32 devices in a mesh: lon: 4 (over z), lat: 4 (over x, core), band: 2 (over y).
Axes of the slice: x: 2, y: 2, z: 4, core: 2. Of those that a mesh axis runs over, the one named last changes fastest.
Arguments:
- spectrum: float32 [64, 64, 576], P('lat', 'lon', 'band'), may hold values from 0.02 to 13, as said below
- sea_mask: int32 [64, 64], P('lat', 'lon'), may hold values 0 or 1
- ice_mask: int32 [64, 64], P('lat', 'lon'), may hold values 0 or 1
- depth_class: int32 [64, 64], P('lat', 'lon'), may hold values from 0 to 7
- speed_table: float32 [8, 16], replicated, may hold values from 0.2 to 0.8
- refraction_table: float32 [8, 16], replicated, may hold values from 0.05 to 0.5
- depth_slope: float32 [2, 64, 64], P(None, 'lat', 'lon'), may hold values from -1 to 1
- wind_speed: float32 [64, 64], P('lat', 'lon'), may hold values from 0.3 to 3
- wind_dir: float32 [64, 64], P('lat', 'lon'), may hold values from -3.140625 to 3.140625
- ice_rate: float32 [16], replicated, may hold values from 0.1 to 1
Outputs:
- spectrum_out: float32 [64, 64, 576], P('lat', 'lon', 'band')
The draws below stay inside these ranges and needn't reach their ends.
Inputs may be any that keep to these rules, and one draw needn't show every extreme that they name: `spectrum`: densities are positive.
All inputs are finite; a program needn't handle non-finite values. No bound on the sum of `sea_mask` or of `ice_mask` on one device may be relied on, other than what follows from the above.
Results may differ from the reference program's by a relative error of at most 0.0003.
Values sent between devices are 32-bit elements; how exact they have to be, the bound alone decides.
No kernel may reach another device: no remote copies, remote signals or barrier semaphores. Data moves between devices by JAX's collectives and lax.ppermute only.
A program may use at most 64 MiB of HBM per device.

```python
import math
import jax
import jax.numpy as jnp
from jax import lax

NFREQ = 16
NDIR = 36
NCLASS = 8
ITERS = 4
NCOMP = 576
NLAT = 64
NLON = 64


def draw_spectrum(key, part):
    base_key, comp_key, point_key = jax.random.split(key, 3)
    noise_draw = jax.random.uniform(base_key, (NLAT, NLON, NCOMP), jnp.float32)
    comp_draw = jax.random.uniform(comp_key, (1, 1, NCOMP), jnp.float32)
    point_draw = jax.random.uniform(point_key, (NLAT, NLON, 1), jnp.float32)
    base_value = jnp.exp(math.log(0.3) + noise_draw * math.log(10.0))
    comp_scale = jnp.exp((comp_draw - 0.5) * math.log(4.0))
    point_scale = jnp.exp((point_draw - 0.5) * math.log(3.0))
    return base_value * comp_scale * point_scale


def with_ends(values, own_key, low, high):
    index_at = [jax.random.randint(jax.random.fold_in(own_key, axis), (), 0, length) for axis, length in enumerate(values.shape)]
    main_axis = values.shape.index(max(values.shape))
    next_to = index_at[:main_axis] + [(index_at[main_axis] + 1) % values.shape[main_axis]] + index_at[main_axis + 1:]
    return values.at[tuple(index_at)].set(low).at[tuple(next_to)].set(high)


def steps_of(key, shape, pieces, least, largest):
    def one(dim, blocks):
        steps = jax.random.uniform(jax.random.fold_in(jax.random.fold_in(key, 6), dim), (blocks,), jnp.float32, least / len(pieces), largest / len(pieces))
        return jnp.repeat(jnp.exp(steps), shape[dim] // blocks).reshape((-1,) + (1,) * (len(shape) - dim - 1))

    gain = one(*pieces[0])
    for cut in pieces[1:]:
        gain = gain * one(*cut)
    return gain


def setup_inputs(seed: int = 0) -> dict:
    splits = jax.random.split(jax.random.key(seed), 11)
    spectrum = draw_spectrum(jax.random.fold_in(splits[10], 71), 0)
    sea_mask = with_ends((jax.random.randint(splits[1], (NLAT, NLON), 0, 10) < 9).astype(jnp.int32), jax.random.fold_in(splits[1], 1), 0, 1)
    ice_mask = with_ends((jax.random.randint(splits[2], (NLAT, NLON), 0, 5) < 1).astype(jnp.int32), jax.random.fold_in(splits[2], 1), 0, 1)
    depth_class = with_ends(jax.random.randint(splits[3], (NLAT, NLON), 0, NCLASS), jax.random.fold_in(splits[3], 1), 0, NCLASS - 1).astype(jnp.int32)
    speed_table = jnp.clip(jax.random.uniform(splits[4], (NCLASS, NFREQ), jnp.float32, 0.2, 0.8), 0.2, 0.8)
    refraction_table = jnp.clip(jax.random.uniform(splits[5], (NCLASS, NFREQ), jnp.float32, 0.05, 0.5), 0.05, 0.5)
    depth_slope = jnp.clip(jax.random.uniform(splits[6], (2, NLAT, NLON), jnp.float32, -1.0, 1.0) * steps_of(splits[6], (2, NLAT, NLON), ((1, 4), (2, 4)), -0.4, 0.0), -1.0, 1.0)
    wind_speed = jnp.clip(jnp.exp(math.log(3.0) - 2.3025851 * jax.random.uniform(splits[7], (NLAT, NLON), jnp.float32) ** steps_of(splits[7], (NLAT, NLON), ((0, 4), (1, 4)), -0.2, 0.2)), 0.3, 3.0)
    wind_dir = jnp.clip(jax.random.uniform(splits[8], (NLAT, NLON), jnp.float32, -3.140625, 3.140625), -3.140625, 3.140625)
    ice_rate = jnp.clip(jnp.exp(jax.random.uniform(splits[9], (NFREQ,), jnp.float32, math.log(0.1), math.log(1.0))), 0.1, 1.0)
    return dict(spectrum=spectrum, sea_mask=sea_mask, ice_mask=ice_mask, depth_class=depth_class, speed_table=speed_table, refraction_table=refraction_table, depth_slope=depth_slope, wind_speed=wind_speed, wind_dir=wind_dir, ice_rate=ice_rate)


freq_ratio = 1.1
wind_gain = 0.12
break_coef = 0.05
south_edge = -30.0
band_span = 60.0


def quickest(behind, center, forward, beyond, courant):
    curvature = jnp.where(courant >= 0.0, forward - 2.0 * center + behind, beyond - 2.0 * forward + center)
    face_value = 0.5 * (center + forward) - 0.5 * courant * (forward - center) - (1.0 - courant * courant) / 6.0 * curvature
    return courant * face_value


def advect(density, cell_speed, axis_dim):
    length = density.shape[axis_dim]

    def piece(array, low, high):
        return lax.slice_in_dim(array, low, high, axis=axis_dim)

    courant = 0.5 * (piece(cell_speed, 1, length - 2) + piece(cell_speed, 2, length - 1))
    fluxes = quickest(piece(density, 0, length - 3), piece(density, 1, length - 2), piece(density, 2, length - 1), piece(density, 3, length), courant)
    faces = fluxes.shape[axis_dim]
    return piece(density, 2, length - 2) - (piece(fluxes, 1, faces) - piece(fluxes, 0, faces - 1))


def rotate(density, offset):
    dir_index = jnp.arange(density.shape[-1]) % NDIR
    target = dir_index + offset
    inner_roll = jnp.roll(density, -offset, axis=-1)
    if offset > 0:
        outer_roll = jnp.roll(density, NDIR - offset, axis=-1)
        return jnp.where(target >= NDIR, outer_roll, inner_roll)
    outer_roll = jnp.roll(density, -(offset + NDIR), axis=-1)
    return jnp.where(target < 0, outer_roll, inner_roll)


def refract(density, courant):
    fluxes = quickest(rotate(density, -1), density, rotate(density, 1), rotate(density, 2), courant)
    return density - (fluxes - rotate(fluxes, -1))


def expand(per_freq, spread):
    return jnp.dot(per_freq, spread, precision=lax.Precision.HIGHEST)


def lookup(classes, lookup_table):
    onehot = (classes[..., None] == jnp.arange(lookup_table.shape[0])).astype(jnp.float32)
    return jnp.dot(onehot, lookup_table, precision=lax.Precision.HIGHEST)


def stretch(rows, total_rows):
    latitude = (south_edge + band_span * (rows.astype(jnp.float32) + 0.5) / total_rows) * (math.pi / 180.0)
    return 1.0 / jnp.cos(latitude)


def sources(density, energy_sum, moment, levels, heading, ice_loss, sea_share, ice_share, wind_speed, wind_dir):
    mean_level = jnp.maximum(moment, 1.0) / jnp.maximum(energy_sum, 1.0)
    energy = energy_sum / NCOMP
    breaking = break_coef * levels * levels / mean_level[..., None] * (energy * energy)[..., None]
    growth = wind_gain * wind_speed[..., None] * levels * jnp.maximum(jnp.cos(heading - wind_dir[..., None]), 0.0)
    damping = ice_share[..., None] * ice_loss
    return sea_share[..., None] * density * jnp.exp(growth - breaking - damping)


def wrap_cols(array):
    return jnp.concatenate([array[:, -2:], array, array[:, :2]], axis=1)


def pad_rows(array):
    return jnp.pad(array, ((2, 2), (0, 0), (0, 0)))


def reference(spectrum, sea_mask, ice_mask, depth_class, speed_table, refraction_table, depth_slope, wind_speed, wind_dir, ice_rate):
    sea_share = sea_mask.astype(jnp.float32)
    ice_share = ice_mask.astype(jnp.float32)
    comp_index = jnp.arange(NCOMP)
    spread = (comp_index[None, :] // NDIR == jnp.arange(NFREQ)[:, None]).astype(jnp.float32)
    heading = 2.0 * math.pi * (comp_index % NDIR).astype(jnp.float32) / NDIR
    levels = jnp.exp(math.log(freq_ratio) * (comp_index // NDIR).astype(jnp.float32))
    ice_loss = jnp.repeat(ice_rate, NDIR)
    group_speed = lookup(depth_class, speed_table) * sea_share[..., None]
    turning = lookup(depth_class, refraction_table) * sea_share[..., None]
    stretch_rows = stretch(jnp.arange(NLAT), NLAT)
    cell_speed = expand(group_speed, spread)
    along_x = cell_speed * jnp.cos(heading) * stretch_rows[:, None, None]
    along_y = cell_speed * jnp.sin(heading)
    face_angle = heading + math.pi / NDIR
    along_t = expand(turning * depth_slope[0][..., None], spread) * jnp.sin(face_angle) - expand(turning * depth_slope[1][..., None], spread) * jnp.cos(face_angle)
    density = spectrum * sea_share[..., None]
    for substep in range(ITERS):
        density = advect(wrap_cols(density), wrap_cols(along_x), 1)
        density = advect(pad_rows(density), pad_rows(along_y), 0)
        density = refract(density, along_t)
    energy_sum = jnp.sum(density, axis=-1)
    moment = jnp.sum(density * levels, axis=-1)
    return sources(density, energy_sum, moment, levels, heading, ice_loss, sea_share, ice_share, wind_speed, wind_dir)
```

```python
import math

import jax
import jax.numpy as jnp
import numpy as np
from jax import lax
from jax.experimental import pallas as pl
from jax.experimental.pallas import tpu as pltpu
from jax.sharding import PartitionSpec as P

NDIR = 36
NCOMP = 576
ITERS = 4
NCLASS = 8
FREQ = 8
HALO = 8
STATIC = NDIR
SLABS = NDIR + 1
SEA, DEPTH, SLOPE_X, SLOPE_Y, ICE, WIND, WDIR = range(7)

freq_ratio = 1.1
wind_gain = 0.12
break_coef = 0.05
south_edge = -30.0
band_span = 60.0

COS = [math.cos(2.0 * math.pi * d / NDIR) for d in range(NDIR)]
SIN = [math.sin(2.0 * math.pi * d / NDIR) for d in range(NDIR)]
COS_FACE = [math.cos(2.0 * math.pi * (d + 0.5) / NDIR) for d in range(NDIR)]
SIN_FACE = [math.sin(2.0 * math.pi * (d + 0.5) / NDIR) for d in range(NDIR)]

TAB_SPEED, TAB_TURN, STRETCH, LIVE, ICE_RATE, LEVEL = 0, 8, 16, 17, 18, 19

f32 = jnp.float32


def lanes():
    return lax.broadcasted_iota(jnp.int32, (8, 128), 1)


def roll(x, shift):
    shift = shift % 128
    return pltpu.roll(x, shift, 1) if shift else x


def pack_kernel(spec, sea, ice, depth, slope, wspeed, wdir, own, to_east, to_west, flat0, flat1, wide):
    grid = spec[...].reshape(256, NDIR * FREQ)
    for low, high in ((0, 128), (128, 256), (256, 288)):
        turned = grid[:, low:high].T
        flat0[low:high, :] = turned[:, :128]
        flat1[low:high, :] = turned[:, 128:]
    wide[...] = jnp.zeros_like(wide)
    group = lax.broadcasted_iota(jnp.int32, (16, 128), 1) // 16
    row = lax.broadcasted_iota(jnp.int32, (16, 128), 0) % 8
    own[STATIC] = jnp.zeros((2, 8, 128), f32)

    def place(field, values):
        wide[:, :16] = values
        moved = pltpu.roll(wide[...], 0, 1, stride=16, stride_axis=0)
        kept = jnp.where(group == row, moved, 0.0)
        for half in range(2):
            own[STATIC, half, field : field + 1, :] = jnp.sum(
                kept[8 * half : 8 * half + 8], axis=0, keepdims=True
            )

    place(SEA, sea[...].astype(f32))
    place(DEPTH, depth[...].astype(f32))
    place(SLOPE_X, slope[0])
    place(SLOPE_Y, slope[1])
    place(ICE, ice[...].astype(f32))
    place(WIND, wspeed[...])
    place(WDIR, wdir[...])
    inner = lanes() % 16
    sea0 = own[STATIC, 0, SEA : SEA + 1, :]
    sea1 = own[STATIC, 1, SEA : SEA + 1, :]
    for slab in range(SLABS):
        if slab < NDIR:
            own0 = flat0[pl.ds(slab, FREQ, stride=NDIR), :] * sea0
            own1 = flat1[pl.ds(slab, FREQ, stride=NDIR), :] * sea1
            own[slab, 0] = own0
            own[slab, 1] = own1
        else:
            own0 = own[slab, 0]
            own1 = own[slab, 1]
        to_east[slab] = jnp.where(inner >= 8, own0, roll(own1, -8))
        to_west[slab] = jnp.where(inner < 8, own0, roll(own1, 8))


def growth_kernel(own, consts, gain):
    for half in range(2):
        point = own[STATIC, half]
        turn = point[WDIR : WDIR + 1]
        cos_w = jnp.cos(turn)
        sin_w = jnp.sin(turn)
        force = wind_gain * point[WIND : WIND + 1] * consts[LEVEL]
        share = point[SEA : SEA + 1]
        for d in range(NDIR):
            along = jnp.maximum(COS[d] * cos_w + SIN[d] * sin_w, 0.0)
            gain[d, half] = jnp.exp(force * along) * share


def join_kernel(own, from_west, from_east, rows):
    inner = lanes() % 16
    even = (lanes() // 16) % 2 == 0

    def body(slab, carry):
        west = from_west[slab]
        east = from_east[slab]
        rim0 = jnp.where(inner < 8, roll(east, 16), roll(west, -16))
        rim1 = jnp.where(inner < 8, roll(east, 8), roll(west, -8))
        own0 = own[slab, 0]
        own1 = own[slab, 1]
        rows[0, slab, 0] = jnp.where(even, own0, rim0)
        rows[0, slab, 1] = jnp.where(even, rim0, own0)
        rows[1, slab, 0] = jnp.where(even, own1, rim1)
        rows[1, slab, 1] = jnp.where(even, rim1, own1)
        return carry

    lax.fori_loop(0, SLABS, body, 0, unroll=True)


def flux(q, diff, curve, k):
    return k * (q + (0.5 - 0.5 * k) * (diff - (1.0 / 3.0 + (1.0 / 3.0) * k) * curve))


def sweep_lon(tiles, kx, cos_d, positive):
    out = []
    for q, face in zip(tiles, kx):
        k = cos_d * face
        diff = roll(q, -1) - q
        if positive:
            curve = diff - roll(diff, 1)
        else:
            curve = roll(diff, -1) - diff
        f = flux(q, diff, curve, k)
        out.append(q - f + roll(f, 1))
    return out


def sweep_lat(tiles, ky, sin_d, positive, live):
    ahead = tiles[1:] + [roll(tiles[0], -32)]
    diff = [n - m for n, m in zip(ahead, tiles)]
    if positive:
        before = [roll(diff[7], 32)] + diff[:7]
        curve = [a - b for a, b in zip(diff, before)]
    else:
        after = diff[1:] + [roll(diff[0], -32)]
        curve = [a - b for a, b in zip(after, diff)]
    fluxes = [flux(q, a, b, sin_d * face) for q, a, b, face in zip(tiles, diff, curve, ky)]
    behind = [roll(fluxes[7], 32)] + fluxes[:7]
    return [(q - f + b) * live for q, f, b in zip(tiles, fluxes, behind)]


def sweep_dir(cells, tx, ty):
    courant = [SIN_FACE[d] * tx - COS_FACE[d] * ty for d in range(NDIR)]
    first = cells[0]
    diff = [None] * NDIR
    for d in range(NDIR):
        diff[d] = cells[(d + 1) % NDIR] - cells[d]
    curve = [diff[d] - diff[d - 1] for d in range(NDIR)]
    fluxes = []
    for d in range(NDIR):
        k = courant[d]
        bend = jnp.where(k >= 0.0, curve[d], curve[(d + 1) % NDIR])
        fluxes.append(flux(cells[d], diff[d], bend, k))
    return [cells[d] - fluxes[d] + fluxes[d - 1] for d in range(NDIR)]


def march_kernel(rows, from_south, from_north, consts, own, sums, q, kx, ky, tx, ty, trig):
    lane = lanes()

    def assemble(slab, carry):
        for p in range(2):
            parts = [
                from_south[slab, p],
                roll(rows[0, slab, p], 32),
                roll(rows[1, slab, p], 64),
                roll(from_north[slab, p], 96),
            ]
            for t in range(p, 8, 2):
                which = ((lane - (16 * t - 8)) % 128) // 32
                mixed = jnp.where(
                    which < 2,
                    jnp.where(which == 0, parts[0], parts[1]),
                    jnp.where(which == 2, parts[2], parts[3]),
                )
                q[slab, t] = roll(mixed, 8 - 16 * t)
        return carry

    lax.fori_loop(0, SLABS, assemble, 0, unroll=2)

    for d in range(NDIR):
        trig[0, d] = jnp.float32(COS[d])
        trig[1, d] = jnp.float32(SIN[d])

    speed = []
    for t in range(8):
        point = q[STATIC, t]
        depth = jnp.broadcast_to(point[DEPTH : DEPTH + 1], (8, 128))
        share = point[SEA : SEA + 1]
        pace = jnp.zeros((8, 128), f32)
        turning = jnp.zeros((8, 128), f32)
        for c in range(NCLASS):
            hit = depth == float(c)
            pace = jnp.where(hit, consts[TAB_SPEED + c], pace)
            turning = jnp.where(hit, consts[TAB_TURN + c], turning)
        pace = pace * share
        turning = turning * share
        speed.append(pace)
        kx[t] = 0.5 * (pace + roll(pace, -1)) * consts[STRETCH, t : t + 1, :]
        tx[t] = turning * point[SLOPE_X : SLOPE_X + 1]
        ty[t] = turning * point[SLOPE_Y : SLOPE_Y + 1]
    for t in range(8):
        ahead = speed[t + 1] if t < 7 else roll(speed[0], -32)
        ky[t] = 0.5 * (speed[t] + ahead)

    live = consts[LIVE]

    def substep(step, carry):
        for quadrant in range(4):
            east = quadrant in (0, 3)
            north = quadrant in (0, 1)

            def one(i, c, quadrant=quadrant, east=east, north=north):
                d = quadrant * 9 + i
                tiles = [q[d, t] for t in range(8)]
                tiles = sweep_lon(tiles, [kx[t] for t in range(8)], trig[0, d], east)
                tiles = sweep_lat(tiles, [ky[t] for t in range(8)], trig[1, d], north, live)
                for t in range(8):
                    q[d, t] = tiles[t]
                return c

            lax.fori_loop(0, 9, one, 0, unroll=3)

        def turn(t, c):
            cells = sweep_dir([q[d, t] for d in range(NDIR)], tx[t], ty[t])
            for d in range(NDIR):
                q[d, t] = cells[d]
            return c

        lax.fori_loop(0, 8, turn, 0)
        return carry

    lax.fori_loop(0, ITERS, substep, 0)

    def take(d, carry):
        sum0, sum1 = carry
        half0 = jnp.zeros((8, 128), f32)
        half1 = jnp.zeros((8, 128), f32)
        for t in range(8):
            moved = roll(q[d, t], 16 * t - 40)
            half0 = jnp.where(lane // 16 == t, moved, half0)
            half1 = jnp.where(lane // 16 == (t + 2) % 8, moved, half1)
        half1 = roll(half1, -32)
        own[d, 0] = half0
        own[d, 1] = half1
        return sum0 + half0, sum1 + half1

    zero = jnp.zeros((8, 128), f32)
    totals = lax.fori_loop(0, NDIR, take, (zero, zero), unroll=3)
    level = consts[LEVEL]
    sums[...] = zero
    for half in range(2):
        sums[half : half + 1, :] = jnp.sum(totals[half], axis=0, keepdims=True)
        sums[2 + half : 3 + half, :] = jnp.sum(totals[half] * level, axis=0, keepdims=True)


def finish_kernel(own, gain, static, sums, other, consts, out, flat0, flat1):
    total = sums[...] + other[...]
    for half, flat in ((0, flat0), (1, flat1)):
        energy = total[half : half + 1]
        moment = total[2 + half : 3 + half]
        mean_level = jnp.maximum(moment, 1.0) / jnp.maximum(energy, 1.0)
        mean = energy / NCOMP
        level = consts[LEVEL]
        breaking = break_coef * level * level / mean_level * (mean * mean)
        damping = static[0, half, ICE : ICE + 1] * consts[ICE_RATE]
        loss = jnp.exp(-breaking - damping)
        for d in range(NDIR):
            flat[pl.ds(d, FREQ, stride=NDIR), :] = own[d, half] * gain[d, half] * loss
        for low, high in ((0, 128), (128, 256), (256, 288)):
            turned = flat[low:high, :].T
            out[8 * half : 8 * half + 8, :, low:high] = turned.reshape(8, 16, high - low)


def vmem(count):
    return [pl.BlockSpec(memory_space=pltpu.VMEM)] * count


PARAMS = pltpu.CompilerParams(vmem_limit_bytes=32 * 2**20)


def call(kernel, ins, outs, scratch=(), name=None):
    return pl.pallas_call(
        kernel,
        out_shape=[jax.ShapeDtypeStruct(shape, f32) for shape in outs],
        in_specs=vmem(ins),
        out_specs=vmem(len(outs)),
        scratch_shapes=list(scratch),
        compiler_params=PARAMS,
        name=name,
    )


def shift(array, axis, step, closed):
    count = lax.axis_size(axis)
    pairs = []
    for i in range(count):
        j = i + step
        if closed or 0 <= j < count:
            pairs.append((i, j % count))
    return lax.ppermute(array, axis, pairs)


def per_device(
    spectrum,
    sea_mask,
    ice_mask,
    depth_class,
    speed_table,
    refraction_table,
    depth_slope,
    wind_speed,
    wind_dir,
    ice_rate,
):
    band = lax.axis_index("band")
    lat = lax.axis_index("lat")
    lats = lax.axis_size("lat")
    rows_dev = spectrum.shape[0]

    def spread(table):
        mine = lax.dynamic_slice_in_dim(table, band * FREQ, FREQ, 1)
        return jnp.broadcast_to(mine[:, :, None], (NCLASS, FREQ, 128))

    group = jnp.arange(128) // 32
    row = lat * rows_dev - HALO + 8 * group[None, :] + jnp.arange(8)[:, None]
    latitude = (south_edge + band_span * (row.astype(f32) + 0.5) / (rows_dev * lats)) * (math.pi / 180.0)
    stretch = 1.0 / jnp.cos(latitude)
    live = 1.0 - (((group == 0) & (lat == 0)) | ((group == 3) & (lat == lats - 1))).astype(f32)
    ice = lax.dynamic_slice_in_dim(ice_rate, band * FREQ, FREQ, 0)
    level = jnp.exp(math.log(freq_ratio) * (band * FREQ + jnp.arange(FREQ)).astype(f32))
    consts = jnp.concatenate(
        [
            spread(speed_table),
            spread(refraction_table),
            stretch[None],
            jnp.broadcast_to(live[None, None, :], (1, 8, 128)),
            jnp.broadcast_to(ice[None, :, None], (1, 8, 128)),
            jnp.broadcast_to(level[None, :, None], (1, 8, 128)),
        ]
    )

    tile = (8, 128)
    own, to_east, to_west = call(
        pack_kernel,
        7,
        [(SLABS, 2) + tile, (SLABS,) + tile, (SLABS,) + tile],
        [pltpu.VMEM((NDIR * FREQ, 128), f32)] * 2 + [pltpu.VMEM((16, 128), f32)],
        name="pack",
    )(spectrum, sea_mask, ice_mask, depth_class, depth_slope, wind_speed, wind_dir)
    from_west = shift(to_east, "lon", 1, True)
    from_east = shift(to_west, "lon", -1, True)
    (gain,) = call(growth_kernel, 2, [(NDIR, 2) + tile], name="growth")(own, consts)
    (rows,) = call(join_kernel, 3, [(2, SLABS, 2) + tile], name="join")(own, from_west, from_east)
    from_south = shift(rows[1], "lat", 1, False)
    from_north = shift(rows[0], "lat", -1, False)
    block = pltpu.VMEM((8,) + tile, f32)
    last, sums = call(
        march_kernel,
        4,
        [(NDIR, 2) + tile, tile],
        [pltpu.VMEM((SLABS, 8) + tile, f32), block, block, block, block, pltpu.SMEM((2, NDIR), f32)],
        name="march",
    )(rows, from_south, from_north, consts)
    other = lax.ppermute(sums, "band", [(i, 1 - i) for i in range(2)])
    (out,) = call(
        finish_kernel,
        6,
        [spectrum.shape],
        [pltpu.VMEM((NDIR * FREQ, 128), f32)] * 2,
        name="finish",
    )(last, gain, own[STATIC:], sums, other, consts)
    return out


def solution(mesh):
    return jax.shard_map(
        per_device,
        mesh=mesh,
        in_specs=(
            P("lat", "lon", "band"),
            P("lat", "lon"),
            P("lat", "lon"),
            P("lat", "lon"),
            P(),
            P(),
            P(None, "lat", "lon"),
            P("lat", "lon"),
            P("lat", "lon"),
            P(),
        ),
        out_specs=P("lat", "lon", "band"),
        check_vma=False,
    )
```

```python
import math

import jax
import jax.numpy as jnp
import numpy as np
from jax import lax
from jax.experimental import pallas as pl
from jax.experimental.pallas import tpu as pltpu
from jax.sharding import PartitionSpec as P

NDIR = 36
NCOMP = 576
ITERS = 4
NCLASS = 8
FREQ = 8
HALO = 8
STATIC = NDIR
SLABS = NDIR + 1
SEA, DEPTH, SLOPE_X, SLOPE_Y, ICE, WIND, WDIR = range(7)

freq_ratio = 1.1
wind_gain = 0.12
break_coef = 0.05
south_edge = -30.0
band_span = 60.0

COS = [math.cos(2.0 * math.pi * d / NDIR) for d in range(NDIR)]
SIN = [math.sin(2.0 * math.pi * d / NDIR) for d in range(NDIR)]
COS_FACE = [math.cos(2.0 * math.pi * (d + 0.5) / NDIR) for d in range(NDIR)]
SIN_FACE = [math.sin(2.0 * math.pi * (d + 0.5) / NDIR) for d in range(NDIR)]

TAB_SPEED, TAB_TURN, STRETCH, LIVE, ICE_RATE, LEVEL = 0, 8, 16, 17, 18, 19

f32 = jnp.float32


def lanes():
    return lax.broadcasted_iota(jnp.int32, (8, 128), 1)


def roll(x, shift):
    shift = shift % 128
    return pltpu.roll(x, shift, 1) if shift else x


def pack_kernel(*refs):
    sources, (own, to_east, to_west), landed = refs[:7], refs[7:10], refs[10:17]
    flat0, flat1, wide, sems = refs[17:]
    copies = [pltpu.make_async_copy(src, dst, sems.at[i]) for i, (src, dst) in enumerate(zip(sources, landed))]
    for copy in copies:
        copy.start()
    wide[...] = jnp.zeros_like(wide)
    group = lax.broadcasted_iota(jnp.int32, (16, 128), 1) // 16
    row = lax.broadcasted_iota(jnp.int32, (16, 128), 0) % 8
    own[STATIC] = jnp.zeros((2, 8, 128), f32)
    for copy in copies:
        copy.wait()
    spec, sea, ice, depth, slope, wspeed, wdir = landed

    def place(field, values):
        wide[:, :16] = values
        moved = pltpu.roll(wide[...], 0, 1, stride=16, stride_axis=0)
        kept = jnp.where(group == row, moved, 0.0)
        for half in range(2):
            own[STATIC, half, field : field + 1, :] = jnp.sum(
                kept[8 * half : 8 * half + 8], axis=0, keepdims=True
            )

    place(SEA, sea[...].astype(f32))
    place(DEPTH, depth[...].astype(f32))
    place(SLOPE_X, slope[0])
    place(SLOPE_Y, slope[1])
    place(ICE, ice[...].astype(f32))
    place(WIND, wspeed[...])
    place(WDIR, wdir[...])
    grid = spec[...].reshape(256, NDIR * FREQ)
    for low, high in ((0, 128), (128, 256), (256, 288)):
        turned = grid[:, low:high].T
        flat0[low:high, :] = turned[:, :128]
        flat1[low:high, :] = turned[:, 128:]
    inner = lanes() % 16
    sea0 = own[STATIC, 0, SEA : SEA + 1, :]
    sea1 = own[STATIC, 1, SEA : SEA + 1, :]
    for slab in range(SLABS):
        if slab < NDIR:
            own0 = flat0[pl.ds(slab, FREQ, stride=NDIR), :] * sea0
            own1 = flat1[pl.ds(slab, FREQ, stride=NDIR), :] * sea1
            own[slab, 0] = own0
            own[slab, 1] = own1
        else:
            own0 = own[slab, 0]
            own1 = own[slab, 1]
        to_east[slab] = jnp.where(inner >= 8, own0, roll(own1, -8))
        to_west[slab] = jnp.where(inner < 8, own0, roll(own1, 8))


def growth_kernel(own, consts, gain):
    for half in range(2):
        point = own[STATIC, half]
        turn = point[WDIR : WDIR + 1]
        cos_w = jnp.cos(turn)
        sin_w = jnp.sin(turn)
        force = wind_gain * point[WIND : WIND + 1] * consts[LEVEL]
        share = point[SEA : SEA + 1]
        for d in range(NDIR):
            along = jnp.maximum(COS[d] * cos_w + SIN[d] * sin_w, 0.0)
            gain[d, half] = jnp.exp(force * along) * share


def join_kernel(own, from_west, from_east, south_rows, north_rows):
    inner = lanes() % 16
    even = (lanes() // 16) % 2 == 0
    for slab in range(SLABS):
        west = from_west[slab]
        east = from_east[slab]
        rim0 = jnp.where(inner < 8, roll(east, 16), roll(west, -16))
        rim1 = jnp.where(inner < 8, roll(east, 8), roll(west, -8))
        own0 = own[slab, 0]
        own1 = own[slab, 1]
        south_rows[slab, 0] = jnp.where(even, own0, rim0)
        south_rows[slab, 1] = jnp.where(even, rim0, own0)
        north_rows[slab, 0] = jnp.where(even, own1, rim1)
        north_rows[slab, 1] = jnp.where(even, rim1, own1)


def place_kernel(south_rows, north_rows, from_south, from_north, consts, q, kx, ky, tx, ty):
    lane = lanes()

    def assemble(slab, carry):
        for p in range(2):
            parts = [
                from_south[slab, p],
                roll(south_rows[slab, p], 32),
                roll(north_rows[slab, p], 64),
                roll(from_north[slab, p], 96),
            ]
            for t in range(p, 8, 2):
                which = ((lane - (16 * t - 8)) % 128) // 32
                mixed = jnp.where(
                    which < 2,
                    jnp.where(which == 0, parts[0], parts[1]),
                    jnp.where(which == 2, parts[2], parts[3]),
                )
                q[slab, t] = roll(mixed, 8 - 16 * t)
        return carry

    assemble(STATIC, 0)
    speed = []
    for t in range(8):
        point = q[STATIC, t]
        depth = jnp.broadcast_to(point[DEPTH : DEPTH + 1], (8, 128))
        share = point[SEA : SEA + 1]
        pace = jnp.zeros((8, 128), f32)
        turning = jnp.zeros((8, 128), f32)
        for c in range(NCLASS):
            hit = depth == float(c)
            pace = jnp.where(hit, consts[TAB_SPEED + c], pace)
            turning = jnp.where(hit, consts[TAB_TURN + c], turning)
        pace = pace * share
        turning = turning * share
        speed.append(pace)
        kx[t] = 0.5 * (pace + roll(pace, -1)) * consts[STRETCH, t : t + 1, :]
        tx[t] = turning * point[SLOPE_X : SLOPE_X + 1]
        ty[t] = turning * point[SLOPE_Y : SLOPE_Y + 1]
    for t in range(8):
        ahead = speed[t + 1] if t < 7 else roll(speed[0], -32)
        ky[t] = 0.5 * (speed[t] + ahead)

    lax.fori_loop(0, NDIR, assemble, 0, unroll=3)


def flux(q, diff, curve, k, u, w):
    return k * (q + u * (diff - w * curve))


def halves(k):
    return 0.5 - 0.5 * k, (1.0 / 3.0) + (1.0 / 3.0) * k


def lon_kernel(q, kx, out):
    def one(t, c):
        face = kx[t]
        for base in range(10):
            if base == 0:
                forth, back = [0], [18]
            elif base == 9:
                forth, back = [27], [9]
            else:
                forth, back = [base, 36 - base], [18 - base, 18 + base]
            k = COS[base] * face
            u, w = halves(k)
            for d in forth:
                cell = q[d, t]
                diff = roll(cell, -1) - cell
                f = flux(cell, diff, diff - roll(diff, 1), k, u, w)
                out[d, t] = cell - f + roll(f, 1)
            for d in back:
                cell = q[d, t]
                ahead = roll(cell, -1)
                diff = cell - ahead
                f = flux(ahead, diff, diff - roll(diff, -1), k, u, w)
                out[d, t] = cell + f - roll(f, 1)
        return c

    lax.fori_loop(0, 8, one, 0)


def lat_kernel(q, ky, consts, out):
    live = consts[LIVE]

    def forth(d, ks, us, ws):
        tiles = [q[d, t] for t in range(8)]
        diff = [tiles[t + 1] - tiles[t] for t in range(7)]
        diff.append(roll(tiles[0], -32) - tiles[7])
        before = roll(diff[7], 32)
        fluxes = []
        for t in range(8):
            fluxes.append(flux(tiles[t], diff[t], diff[t] - before, ks[t], us[t], ws[t]))
            before = diff[t]
        behind = roll(fluxes[7], 32)
        for t in range(8):
            out[d, t] = (tiles[t] - fluxes[t] + behind) * live
            behind = fluxes[t]

    def back(d, ks, us, ws):
        tiles = [q[d, t] for t in range(8)]
        ahead = tiles[1:] + [roll(tiles[0], -32)]
        diff = [tiles[t] - ahead[t] for t in range(8)]
        after = diff[1:] + [roll(diff[0], -32)]
        fluxes = [flux(ahead[t], diff[t], diff[t] - after[t], ks[t], us[t], ws[t]) for t in range(8)]
        behind = roll(fluxes[7], 32)
        for t in range(8):
            out[d, t] = (tiles[t] + fluxes[t] - behind) * live
            behind = fluxes[t]

    for base in range(10):
        ks = [SIN[base] * ky[t] for t in range(8)]
        us, ws = zip(*[halves(k) for k in ks])
        if base == 0:
            north, south = [0], [18]
        elif base == 9:
            north, south = [9], [27]
        else:
            north, south = [base, 18 - base], [18 + base, 36 - base]
        for d in north:
            forth(d, ks, us, ws)
        for d in south:
            back(d, ks, us, ws)


def turn_kernel(q, tx, ty, out):
    def one(t, c):
        x = tx[t]
        y = ty[t]

        def courant(d):
            return SIN_FACE[d] * x - COS_FACE[d] * y

        def face(d, cell, diff, curve, curve_ahead):
            k = courant(d)
            u, w = halves(k)
            return flux(cell, diff, jnp.where(k >= 0.0, curve, curve_ahead), k, u, w)

        cell, ahead = q[0, t], q[1, t]
        before, last = q[NDIR - 1, t], q[NDIR - 2, t]
        diff0 = before - last
        diff1 = cell - before
        diff2 = ahead - cell
        curve1 = diff1 - diff0
        curve2 = diff2 - diff1
        f_before = face(NDIR - 1, before, diff1, curve1, curve2)
        diff, curve = diff2, curve2
        for d in range(NDIR):
            beyond = q[(d + 2) % NDIR, t]
            diff_ahead = beyond - ahead
            curve_ahead = diff_ahead - diff
            f = face(d, cell, diff, curve, curve_ahead)
            out[d, t] = cell - f + f_before
            cell, ahead, diff, curve, f_before = ahead, beyond, diff_ahead, curve_ahead, f
        return c

    lax.fori_loop(0, 8, one, 0)


def gather_kernel(q, consts, own, sums):
    lane = lanes()
    zero = jnp.zeros((8, 128), f32)

    def take(d, carry):
        sum0, sum1 = carry
        half0 = zero
        half1 = zero
        for t in range(8):
            moved = roll(q[d, t], 16 * t - 40)
            half0 = jnp.where(lane // 16 == t, moved, half0)
            half1 = jnp.where(lane // 16 == (t + 2) % 8, moved, half1)
        half1 = roll(half1, -32)
        own[d, 0] = half0
        own[d, 1] = half1
        return sum0 + half0, sum1 + half1

    totals = lax.fori_loop(0, NDIR, take, (zero, zero), unroll=3)
    level = consts[LEVEL]
    sums[...] = zero
    for half in range(2):
        sums[half : half + 1, :] = jnp.sum(totals[half], axis=0, keepdims=True)
        sums[2 + half : 3 + half, :] = jnp.sum(totals[half] * level, axis=0, keepdims=True)


def finish_kernel(own, gain, static, sums, other, consts, out, flat0, flat1):
    total = sums[...] + other[...]
    for half, flat in ((0, flat0), (1, flat1)):
        energy = total[half : half + 1]
        moment = total[2 + half : 3 + half]
        mean_level = jnp.maximum(moment, 1.0) / jnp.maximum(energy, 1.0)
        mean = energy / NCOMP
        level = consts[LEVEL]
        breaking = break_coef * level * level / mean_level * (mean * mean)
        damping = static[0, half, ICE : ICE + 1] * consts[ICE_RATE]
        loss = jnp.exp(-breaking - damping)
        for d in range(NDIR):
            flat[pl.ds(d, FREQ, stride=NDIR), :] = own[d, half] * gain[d, half] * loss
        for low, high in ((0, 128), (128, 256), (256, 288)):
            turned = flat[low:high, :].T
            out[8 * half : 8 * half + 8, :, low:high] = turned.reshape(8, 16, high - low)


PARAMS = pltpu.CompilerParams(vmem_limit_bytes=32 * 2**20)


def call(kernel, ins, outs, scratch=(), name=None, space=pltpu.VMEM):
    return pl.pallas_call(
        kernel,
        out_shape=[jax.ShapeDtypeStruct(shape, f32) for shape in outs],
        in_specs=[pl.BlockSpec(memory_space=space)] * ins,
        out_specs=[pl.BlockSpec(memory_space=pltpu.VMEM)] * len(outs),
        scratch_shapes=list(scratch),
        compiler_params=PARAMS,
        name=name,
    )


def shift(array, axis, step, closed):
    count = lax.axis_size(axis)
    pairs = []
    for i in range(count):
        j = i + step
        if closed or 0 <= j < count:
            pairs.append((i, j % count))
    return lax.ppermute(array, axis, pairs)


def per_device(
    spectrum,
    sea_mask,
    ice_mask,
    depth_class,
    speed_table,
    refraction_table,
    depth_slope,
    wind_speed,
    wind_dir,
    ice_rate,
):
    band = lax.axis_index("band")
    lat = lax.axis_index("lat")
    lats = lax.axis_size("lat")
    rows_dev = spectrum.shape[0]

    def spread(table):
        mine = lax.dynamic_slice_in_dim(table, band * FREQ, FREQ, 1)
        return jnp.broadcast_to(mine[:, :, None], (NCLASS, FREQ, 128))

    group = jnp.arange(128) // 32
    row = lat * rows_dev - HALO + 8 * group[None, :] + jnp.arange(8)[:, None]
    latitude = (south_edge + band_span * (row.astype(f32) + 0.5) / (rows_dev * lats)) * (math.pi / 180.0)
    stretch = 1.0 / jnp.cos(latitude)
    live = 1.0 - (((group == 0) & (lat == 0)) | ((group == 3) & (lat == lats - 1))).astype(f32)
    ice = lax.dynamic_slice_in_dim(ice_rate, band * FREQ, FREQ, 0)
    level = jnp.exp(math.log(freq_ratio) * (band * FREQ + jnp.arange(FREQ)).astype(f32))
    consts = jnp.concatenate(
        [
            spread(speed_table),
            spread(refraction_table),
            stretch[None],
            jnp.broadcast_to(live[None, None, :], (1, 8, 128)),
            jnp.broadcast_to(ice[None, :, None], (1, 8, 128)),
            jnp.broadcast_to(level[None, :, None], (1, 8, 128)),
        ]
    )

    tile = (8, 128)
    inputs = [spectrum, sea_mask, ice_mask, depth_class, depth_slope, wind_speed, wind_dir]
    own, to_east, to_west = call(
        pack_kernel,
        7,
        [(SLABS, 2) + tile, (SLABS,) + tile, (SLABS,) + tile],
        [pltpu.VMEM(x.shape, x.dtype) for x in inputs]
        + [pltpu.VMEM((NDIR * FREQ, 128), f32)] * 2
        + [pltpu.VMEM((16, 128), f32), pltpu.SemaphoreType.DMA((7,))],
        name="pack",
        space=pltpu.HBM,
    )(*[pltpu.with_memory_space_constraint(x, pltpu.HBM) for x in inputs])
    from_west = shift(to_east, "lon", 1, True)
    from_east = shift(to_west, "lon", -1, True)
    (gain,) = call(growth_kernel, 2, [(NDIR, 2) + tile], name="growth")(own, consts)
    south_rows, north_rows = call(join_kernel, 3, [(SLABS, 2) + tile] * 2, name="join")(own, from_west, from_east)
    from_south = shift(north_rows, "lat", 1, False)
    from_north = shift(south_rows, "lat", -1, False)
    block = (8,) + tile
    q, kx, ky, tx, ty = call(place_kernel, 5, [(SLABS,) + block] + [block] * 4, name="place")(
        south_rows, north_rows, from_south, from_north, consts
    )
    cells = [(NDIR,) + block]
    for substep in range(ITERS):
        (q,) = call(lon_kernel, 2, cells, name="lon")(q, kx)
        (q,) = call(lat_kernel, 3, cells, name="lat")(q, ky, consts)
        (q,) = call(turn_kernel, 3, cells, name="turn")(q, tx, ty)
    last, sums = call(gather_kernel, 2, [(NDIR, 2) + tile, tile], name="gather")(q, consts)
    other = lax.ppermute(sums, "band", [(i, 1 - i) for i in range(2)])
    (out,) = call(
        finish_kernel,
        6,
        [spectrum.shape],
        [pltpu.VMEM((NDIR * FREQ, 128), f32)] * 2,
        name="finish",
    )(last, gain, own[STATIC:], sums, other, consts)
    return out


def solution(mesh):
    return jax.shard_map(
        per_device,
        mesh=mesh,
        in_specs=(
            P("lat", "lon", "band"),
            P("lat", "lon"),
            P("lat", "lon"),
            P("lat", "lon"),
            P(),
            P(),
            P(None, "lat", "lon"),
            P("lat", "lon"),
            P("lat", "lon"),
            P(),
        ),
        out_specs=P("lat", "lon", "band"),
        check_vma=False,
    )
```

```python
import math

import jax
import jax.numpy as jnp
import numpy as np
from jax import lax
from jax.experimental import pallas as pl
from jax.experimental.pallas import tpu as pltpu
from jax.sharding import PartitionSpec as P

NDIR = 36
NCOMP = 576
ITERS = 4
NCLASS = 8
FREQ = 8
HALO = 8
STATIC = NDIR
SLABS = NDIR + 1
SEA, DEPTH, SLOPE_X, SLOPE_Y, ICE, WIND, WDIR = range(7)

freq_ratio = 1.1
wind_gain = 0.12
break_coef = 0.05
south_edge = -30.0
band_span = 60.0

COS = [math.cos(2.0 * math.pi * d / NDIR) for d in range(NDIR)]
SIN = [math.sin(2.0 * math.pi * d / NDIR) for d in range(NDIR)]
COS_FACE = [math.cos(2.0 * math.pi * (d + 0.5) / NDIR) for d in range(NDIR)]
SIN_FACE = [math.sin(2.0 * math.pi * (d + 0.5) / NDIR) for d in range(NDIR)]

TAB_SPEED, TAB_TURN, STRETCH, LIVE, ICE_RATE, LEVEL = 0, 8, 16, 17, 18, 19

f32 = jnp.float32


def lanes():
    return lax.broadcasted_iota(jnp.int32, (8, 128), 1)


def roll(x, shift):
    shift = shift % 128
    return pltpu.roll(x, shift, 1) if shift else x


def is_even(axis):
    return lax.axis_index(axis) % 2 == 0


def pack_kernel(*refs):
    sources, (own, to_first, to_second), landed = refs[:7], refs[7:10], refs[10:17]
    flat0, flat1, wide, sems = refs[17:]
    copies = [pltpu.make_async_copy(src, dst, sems.at[i]) for i, (src, dst) in enumerate(zip(sources, landed))]
    for copy in copies:
        copy.start()
    wide[...] = jnp.zeros_like(wide)
    group = lax.broadcasted_iota(jnp.int32, (16, 128), 1) // 16
    row = lax.broadcasted_iota(jnp.int32, (16, 128), 0) % 8
    own[STATIC] = jnp.zeros((2, 8, 128), f32)
    for copy in copies:
        copy.wait()
    spec, sea, ice, depth, slope, wspeed, wdir = landed

    def place(field, values):
        wide[:, :16] = values
        moved = pltpu.roll(wide[...], 0, 1, stride=16, stride_axis=0)
        kept = jnp.where(group == row, moved, 0.0)
        for half in range(2):
            own[STATIC, half, field : field + 1, :] = jnp.sum(
                kept[8 * half : 8 * half + 8], axis=0, keepdims=True
            )

    place(SEA, sea[...].astype(f32))
    place(DEPTH, depth[...].astype(f32))
    place(SLOPE_X, slope[0])
    place(SLOPE_Y, slope[1])
    place(ICE, ice[...].astype(f32))
    place(WIND, wspeed[...])
    place(WDIR, wdir[...])
    grid = spec[...].reshape(256, NDIR * FREQ)
    for low, high in ((0, 128), (128, 256), (256, 288)):
        turned = grid[:, low:high].T
        flat0[low:high, :] = turned[:, :128]
        flat1[low:high, :] = turned[:, 128:]
    inner = lanes() % 16
    even = is_even("lon")
    sea0 = own[STATIC, 0, SEA : SEA + 1, :]
    sea1 = own[STATIC, 1, SEA : SEA + 1, :]
    for slab in range(SLABS):
        if slab < NDIR:
            own0 = flat0[pl.ds(slab, FREQ, stride=NDIR), :] * sea0
            own1 = flat1[pl.ds(slab, FREQ, stride=NDIR), :] * sea1
            own[slab, 0] = own0
            own[slab, 1] = own1
        else:
            own0 = own[slab, 0]
            own1 = own[slab, 1]
        to_east = jnp.where(inner >= 8, own0, roll(own1, -8))
        to_west = jnp.where(inner < 8, own0, roll(own1, 8))
        to_first[slab] = jnp.where(even, to_east, to_west)
        to_second[slab] = jnp.where(even, to_west, to_east)


def growth_kernel(own, consts, gain):
    for half in range(2):
        point = own[STATIC, half]
        turn = point[WDIR : WDIR + 1]
        cos_w = jnp.cos(turn)
        sin_w = jnp.sin(turn)
        force = wind_gain * point[WIND : WIND + 1] * consts[LEVEL]
        share = point[SEA : SEA + 1]
        for d in range(NDIR):
            along = jnp.maximum(COS[d] * cos_w + SIN[d] * sin_w, 0.0)
            gain[d, half] = jnp.exp(force * along) * share


def join_kernel(own, from_first, from_second, to_first, to_second):
    inner = lanes() % 16
    even_group = (lanes() // 16) % 2 == 0
    even_lon = is_even("lon")
    even_lat = is_even("lat")
    for slab in range(SLABS):
        first, second = from_first[slab], from_second[slab]
        east = jnp.where(even_lon, first, second)
        west = jnp.where(even_lon, second, first)
        rim0 = jnp.where(inner < 8, roll(east, 16), roll(west, -16))
        rim1 = jnp.where(inner < 8, roll(east, 8), roll(west, -8))
        own0 = own[slab, 0]
        own1 = own[slab, 1]
        for p in range(2):
            pick = even_group if p == 0 else ~even_group
            south_rows = jnp.where(pick, own0, rim0)
            north_rows = jnp.where(pick, own1, rim1)
            to_first[slab, p] = jnp.where(even_lat, north_rows, south_rows)
            to_second[slab, p] = jnp.where(even_lat, south_rows, north_rows)


def place_kernel(to_first, to_second, from_first, from_second, consts, q, kx, ky, tx, ty):
    lane = lanes()
    even = is_even("lat")

    def assemble(slab):
        for p in range(2):
            to1, to2 = to_first[slab, p], to_second[slab, p]
            from1, from2 = from_first[slab, p], from_second[slab, p]
            parts = [
                jnp.where(even, from2, from1),
                roll(jnp.where(even, to2, to1), 32),
                roll(jnp.where(even, to1, to2), 64),
                roll(jnp.where(even, from1, from2), 96),
            ]
            for t in range(p, 8, 2):
                which = ((lane - (16 * t - 8)) % 128) // 32
                mixed = jnp.where(
                    which < 2,
                    jnp.where(which == 0, parts[0], parts[1]),
                    jnp.where(which == 2, parts[2], parts[3]),
                )
                q[slab, t] = roll(mixed, 8 - 16 * t)

    assemble(STATIC)
    speed = []
    for t in range(8):
        point = q[STATIC, t]
        depth = jnp.broadcast_to(point[DEPTH : DEPTH + 1], (8, 128))
        share = point[SEA : SEA + 1]
        pace = jnp.zeros((8, 128), f32)
        turning = jnp.zeros((8, 128), f32)
        for c in range(NCLASS):
            hit = depth == float(c)
            pace = jnp.where(hit, consts[TAB_SPEED + c], pace)
            turning = jnp.where(hit, consts[TAB_TURN + c], turning)
        pace = pace * share
        turning = turning * share
        speed.append(pace)
        kx[t] = 0.5 * (pace + roll(pace, -1)) * consts[STRETCH, t : t + 1, :]
        tx[t] = turning * point[SLOPE_X : SLOPE_X + 1]
        ty[t] = turning * point[SLOPE_Y : SLOPE_Y + 1]
    for t in range(8):
        ahead = speed[t + 1] if t < 7 else roll(speed[0], -32)
        ky[t] = 0.5 * (speed[t] + ahead)

    for d in range(NDIR):
        assemble(d)


def flux(q, diff, curve, k, u, w):
    return k * (q + u * (diff - w * curve))


def halves(k):
    return 0.5 - 0.5 * k, (1.0 / 3.0) + (1.0 / 3.0) * k


def lon_kernel(q, kx, out):
    for t in range(8):
        face = kx[t]
        for base in range(10):
            if base == 0:
                forth, back = [0], [18]
            elif base == 9:
                forth, back = [27], [9]
            else:
                forth, back = [base, 36 - base], [18 - base, 18 + base]
            k = COS[base] * face
            u, w = halves(k)
            for d in forth:
                cell = q[d, t]
                diff = roll(cell, -1) - cell
                f = flux(cell, diff, diff - roll(diff, 1), k, u, w)
                out[d, t] = cell - f + roll(f, 1)
            for d in back:
                cell = q[d, t]
                ahead = roll(cell, -1)
                diff = cell - ahead
                f = flux(ahead, diff, diff - roll(diff, -1), k, u, w)
                out[d, t] = cell + f - roll(f, 1)


def lat_kernel(q, ky, consts, out):
    live = consts[LIVE]

    def forth(d, ks, us, ws):
        tiles = [q[d, t] for t in range(8)]
        diff = [tiles[t + 1] - tiles[t] for t in range(7)]
        diff.append(roll(tiles[0], -32) - tiles[7])
        before = roll(diff[7], 32)
        fluxes = []
        for t in range(8):
            fluxes.append(flux(tiles[t], diff[t], diff[t] - before, ks[t], us[t], ws[t]))
            before = diff[t]
        behind = roll(fluxes[7], 32)
        for t in range(8):
            out[d, t] = (tiles[t] - fluxes[t] + behind) * live
            behind = fluxes[t]

    def back(d, ks, us, ws):
        tiles = [q[d, t] for t in range(8)]
        ahead = tiles[1:] + [roll(tiles[0], -32)]
        diff = [tiles[t] - ahead[t] for t in range(8)]
        after = diff[1:] + [roll(diff[0], -32)]
        fluxes = [flux(ahead[t], diff[t], diff[t] - after[t], ks[t], us[t], ws[t]) for t in range(8)]
        behind = roll(fluxes[7], 32)
        for t in range(8):
            out[d, t] = (tiles[t] + fluxes[t] - behind) * live
            behind = fluxes[t]

    for base in range(10):
        ks = [SIN[base] * ky[t] for t in range(8)]
        us, ws = zip(*[halves(k) for k in ks])
        if base == 0:
            north, south = [0], [18]
        elif base == 9:
            north, south = [9], [27]
        else:
            north, south = [base, 18 - base], [18 + base, 36 - base]
        for d in north:
            forth(d, ks, us, ws)
        for d in south:
            back(d, ks, us, ws)


def turn_kernel(q, tx, ty, out):
    def one(t):
        x = tx[t]
        y = ty[t]

        def courant(d):
            return SIN_FACE[d] * x - COS_FACE[d] * y

        def face(d, cell, diff, curve, curve_ahead):
            k = courant(d)
            u, w = halves(k)
            return flux(cell, diff, jnp.where(k >= 0.0, curve, curve_ahead), k, u, w)

        cell, ahead = q[0, t], q[1, t]
        before, last = q[NDIR - 1, t], q[NDIR - 2, t]
        diff0 = before - last
        diff1 = cell - before
        diff2 = ahead - cell
        curve1 = diff1 - diff0
        curve2 = diff2 - diff1
        f_before = face(NDIR - 1, before, diff1, curve1, curve2)
        diff, curve = diff2, curve2
        for d in range(NDIR):
            beyond = q[(d + 2) % NDIR, t]
            diff_ahead = beyond - ahead
            curve_ahead = diff_ahead - diff
            f = face(d, cell, diff, curve, curve_ahead)
            out[d, t] = cell - f + f_before
            cell, ahead, diff, curve, f_before = ahead, beyond, diff_ahead, curve_ahead, f

    for t in range(8):
        one(t)


def gather_kernel(q, consts, own, sums):
    lane = lanes()
    zero = jnp.zeros((8, 128), f32)

    totals = [zero, zero]
    for d in range(NDIR):
        halves_of = [zero, zero]
        for t in range(8):
            moved = roll(q[d, t], 16 * t - 40)
            halves_of[0] = jnp.where(lane // 16 == t, moved, halves_of[0])
            halves_of[1] = jnp.where(lane // 16 == (t + 2) % 8, moved, halves_of[1])
        halves_of[1] = roll(halves_of[1], -32)
        for half in range(2):
            own[d, half] = halves_of[half]
            totals[half] = totals[half] + halves_of[half]
    level = consts[LEVEL]
    sums[...] = zero
    for half in range(2):
        sums[half : half + 1, :] = jnp.sum(totals[half], axis=0, keepdims=True)
        sums[2 + half : 3 + half, :] = jnp.sum(totals[half] * level, axis=0, keepdims=True)


def finish_kernel(own, gain, static, sums, other, consts, out, flat0, flat1):
    total = sums[...] + other[...]
    for half, flat in ((0, flat0), (1, flat1)):
        energy = total[half : half + 1]
        moment = total[2 + half : 3 + half]
        mean_level = jnp.maximum(moment, 1.0) / jnp.maximum(energy, 1.0)
        mean = energy / NCOMP
        level = consts[LEVEL]
        breaking = break_coef * level * level / mean_level * (mean * mean)
        damping = static[0, half, ICE : ICE + 1] * consts[ICE_RATE]
        loss = jnp.exp(-breaking - damping)
        for d in range(NDIR):
            flat[pl.ds(d, FREQ, stride=NDIR), :] = own[d, half] * gain[d, half] * loss
        for low, high in ((0, 128), (128, 256), (256, 288)):
            turned = flat[low:high, :].T
            out[8 * half : 8 * half + 8, :, low:high] = turned.reshape(8, 16, high - low)


PARAMS = pltpu.CompilerParams(vmem_limit_bytes=32 * 2**20)


def call(kernel, ins, outs, scratch=(), name=None, space=pltpu.VMEM):
    return pl.pallas_call(
        kernel,
        out_shape=[jax.ShapeDtypeStruct(shape, f32) for shape in outs],
        in_specs=[pl.BlockSpec(memory_space=space)] * ins,
        out_specs=[pl.BlockSpec(memory_space=pltpu.VMEM)] * len(outs),
        scratch_shapes=list(scratch),
        compiler_params=PARAMS,
        name=name,
    )


def swap(array, axis, first, closed=False):
    count = lax.axis_size(axis)
    pairs = []
    for i in range(first, count, 2):
        if i + 1 < count or closed:
            j = (i + 1) % count
            pairs += [(i, j), (j, i)]
    return lax.ppermute(array, axis, pairs)


def per_device(
    spectrum,
    sea_mask,
    ice_mask,
    depth_class,
    speed_table,
    refraction_table,
    depth_slope,
    wind_speed,
    wind_dir,
    ice_rate,
):
    band = lax.axis_index("band")
    lat = lax.axis_index("lat")
    lats = lax.axis_size("lat")
    rows_dev = spectrum.shape[0]

    def spread(table):
        mine = lax.dynamic_slice_in_dim(table, band * FREQ, FREQ, 1)
        return jnp.broadcast_to(mine[:, :, None], (NCLASS, FREQ, 128))

    group = jnp.arange(128) // 32
    row = lat * rows_dev - HALO + 8 * group[None, :] + jnp.arange(8)[:, None]
    latitude = (south_edge + band_span * (row.astype(f32) + 0.5) / (rows_dev * lats)) * (math.pi / 180.0)
    stretch = 1.0 / jnp.cos(latitude)
    live = 1.0 - (((group == 0) & (lat == 0)) | ((group == 3) & (lat == lats - 1))).astype(f32)
    ice = lax.dynamic_slice_in_dim(ice_rate, band * FREQ, FREQ, 0)
    level = jnp.exp(math.log(freq_ratio) * (band * FREQ + jnp.arange(FREQ)).astype(f32))
    consts = jnp.concatenate(
        [
            spread(speed_table),
            spread(refraction_table),
            stretch[None],
            jnp.broadcast_to(live[None, None, :], (1, 8, 128)),
            jnp.broadcast_to(ice[None, :, None], (1, 8, 128)),
            jnp.broadcast_to(level[None, :, None], (1, 8, 128)),
        ]
    )

    tile = (8, 128)
    inputs = [spectrum, sea_mask, ice_mask, depth_class, depth_slope, wind_speed, wind_dir]
    own, to_first, to_second = call(
        pack_kernel,
        7,
        [(SLABS, 2) + tile, (SLABS,) + tile, (SLABS,) + tile],
        [pltpu.VMEM(x.shape, x.dtype) for x in inputs]
        + [pltpu.VMEM((NDIR * FREQ, 128), f32)] * 2
        + [pltpu.VMEM((16, 128), f32), pltpu.SemaphoreType.DMA((7,))],
        name="pack",
        space=pltpu.HBM,
    )(*[pltpu.with_memory_space_constraint(x, pltpu.HBM) for x in inputs])
    from_second = swap(to_second, "lon", 1, True)
    from_first = swap(to_first, "lon", 0, True)
    (gain,) = call(growth_kernel, 2, [(NDIR, 2) + tile], name="growth")(own, consts)
    to_first, to_second = call(join_kernel, 3, [(SLABS, 2) + tile] * 2, name="join")(own, from_first, from_second)
    from_second = swap(to_second, "lat", 1)
    from_first = swap(to_first, "lat", 0)
    block = (8,) + tile
    q, kx, ky, tx, ty = call(place_kernel, 5, [(SLABS,) + block] + [block] * 4, name="place")(
        to_first, to_second, from_first, from_second, consts
    )
    cells = [(NDIR,) + block]
    for substep in range(ITERS):
        (q,) = call(lon_kernel, 2, cells, name="lon")(q, kx)
        (q,) = call(lat_kernel, 3, cells, name="lat")(q, ky, consts)
        (q,) = call(turn_kernel, 3, cells, name="turn")(q, tx, ty)
    last, sums = call(gather_kernel, 2, [(NDIR, 2) + tile, tile], name="gather")(q, consts)
    other = swap(sums, "band", 0)
    (out,) = call(
        finish_kernel,
        6,
        [spectrum.shape],
        [pltpu.VMEM((NDIR * FREQ, 128), f32)] * 2,
        name="finish",
    )(last, gain, own[STATIC:], sums, other, consts)
    return out


def solution(mesh):
    return jax.shard_map(
        per_device,
        mesh=mesh,
        in_specs=(
            P("lat", "lon", "band"),
            P("lat", "lon"),
            P("lat", "lon"),
            P("lat", "lon"),
            P(),
            P(),
            P(None, "lat", "lon"),
            P("lat", "lon"),
            P("lat", "lon"),
            P(),
        ),
        out_specs=P("lat", "lon", "band"),
        check_vma=False,
    )
```

```python
import math

import jax
import jax.numpy as jnp
import numpy as np
from jax import lax
from jax.experimental import pallas as pl
from jax.experimental.pallas import tpu as pltpu
from jax.sharding import PartitionSpec as P

NDIR = 36
NCOMP = 576
ITERS = 4
NCLASS = 8
FREQ = 8
HALO = 8
STATIC = NDIR
SLABS = NDIR + 1
SEA, DEPTH, SLOPE_X, SLOPE_Y, ICE, WIND, WDIR = range(7)

freq_ratio = 1.1
wind_gain = 0.12
break_coef = 0.05
south_edge = -30.0
band_span = 60.0

COS = [math.cos(2.0 * math.pi * d / NDIR) for d in range(NDIR)]
SIN = [math.sin(2.0 * math.pi * d / NDIR) for d in range(NDIR)]
COS_FACE = [math.cos(2.0 * math.pi * (d + 0.5) / NDIR) for d in range(NDIR)]
SIN_FACE = [math.sin(2.0 * math.pi * (d + 0.5) / NDIR) for d in range(NDIR)]

TAB_SPEED, TAB_TURN, STRETCH, LIVE, ICE_RATE, LEVEL = 0, 8, 16, 17, 18, 19

f32 = jnp.float32
bf16 = jnp.bfloat16


def lanes():
    return lax.broadcasted_iota(jnp.int32, (8, 128), 1)


def roll(x, shift):
    shift = shift % 128
    return pltpu.roll(x, shift, 1) if shift else x


def is_even(axis):
    return lax.axis_index(axis) % 2 == 0


def pack_kernel(*refs):
    sources, (own, to_first, to_second, rows_first, rows_second), landed = refs[:7], refs[7:12], refs[12:19]
    flat0, flat1, wide, sems = refs[19:]
    copies = [pltpu.make_async_copy(src, dst, sems.at[i]) for i, (src, dst) in enumerate(zip(sources, landed))]
    for copy in copies:
        copy.start()
    wide[...] = jnp.zeros_like(wide)
    group = lax.broadcasted_iota(jnp.int32, (16, 128), 1) // 16
    row = lax.broadcasted_iota(jnp.int32, (16, 128), 0) % 8
    own[:, STATIC] = jnp.zeros((2, 8, 128), f32)
    for copy in copies:
        copy.wait()
    spec, sea, ice, depth, slope, wspeed, wdir = landed

    def place(field, values):
        wide[:, :16] = values
        moved = pltpu.roll(wide[...], 0, 1, stride=16, stride_axis=0)
        kept = jnp.where(group == row, moved, 0.0)
        for half in range(2):
            own[half, STATIC, field : field + 1, :] = jnp.sum(
                kept[8 * half : 8 * half + 8], axis=0, keepdims=True
            )

    place(SEA, sea[...].astype(f32))
    place(DEPTH, depth[...].astype(f32))
    place(SLOPE_X, slope[0])
    place(SLOPE_Y, slope[1])
    place(ICE, ice[...].astype(f32))
    place(WIND, wspeed[...])
    place(WDIR, wdir[...])
    grid = spec[...].reshape(256, NDIR * FREQ)
    for low, high in ((0, 128), (128, 256), (256, 288)):
        turned = grid[:, low:high].T
        flat0[low:high, :] = turned[:, :128]
        flat1[low:high, :] = turned[:, 128:]
    inner = lanes() % 16
    even = is_even("lon")
    even_lat = is_even("lat")
    sea0 = own[0, STATIC, SEA : SEA + 1, :]
    sea1 = own[1, STATIC, SEA : SEA + 1, :]
    for slab in range(SLABS):
        if slab < NDIR:
            own0 = flat0[pl.ds(slab, FREQ, stride=NDIR), :] * sea0
            own1 = flat1[pl.ds(slab, FREQ, stride=NDIR), :] * sea1
            own[0, slab] = own0
            own[1, slab] = own1
        else:
            own0 = own[0, slab]
            own1 = own[1, slab]
        to_east = jnp.where(inner >= 8, own0, roll(own1, -8))
        to_west = jnp.where(inner < 8, own0, roll(own1, 8))
        to_first[slab] = jnp.where(even, to_east, to_west)
        to_second[slab] = jnp.where(even, to_west, to_east)
        rows_first[slab] = jnp.where(even_lat, own1, own0)
        rows_second[slab] = jnp.where(even_lat, own0, own1)


def growth_kernel(own, consts, gain):
    for half in range(2):
        point = own[half, STATIC]
        turn = point[WDIR : WDIR + 1]
        cos_w = jnp.cos(turn)
        sin_w = jnp.sin(turn)
        force = wind_gain * point[WIND : WIND + 1] * consts[LEVEL]
        share = point[SEA : SEA + 1]
        for d in range(NDIR):
            along = jnp.maximum(COS[d] * cos_w + SIN[d] * sin_w, 0.0)
            gain[d, half] = jnp.exp(force * along) * share


def tables_kernel(place, shifts, gather):
    chunk = lax.broadcasted_iota(jnp.int32, (16, 128), 0)
    lane = lax.broadcasted_iota(jnp.int32, (16, 128), 1)
    low = chunk < 8
    targets = [
        40 + chunk,
        72 + chunk,
        jnp.where(low, 64 + chunk, 24 + chunk),
        jnp.where(low, 56 + chunk, 80 + chunk),
        8 + chunk,
        jnp.where(low, chunk, 16 + chunk),
        104 + chunk,
        jnp.where(low, 120 + chunk, 88 + chunk),
    ]
    place[...] = jnp.zeros_like(place)
    for s, target in enumerate(targets):
        stripe = (lane == target).astype(f32).astype(bf16)
        for part in range(2):
            for t in range(8):
                row = part * 1024 + s * 128 + 16 * t
                place[row : row + 16, 128 * t : 128 * t + 128] = stripe
    row = lax.broadcasted_iota(jnp.int32, (128, 128), 0)
    col = lax.broadcasted_iota(jnp.int32, (128, 128), 1)
    for sign, taps in ((0, FORTH_TAPS), (1, BACK_TAPS)):
        for i, tap in enumerate(taps):
            moved = (row == (col + tap) % 128).astype(f32).astype(bf16)
            for part in range(2):
                shifts[sign, 128 * part : 128 * part + 128, 128 * i : 128 * i + 128] = moved
    for t in range(8):
        for half in range(2):
            from_row = 40 + 32 * half + col % 16
            moved = ((col // 16 == t) & (row == from_row)).astype(f32).astype(bf16)
            for part in range(2):
                at = part * 1024 + 128 * t
                gather[at : at + 128, 128 * half : 128 * half + 128] = moved


def corner_kernel(from_first, from_second, to_first, to_second):
    low = lanes() % 16 < 8
    even_lon = is_even("lon")
    even_lat = is_even("lat")
    for slab in range(SLABS):
        first, second = from_first[slab], from_second[slab]
        east = jnp.where(even_lon, first, second)
        west = jnp.where(even_lon, second, first)
        north = jnp.where(low, west, east)
        south = jnp.where(low, east, west)
        to_first[slab] = jnp.where(even_lat, north, south)
        to_second[slab] = jnp.where(even_lat, south, north)


def split(x):
    high = x.astype(bf16)
    return high, (x - high.astype(f32)).astype(bf16)


def place_kernel(
    own, cols_first, cols_second, rows_first, rows_second, rims_first, rims_second, consts, matrix,
    q, taps, ky, tx, ty, lhs,
):
    even_lon = is_even("lon")
    even_lat = is_even("lat")
    blank = jnp.zeros((8, 128), f32)

    def fill(s, array):
        x = jnp.concatenate([array.reshape(8 * SLABS, 128), blank], axis=0)
        high, low = split(x)
        lhs[:, 128 * s : 128 * s + 128] = high
        lhs[:, 1024 + 128 * s : 1024 + 128 * s + 128] = low

    def pick(flag, first, second):
        return jnp.where(flag, first[...], second[...])

    fill(0, own[0])
    fill(1, own[1])
    fill(2, pick(even_lon, cols_second, cols_first))
    fill(3, pick(even_lon, cols_first, cols_second))
    fill(4, pick(even_lat, rows_second, rows_first))
    fill(5, pick(even_lat, rims_second, rims_first))
    fill(6, pick(even_lat, rows_first, rows_second))
    fill(7, pick(even_lat, rims_first, rims_second))
    for pair in range(4):
        moved = jnp.dot(lhs[...], matrix[:, 256 * pair : 256 * pair + 256], preferred_element_type=f32)
        for i in range(2):
            q[:, 2 * pair + i] = moved[: 8 * SLABS, 128 * i : 128 * i + 128].reshape(SLABS, 8, 128)

    speed = []
    for t in range(8):
        point = q[STATIC, t]
        depth = jnp.broadcast_to(point[DEPTH : DEPTH + 1], (8, 128))
        share = point[SEA : SEA + 1]
        pace = jnp.zeros((8, 128), f32)
        turning = jnp.zeros((8, 128), f32)
        for c in range(NCLASS):
            hit = depth == float(c)
            pace = jnp.where(hit, consts[TAB_SPEED + c], pace)
            turning = jnp.where(hit, consts[TAB_TURN + c], turning)
        pace = pace * share
        turning = turning * share
        speed.append(pace)
        tx[t] = turning * point[SLOPE_X : SLOPE_X + 1]
        ty[t] = turning * point[SLOPE_Y : SLOPE_Y + 1]
        stretch = consts[STRETCH, t : t + 1, :]
        right = 0.5 * (pace + roll(pace, -1)) * stretch
        left = 0.5 * (pace + roll(pace, 1)) * stretch
        for base in range(10):
            a1, b1, c1 = weights(COS[base] * right)
            a0, b0, c0 = weights(COS[base] * left)
            taps[base, 0, 0, t] = 1.0 - a1 + b0
            taps[base, 0, 1, t] = -b1
            taps[base, 0, 2, t] = a0 - c1
            taps[base, 0, 3, t] = c0
            taps[base, 1, 0, t] = 1.0 + b1 - a0
            taps[base, 1, 1, t] = a1 - c0
            taps[base, 1, 2, t] = -b0
            taps[base, 1, 3, t] = c1
    for t in range(8):
        ahead = speed[t + 1] if t < 7 else roll(speed[0], -32)
        ky[t] = 0.5 * (speed[t] + ahead)


def flux(q, diff, curve, k, u, w):
    return k * (q + u * (diff - w * curve))


def halves(k):
    return 0.5 - 0.5 * k, (1.0 / 3.0) + (1.0 / 3.0) * k


def weights(k):
    u, w = halves(k)
    bend = k * u * w
    return k - k * u + 2.0 * bend, k * u - bend, -bend


FORTH_TAPS = (1, -1, -2)
BACK_TAPS = (1, -1, 2)


def lon_kernel(q, taps, shifts, out, moved):
    for quadrant, sign in ((0, 0), (3, 0), (1, 1), (2, 1)):
        x = q[9 * quadrant : 9 * quadrant + 9].reshape(576, 128)
        lhs = jnp.concatenate(split(x), axis=1)
        moved[quadrant] = jnp.dot(lhs, shifts[sign], preferred_element_type=f32)
    for sign in range(2):
        for base in range(10):
            if base == 0:
                dirs = [[0], [18]][sign]
            elif base == 9:
                dirs = [[27], [9]][sign]
            else:
                dirs = [[base, 36 - base], [18 - base, 18 + base]][sign]
            for t in range(8):
                tap = [taps[base, sign, i, t] for i in range(4)]
                for d in dirs:
                    at = 64 * (d % 9) + 8 * t
                    near = [moved[d // 9, at : at + 8, 128 * i : 128 * i + 128] for i in range(3)]
                    out[d, t] = (tap[0] * q[d, t] + tap[1] * near[0]) + (tap[2] * near[1] + tap[3] * near[2])


def lat_kernel(q, ky, consts, out):
    live = consts[LIVE]

    def forth(d, ks, us, ws):
        tiles = [q[d, t] for t in range(8)]
        diff = [tiles[t + 1] - tiles[t] for t in range(7)]
        diff.append(roll(tiles[0], -32) - tiles[7])
        before = roll(diff[7], 32)
        fluxes = []
        for t in range(8):
            fluxes.append(flux(tiles[t], diff[t], diff[t] - before, ks[t], us[t], ws[t]))
            before = diff[t]
        behind = roll(fluxes[7], 32)
        for t in range(8):
            out[d, t] = (tiles[t] - fluxes[t] + behind) * live
            behind = fluxes[t]

    def back(d, ks, us, ws):
        tiles = [q[d, t] for t in range(8)]
        ahead = tiles[1:] + [roll(tiles[0], -32)]
        diff = [tiles[t] - ahead[t] for t in range(8)]
        after = diff[1:] + [roll(diff[0], -32)]
        fluxes = [flux(ahead[t], diff[t], diff[t] - after[t], ks[t], us[t], ws[t]) for t in range(8)]
        behind = roll(fluxes[7], 32)
        for t in range(8):
            out[d, t] = (tiles[t] + fluxes[t] - behind) * live
            behind = fluxes[t]

    for base in range(10):
        ks = [SIN[base] * ky[t] for t in range(8)]
        us, ws = zip(*[halves(k) for k in ks])
        if base == 0:
            north, south = [0], [18]
        elif base == 9:
            north, south = [9], [27]
        else:
            north, south = [base, 18 - base], [18 + base, 36 - base]
        for d in north:
            forth(d, ks, us, ws)
        for d in south:
            back(d, ks, us, ws)


def turn_kernel(q, tx, ty, out):
    def one(t):
        x = tx[t]
        y = ty[t]

        def courant(d):
            return SIN_FACE[d] * x - COS_FACE[d] * y

        def face(d, cell, diff, curve, curve_ahead):
            k = courant(d)
            u, w = halves(k)
            return flux(cell, diff, jnp.where(k >= 0.0, curve, curve_ahead), k, u, w)

        cell, ahead = q[0, t], q[1, t]
        before, last = q[NDIR - 1, t], q[NDIR - 2, t]
        diff0 = before - last
        diff1 = cell - before
        diff2 = ahead - cell
        curve1 = diff1 - diff0
        curve2 = diff2 - diff1
        f_before = face(NDIR - 1, before, diff1, curve1, curve2)
        diff, curve = diff2, curve2
        for d in range(NDIR):
            beyond = q[(d + 2) % NDIR, t]
            diff_ahead = beyond - ahead
            curve_ahead = diff_ahead - diff
            f = face(d, cell, diff, curve, curve_ahead)
            out[d, t] = cell - f + f_before
            cell, ahead, diff, curve, f_before = ahead, beyond, diff_ahead, curve_ahead, f

    for t in range(8):
        one(t)


def gather_kernel(q, consts, matrix, own, sums, lhs):
    zero = jnp.zeros((8, 128), f32)
    for t in range(8):
        high, low = split(q[:, t].reshape(8 * NDIR, 128))
        lhs[:, 128 * t : 128 * t + 128] = high
        lhs[:, 1024 + 128 * t : 1024 + 128 * t + 128] = low
    moved = jnp.dot(lhs[...], matrix[...], preferred_element_type=f32)
    totals = [zero, zero]
    for half in range(2):
        own[half] = moved[:, 128 * half : 128 * half + 128].reshape(NDIR, 8, 128)
        totals[half] = jnp.sum(own[half], axis=0)
    level = consts[LEVEL]
    sums[...] = zero
    for half in range(2):
        sums[half : half + 1, :] = jnp.sum(totals[half], axis=0, keepdims=True)
        sums[2 + half : 3 + half, :] = jnp.sum(totals[half] * level, axis=0, keepdims=True)


def finish_kernel(own, gain, static, sums, other, consts, out, flat0, flat1):
    total = sums[...] + other[...]
    for half, flat in ((0, flat0), (1, flat1)):
        energy = total[half : half + 1]
        moment = total[2 + half : 3 + half]
        mean_level = jnp.maximum(moment, 1.0) / jnp.maximum(energy, 1.0)
        mean = energy / NCOMP
        level = consts[LEVEL]
        breaking = break_coef * level * level / mean_level * (mean * mean)
        damping = static[half, 0, ICE : ICE + 1] * consts[ICE_RATE]
        loss = jnp.exp(-breaking - damping)
        for d in range(NDIR):
            flat[pl.ds(d, FREQ, stride=NDIR), :] = own[half, d] * gain[d, half] * loss
        for low, high in ((0, 128), (128, 256), (256, 288)):
            turned = flat[low:high, :].T
            out[8 * half : 8 * half + 8, :, low:high] = turned.reshape(8, 16, high - low)


PARAMS = pltpu.CompilerParams(vmem_limit_bytes=40 * 2**20)


def call(kernel, ins, outs, scratch=(), name=None, space=pltpu.VMEM, dtype=f32):
    return pl.pallas_call(
        kernel,
        out_shape=[jax.ShapeDtypeStruct(shape, dtype) for shape in outs],
        in_specs=[pl.BlockSpec(memory_space=space)] * ins,
        out_specs=[pl.BlockSpec(memory_space=pltpu.VMEM)] * len(outs),
        scratch_shapes=list(scratch),
        compiler_params=PARAMS,
        name=name,
    )


def swap(array, axis, first, closed=False):
    count = lax.axis_size(axis)
    pairs = []
    for i in range(first, count, 2):
        if i + 1 < count or closed:
            j = (i + 1) % count
            pairs += [(i, j), (j, i)]
    return lax.ppermute(array, axis, pairs)


def per_device(
    spectrum,
    sea_mask,
    ice_mask,
    depth_class,
    speed_table,
    refraction_table,
    depth_slope,
    wind_speed,
    wind_dir,
    ice_rate,
):
    band = lax.axis_index("band")
    lat = lax.axis_index("lat")
    lats = lax.axis_size("lat")
    rows_dev = spectrum.shape[0]

    def spread(table):
        mine = lax.dynamic_slice_in_dim(table, band * FREQ, FREQ, 1)
        return jnp.broadcast_to(mine[:, :, None], (NCLASS, FREQ, 128))

    group = jnp.arange(128) // 32
    row = lat * rows_dev - HALO + 8 * group[None, :] + jnp.arange(8)[:, None]
    latitude = (south_edge + band_span * (row.astype(f32) + 0.5) / (rows_dev * lats)) * (math.pi / 180.0)
    stretch = 1.0 / jnp.cos(latitude)
    live = 1.0 - (((group == 0) & (lat == 0)) | ((group == 3) & (lat == lats - 1))).astype(f32)
    ice = lax.dynamic_slice_in_dim(ice_rate, band * FREQ, FREQ, 0)
    level = jnp.exp(math.log(freq_ratio) * (band * FREQ + jnp.arange(FREQ)).astype(f32))
    consts = jnp.concatenate(
        [
            spread(speed_table),
            spread(refraction_table),
            stretch[None],
            jnp.broadcast_to(live[None, None, :], (1, 8, 128)),
            jnp.broadcast_to(ice[None, :, None], (1, 8, 128)),
            jnp.broadcast_to(level[None, :, None], (1, 8, 128)),
        ]
    )

    tile = (8, 128)
    inputs = [spectrum, sea_mask, ice_mask, depth_class, depth_slope, wind_speed, wind_dir]
    slabs = (SLABS,) + tile
    own, to_first, to_second, edge_first, edge_second = call(
        pack_kernel,
        7,
        [(2,) + slabs] + [slabs] * 4,
        [pltpu.VMEM(x.shape, x.dtype) for x in inputs]
        + [pltpu.VMEM((NDIR * FREQ, 128), f32)] * 2
        + [pltpu.VMEM((16, 128), f32), pltpu.SemaphoreType.DMA((7,))],
        name="pack",
        space=pltpu.HBM,
    )(*[pltpu.with_memory_space_constraint(x, pltpu.HBM) for x in inputs])
    cols_second = swap(to_second, "lon", 1, True)
    cols_first = swap(to_first, "lon", 0, True)
    rows_second = swap(edge_second, "lat", 1)
    rows_first = swap(edge_first, "lat", 0)
    (gain,) = call(growth_kernel, 2, [(NDIR, 2) + tile], name="growth")(own, consts)
    place, shifts, gather = call(
        tables_kernel, 0, [(2048, 1024), (2, 256, 384), (2048, 256)], name="tables", dtype=bf16
    )()
    to_first, to_second = call(corner_kernel, 2, [slabs] * 2, name="corner")(cols_first, cols_second)
    rims_second = swap(to_second, "lat", 1)
    rims_first = swap(to_first, "lat", 0)
    block = (8,) + tile
    q, taps, ky, tx, ty = call(
        place_kernel,
        9,
        [(SLABS,) + block, (10, 2, 4) + block] + [block] * 3,
        [pltpu.VMEM((8 * SLABS + 8, 2048), bf16)],
        name="place",
    )(own, cols_first, cols_second, rows_first, rows_second, rims_first, rims_second, consts, place)
    cells = [(NDIR,) + block]
    for substep in range(ITERS):
        (q,) = call(lon_kernel, 3, cells, [pltpu.VMEM((4, 576, 384), f32)], name="lon")(q, taps, shifts)
        (q,) = call(lat_kernel, 3, cells, name="lat")(q, ky, consts)
        (q,) = call(turn_kernel, 3, cells, name="turn")(q, tx, ty)
    last, sums = call(
        gather_kernel, 3, [(2, NDIR) + tile, tile], [pltpu.VMEM((8 * NDIR, 2048), bf16)], name="gather"
    )(q, consts, gather)
    other = swap(sums, "band", 0)
    (out,) = call(
        finish_kernel,
        6,
        [spectrum.shape],
        [pltpu.VMEM((NDIR * FREQ, 128), f32)] * 2,
        name="finish",
    )(last, gain, own[:, STATIC:], sums, other, consts)
    return out


def solution(mesh):
    return jax.shard_map(
        per_device,
        mesh=mesh,
        in_specs=(
            P("lat", "lon", "band"),
            P("lat", "lon"),
            P("lat", "lon"),
            P("lat", "lon"),
            P(),
            P(),
            P(None, "lat", "lon"),
            P("lat", "lon"),
            P("lat", "lon"),
            P(),
        ),
        out_specs=P("lat", "lon", "band"),
        check_vma=False,
    )
```

```python
import functools
import math

import jax
import jax.numpy as jnp
import numpy as np
from jax import lax
from jax.experimental import pallas as pl
from jax.experimental.pallas import tpu as pltpu
from jax.sharding import PartitionSpec as P

NDIR = 36
NCOMP = 576
ITERS = 4
NCLASS = 8
FREQ = 8
HALO = 8
ROWS = 16
STATIC = NDIR
SLABS = NDIR + 1
SEA, DEPTH, SLOPE_X, SLOPE_Y, ICE, WIND, WDIR = range(7)

freq_ratio = 1.1
wind_gain = 0.12
break_coef = 0.05
south_edge = -30.0
band_span = 60.0

COS = [math.cos(2.0 * math.pi * d / NDIR) for d in range(NDIR)]
SIN = [math.sin(2.0 * math.pi * d / NDIR) for d in range(NDIR)]
COS_FACE = [math.cos(2.0 * math.pi * (d + 0.5) / NDIR) for d in range(NDIR)]
SIN_FACE = [math.sin(2.0 * math.pi * (d + 0.5) / NDIR) for d in range(NDIR)]

TAB_SPEED, TAB_TURN, STRETCH, LIVE, ICE_RATE, LEVEL = 0, 8, 16, 17, 18, 19

f32 = jnp.float32
bf16 = jnp.bfloat16


def lanes():
    return lax.broadcasted_iota(jnp.int32, (8, 128), 1)


def roll(x, shift):
    shift = shift % 128
    return pltpu.roll(x, shift, 1) if shift else x


def is_even(axis):
    return lax.axis_index(axis) % 2 == 0


def pack_kernel(*refs):
    sources, own, tables = refs[:10], refs[10], refs[11:14]
    landed = refs[14:21]
    flat0, flat1, wide, sems = refs[21:]
    copies = [
        pltpu.make_async_copy(src, dst, sems.at[i]) for i, (src, dst) in enumerate(zip(sources, landed + tables))
    ]
    for copy in copies:
        copy.start()
    wide[...] = jnp.zeros_like(wide)
    group = lax.broadcasted_iota(jnp.int32, (16, 128), 1) // 16
    row = lax.broadcasted_iota(jnp.int32, (16, 128), 0) % 8
    own[:, STATIC] = jnp.zeros((2, 8, 128), f32)
    for copy in copies:
        copy.wait()
    spec, sea, ice, depth, slope, wspeed, wdir = landed

    def place(field, values):
        wide[:, :16] = values
        moved = pltpu.roll(wide[...], 0, 1, stride=16, stride_axis=0)
        kept = jnp.where(group == row, moved, 0.0)
        for half in range(2):
            own[half, STATIC, field : field + 1, :] = jnp.sum(
                kept[8 * half : 8 * half + 8], axis=0, keepdims=True
            )

    place(SEA, sea[...].astype(f32))
    place(DEPTH, depth[...].astype(f32))
    place(SLOPE_X, slope[0])
    place(SLOPE_Y, slope[1])
    place(ICE, ice[...].astype(f32))
    place(WIND, wspeed[...])
    place(WDIR, wdir[...])
    grid = spec[...].reshape(256, NDIR * FREQ)
    for low, high in ((0, 128), (128, 256), (256, 288)):
        turned = grid[:, low:high].T
        flat0[low:high, :] = turned[:, :128]
        flat1[low:high, :] = turned[:, 128:]
    sea0 = own[0, STATIC, SEA : SEA + 1, :]
    sea1 = own[1, STATIC, SEA : SEA + 1, :]
    for d in range(NDIR):
        own[0, d] = flat0[pl.ds(d, FREQ, stride=NDIR), :] * sea0
        own[1, d] = flat1[pl.ds(d, FREQ, stride=NDIR), :] * sea1


def column_kernel(second, own, message):
    inner = lanes() % 16
    to_east = is_even("lon") != second
    for slab in range(SLABS):
        own0, own1 = own[0, slab], own[1, slab]
        east = jnp.where(inner >= 8, own0, roll(own1, -8))
        west = jnp.where(inner < 8, own0, roll(own1, 8))
        message[slab] = jnp.where(to_east, east, west)


def edge_kernel(second, own, edge):
    even = is_even("lat")
    if second:
        edge[...] = jnp.where(even, own[0], own[1])
    else:
        edge[...] = jnp.where(even, own[1], own[0])


def growth_kernel(own, consts, gain):
    for half in range(2):
        point = own[half, STATIC]
        turn = point[WDIR : WDIR + 1]
        cos_w = jnp.cos(turn)
        sin_w = jnp.sin(turn)
        force = wind_gain * point[WIND : WIND + 1] * consts[LEVEL]
        share = point[SEA : SEA + 1]
        for d in range(NDIR):
            along = jnp.maximum(COS[d] * cos_w + SIN[d] * sin_w, 0.0)
            gain[d, half] = jnp.exp(force * along) * share


def tables_kernel(speed_table, refraction_table, ice_rate, place, rims, shifts, gather, spread, consts):
    first = lax.axis_index("band") * FREQ
    sub = lax.broadcasted_iota(jnp.int32, (8, 128), 0)
    mine = lanes() == first + sub

    def column(row):
        picked = jnp.where(mine, jnp.broadcast_to(row, (8, 128)), 0.0)
        return jnp.broadcast_to(jnp.sum(picked, axis=1, keepdims=True), (8, 128))

    def widen(values):
        return jnp.concatenate([values, jnp.zeros((values.shape[0], 112), f32)], axis=1)

    for at, table in ((TAB_SPEED, speed_table), (TAB_TURN, refraction_table)):
        wide = widen(table[...])
        for c in range(NCLASS):
            consts[at + c] = column(wide[c : c + 1])
    consts[ICE_RATE] = column(widen(ice_rate[...].reshape(1, 16)))
    consts[LEVEL] = jnp.exp(math.log(freq_ratio) * (first + sub).astype(f32))
    lat = lax.axis_index("lat")
    lats = lax.axis_size("lat")
    group = lanes() // 32
    rows = lat * ROWS - HALO + 8 * group + sub
    latitude = (south_edge + band_span * (rows.astype(f32) + 0.5) / (ROWS * lats)) * (math.pi / 180.0)
    consts[STRETCH] = 1.0 / jnp.cos(latitude)
    ghost = ((group == 0) & (lat == 0)) | ((group == 3) & (lat == lats - 1))
    consts[LIVE] = jnp.where(ghost, 0.0, 1.0)
    comp = lax.broadcasted_iota(jnp.int32, (16, NDIR * FREQ), 1) // NDIR
    freq = lax.broadcasted_iota(jnp.int32, (16, NDIR * FREQ), 0) % FREQ
    spread[...] = (comp == freq).astype(f32).astype(bf16)

    chunk = lax.broadcasted_iota(jnp.int32, (16, 128), 0)
    lane = lax.broadcasted_iota(jnp.int32, (16, 128), 1)
    low = chunk < 8
    targets = [
        40 + chunk,
        72 + chunk,
        jnp.where(low, 64 + chunk, 24 + chunk),
        jnp.where(low, 56 + chunk, 80 + chunk),
        8 + chunk,
        104 + chunk,
    ]
    corners = [jnp.where(low, chunk, 16 + chunk), jnp.where(low, 120 + chunk, 88 + chunk)]
    for matrix, lists in ((place, targets), (rims, corners)):
        matrix[...] = jnp.zeros_like(matrix)
        for s, target in enumerate(lists):
            stripe = (lane == target).astype(f32).astype(bf16)
            for part in range(2):
                for t in range(8):
                    row = part * 128 * len(lists) + s * 128 + 16 * t
                    matrix[row : row + 16, 128 * t : 128 * t + 128] = stripe
    row = lax.broadcasted_iota(jnp.int32, (128, 128), 0)
    col = lax.broadcasted_iota(jnp.int32, (128, 128), 1)
    for sign, taps in ((0, FORTH_TAPS), (1, BACK_TAPS)):
        for i, tap in enumerate(taps):
            moved = (row == (col + tap) % 128).astype(f32).astype(bf16)
            for part in range(2):
                shifts[sign, 128 * part : 128 * part + 128, 128 * i : 128 * i + 128] = moved
    for t in range(8):
        for half in range(2):
            from_row = 40 + 32 * half + col % 16
            moved = ((col // 16 == t) & (row == from_row)).astype(f32).astype(bf16)
            for part in range(2):
                at = part * 1024 + 128 * t
                gather[at : at + 128, 128 * half : 128 * half + 128] = moved


def corner_kernel(second, cols_second, cols_first, rim):
    low = lanes() % 16 < 8
    even_lon = is_even("lon")
    even_lat = is_even("lat")
    to_north = ~even_lat if second else even_lat
    west_low = low == to_north
    for slab in range(SLABS):
        one, two = cols_first[slab], cols_second[slab]
        east = jnp.where(even_lon, one, two)
        west = jnp.where(even_lon, two, one)
        rim[slab] = jnp.where(west_low, west, east)


def split(x):
    high = x.astype(bf16)
    return high, (x - high.astype(f32)).astype(bf16)


def fill_parts(lhs, count, s, array):
    x = jnp.concatenate([array.reshape(8 * SLABS, 128), jnp.zeros((8, 128), f32)], axis=0)
    high, low = split(x)
    lhs[:, 128 * s : 128 * s + 128] = high
    lhs[:, 128 * (count + s) : 128 * (count + s) + 128] = low


def place_kernel(own, cols_second, cols_first, rows_second, rows_first, matrix, q, lhs):
    even_lon = is_even("lon")
    even_lat = is_even("lat")
    fill_parts(lhs, 6, 0, own[0])
    fill_parts(lhs, 6, 1, own[1])
    fill_parts(lhs, 6, 2, jnp.where(even_lon, cols_second[...], cols_first[...]))
    fill_parts(lhs, 6, 3, jnp.where(even_lon, cols_first[...], cols_second[...]))
    fill_parts(lhs, 6, 4, jnp.where(even_lat, rows_second[...], rows_first[...]))
    fill_parts(lhs, 6, 5, jnp.where(even_lat, rows_first[...], rows_second[...]))
    for pair in range(4):
        moved = jnp.dot(lhs[...], matrix[:, 256 * pair : 256 * pair + 256], preferred_element_type=f32)
        for i in range(2):
            q[:, 2 * pair + i] = moved[: 8 * SLABS, 128 * i : 128 * i + 128].reshape(SLABS, 8, 128)


def lookup(point, consts, at):
    depth = jnp.broadcast_to(point[DEPTH : DEPTH + 1], (8, 128))
    value = jnp.zeros((8, 128), f32)
    for c in range(NCLASS):
        value = jnp.where(depth == float(c), consts[at + c], value)
    return value * point[SEA : SEA + 1]


def rims_kernel(partial, rims_second, rims_first, consts, matrix, q, taps, ky, tx, ty, lhs):
    even_lat = is_even("lat")
    fill_parts(lhs, 2, 0, jnp.where(even_lat, rims_second[...], rims_first[...]))
    fill_parts(lhs, 2, 1, jnp.where(even_lat, rims_first[...], rims_second[...]))
    for pair in range(4):
        moved = jnp.dot(lhs[...], matrix[:, 256 * pair : 256 * pair + 256], preferred_element_type=f32)
        for i in range(2):
            t = 2 * pair + i
            q[:, t] = partial[:, t] + moved[: 8 * SLABS, 128 * i : 128 * i + 128].reshape(SLABS, 8, 128)

    speed = []
    for t in range(8):
        point = q[STATIC, t]
        pace = lookup(point, consts, TAB_SPEED)
        turning = lookup(point, consts, TAB_TURN)
        speed.append(pace)
        tx[t] = turning * point[SLOPE_X : SLOPE_X + 1]
        ty[t] = turning * point[SLOPE_Y : SLOPE_Y + 1]
        stretch = consts[STRETCH, t : t + 1, :]
        right = 0.5 * (pace + roll(pace, -1)) * stretch
        left = 0.5 * (pace + roll(pace, 1)) * stretch
        for base in range(10):
            a1, b1, c1 = weights(COS[base] * right)
            a0, b0, c0 = weights(COS[base] * left)
            taps[base, 0, 0, t] = 1.0 - a1 + b0
            taps[base, 0, 1, t] = -b1
            taps[base, 0, 2, t] = a0 - c1
            taps[base, 0, 3, t] = c0
            taps[base, 1, 0, t] = 1.0 + b1 - a0
            taps[base, 1, 1, t] = a1 - c0
            taps[base, 1, 2, t] = -b0
            taps[base, 1, 3, t] = c1
    for t in range(8):
        ahead = speed[t + 1] if t < 7 else roll(speed[0], -32)
        ky[t] = 0.5 * (speed[t] + ahead)


def flux(q, diff, curve, k, u, w):
    return k * (q + u * (diff - w * curve))


def halves(k):
    return 0.5 - 0.5 * k, (1.0 / 3.0) + (1.0 / 3.0) * k


def weights(k):
    u, w = halves(k)
    bend = k * u * w
    return k - k * u + 2.0 * bend, k * u - bend, -bend


FORTH_TAPS = (1, -1, -2)
BACK_TAPS = (1, -1, 2)


def lon_kernel(q, taps, shifts, out, moved):
    for quadrant, sign in ((0, 0), (3, 0), (1, 1), (2, 1)):
        x = q[9 * quadrant : 9 * quadrant + 9].reshape(576, 128)
        lhs = jnp.concatenate(split(x), axis=1)
        moved[quadrant] = jnp.dot(lhs, shifts[sign], preferred_element_type=f32)
    for sign in range(2):
        for base in range(10):
            if base == 0:
                dirs = [[0], [18]][sign]
            elif base == 9:
                dirs = [[27], [9]][sign]
            else:
                dirs = [[base, 36 - base], [18 - base, 18 + base]][sign]
            for t in range(8):
                tap = [taps[base, sign, i, t] for i in range(4)]
                for d in dirs:
                    at = 64 * (d % 9) + 8 * t
                    near = [moved[d // 9, at : at + 8, 128 * i : 128 * i + 128] for i in range(3)]
                    out[d, t] = (tap[0] * q[d, t] + tap[1] * near[0]) + (tap[2] * near[1] + tap[3] * near[2])


def lat_kernel(q, ky, consts, out):
    live = consts[LIVE]

    def forth(d, ks, us, ws):
        tiles = [q[d, t] for t in range(8)]
        diff = [tiles[t + 1] - tiles[t] for t in range(7)]
        diff.append(roll(tiles[0], -32) - tiles[7])
        before = roll(diff[7], 32)
        fluxes = []
        for t in range(8):
            fluxes.append(flux(tiles[t], diff[t], diff[t] - before, ks[t], us[t], ws[t]))
            before = diff[t]
        behind = roll(fluxes[7], 32)
        for t in range(8):
            out[d, t] = (tiles[t] - fluxes[t] + behind) * live
            behind = fluxes[t]

    def back(d, ks, us, ws):
        tiles = [q[d, t] for t in range(8)]
        ahead = tiles[1:] + [roll(tiles[0], -32)]
        diff = [tiles[t] - ahead[t] for t in range(8)]
        after = diff[1:] + [roll(diff[0], -32)]
        fluxes = [flux(ahead[t], diff[t], diff[t] - after[t], ks[t], us[t], ws[t]) for t in range(8)]
        behind = roll(fluxes[7], 32)
        for t in range(8):
            out[d, t] = (tiles[t] + fluxes[t] - behind) * live
            behind = fluxes[t]

    for base in range(10):
        ks = [SIN[base] * ky[t] for t in range(8)]
        us, ws = zip(*[halves(k) for k in ks])
        if base == 0:
            north, south = [0], [18]
        elif base == 9:
            north, south = [9], [27]
        else:
            north, south = [base, 18 - base], [18 + base, 36 - base]
        for d in north:
            forth(d, ks, us, ws)
        for d in south:
            back(d, ks, us, ws)


def turn_around(get, put, x, y):
    def factors(d):
        k = SIN_FACE[d] * x - COS_FACE[d] * y
        half, third = 0.5 * k, (1.0 / 3.0) * k
        return k, 0.5 - half, 1.0 / 3.0 + third, 0.5 + half, 1.0 / 3.0 - third

    half_turn = NDIR // 2
    k, u, w, u_back, w_back = factors(half_turn - 1)
    state = []
    ends = []
    for at in (0, half_turn):
        cell, ahead = get(at), get(at + 1)
        before, last = get((at - 1) % NDIR), get((at - 2) % NDIR)
        diff = ahead - cell
        diff1 = cell - before
        curve = diff - diff1
        curve1 = diff1 - (before - last)
        if at == 0:
            f = flux(before, diff1, jnp.where(k >= 0.0, curve, curve1), k, u_back, w_back)
        else:
            f = flux(before, diff1, jnp.where(k >= 0.0, curve1, curve), k, u, w)
        state.append([cell, ahead, diff, curve])
        ends.append(f)
    f_first, f_second = -ends[0], -ends[1]
    for d in range(half_turn):
        if d < half_turn - 1:
            k, u, w, u_back, w_back = factors(d)
            positive = k >= 0.0
        for at in (0, half_turn):
            cell, ahead, diff, curve = state[at // half_turn]
            beyond = get((at + d + 2) % NDIR)
            diff_ahead = beyond - ahead
            curve_ahead = diff_ahead - diff
            if at == 0:
                if d < half_turn - 1:
                    f = flux(cell, diff, jnp.where(positive, curve, curve_ahead), k, u, w)
                else:
                    f = ends[1]
                put(d, cell - f + f_first)
                f_first = f
            else:
                if d < half_turn - 1:
                    f = flux(cell, diff, jnp.where(positive, curve_ahead, curve), k, u_back, w_back)
                else:
                    f = ends[0]
                put(at + d, cell + f - f_second)
                f_second = f
            state[at // half_turn] = [ahead, beyond, diff_ahead, curve_ahead]


def turn_kernel(q, tx, ty, out):
    for t in range(8):

        def put(d, value, t=t):
            out[d, t] = value

        turn_around(lambda d, t=t: q[d, t], put, tx[t], ty[t])


def gather_kernel(q, consts, matrix, own, sums, lhs):
    zero = jnp.zeros((8, 128), f32)
    for t in range(8):
        high, low = split(q[:, t].reshape(8 * NDIR, 128))
        lhs[:, 128 * t : 128 * t + 128] = high
        lhs[:, 1024 + 128 * t : 1024 + 128 * t + 128] = low
    moved = jnp.dot(lhs[...], matrix[...], preferred_element_type=f32)
    totals = [zero, zero]
    for half in range(2):
        own[half] = moved[:, 128 * half : 128 * half + 128].reshape(NDIR, 8, 128)
        totals[half] = jnp.sum(own[half], axis=0)
    level = consts[LEVEL]
    sums[...] = zero
    for half in range(2):
        sums[half : half + 1, :] = jnp.sum(totals[half], axis=0, keepdims=True)
        sums[2 + half : 3 + half, :] = jnp.sum(totals[half] * level, axis=0, keepdims=True)


def last_turn_kernel(own, static, gain, consts, early, flat0, flat1):
    for half, flat in ((0, flat0), (1, flat1)):
        point = static[half, 0]
        turning = lookup(point, consts, TAB_TURN)

        def put(d, value, half=half, flat=flat):
            flat[pl.ds(d, FREQ, stride=NDIR), :] = value * gain[d, half]

        turn_around(
            lambda d, half=half: own[half, d],
            put,
            turning * point[SLOPE_X : SLOPE_X + 1],
            turning * point[SLOPE_Y : SLOPE_Y + 1],
        )
        for low, high in ((0, 128), (128, 256), (256, 288)):
            early[128 * half : 128 * half + 128, low:high] = flat[low:high, :].T


def finish_kernel(early, static, sums, other, consts, spread, out):
    total = sums[...] + other[...]
    for half in range(2):
        energy = total[half : half + 1]
        moment = total[2 + half : 3 + half]
        mean_level = jnp.maximum(moment, 1.0) / jnp.maximum(energy, 1.0)
        mean = energy / NCOMP
        level = consts[LEVEL]
        breaking = break_coef * level * level / mean_level * (mean * mean)
        damping = static[half, 0, ICE : ICE + 1] * consts[ICE_RATE]
        loss = jnp.exp(-breaking - damping)
        parts = jnp.concatenate(split(loss.T), axis=1)
        wide = jnp.dot(parts, spread[...], preferred_element_type=f32)
        result = early[128 * half : 128 * half + 128, :] * wide
        out[8 * half : 8 * half + 8] = result.reshape(8, 16, NDIR * FREQ)


PARAMS = pltpu.CompilerParams(vmem_limit_bytes=40 * 2**20)


def call(kernel, ins, outs, scratch=(), name=None, space=pltpu.VMEM, dtype=f32):
    types = dtype if isinstance(dtype, list) else [dtype] * len(outs)
    return pl.pallas_call(
        kernel,
        out_shape=[jax.ShapeDtypeStruct(shape, kind) for shape, kind in zip(outs, types)],
        in_specs=[pl.BlockSpec(memory_space=space)] * ins,
        out_specs=[pl.BlockSpec(memory_space=pltpu.VMEM)] * len(outs),
        scratch_shapes=list(scratch),
        compiler_params=PARAMS,
        name=name,
    )


def swap(array, axis, first, closed=False):
    count = lax.axis_size(axis)
    pairs = []
    for i in range(first, count, 2):
        if i + 1 < count or closed:
            j = (i + 1) % count
            pairs += [(i, j), (j, i)]
    return lax.ppermute(array, axis, pairs)


def per_device(
    spectrum,
    sea_mask,
    ice_mask,
    depth_class,
    speed_table,
    refraction_table,
    depth_slope,
    wind_speed,
    wind_dir,
    ice_rate,
):
    tile = (8, 128)
    block = (8,) + tile
    slabs = (SLABS,) + tile
    inputs = [spectrum, sea_mask, ice_mask, depth_class, depth_slope, wind_speed, wind_dir]
    tables = [speed_table, refraction_table, ice_rate]
    own, speeds, turnings, ices = call(
        pack_kernel,
        10,
        [(2,) + slabs] + [x.shape for x in tables],
        [pltpu.VMEM(x.shape, x.dtype) for x in inputs]
        + [pltpu.VMEM((NDIR * FREQ, 128), f32)] * 2
        + [pltpu.VMEM((16, 128), f32), pltpu.SemaphoreType.DMA((10,))],
        name="pack",
        space=pltpu.HBM,
    )(*[pltpu.with_memory_space_constraint(x, pltpu.HBM) for x in inputs + tables])
    (to_second,) = call(functools.partial(column_kernel, True), 1, [slabs], name="column_far")(own)
    cols_second = swap(to_second, "lon", 1, True)
    (to_first,) = call(functools.partial(column_kernel, False), 1, [slabs], name="column_near")(own)
    cols_first = swap(to_first, "lon", 0, True)
    (edge_second,) = call(functools.partial(edge_kernel, True), 1, [slabs], name="edge_far")(own)
    rows_second = swap(edge_second, "lat", 1)
    (edge_first,) = call(functools.partial(edge_kernel, False), 1, [slabs], name="edge_near")(own)
    rows_first = swap(edge_first, "lat", 0)
    place, rims, shifts, gather, spread, consts = call(
        tables_kernel,
        3,
        [(1536, 1024), (512, 1024), (2, 256, 384), (2048, 256), (16, NDIR * FREQ), (20,) + tile],
        name="tables",
        dtype=[bf16] * 5 + [f32],
    )(speeds, turnings, ices)
    (gain,) = call(growth_kernel, 2, [(NDIR, 2) + tile], name="growth")(own, consts)
    (to_second,) = call(functools.partial(corner_kernel, True), 2, [slabs], name="corner_far")(cols_second, cols_first)
    rims_second = swap(to_second, "lat", 1)
    (to_first,) = call(functools.partial(corner_kernel, False), 2, [slabs], name="corner_near")(cols_second, cols_first)
    rims_first = swap(to_first, "lat", 0)
    (partial,) = call(
        place_kernel,
        6,
        [(SLABS,) + block],
        [pltpu.VMEM((8 * SLABS + 8, 1536), bf16)],
        name="place",
    )(own, cols_second, cols_first, rows_second, rows_first, place)
    q, taps, ky, tx, ty = call(
        rims_kernel,
        5,
        [(SLABS,) + block, (10, 2, 4) + block] + [block] * 3,
        [pltpu.VMEM((8 * SLABS + 8, 512), bf16)],
        name="rims",
    )(partial, rims_second, rims_first, consts, rims)
    cells = [(NDIR,) + block]
    for substep in range(ITERS):
        (q,) = call(lon_kernel, 3, cells, [pltpu.VMEM((4, 576, 384), f32)], name="lon")(q, taps, shifts)
        (q,) = call(lat_kernel, 3, cells, name="lat")(q, ky, consts)
        if substep < ITERS - 1:
            (q,) = call(turn_kernel, 3, cells, name="turn")(q, tx, ty)
    last, sums = call(
        gather_kernel, 3, [(2, NDIR) + tile, tile], [pltpu.VMEM((8 * NDIR, 2048), bf16)], name="gather"
    )(q, consts, gather)
    other = swap(sums, "band", 0)
    static = own[:, STATIC:]
    (early,) = call(
        last_turn_kernel,
        4,
        [(256, NDIR * FREQ)],
        [pltpu.VMEM((NDIR * FREQ, 128), f32)] * 2,
        name="last_turn",
    )(last, static, gain, consts)
    (out,) = call(finish_kernel, 6, [spectrum.shape], name="finish")(early, static, sums, other, consts, spread)
    return out


def solution(mesh):
    return jax.shard_map(
        per_device,
        mesh=mesh,
        in_specs=(
            P("lat", "lon", "band"),
            P("lat", "lon"),
            P("lat", "lon"),
            P("lat", "lon"),
            P(),
            P(),
            P(None, "lat", "lon"),
            P("lat", "lon"),
            P("lat", "lon"),
            P(),
        ),
        out_specs=P("lat", "lon", "band"),
        check_vma=False,
    )
```

```python
import functools
import math

import jax
import jax.numpy as jnp
import numpy as np
from jax import lax
from jax.experimental import pallas as pl
from jax.experimental.pallas import tpu as pltpu
from jax.sharding import PartitionSpec as P

NDIR = 36
NCOMP = 576
ITERS = 4
NCLASS = 8
FREQ = 8
HALO = 8
ROWS = 16
STATIC = NDIR
SLABS = NDIR + 1
SEA, DEPTH, SLOPE_X, SLOPE_Y, ICE, WIND, WDIR = range(7)

freq_ratio = 1.1
wind_gain = 0.12
break_coef = 0.05
south_edge = -30.0
band_span = 60.0

COS = [math.cos(2.0 * math.pi * d / NDIR) for d in range(NDIR)]
SIN = [math.sin(2.0 * math.pi * d / NDIR) for d in range(NDIR)]
COS_FACE = [math.cos(2.0 * math.pi * (d + 0.5) / NDIR) for d in range(NDIR)]
SIN_FACE = [math.sin(2.0 * math.pi * (d + 0.5) / NDIR) for d in range(NDIR)]

TAB_SPEED, TAB_TURN, STRETCH, LIVE, ICE_RATE, LEVEL = 0, 8, 16, 17, 18, 19

f32 = jnp.float32
bf16 = jnp.bfloat16


def lanes():
    return lax.broadcasted_iota(jnp.int32, (8, 128), 1)


def roll(x, shift):
    shift = shift % 128
    return pltpu.roll(x, shift, 1) if shift else x


def is_even(axis):
    return lax.axis_index(axis) % 2 == 0


def pack_kernel(*refs):
    sources, own, tables = refs[:10], refs[10], refs[11:14]
    landed = refs[14:21]
    flat0, flat1, wide, sems = refs[21:]
    copies = [
        pltpu.make_async_copy(src, dst, sems.at[i]) for i, (src, dst) in enumerate(zip(sources, landed + tables))
    ]
    for copy in copies:
        copy.start()
    wide[...] = jnp.zeros_like(wide)
    group = lax.broadcasted_iota(jnp.int32, (16, 128), 1) // 16
    row = lax.broadcasted_iota(jnp.int32, (16, 128), 0) % 8
    own[:, STATIC] = jnp.zeros((2, 8, 128), f32)
    for copy in copies:
        copy.wait()
    spec, sea, ice, depth, slope, wspeed, wdir = landed

    def place(field, values):
        wide[:, :16] = values
        moved = pltpu.roll(wide[...], 0, 1, stride=16, stride_axis=0)
        kept = jnp.where(group == row, moved, 0.0)
        for half in range(2):
            own[half, STATIC, field : field + 1, :] = jnp.sum(
                kept[8 * half : 8 * half + 8], axis=0, keepdims=True
            )

    place(SEA, sea[...].astype(f32))
    place(DEPTH, depth[...].astype(f32))
    place(SLOPE_X, slope[0])
    place(SLOPE_Y, slope[1])
    place(ICE, ice[...].astype(f32))
    place(WIND, wspeed[...])
    place(WDIR, wdir[...])
    grid = spec[...].reshape(256, NDIR * FREQ)
    for low, high in ((0, 128), (128, 256), (256, 288)):
        turned = grid[:, low:high].T
        flat0[low:high, :] = turned[:, :128]
        flat1[low:high, :] = turned[:, 128:]
    sea0 = own[0, STATIC, SEA : SEA + 1, :]
    sea1 = own[1, STATIC, SEA : SEA + 1, :]
    for d in range(NDIR):
        own[0, d] = flat0[pl.ds(d, FREQ, stride=NDIR), :] * sea0
        own[1, d] = flat1[pl.ds(d, FREQ, stride=NDIR), :] * sea1


def column_kernel(second, own, message):
    inner = lanes() % 16
    to_east = is_even("lon") != second
    for slab in range(SLABS):
        own0, own1 = own[0, slab], own[1, slab]
        east = jnp.where(inner >= 8, own0, roll(own1, -8))
        west = jnp.where(inner < 8, own0, roll(own1, 8))
        message[slab] = jnp.where(to_east, east, west)


def edge_kernel(second, own, edge):
    even = is_even("lat")
    if second:
        edge[...] = jnp.where(even, own[0], own[1])
    else:
        edge[...] = jnp.where(even, own[1], own[0])


def growth_kernel(own, consts, gain):
    for half in range(2):
        point = own[half, STATIC]
        turn = point[WDIR : WDIR + 1]
        cos_w = jnp.cos(turn)
        sin_w = jnp.sin(turn)
        force = wind_gain * point[WIND : WIND + 1] * consts[LEVEL]
        share = point[SEA : SEA + 1]
        for d in range(NDIR):
            along = jnp.maximum(COS[d] * cos_w + SIN[d] * sin_w, 0.0)
            gain[d, half] = jnp.exp(force * along) * share


def tables_kernel(speed_table, refraction_table, ice_rate, place, rims, shifts, gather, spread, consts):
    first = lax.axis_index("band") * FREQ
    sub = lax.broadcasted_iota(jnp.int32, (8, 128), 0)
    mine = lanes() == first + sub

    def column(row):
        picked = jnp.where(mine, jnp.broadcast_to(row, (8, 128)), 0.0)
        return jnp.broadcast_to(jnp.sum(picked, axis=1, keepdims=True), (8, 128))

    def widen(values):
        return jnp.concatenate([values, jnp.zeros((values.shape[0], 112), f32)], axis=1)

    for at, table in ((TAB_SPEED, speed_table), (TAB_TURN, refraction_table)):
        wide = widen(table[...])
        for c in range(NCLASS):
            consts[at + c] = column(wide[c : c + 1])
    consts[ICE_RATE] = column(widen(ice_rate[...].reshape(1, 16)))
    consts[LEVEL] = jnp.exp(math.log(freq_ratio) * (first + sub).astype(f32))
    lat = lax.axis_index("lat")
    lats = lax.axis_size("lat")
    group = lanes() // 32
    rows = lat * ROWS - HALO + 8 * group + sub
    latitude = (south_edge + band_span * (rows.astype(f32) + 0.5) / (ROWS * lats)) * (math.pi / 180.0)
    consts[STRETCH] = 1.0 / jnp.cos(latitude)
    ghost = ((group == 0) & (lat == 0)) | ((group == 3) & (lat == lats - 1))
    consts[LIVE] = jnp.where(ghost, 0.0, 1.0)
    comp = lax.broadcasted_iota(jnp.int32, (16, NDIR * FREQ), 1) // NDIR
    freq = lax.broadcasted_iota(jnp.int32, (16, NDIR * FREQ), 0) % FREQ
    spread[...] = (comp == freq).astype(f32).astype(bf16)

    chunk = lax.broadcasted_iota(jnp.int32, (16, 128), 0)
    lane = lax.broadcasted_iota(jnp.int32, (16, 128), 1)
    low = chunk < 8
    targets = [
        40 + chunk,
        72 + chunk,
        jnp.where(low, 64 + chunk, 24 + chunk),
        jnp.where(low, 56 + chunk, 80 + chunk),
        8 + chunk,
        104 + chunk,
    ]
    corners = [jnp.where(low, chunk, 16 + chunk), jnp.where(low, 120 + chunk, 88 + chunk)]
    for matrix, lists in ((place, targets), (rims, corners)):
        matrix[...] = jnp.zeros_like(matrix)
        for s, target in enumerate(lists):
            stripe = (lane == target).astype(f32).astype(bf16)
            for part in range(2):
                for t in range(8):
                    row = part * 128 * len(lists) + s * 128 + 16 * t
                    matrix[row : row + 16, 128 * t : 128 * t + 128] = stripe
    row = lax.broadcasted_iota(jnp.int32, (128, 128), 0)
    col = lax.broadcasted_iota(jnp.int32, (128, 128), 1)
    for sign, taps in ((0, FORTH_TAPS), (1, BACK_TAPS)):
        for i, tap in enumerate(taps):
            moved = (row == (col + tap) % 128).astype(f32).astype(bf16)
            for part in range(2):
                shifts[sign, 128 * part : 128 * part + 128, 128 * i : 128 * i + 128] = moved
    for t in range(8):
        for half in range(2):
            from_row = 40 + 32 * half + col % 16
            moved = ((col // 16 == t) & (row == from_row)).astype(f32).astype(bf16)
            for part in range(2):
                at = part * 1024 + 128 * t
                gather[at : at + 128, 128 * half : 128 * half + 128] = moved


def corner_kernel(cols_second, cols_first, rows_second, rows_first, consts, rim):
    del rows_second, rows_first, consts
    low = lanes() % 16 < 8
    even_lon = is_even("lon")
    west_low = low == is_even("lat")
    for slab in range(SLABS):
        one, two = cols_first[slab], cols_second[slab]
        east = jnp.where(even_lon, one, two)
        west = jnp.where(even_lon, two, one)
        rim[0, slab] = jnp.where(west_low, west, east)
        rim[1, slab] = jnp.where(west_low, east, west)


def relay_kernel(rims_pair, beyond):
    beyond[...] = rims_pair[1]


def split(x):
    high = x.astype(bf16)
    return high, (x - high.astype(f32)).astype(bf16)


def fill_parts(lhs, count, s, array):
    x = jnp.concatenate([array.reshape(8 * SLABS, 128), jnp.zeros((8, 128), f32)], axis=0)
    high, low = split(x)
    lhs[:, 128 * s : 128 * s + 128] = high
    lhs[:, 128 * (count + s) : 128 * (count + s) + 128] = low


def place_kernel(own, cols_second, cols_first, rows_second, rows_first, matrix, q, lhs):
    even_lon = is_even("lon")
    even_lat = is_even("lat")
    fill_parts(lhs, 6, 0, own[0])
    fill_parts(lhs, 6, 1, own[1])
    fill_parts(lhs, 6, 2, jnp.where(even_lon, cols_second[...], cols_first[...]))
    fill_parts(lhs, 6, 3, jnp.where(even_lon, cols_first[...], cols_second[...]))
    fill_parts(lhs, 6, 4, jnp.where(even_lat, rows_second[...], rows_first[...]))
    fill_parts(lhs, 6, 5, jnp.where(even_lat, rows_first[...], rows_second[...]))
    for pair in range(4):
        moved = jnp.dot(lhs[...], matrix[:, 256 * pair : 256 * pair + 256], preferred_element_type=f32)
        for i in range(2):
            q[:, 2 * pair + i] = moved[: 8 * SLABS, 128 * i : 128 * i + 128].reshape(SLABS, 8, 128)


def lookup(point, consts, at):
    depth = jnp.broadcast_to(point[DEPTH : DEPTH + 1], (8, 128))
    value = jnp.zeros((8, 128), f32)
    for c in range(NCLASS):
        value = jnp.where(depth == float(c), consts[at + c], value)
    return value * point[SEA : SEA + 1]


def rims_kernel(partial, rims_second, rims_pair, consts, matrix, q, taps, ky, tx, ty, lhs):
    even_lat = is_even("lat")
    fill_parts(lhs, 2, 0, jnp.where(even_lat, rims_second[...], rims_pair[0]))
    fill_parts(lhs, 2, 1, jnp.where(even_lat, rims_pair[0], rims_second[...]))
    for pair in range(4):
        moved = jnp.dot(lhs[...], matrix[:, 256 * pair : 256 * pair + 256], preferred_element_type=f32)
        for i in range(2):
            t = 2 * pair + i
            q[:, t] = partial[:, t] + moved[: 8 * SLABS, 128 * i : 128 * i + 128].reshape(SLABS, 8, 128)

    speed = []
    for t in range(8):
        point = q[STATIC, t]
        pace = lookup(point, consts, TAB_SPEED)
        turning = lookup(point, consts, TAB_TURN)
        speed.append(pace)
        tx[t] = turning * point[SLOPE_X : SLOPE_X + 1]
        ty[t] = turning * point[SLOPE_Y : SLOPE_Y + 1]
        stretch = consts[STRETCH, t : t + 1, :]
        right = 0.5 * (pace + roll(pace, -1)) * stretch
        left = 0.5 * (pace + roll(pace, 1)) * stretch
        for base in range(10):
            a1, b1, c1 = weights(COS[base] * right)
            a0, b0, c0 = weights(COS[base] * left)
            taps[base, 0, 0, t] = 1.0 - a1 + b0
            taps[base, 0, 1, t] = -b1
            taps[base, 0, 2, t] = a0 - c1
            taps[base, 0, 3, t] = c0
            taps[base, 1, 0, t] = 1.0 + b1 - a0
            taps[base, 1, 1, t] = a1 - c0
            taps[base, 1, 2, t] = -b0
            taps[base, 1, 3, t] = c1
    for t in range(8):
        ahead = speed[t + 1] if t < 7 else roll(speed[0], -32)
        ky[t] = 0.5 * (speed[t] + ahead)


def flux(q, diff, curve, k, u, w):
    return k * (q + u * (diff - w * curve))


def halves(k):
    return 0.5 - 0.5 * k, (1.0 / 3.0) + (1.0 / 3.0) * k


def weights(k):
    u, w = halves(k)
    bend = k * u * w
    return k - k * u + 2.0 * bend, k * u - bend, -bend


FORTH_TAPS = (-1, -2)
BACK_TAPS = (-1, 2)


def lon_kernel(q, taps, shifts, out, moved):
    for quadrant, sign in ((0, 0), (3, 0), (1, 1), (2, 1)):
        x = q[9 * quadrant : 9 * quadrant + 9].reshape(576, 128)
        lhs = jnp.concatenate(split(x), axis=1)
        moved[quadrant] = jnp.dot(lhs, shifts[sign], preferred_element_type=f32)
    for sign in range(2):
        for base in range(10):
            if base == 0:
                dirs = [[0], [18]][sign]
            elif base == 9:
                dirs = [[27], [9]][sign]
            else:
                dirs = [[base, 36 - base], [18 - base, 18 + base]][sign]
            for t in range(8):
                tap = [taps[base, sign, i, t] for i in range(4)]
                for d in dirs:
                    at = 64 * (d % 9) + 8 * t
                    cell = q[d, t]
                    near = [moved[d // 9, at : at + 8, 128 * i : 128 * i + 128] for i in range(2)]
                    out[d, t] = (tap[0] * cell + tap[1] * roll(cell, -1)) + (tap[2] * near[0] + tap[3] * near[1])


def lat_kernel(q, ky, consts, out, sums=None):
    live = consts[LIVE]
    totals = [jnp.zeros((8, 128), f32)] * 8

    def put(d, t, value):
        out[d, t] = value
        if sums is not None:
            totals[t] = totals[t] + value

    def forth(d, ks, us, ws):
        tiles = [q[d, t] for t in range(8)]
        diff = [tiles[t + 1] - tiles[t] for t in range(7)]
        diff.append(roll(tiles[0], -32) - tiles[7])
        before = roll(diff[7], 32)
        fluxes = []
        for t in range(8):
            fluxes.append(flux(tiles[t], diff[t], diff[t] - before, ks[t], us[t], ws[t]))
            before = diff[t]
        behind = roll(fluxes[7], 32)
        for t in range(8):
            put(d, t, (tiles[t] - fluxes[t] + behind) * live)
            behind = fluxes[t]

    def back(d, ks, us, ws):
        tiles = [q[d, t] for t in range(8)]
        ahead = tiles[1:] + [roll(tiles[0], -32)]
        diff = [tiles[t] - ahead[t] for t in range(8)]
        after = diff[1:] + [roll(diff[0], -32)]
        fluxes = [flux(ahead[t], diff[t], diff[t] - after[t], ks[t], us[t], ws[t]) for t in range(8)]
        behind = roll(fluxes[7], 32)
        for t in range(8):
            put(d, t, (tiles[t] + fluxes[t] - behind) * live)
            behind = fluxes[t]

    for base in range(10):
        ks = [SIN[base] * ky[t] for t in range(8)]
        us, ws = zip(*[halves(k) for k in ks])
        if base == 0:
            north, south = [0], [18]
        elif base == 9:
            north, south = [9], [27]
        else:
            north, south = [base, 18 - base], [18 + base, 36 - base]
        for d in north:
            forth(d, ks, us, ws)
        for d in south:
            back(d, ks, us, ws)
    if sums is None:
        return
    lane = lanes()
    halves_of = [jnp.zeros((8, 128), f32)] * 2
    for t in range(8):
        moved = roll(totals[t], 16 * t - 40)
        halves_of[0] = jnp.where(lane // 16 == t, moved, halves_of[0])
        halves_of[1] = jnp.where(lane // 16 == (t + 2) % 8, moved, halves_of[1])
    halves_of[1] = roll(halves_of[1], -32)
    sums[...] = jnp.zeros((8, 128), f32)
    for half in range(2):
        sums[half : half + 1, :] = jnp.sum(halves_of[half], axis=0, keepdims=True)
        sums[2 + half : 3 + half, :] = jnp.sum(halves_of[half] * consts[LEVEL], axis=0, keepdims=True)


def turn_around(get, put, x, y):
    def factors(d):
        k = SIN_FACE[d] * x - COS_FACE[d] * y
        half, third = 0.5 * k, (1.0 / 3.0) * k
        return k, 0.5 - half, 1.0 / 3.0 + third, 0.5 + half, 1.0 / 3.0 - third

    half_turn = NDIR // 2
    k, u, w, u_back, w_back = factors(half_turn - 1)
    state = []
    ends = []
    for at in (0, half_turn):
        cell, ahead = get(at), get(at + 1)
        before, last = get((at - 1) % NDIR), get((at - 2) % NDIR)
        diff = ahead - cell
        diff1 = cell - before
        curve = diff - diff1
        curve1 = diff1 - (before - last)
        if at == 0:
            f = flux(before, diff1, jnp.where(k >= 0.0, curve, curve1), k, u_back, w_back)
        else:
            f = flux(before, diff1, jnp.where(k >= 0.0, curve1, curve), k, u, w)
        state.append([cell, ahead, diff, curve])
        ends.append(f)
    f_first, f_second = -ends[0], -ends[1]
    for d in range(half_turn):
        if d < half_turn - 1:
            k, u, w, u_back, w_back = factors(d)
            positive = k >= 0.0
        for at in (0, half_turn):
            cell, ahead, diff, curve = state[at // half_turn]
            beyond = get((at + d + 2) % NDIR)
            diff_ahead = beyond - ahead
            curve_ahead = diff_ahead - diff
            if at == 0:
                if d < half_turn - 1:
                    f = flux(cell, diff, jnp.where(positive, curve, curve_ahead), k, u, w)
                else:
                    f = ends[1]
                put(d, cell - f + f_first)
                f_first = f
            else:
                if d < half_turn - 1:
                    f = flux(cell, diff, jnp.where(positive, curve_ahead, curve), k, u_back, w_back)
                else:
                    f = ends[0]
                put(at + d, cell + f - f_second)
                f_second = f
            state[at // half_turn] = [ahead, beyond, diff_ahead, curve_ahead]


def turn_kernel(q, tx, ty, out):
    for t in range(8):

        def put(d, value, t=t):
            out[d, t] = value

        turn_around(lambda d, t=t: q[d, t], put, tx[t], ty[t])


def gather_kernel(q, matrix, own, lhs):
    for t in range(8):
        high, low = split(q[:, t].reshape(8 * NDIR, 128))
        lhs[:, 128 * t : 128 * t + 128] = high
        lhs[:, 1024 + 128 * t : 1024 + 128 * t + 128] = low
    moved = jnp.dot(lhs[...], matrix[...], preferred_element_type=f32)
    for half in range(2):
        own[half] = moved[:, 128 * half : 128 * half + 128].reshape(NDIR, 8, 128)


def last_turn_kernel(own, static, gain, consts, early, flat0, flat1):
    for half, flat in ((0, flat0), (1, flat1)):
        point = static[half, 0]
        turning = lookup(point, consts, TAB_TURN)

        def put(d, value, half=half, flat=flat):
            flat[pl.ds(d, FREQ, stride=NDIR), :] = value * gain[d, half]

        turn_around(
            lambda d, half=half: own[half, d],
            put,
            turning * point[SLOPE_X : SLOPE_X + 1],
            turning * point[SLOPE_Y : SLOPE_Y + 1],
        )
        for low, high in ((0, 128), (128, 256), (256, 288)):
            early[128 * half : 128 * half + 128, low:high] = flat[low:high, :].T


def finish_kernel(early, static, sums, other, consts, spread, out, ready, sems):
    total = sums[...] + other[...]
    for half in range(2):
        energy = total[half : half + 1]
        moment = total[2 + half : 3 + half]
        mean_level = jnp.maximum(moment, 1.0) / jnp.maximum(energy, 1.0)
        mean = energy / NCOMP
        level = consts[LEVEL]
        breaking = break_coef * level * level / mean_level * (mean * mean)
        damping = static[half, 0, ICE : ICE + 1] * consts[ICE_RATE]
        loss = jnp.exp(-breaking - damping)
        parts = jnp.concatenate(split(loss.T), axis=1)
        wide = jnp.dot(parts, spread[...], preferred_element_type=f32)
        result = early[128 * half : 128 * half + 128, :] * wide
        mine = pl.ds(8 * half, 8)
        ready[mine] = result.reshape(8, 16, NDIR * FREQ)
        pltpu.make_async_copy(ready.at[mine], out.at[mine], sems.at[half]).start()
    for half in range(2):
        mine = pl.ds(8 * half, 8)
        pltpu.make_async_copy(ready.at[mine], out.at[mine], sems.at[half]).wait()


PARAMS = pltpu.CompilerParams(vmem_limit_bytes=40 * 2**20)


def call(kernel, ins, outs, scratch=(), name=None, space=pltpu.VMEM, dtype=f32, result=pltpu.VMEM):
    types = dtype if isinstance(dtype, list) else [dtype] * len(outs)
    return pl.pallas_call(
        kernel,
        out_shape=[jax.ShapeDtypeStruct(shape, kind) for shape, kind in zip(outs, types)],
        in_specs=[pl.BlockSpec(memory_space=space)] * ins,
        out_specs=[pl.BlockSpec(memory_space=result)] * len(outs),
        scratch_shapes=list(scratch),
        compiler_params=PARAMS,
        name=name,
    )


def swap(array, axis, first, closed=False):
    count = lax.axis_size(axis)
    pairs = []
    for i in range(first, count, 2):
        if i + 1 < count or closed:
            j = (i + 1) % count
            pairs += [(i, j), (j, i)]
    return lax.ppermute(array, axis, pairs)


def skip(array, axis):
    count = lax.axis_size(axis)
    pairs = [(i, i + 2) for i in range(0, count - 2, 2)] + [(i, i - 2) for i in range(3, count, 2)]
    return lax.ppermute(array, axis, pairs)


def per_device(
    spectrum,
    sea_mask,
    ice_mask,
    depth_class,
    speed_table,
    refraction_table,
    depth_slope,
    wind_speed,
    wind_dir,
    ice_rate,
):
    tile = (8, 128)
    block = (8,) + tile
    slabs = (SLABS,) + tile
    inputs = [spectrum, sea_mask, ice_mask, depth_class, depth_slope, wind_speed, wind_dir]
    tables = [speed_table, refraction_table, ice_rate]
    own, speeds, turnings, ices = call(
        pack_kernel,
        10,
        [(2,) + slabs] + [x.shape for x in tables],
        [pltpu.VMEM(x.shape, x.dtype) for x in inputs]
        + [pltpu.VMEM((NDIR * FREQ, 128), f32)] * 2
        + [pltpu.VMEM((16, 128), f32), pltpu.SemaphoreType.DMA((10,))],
        name="pack",
        space=pltpu.HBM,
    )(*[pltpu.with_memory_space_constraint(x, pltpu.HBM) for x in inputs + tables])
    (to_second,) = call(functools.partial(column_kernel, True), 1, [slabs], name="column_far")(own)
    cols_second = swap(to_second, "lon", 1, True)
    (to_first,) = call(functools.partial(column_kernel, False), 1, [slabs], name="column_near")(own)
    cols_first = swap(to_first, "lon", 0, True)
    (edge_second,) = call(functools.partial(edge_kernel, True), 1, [slabs], name="edge_far")(own)
    rows_second = swap(edge_second, "lat", 1)
    (edge_first,) = call(functools.partial(edge_kernel, False), 1, [slabs], name="edge_near")(own)
    rows_first = swap(edge_first, "lat", 0)
    place, rims, shifts, gather, spread, consts = call(
        tables_kernel,
        3,
        [(1536, 1024), (512, 1024), (2, 256, 256), (2048, 256), (16, NDIR * FREQ), (20,) + tile],
        name="tables",
        dtype=[bf16] * 5 + [f32],
    )(speeds, turnings, ices)
    (gain,) = call(growth_kernel, 2, [(NDIR, 2) + tile], name="growth")(own, consts)
    (rim,) = call(corner_kernel, 5, [(2,) + slabs], name="corner")(
        cols_second, cols_first, rows_second, rows_first, consts
    )
    rims_pair = swap(rim, "lat", 0)
    (beyond,) = call(relay_kernel, 1, [slabs], name="relay")(rims_pair)
    rims_second = skip(beyond, "lat")
    (partial,) = call(
        place_kernel,
        6,
        [(SLABS,) + block],
        [pltpu.VMEM((8 * SLABS + 8, 1536), bf16)],
        name="place",
    )(own, cols_second, cols_first, rows_second, rows_first, place)
    q, taps, ky, tx, ty = call(
        rims_kernel,
        5,
        [(SLABS,) + block, (10, 2, 4) + block] + [block] * 3,
        [pltpu.VMEM((8 * SLABS + 8, 512), bf16)],
        name="rims",
    )(partial, rims_second, rims_pair, consts, rims)
    cells = [(NDIR,) + block]
    for substep in range(ITERS):
        (q,) = call(lon_kernel, 3, cells, [pltpu.VMEM((4, 576, 256), f32)], name="lon")(q, taps, shifts)
        if substep == ITERS - 1:
            q, sums = call(lat_kernel, 3, cells + [tile], name="lat_sums")(q, ky, consts)
        else:
            (q,) = call(lat_kernel, 3, cells, name="lat")(q, ky, consts)
            (q,) = call(turn_kernel, 3, cells, name="turn")(q, tx, ty)
    other = swap(sums, "band", 0)
    (last,) = call(
        gather_kernel, 2, [(2, NDIR) + tile], [pltpu.VMEM((8 * NDIR, 2048), bf16)], name="gather"
    )(q, gather)
    static = own[:, STATIC:]
    (early,) = call(
        last_turn_kernel,
        4,
        [(256, NDIR * FREQ)],
        [pltpu.VMEM((NDIR * FREQ, 128), f32)] * 2,
        name="last_turn",
    )(last, static, gain, consts)
    (out,) = call(
        finish_kernel,
        6,
        [spectrum.shape],
        [pltpu.VMEM(spectrum.shape, f32), pltpu.SemaphoreType.DMA((2,))],
        name="finish",
        result=pltpu.HBM,
    )(early, static, sums, other, consts, spread)
    return out


def solution(mesh):
    return jax.shard_map(
        per_device,
        mesh=mesh,
        in_specs=(
            P("lat", "lon", "band"),
            P("lat", "lon"),
            P("lat", "lon"),
            P("lat", "lon"),
            P(),
            P(),
            P(None, "lat", "lon"),
            P("lat", "lon"),
            P("lat", "lon"),
            P(),
        ),
        out_specs=P("lat", "lon", "band"),
        check_vma=False,
    )
```

```python
import functools
import math

import jax
import jax.numpy as jnp
import numpy as np
from jax import lax
from jax.experimental import pallas as pl
from jax.experimental.pallas import tpu as pltpu
from jax.sharding import PartitionSpec as P

NDIR = 36
NCOMP = 576
ITERS = 4
NCLASS = 8
FREQ = 8
HALO = 8
ROWS = 16
STATIC = NDIR
SLABS = NDIR + 1
SEA, DEPTH, SLOPE_X, SLOPE_Y, ICE, WIND, WDIR = range(7)

freq_ratio = 1.1
wind_gain = 0.12
break_coef = 0.05
south_edge = -30.0
band_span = 60.0

COS = [math.cos(2.0 * math.pi * d / NDIR) for d in range(NDIR)]
SIN = [math.sin(2.0 * math.pi * d / NDIR) for d in range(NDIR)]
COS_FACE = [math.cos(2.0 * math.pi * (d + 0.5) / NDIR) for d in range(NDIR)]
SIN_FACE = [math.sin(2.0 * math.pi * (d + 0.5) / NDIR) for d in range(NDIR)]

TAB_SPEED, TAB_TURN, STRETCH, LIVE, ICE_RATE, LEVEL = 0, 8, 16, 17, 18, 19

f32 = jnp.float32
bf16 = jnp.bfloat16


def lanes():
    return lax.broadcasted_iota(jnp.int32, (8, 128), 1)


def roll(x, shift):
    shift = shift % 128
    return pltpu.roll(x, shift, 1) if shift else x


def is_even(axis):
    return lax.axis_index(axis) % 2 == 0


def pack_kernel(*refs):
    sources, own, tables = refs[:10], refs[10], refs[11:14]
    landed = refs[14:21]
    flat0, flat1, wide, sems = refs[21:]
    copies = [
        pltpu.make_async_copy(src, dst, sems.at[i]) for i, (src, dst) in enumerate(zip(sources, landed + tables))
    ]
    for copy in copies:
        copy.start()
    wide[...] = jnp.zeros_like(wide)
    group = lax.broadcasted_iota(jnp.int32, (16, 128), 1) // 16
    row = lax.broadcasted_iota(jnp.int32, (16, 128), 0) % 8
    own[:, STATIC] = jnp.zeros((2, 8, 128), f32)
    for copy in copies:
        copy.wait()
    spec, sea, ice, depth, slope, wspeed, wdir = landed

    def place(field, values):
        wide[:, :16] = values
        moved = pltpu.roll(wide[...], 0, 1, stride=16, stride_axis=0)
        kept = jnp.where(group == row, moved, 0.0)
        for half in range(2):
            own[half, STATIC, field : field + 1, :] = jnp.sum(
                kept[8 * half : 8 * half + 8], axis=0, keepdims=True
            )

    place(SEA, sea[...].astype(f32))
    place(DEPTH, depth[...].astype(f32))
    place(SLOPE_X, slope[0])
    place(SLOPE_Y, slope[1])
    place(ICE, ice[...].astype(f32))
    place(WIND, wspeed[...])
    place(WDIR, wdir[...])
    grid = spec[...].reshape(256, NDIR * FREQ)
    for low, high in ((0, 128), (128, 256), (256, 288)):
        turned = grid[:, low:high].T
        flat0[low:high, :] = turned[:, :128]
        flat1[low:high, :] = turned[:, 128:]
    sea0 = own[0, STATIC, SEA : SEA + 1, :]
    sea1 = own[1, STATIC, SEA : SEA + 1, :]
    for d in range(NDIR):
        own[0, d] = flat0[pl.ds(d, FREQ, stride=NDIR), :] * sea0
        own[1, d] = flat1[pl.ds(d, FREQ, stride=NDIR), :] * sea1


WEST_PAIRS = [(33, 0), (34, 1), (35, 2)]
EAST_PAIRS = [(15, 18), (16, 19), (17, 20)]


def slots(pairs):
    paired = [d for pair in pairs for d in pair]
    return [d for d in range(SLABS) if d not in paired]


SENT = SLABS - 3


def column_kernel(second, own, message):
    inner = lanes() % 16
    to_east = is_even("lon") != second
    from_own0 = (inner >= 8) == to_east
    shift = jnp.where(to_east, 120, 8)

    def edge(slab):
        return jnp.where(from_own0, own[0, slab], pltpu.roll(own[1, slab], shift, 1))

    for i, (east, west) in enumerate(zip(slots(EAST_PAIRS), slots(WEST_PAIRS))):
        if east == west:
            message[i] = edge(east)
        else:
            message[i] = edge(jnp.where(to_east, east, west))
    near = (inner % 8 >= 4) == to_east
    for i, (east, west) in enumerate(zip(EAST_PAIRS, WEST_PAIRS)):
        one = edge(jnp.where(to_east, east[0], west[0]))
        two = edge(jnp.where(to_east, east[1], west[1]))
        message[SENT - 3 + i] = jnp.where(near, one, pltpu.roll(two, jnp.where(to_east, 124, 4), 1))


NORTH_PAIRS = [(24, 27), (25, 28), (26, 29)]
SOUTH_PAIRS = [(6, 9), (7, 10), (8, 11)]


def edge_kernel(second, own, message):
    to_north = is_even("lat") != second
    for i, (north, south) in enumerate(zip(slots(NORTH_PAIRS), slots(SOUTH_PAIRS))):
        message[i] = jnp.where(to_north, own[1, north], own[0, south])
    near = (lanes() >= 64) == to_north
    for i, (north, south) in enumerate(zip(NORTH_PAIRS, SOUTH_PAIRS)):
        one = jnp.where(to_north, own[1, north[0]], own[0, south[0]])
        two = jnp.where(to_north, own[1, north[1]], own[0, south[1]])
        message[SENT - 3 + i] = jnp.where(near, one, roll(two, 64))


def growth_kernel(own, consts, gain):
    for half in range(2):
        point = own[half, STATIC]
        turn = point[WDIR : WDIR + 1]
        cos_w = jnp.cos(turn)
        sin_w = jnp.sin(turn)
        force = wind_gain * point[WIND : WIND + 1] * consts[LEVEL]
        share = point[SEA : SEA + 1]
        for d in range(NDIR):
            along = jnp.maximum(COS[d] * cos_w + SIN[d] * sin_w, 0.0)
            gain[d, half] = jnp.exp(force * along) * share


def tables_kernel(speed_table, refraction_table, ice_rate, place, rims, shifts, gather, spread, consts):
    first = lax.axis_index("band") * FREQ
    sub = lax.broadcasted_iota(jnp.int32, (8, 128), 0)
    mine = lanes() == first + sub

    def column(row):
        picked = jnp.where(mine, jnp.broadcast_to(row, (8, 128)), 0.0)
        return jnp.broadcast_to(jnp.sum(picked, axis=1, keepdims=True), (8, 128))

    def widen(values):
        return jnp.concatenate([values, jnp.zeros((values.shape[0], 112), f32)], axis=1)

    for at, table in ((TAB_SPEED, speed_table), (TAB_TURN, refraction_table)):
        wide = widen(table[...])
        for c in range(NCLASS):
            consts[at + c] = column(wide[c : c + 1])
    consts[ICE_RATE] = column(widen(ice_rate[...].reshape(1, 16)))
    consts[LEVEL] = jnp.exp(math.log(freq_ratio) * (first + sub).astype(f32))
    lat = lax.axis_index("lat")
    lats = lax.axis_size("lat")
    group = lanes() // 32
    rows = lat * ROWS - HALO + 8 * group + sub
    latitude = (south_edge + band_span * (rows.astype(f32) + 0.5) / (ROWS * lats)) * (math.pi / 180.0)
    consts[STRETCH] = 1.0 / jnp.cos(latitude)
    ghost = ((group == 0) & (lat == 0)) | ((group == 3) & (lat == lats - 1))
    consts[LIVE] = jnp.where(ghost, 0.0, 1.0)
    comp = lax.broadcasted_iota(jnp.int32, (32, 384), 1) // NDIR
    freq = lax.broadcasted_iota(jnp.int32, (32, 384), 0) % 16
    for half in range(2):
        spread[:, 384 * half : 384 * half + 384] = (comp == freq - 8 * half).astype(f32).astype(bf16)

    chunk = lax.broadcasted_iota(jnp.int32, (16, 128), 0)
    lane = lax.broadcasted_iota(jnp.int32, (16, 128), 1)
    low = chunk < 8
    targets = [
        40 + chunk,
        72 + chunk,
        jnp.where(low, 64 + chunk, 24 + chunk),
        jnp.where(low, 56 + chunk, 80 + chunk),
        8 + chunk,
        104 + chunk,
    ]
    corners = [jnp.where(low, chunk, 16 + chunk), jnp.where(low, 120 + chunk, 88 + chunk)]
    for matrix, lists in ((place, targets), (rims, corners)):
        matrix[...] = jnp.zeros_like(matrix)
        for s, target in enumerate(lists):
            stripe = (lane == target).astype(f32).astype(bf16)
            for part in range(2):
                for t in range(8):
                    row = part * 128 * len(lists) + s * 128 + 16 * t
                    matrix[row : row + 16, 128 * t : 128 * t + 128] = stripe
    row = lax.broadcasted_iota(jnp.int32, (128, 128), 0)
    col = lax.broadcasted_iota(jnp.int32, (128, 128), 1)
    for sign, taps in ((0, FORTH_TAPS), (1, BACK_TAPS)):
        for i, tap in enumerate(taps):
            moved = (row == (col + tap) % 128).astype(f32).astype(bf16)
            for part in range(2):
                shifts[sign, 128 * part : 128 * part + 128, 128 * i : 128 * i + 128] = moved
    for t in range(8):
        for half in range(2):
            from_row = 40 + 32 * half + col % 16
            moved = ((col // 16 == t) & (row == from_row)).astype(f32).astype(bf16)
            for part in range(2):
                at = part * 1024 + 128 * t
                gather[at : at + 128, 128 * half : 128 * half + 128] = moved


def unpack(even, first, second, pairs, out, back):
    full = slots(pairs)
    for i in range(SENT):
        got = jnp.where(even, first[i], second[i])
        if i < len(full):
            out[full[i]] = got
        else:
            pair = pairs[i - len(full)]
            out[pair[0]] = got
            out[pair[1]] = roll(got, back)


def unpack_kernel(cols_second, cols_first, rows_second, rows_first, consts, west, east):
    del rows_second, rows_first, consts
    even = is_even("lon")
    unpack(even, cols_second, cols_first, EAST_PAIRS, west, 4)
    unpack(even, cols_first, cols_second, WEST_PAIRS, east, -4)


def unpack_rows_kernel(rows_second, rows_first, south, north):
    even = is_even("lat")
    unpack(even, rows_second, rows_first, NORTH_PAIRS, south, 64)
    unpack(even, rows_first, rows_second, SOUTH_PAIRS, north, 64)


def rim_kernel(second, west, east, rim):
    west_low = (lanes() % 16 < 8) == (is_even("lat") != second)
    for slab in range(SLABS):
        rim[slab] = jnp.where(west_low, west[slab], east[slab])


def split(x):
    high = x.astype(bf16)
    return high, (x - high.astype(f32)).astype(bf16)


def fill_parts(lhs, count, s, array):
    x = jnp.concatenate([array.reshape(8 * SLABS, 128), jnp.zeros((8, 128), f32)], axis=0)
    high, low = split(x)
    lhs[:, 128 * s : 128 * s + 128] = high
    lhs[:, 128 * (count + s) : 128 * (count + s) + 128] = low


def place_kernel(own, west, east, south, north, matrix, q, lhs):
    fill_parts(lhs, 6, 0, own[0])
    fill_parts(lhs, 6, 1, own[1])
    fill_parts(lhs, 6, 2, west[...])
    fill_parts(lhs, 6, 3, east[...])
    fill_parts(lhs, 6, 4, south[...])
    fill_parts(lhs, 6, 5, north[...])
    for pair in range(4):
        moved = jnp.dot(lhs[...], matrix[:, 256 * pair : 256 * pair + 256], preferred_element_type=f32)
        for i in range(2):
            q[:, 2 * pair + i] = moved[: 8 * SLABS, 128 * i : 128 * i + 128].reshape(SLABS, 8, 128)


def lookup(point, consts, at):
    depth = jnp.broadcast_to(point[DEPTH : DEPTH + 1], (8, 128))
    value = jnp.zeros((8, 128), f32)
    for c in range(NCLASS):
        value = jnp.where(depth == float(c), consts[at + c], value)
    return value * point[SEA : SEA + 1]


def rims_kernel(partial, rims_second, rims_first, consts, matrix, q, taps, ky, tx, ty, lhs):
    even_lat = is_even("lat")
    south = jnp.where(even_lat, rims_second[...], rims_first[...])
    north = jnp.where(even_lat, rims_first[...], rims_second[...])
    for s, array in ((0, south), (1, north)):
        high, low = split(array[:NDIR].reshape(8 * NDIR, 128))
        lhs[:, 128 * s : 128 * s + 128] = high
        lhs[:, 128 * (2 + s) : 128 * (2 + s) + 128] = low
    lane = lanes()
    south, north = south[STATIC], north[STATIC]
    speed = []
    for t in range(8):
        if t % 2 == 0:
            moved = jnp.dot(lhs[...], matrix[:, 128 * t : 128 * t + 256], preferred_element_type=f32)
            for i in range(2):
                q[:, t + i] = partial[:NDIR, t + i] + moved[:, 128 * i : 128 * i + 128].reshape(NDIR, 8, 128)
        point = partial[STATIC, t]
        for low, array, shift in ((0, south, 0), (24, south, 16), (96, north, 88), (120, north, 120)):
            point = jnp.where((lane >= low) & (lane < low + 8), roll(array, shift - 16 * t), point)
        pace = lookup(point, consts, TAB_SPEED)
        turning = lookup(point, consts, TAB_TURN)
        speed.append(pace)
        tx[t] = turning * point[SLOPE_X : SLOPE_X + 1]
        ty[t] = turning * point[SLOPE_Y : SLOPE_Y + 1]
        stretch = consts[STRETCH, t : t + 1, :]
        right = 0.5 * (pace + roll(pace, -1)) * stretch
        left = 0.5 * (pace + roll(pace, 1)) * stretch
        for base in range(10):
            a1, b1, c1 = weights(COS[base] * right)
            a0, b0, c0 = weights(COS[base] * left)
            taps[base, 0, 0, t] = 1.0 - a1 + b0
            taps[base, 0, 1, t] = -b1
            taps[base, 0, 2, t] = a0 - c1
            taps[base, 0, 3, t] = c0
            taps[base, 1, 0, t] = 1.0 + b1 - a0
            taps[base, 1, 1, t] = a1 - c0
            taps[base, 1, 2, t] = -b0
            taps[base, 1, 3, t] = c1
    for t in range(8):
        ahead = speed[t + 1] if t < 7 else roll(speed[0], -32)
        ky[t] = 0.5 * (speed[t] + ahead)


def flux(q, diff, curve, k, u, w):
    return k * (q + u * (diff - w * curve))


def halves(k):
    return 0.5 - 0.5 * k, (1.0 / 3.0) + (1.0 / 3.0) * k


def weights(k):
    u, w = halves(k)
    bend = k * u * w
    return k - k * u + 2.0 * bend, k * u - bend, -bend


FORTH_TAPS = (-1, -2)
BACK_TAPS = (-1, 2)


def lon_kernel(q, taps, shifts, out, moved):
    for quadrant, sign in ((0, 0), (3, 0), (1, 1), (2, 1)):
        x = q[9 * quadrant : 9 * quadrant + 9].reshape(576, 128)
        lhs = jnp.concatenate(split(x), axis=1)
        moved[quadrant] = jnp.dot(lhs, shifts[sign], preferred_element_type=f32)
    for sign in range(2):
        for base in range(10):
            if base == 0:
                dirs = [[0], [18]][sign]
            elif base == 9:
                dirs = [[27], [9]][sign]
            else:
                dirs = [[base, 36 - base], [18 - base, 18 + base]][sign]
            for t in range(8):
                tap = [taps[base, sign, i, t] for i in range(4)]
                for d in dirs:
                    at = 64 * (d % 9) + 8 * t
                    cell = q[d, t]
                    near = [moved[d // 9, at : at + 8, 128 * i : 128 * i + 128] for i in range(2)]
                    out[d, t] = (tap[0] * cell + tap[1] * roll(cell, -1)) + (tap[2] * near[0] + tap[3] * near[1])


def lat_kernel(q, ky, consts, out, sums=None):
    live = consts[LIVE]
    totals = [jnp.zeros((8, 128), f32)] * 8

    def put(d, t, value):
        out[d, t] = value
        if sums is not None:
            totals[t] = totals[t] + value

    def forth(d, ks, us, ws):
        tiles = [q[d, t] for t in range(8)]
        diff = [tiles[t + 1] - tiles[t] for t in range(7)]
        diff.append(roll(tiles[0], -32) - tiles[7])
        before = roll(diff[7], 32)
        fluxes = []
        for t in range(8):
            fluxes.append(flux(tiles[t], diff[t], diff[t] - before, ks[t], us[t], ws[t]))
            before = diff[t]
        behind = roll(fluxes[7], 32)
        for t in range(8):
            put(d, t, (tiles[t] - fluxes[t] + behind) * live)
            behind = fluxes[t]

    def back(d, ks, us, ws):
        tiles = [q[d, t] for t in range(8)]
        ahead = tiles[1:] + [roll(tiles[0], -32)]
        diff = [tiles[t] - ahead[t] for t in range(8)]
        after = diff[1:] + [roll(diff[0], -32)]
        fluxes = [flux(ahead[t], diff[t], diff[t] - after[t], ks[t], us[t], ws[t]) for t in range(8)]
        behind = roll(fluxes[7], 32)
        for t in range(8):
            put(d, t, (tiles[t] + fluxes[t] - behind) * live)
            behind = fluxes[t]

    for base in range(10):
        ks = [SIN[base] * ky[t] for t in range(8)]
        us, ws = zip(*[halves(k) for k in ks])
        if base == 0:
            north, south = [0], [18]
        elif base == 9:
            north, south = [9], [27]
        else:
            north, south = [base, 18 - base], [18 + base, 36 - base]
        for d in north:
            forth(d, ks, us, ws)
        for d in south:
            back(d, ks, us, ws)
    if sums is None:
        return
    lane = lanes()
    halves_of = [jnp.zeros((8, 128), f32)] * 2
    for t in range(8):
        moved = roll(totals[t], 16 * t - 40)
        halves_of[0] = jnp.where(lane // 16 == t, moved, halves_of[0])
        halves_of[1] = jnp.where(lane // 16 == (t + 2) % 8, moved, halves_of[1])
    halves_of[1] = roll(halves_of[1], -32)
    sums[...] = jnp.zeros((8, 128), f32)
    for half in range(2):
        sums[half : half + 1, :] = jnp.sum(halves_of[half], axis=0, keepdims=True)
        sums[2 + half : 3 + half, :] = jnp.sum(halves_of[half] * consts[LEVEL], axis=0, keepdims=True)


def turn_around(get, put, x, y):
    def factors(d):
        k = SIN_FACE[d] * x - COS_FACE[d] * y
        half, third = 0.5 * k, (1.0 / 3.0) * k
        return k, 0.5 - half, 1.0 / 3.0 + third, 0.5 + half, 1.0 / 3.0 - third

    half_turn = NDIR // 2
    k, u, w, u_back, w_back = factors(half_turn - 1)
    state = []
    ends = []
    for at in (0, half_turn):
        cell, ahead = get(at), get(at + 1)
        before, last = get((at - 1) % NDIR), get((at - 2) % NDIR)
        diff = ahead - cell
        diff1 = cell - before
        curve = diff - diff1
        curve1 = diff1 - (before - last)
        if at == 0:
            f = flux(before, diff1, jnp.where(k >= 0.0, curve, curve1), k, u_back, w_back)
        else:
            f = flux(before, diff1, jnp.where(k >= 0.0, curve1, curve), k, u, w)
        state.append([cell, ahead, diff, curve])
        ends.append(f)
    f_first, f_second = -ends[0], -ends[1]
    for d in range(half_turn):
        if d < half_turn - 1:
            k, u, w, u_back, w_back = factors(d)
            positive = k >= 0.0
        for at in (0, half_turn):
            cell, ahead, diff, curve = state[at // half_turn]
            beyond = get((at + d + 2) % NDIR)
            diff_ahead = beyond - ahead
            curve_ahead = diff_ahead - diff
            if at == 0:
                if d < half_turn - 1:
                    f = flux(cell, diff, jnp.where(positive, curve, curve_ahead), k, u, w)
                else:
                    f = ends[1]
                put(d, cell - f + f_first)
                f_first = f
            else:
                if d < half_turn - 1:
                    f = flux(cell, diff, jnp.where(positive, curve_ahead, curve), k, u_back, w_back)
                else:
                    f = ends[0]
                put(at + d, cell + f - f_second)
                f_second = f
            state[at // half_turn] = [ahead, beyond, diff_ahead, curve_ahead]


def turn_kernel(q, tx, ty, out):
    for t in range(8):

        def put(d, value, t=t):
            out[d, t] = value

        turn_around(lambda d, t=t: q[d, t], put, tx[t], ty[t])


def gather_kernel(q, matrix, own, lhs):
    for t in range(8):
        high, low = split(q[:, t].reshape(8 * NDIR, 128))
        lhs[:, 128 * t : 128 * t + 128] = high
        lhs[:, 1024 + 128 * t : 1024 + 128 * t + 128] = low
    moved = jnp.dot(lhs[...], matrix[...], preferred_element_type=f32)
    for half in range(2):
        own[half] = moved[:, 128 * half : 128 * half + 128].reshape(NDIR, 8, 128)


def last_turn_kernel(own, static, gain, consts, early, flat0, flat1):
    for half, flat in ((0, flat0), (1, flat1)):
        point = static[half, 0]
        turning = lookup(point, consts, TAB_TURN)

        def put(d, value, half=half, flat=flat):
            flat[pl.ds(d, FREQ, stride=NDIR), :] = value * gain[d, half]

        turn_around(
            lambda d, half=half: own[half, d],
            put,
            turning * point[SLOPE_X : SLOPE_X + 1],
            turning * point[SLOPE_Y : SLOPE_Y + 1],
        )
        for low, high in ((0, 128), (128, 256), (256, 288)):
            early[128 * half : 128 * half + 128, low:high] = flat[low:high, :].T


def finish_kernel(early, static, sums, other, consts, spread, out, ready, sems):
    total = sums[...] + other[...]
    level = consts[LEVEL]
    losses = []
    for half in range(2):
        energy = total[half : half + 1]
        moment = total[2 + half : 3 + half]
        mean_level = jnp.maximum(moment, 1.0) / jnp.maximum(energy, 1.0)
        mean = energy / NCOMP
        breaking = break_coef * level * level / mean_level * (mean * mean)
        damping = static[half, 0, ICE : ICE + 1] * consts[ICE_RATE]
        losses.append(jnp.exp(-breaking - damping))
    turned = jnp.concatenate(losses, axis=0).T
    wide = jnp.dot(jnp.concatenate(split(turned), axis=1), spread[...], preferred_element_type=f32)
    for half in range(2):
        loss = wide[:, 384 * half : 384 * half + NDIR * FREQ]
        result = early[128 * half : 128 * half + 128, :] * loss
        mine = pl.ds(8 * half, 8)
        ready[mine] = result.reshape(8, 16, NDIR * FREQ)
        pltpu.make_async_copy(ready.at[mine], out.at[mine], sems.at[half]).start()
    for half in range(2):
        mine = pl.ds(8 * half, 8)
        pltpu.make_async_copy(ready.at[mine], out.at[mine], sems.at[half]).wait()


PARAMS = pltpu.CompilerParams(vmem_limit_bytes=40 * 2**20)


def call(kernel, ins, outs, scratch=(), name=None, space=pltpu.VMEM, dtype=f32, result=pltpu.VMEM):
    types = dtype if isinstance(dtype, list) else [dtype] * len(outs)
    return pl.pallas_call(
        kernel,
        out_shape=[jax.ShapeDtypeStruct(shape, kind) for shape, kind in zip(outs, types)],
        in_specs=[pl.BlockSpec(memory_space=space)] * ins,
        out_specs=[pl.BlockSpec(memory_space=result)] * len(outs),
        scratch_shapes=list(scratch),
        compiler_params=PARAMS,
        name=name,
    )


def swap(array, axis, first, closed=False):
    count = lax.axis_size(axis)
    pairs = []
    for i in range(first, count, 2):
        if i + 1 < count or closed:
            j = (i + 1) % count
            pairs += [(i, j), (j, i)]
    return lax.ppermute(array, axis, pairs)


def per_device(
    spectrum,
    sea_mask,
    ice_mask,
    depth_class,
    speed_table,
    refraction_table,
    depth_slope,
    wind_speed,
    wind_dir,
    ice_rate,
):
    tile = (8, 128)
    block = (8,) + tile
    slabs = (SLABS,) + tile
    sent = (SENT,) + tile
    inputs = [spectrum, sea_mask, ice_mask, depth_class, depth_slope, wind_speed, wind_dir]
    tables = [speed_table, refraction_table, ice_rate]
    own, speeds, turnings, ices = call(
        pack_kernel,
        10,
        [(2,) + slabs] + [x.shape for x in tables],
        [pltpu.VMEM(x.shape, x.dtype) for x in inputs]
        + [pltpu.VMEM((NDIR * FREQ, 128), f32)] * 2
        + [pltpu.VMEM((16, 128), f32), pltpu.SemaphoreType.DMA((10,))],
        name="pack",
        space=pltpu.HBM,
    )(*[pltpu.with_memory_space_constraint(x, pltpu.HBM) for x in inputs + tables])
    (to_second,) = call(functools.partial(column_kernel, True), 1, [sent], name="column_far")(own)
    cols_second = swap(to_second, "lon", 1, True)
    (to_first,) = call(functools.partial(column_kernel, False), 1, [sent], name="column_near")(own)
    cols_first = swap(to_first, "lon", 0, True)
    (edge_second,) = call(functools.partial(edge_kernel, True), 1, [sent], name="edge_far")(own)
    rows_second = swap(edge_second, "lat", 1)
    (edge_first,) = call(functools.partial(edge_kernel, False), 1, [sent], name="edge_near")(own)
    rows_first = swap(edge_first, "lat", 0)
    place, rims, shifts, gather, spread, consts = call(
        tables_kernel,
        3,
        [(1536, 1024), (512, 1024), (2, 256, 256), (2048, 256), (32, 768), (20,) + tile],
        name="tables",
        dtype=[bf16] * 5 + [f32],
    )(speeds, turnings, ices)
    (gain,) = call(growth_kernel, 2, [(NDIR, 2) + tile], name="growth")(own, consts)
    west, east = call(unpack_kernel, 5, [slabs] * 2, name="unpack")(
        cols_second, cols_first, rows_second, rows_first, consts
    )
    (rim_second,) = call(functools.partial(rim_kernel, True), 2, [slabs], name="rim_far")(west, east)
    rims_second = swap(rim_second, "lat", 1)
    (rim_first,) = call(functools.partial(rim_kernel, False), 2, [slabs], name="rim_near")(west, east)
    rims_first = swap(rim_first, "lat", 0)
    south, north = call(unpack_rows_kernel, 2, [slabs] * 2, name="unpack_rows")(rows_second, rows_first)
    (partial,) = call(
        place_kernel,
        6,
        [(SLABS,) + block],
        [pltpu.VMEM((8 * SLABS + 8, 1536), bf16)],
        name="place",
    )(own, west, east, south, north, place)
    q, taps, ky, tx, ty = call(
        rims_kernel,
        5,
        [(NDIR,) + block, (10, 2, 4) + block] + [block] * 3,
        [pltpu.VMEM((8 * NDIR, 512), bf16)],
        name="rims",
    )(partial, rims_second, rims_first, consts, rims)
    cells = [(NDIR,) + block]
    for substep in range(ITERS):
        (q,) = call(lon_kernel, 3, cells, [pltpu.VMEM((4, 576, 256), f32)], name="lon")(q, taps, shifts)
        if substep == ITERS - 1:
            q, sums = call(lat_kernel, 3, cells + [tile], name="lat_sums")(q, ky, consts)
        else:
            (q,) = call(lat_kernel, 3, cells, name="lat")(q, ky, consts)
            (q,) = call(turn_kernel, 3, cells, name="turn")(q, tx, ty)
    other = swap(sums, "band", 0)
    (last,) = call(
        gather_kernel, 2, [(2, NDIR) + tile], [pltpu.VMEM((8 * NDIR, 2048), bf16)], name="gather"
    )(q, gather)
    static = own[:, STATIC:]
    (early,) = call(
        last_turn_kernel,
        4,
        [(256, NDIR * FREQ)],
        [pltpu.VMEM((NDIR * FREQ, 128), f32)] * 2,
        name="last_turn",
    )(last, static, gain, consts)
    (out,) = call(
        finish_kernel,
        6,
        [spectrum.shape],
        [pltpu.VMEM(spectrum.shape, f32), pltpu.SemaphoreType.DMA((2,))],
        name="finish",
        result=pltpu.HBM,
    )(early, static, sums, other, consts, spread)
    return out


def solution(mesh):
    return jax.shard_map(
        per_device,
        mesh=mesh,
        in_specs=(
            P("lat", "lon", "band"),
            P("lat", "lon"),
            P("lat", "lon"),
            P("lat", "lon"),
            P(),
            P(),
            P(None, "lat", "lon"),
            P("lat", "lon"),
            P("lat", "lon"),
            P(),
        ),
        out_specs=P("lat", "lon", "band"),
        check_vma=False,
    )
```

```python
import functools
import math

import jax
import jax.numpy as jnp
import numpy as np
from jax import lax
from jax.experimental import pallas as pl
from jax.experimental.pallas import tpu as pltpu
from jax.sharding import PartitionSpec as P

NDIR = 36
NCOMP = 576
ITERS = 4
NCLASS = 8
FREQ = 8
HALO = 8
ROWS = 16
STATIC = NDIR
SLABS = NDIR + 1
SEA, DEPTH, SLOPE_X, SLOPE_Y, ICE, WIND, WDIR = range(7)

freq_ratio = 1.1
wind_gain = 0.12
break_coef = 0.05
south_edge = -30.0
band_span = 60.0

COS = [math.cos(2.0 * math.pi * d / NDIR) for d in range(NDIR)]
SIN = [math.sin(2.0 * math.pi * d / NDIR) for d in range(NDIR)]
COS_FACE = [math.cos(2.0 * math.pi * (d + 0.5) / NDIR) for d in range(NDIR)]
SIN_FACE = [math.sin(2.0 * math.pi * (d + 0.5) / NDIR) for d in range(NDIR)]

TAB_SPEED, TAB_TURN, STRETCH, LIVE, ICE_RATE, LEVEL = 0, 8, 16, 17, 18, 19

f32 = jnp.float32
bf16 = jnp.bfloat16


def lanes():
    return lax.broadcasted_iota(jnp.int32, (8, 128), 1)


def roll(x, shift):
    shift = shift % 128
    return pltpu.roll(x, shift, 1) if shift else x


def is_even(axis):
    return lax.axis_index(axis) % 2 == 0


def pack_kernel(*refs):
    sources, own, tables = refs[:10], refs[10], refs[11:14]
    landed = refs[14:21]
    flat0, flat1, wide, sems = refs[21:]
    copies = [
        pltpu.make_async_copy(src, dst, sems.at[i])
        for i, (src, dst) in enumerate(zip(sources[1:], landed[1:] + tables))
    ]
    for i in range(4):
        mine = pl.ds(4 * i, 4)
        copies.append(pltpu.make_async_copy(sources[0].at[mine], landed[0].at[mine], sems.at[9 + i]))
    for copy in copies:
        copy.start()
    wide[...] = jnp.zeros_like(wide)
    group = lax.broadcasted_iota(jnp.int32, (16, 128), 1) // 16
    row = lax.broadcasted_iota(jnp.int32, (16, 128), 0) % 8
    own[:, STATIC] = jnp.zeros((2, 8, 128), f32)
    for copy in copies:
        copy.wait()
    spec, sea, ice, depth, slope, wspeed, wdir = landed

    def place(field, values):
        wide[:, :16] = values
        moved = pltpu.roll(wide[...], 0, 1, stride=16, stride_axis=0)
        kept = jnp.where(group == row, moved, 0.0)
        for half in range(2):
            own[half, STATIC, field : field + 1, :] = jnp.sum(
                kept[8 * half : 8 * half + 8], axis=0, keepdims=True
            )

    place(SEA, sea[...].astype(f32))
    place(DEPTH, depth[...].astype(f32))
    place(SLOPE_X, slope[0])
    place(SLOPE_Y, slope[1])
    place(ICE, ice[...].astype(f32))
    place(WIND, wspeed[...])
    place(WDIR, wdir[...])
    grid = spec[...].reshape(256, NDIR * FREQ)
    for low, high in ((0, 128), (128, 256), (256, 288)):
        turned = grid[:, low:high].T
        flat0[low:high, :] = turned[:, :128]
        flat1[low:high, :] = turned[:, 128:]
    sea0 = own[0, STATIC, SEA : SEA + 1, :]
    sea1 = own[1, STATIC, SEA : SEA + 1, :]
    for d in range(NDIR):
        own[0, d] = flat0[pl.ds(d, FREQ, stride=NDIR), :] * sea0
        own[1, d] = flat1[pl.ds(d, FREQ, stride=NDIR), :] * sea1


WEST_PAIRS = [(33, 0), (34, 1), (35, 2)]
EAST_PAIRS = [(15, 18), (16, 19), (17, 20)]


def slots(pairs):
    paired = [d for pair in pairs for d in pair]
    return [d for d in range(SLABS) if d not in paired]


SENT = SLABS - 3


def column_kernel(second, own, message):
    inner = lanes() % 16
    to_east = is_even("lon") != second
    from_own0 = (inner >= 8) == to_east
    shift = jnp.where(to_east, 120, 8)

    def edge(slab):
        return jnp.where(from_own0, own[0, slab], pltpu.roll(own[1, slab], shift, 1))

    for i, (east, west) in enumerate(zip(slots(EAST_PAIRS), slots(WEST_PAIRS))):
        if east == west:
            message[i] = edge(east)
        else:
            message[i] = edge(jnp.where(to_east, east, west))
    near = (inner % 8 >= 4) == to_east
    for i, (east, west) in enumerate(zip(EAST_PAIRS, WEST_PAIRS)):
        one = edge(jnp.where(to_east, east[0], west[0]))
        two = edge(jnp.where(to_east, east[1], west[1]))
        message[SENT - 3 + i] = jnp.where(near, one, pltpu.roll(two, jnp.where(to_east, 124, 4), 1))


NORTH_PAIRS = [(24, 27), (25, 28), (26, 29)]
SOUTH_PAIRS = [(6, 9), (7, 10), (8, 11)]


def edge_kernel(second, own, message):
    to_north = is_even("lat") != second
    for i, (north, south) in enumerate(zip(slots(NORTH_PAIRS), slots(SOUTH_PAIRS))):
        message[i] = jnp.where(to_north, own[1, north], own[0, south])
    near = (lanes() >= 64) == to_north
    for i, (north, south) in enumerate(zip(NORTH_PAIRS, SOUTH_PAIRS)):
        one = jnp.where(to_north, own[1, north[0]], own[0, south[0]])
        two = jnp.where(to_north, own[1, north[1]], own[0, south[1]])
        message[SENT - 3 + i] = jnp.where(near, one, roll(two, 64))


def growth_kernel(own, consts, gain):
    for half in range(2):
        point = own[half, STATIC]
        turn = point[WDIR : WDIR + 1]
        cos_w = jnp.cos(turn)
        sin_w = jnp.sin(turn)
        force = wind_gain * point[WIND : WIND + 1] * consts[LEVEL]
        share = point[SEA : SEA + 1]
        for d in range(NDIR):
            along = jnp.maximum(COS[d] * cos_w + SIN[d] * sin_w, 0.0)
            gain[d, half] = jnp.exp(force * along) * share


def tables_kernel(speed_table, refraction_table, ice_rate, place, rims, shifts, gather, spread, consts):
    first = lax.axis_index("band") * FREQ
    sub = lax.broadcasted_iota(jnp.int32, (8, 128), 0)
    mine = lanes() == first + sub

    def column(row):
        picked = jnp.where(mine, jnp.broadcast_to(row, (8, 128)), 0.0)
        return jnp.broadcast_to(jnp.sum(picked, axis=1, keepdims=True), (8, 128))

    def widen(values):
        return jnp.concatenate([values, jnp.zeros((values.shape[0], 112), f32)], axis=1)

    for at, table in ((TAB_SPEED, speed_table), (TAB_TURN, refraction_table)):
        wide = widen(table[...])
        for c in range(NCLASS):
            consts[at + c] = column(wide[c : c + 1])
    consts[ICE_RATE] = column(widen(ice_rate[...].reshape(1, 16)))
    consts[LEVEL] = jnp.exp(math.log(freq_ratio) * (first + sub).astype(f32))
    lat = lax.axis_index("lat")
    lats = lax.axis_size("lat")
    group = lanes() // 32
    rows = lat * ROWS - HALO + 8 * group + sub
    latitude = (south_edge + band_span * (rows.astype(f32) + 0.5) / (ROWS * lats)) * (math.pi / 180.0)
    consts[STRETCH] = 1.0 / jnp.cos(latitude)
    ghost = ((group == 0) & (lat == 0)) | ((group == 3) & (lat == lats - 1))
    consts[LIVE] = jnp.where(ghost, 0.0, 1.0)
    comp = lax.broadcasted_iota(jnp.int32, (32, 384), 1) // NDIR
    freq = lax.broadcasted_iota(jnp.int32, (32, 384), 0) % 16
    for half in range(2):
        spread[:, 384 * half : 384 * half + 384] = (comp == freq - 8 * half).astype(f32).astype(bf16)

    chunk = lax.broadcasted_iota(jnp.int32, (16, 128), 0)
    lane = lax.broadcasted_iota(jnp.int32, (16, 128), 1)
    low = chunk < 8
    targets = [
        40 + chunk,
        72 + chunk,
        jnp.where(low, 64 + chunk, 24 + chunk),
        jnp.where(low, 56 + chunk, 80 + chunk),
        8 + chunk,
        104 + chunk,
    ]
    corners = [jnp.where(low, chunk, 16 + chunk), jnp.where(low, 120 + chunk, 88 + chunk)]
    for matrix, lists in ((place, targets), (rims, corners)):
        matrix[...] = jnp.zeros_like(matrix)
        for s, target in enumerate(lists):
            stripe = (lane == target).astype(f32).astype(bf16)
            for part in range(2):
                for t in range(8):
                    row = part * 128 * len(lists) + s * 128 + 16 * t
                    matrix[row : row + 16, 128 * t : 128 * t + 128] = stripe
    row = lax.broadcasted_iota(jnp.int32, (128, 128), 0)
    col = lax.broadcasted_iota(jnp.int32, (128, 128), 1)
    for sign, taps in ((0, FORTH_TAPS), (1, BACK_TAPS)):
        for i, tap in enumerate(taps):
            moved = (row == (col + tap) % 128).astype(f32).astype(bf16)
            for part in range(2):
                shifts[sign, 128 * part : 128 * part + 128, 128 * i : 128 * i + 128] = moved
    for t in range(8):
        for half in range(2):
            from_row = 40 + 32 * half + col % 16
            moved = ((col // 16 == t) & (row == from_row)).astype(f32).astype(bf16)
            for part in range(2):
                at = part * 1024 + 128 * t
                gather[at : at + 128, 128 * half : 128 * half + 128] = moved


def unpack(even, first, second, pairs, out, back):
    full = slots(pairs)
    for i in range(SENT):
        got = jnp.where(even, first[i], second[i])
        if i < len(full):
            out[full[i]] = got
        else:
            pair = pairs[i - len(full)]
            out[pair[0]] = got
            out[pair[1]] = roll(got, back)


def unpack_kernel(cols_second, cols_first, rows_second, rows_first, consts, west, east):
    del rows_second, rows_first, consts
    even = is_even("lon")
    unpack(even, cols_second, cols_first, EAST_PAIRS, west, 4)
    unpack(even, cols_first, cols_second, WEST_PAIRS, east, -4)


def unpack_rows_kernel(rows_second, rows_first, south, north):
    even = is_even("lat")
    unpack(even, rows_second, rows_first, NORTH_PAIRS, south, 64)
    unpack(even, rows_first, rows_second, SOUTH_PAIRS, north, 64)


def rim_kernel(second, west, east, rim):
    west_low = (lanes() % 16 < 8) == (is_even("lat") != second)
    for slab in range(SLABS):
        rim[slab] = jnp.where(west_low, west[slab], east[slab])


def split(x):
    high = x.astype(bf16)
    return high, (x - high.astype(f32)).astype(bf16)


def fill_parts(lhs, count, s, array):
    x = jnp.concatenate([array.reshape(8 * SLABS, 128), jnp.zeros((8, 128), f32)], axis=0)
    high, low = split(x)
    lhs[:, 128 * s : 128 * s + 128] = high
    lhs[:, 128 * (count + s) : 128 * (count + s) + 128] = low


def place_kernel(own, west, east, south, north, matrix, q, lhs):
    fill_parts(lhs, 6, 0, own[0])
    fill_parts(lhs, 6, 1, own[1])
    fill_parts(lhs, 6, 2, west[...])
    fill_parts(lhs, 6, 3, east[...])
    fill_parts(lhs, 6, 4, south[...])
    fill_parts(lhs, 6, 5, north[...])
    for pair in range(4):
        moved = jnp.dot(lhs[...], matrix[:, 256 * pair : 256 * pair + 256], preferred_element_type=f32)
        for i in range(2):
            q[:, 2 * pair + i] = moved[: 8 * SLABS, 128 * i : 128 * i + 128].reshape(SLABS, 8, 128)


def lookup(point, consts, at):
    depth = jnp.broadcast_to(point[DEPTH : DEPTH + 1], (8, 128))
    value = jnp.zeros((8, 128), f32)
    for c in range(NCLASS):
        value = jnp.where(depth == float(c), consts[at + c], value)
    return value * point[SEA : SEA + 1]


def rims_kernel(partial, rims_second, rims_first, consts, matrix, q, taps, ky, tx, ty, lhs):
    even_lat = is_even("lat")
    south = jnp.where(even_lat, rims_second[...], rims_first[...])
    north = jnp.where(even_lat, rims_first[...], rims_second[...])
    for s, array in ((0, south), (1, north)):
        high, low = split(array[:NDIR].reshape(8 * NDIR, 128))
        lhs[:, 128 * s : 128 * s + 128] = high
        lhs[:, 128 * (2 + s) : 128 * (2 + s) + 128] = low
    lane = lanes()
    south, north = south[STATIC], north[STATIC]
    speed = []
    for t in range(8):
        if t % 2 == 0:
            moved = jnp.dot(lhs[...], matrix[:, 128 * t : 128 * t + 256], preferred_element_type=f32)
            for i in range(2):
                q[:, t + i] = partial[:NDIR, t + i] + moved[:, 128 * i : 128 * i + 128].reshape(NDIR, 8, 128)
        point = partial[STATIC, t]
        for low, array, shift in ((0, south, 0), (24, south, 16), (96, north, 88), (120, north, 120)):
            point = jnp.where((lane >= low) & (lane < low + 8), roll(array, shift - 16 * t), point)
        pace = lookup(point, consts, TAB_SPEED)
        turning = lookup(point, consts, TAB_TURN)
        speed.append(pace)
        tx[t] = turning * point[SLOPE_X : SLOPE_X + 1]
        ty[t] = turning * point[SLOPE_Y : SLOPE_Y + 1]
        stretch = consts[STRETCH, t : t + 1, :]
        right = 0.5 * (pace + roll(pace, -1)) * stretch
        left = 0.5 * (pace + roll(pace, 1)) * stretch
        for base in range(10):
            a1, b1, c1 = weights(COS[base] * right)
            a0, b0, c0 = weights(COS[base] * left)
            taps[base, 0, 0, t] = 1.0 - a1 + b0
            taps[base, 0, 1, t] = -b1
            taps[base, 0, 2, t] = a0 - c1
            taps[base, 0, 3, t] = c0
            taps[base, 1, 0, t] = 1.0 + b1 - a0
            taps[base, 1, 1, t] = a1 - c0
            taps[base, 1, 2, t] = -b0
            taps[base, 1, 3, t] = c1
    for t in range(8):
        ahead = speed[t + 1] if t < 7 else roll(speed[0], -32)
        ky[t] = 0.5 * (speed[t] + ahead)


def flux(q, diff, curve, k, u, w):
    return k * (q + u * (diff - w * curve))


def halves(k):
    return 0.5 - 0.5 * k, (1.0 / 3.0) + (1.0 / 3.0) * k


def weights(k):
    u, w = halves(k)
    bend = k * u * w
    return k - k * u + 2.0 * bend, k * u - bend, -bend


FORTH_TAPS = (1, -1, -2)
BACK_TAPS = (1, -1, 2)


def lat_north(tiles, ks, us, ws):
    diff = [tiles[t + 1] - tiles[t] for t in range(7)]
    diff.append(roll(tiles[0], -32) - tiles[7])
    before = roll(diff[7], 32)
    fluxes = []
    for t in range(8):
        fluxes.append(flux(tiles[t], diff[t], diff[t] - before, ks[t], us[t], ws[t]))
        before = diff[t]
    behind = roll(fluxes[7], 32)
    out = []
    for t in range(8):
        out.append(tiles[t] - fluxes[t] + behind)
        behind = fluxes[t]
    return out


def lat_south(tiles, ks, us, ws):
    ahead = tiles[1:] + [roll(tiles[0], -32)]
    diff = [tiles[t] - ahead[t] for t in range(8)]
    after = diff[1:] + [roll(diff[0], -32)]
    fluxes = [flux(ahead[t], diff[t], diff[t] - after[t], ks[t], us[t], ws[t]) for t in range(8)]
    behind = roll(fluxes[7], 32)
    out = []
    for t in range(8):
        out.append(tiles[t] + fluxes[t] - behind)
        behind = fluxes[t]
    return out


def sweep_kernel(with_sums, q, taps, ky, consts, shifts, *refs):
    if with_sums:
        out, sums, moved = refs
    else:
        out, moved = refs
    live = consts[LIVE]
    totals = [jnp.zeros((8, 128), f32)] * 8

    def shifted(quadrant, sign):
        x = q[9 * quadrant : 9 * quadrant + 9].reshape(576, 128)
        lhs = jnp.concatenate(split(x), axis=1)
        moved[quadrant] = jnp.dot(lhs, shifts[sign], preferred_element_type=f32)

    def lon(d, t, tap):
        at = 64 * (d % 9) + 8 * t
        near = [moved[d // 9, at : at + 8, 128 * i : 128 * i + 128] for i in range(3)]
        return (tap[0] * q[d, t] + tap[1] * near[0]) + (tap[2] * near[1] + tap[3] * near[2])

    def both(sign, base):
        if base == 0:
            dirs = [[0], [18]][sign]
        elif base == 9:
            dirs = [[27], [9]][sign]
        else:
            dirs = [[base, 36 - base], [18 - base, 18 + base]][sign]
        tiles = [[] for _ in dirs]
        for t in range(8):
            tap = [taps[base, sign, i, t] for i in range(4)]
            for cells, d in zip(tiles, dirs):
                cells.append(lon(d, t, tap))
        ks = [SIN[base] * ky[t] for t in range(8)]
        us, ws = zip(*[halves(k) for k in ks])
        for cells, d in zip(tiles, dirs):
            lat = lat_north if d < 18 else lat_south
            for t, value in enumerate(lat(cells, ks, us, ws)):
                value = value * live
                out[d, t] = value
                if with_sums:
                    totals[t] = totals[t] + value

    shifted(0, 0)
    shifted(3, 0)
    shifted(1, 1)
    for base in range(5):
        both(0, base)
    shifted(2, 1)
    for base in range(5, 10):
        both(0, base)
    for base in range(10):
        both(1, base)
    if not with_sums:
        return
    lane = lanes()
    halves_of = [jnp.zeros((8, 128), f32)] * 2
    for t in range(8):
        rolled = roll(totals[t], 16 * t - 40)
        halves_of[0] = jnp.where(lane // 16 == t, rolled, halves_of[0])
        halves_of[1] = jnp.where(lane // 16 == (t + 2) % 8, rolled, halves_of[1])
    halves_of[1] = roll(halves_of[1], -32)
    sums[...] = jnp.zeros((8, 128), f32)
    for half in range(2):
        sums[half : half + 1, :] = jnp.sum(halves_of[half], axis=0, keepdims=True)
        sums[2 + half : 3 + half, :] = jnp.sum(halves_of[half] * consts[LEVEL], axis=0, keepdims=True)


def turn_around(get, put, x, y):
    def factors(d):
        k = SIN_FACE[d] * x - COS_FACE[d] * y
        half, third = 0.5 * k, (1.0 / 3.0) * k
        return k, 0.5 - half, 1.0 / 3.0 + third, 0.5 + half, 1.0 / 3.0 - third

    half_turn = NDIR // 2
    k, u, w, u_back, w_back = factors(half_turn - 1)
    state = []
    ends = []
    for at in (0, half_turn):
        cell, ahead = get(at), get(at + 1)
        before, last = get((at - 1) % NDIR), get((at - 2) % NDIR)
        diff = ahead - cell
        diff1 = cell - before
        curve = diff - diff1
        curve1 = diff1 - (before - last)
        if at == 0:
            f = flux(before, diff1, jnp.where(k >= 0.0, curve, curve1), k, u_back, w_back)
        else:
            f = flux(before, diff1, jnp.where(k >= 0.0, curve1, curve), k, u, w)
        state.append([cell, ahead, diff, curve])
        ends.append(f)
    f_first, f_second = -ends[0], -ends[1]
    for d in range(half_turn):
        if d < half_turn - 1:
            k, u, w, u_back, w_back = factors(d)
            positive = k >= 0.0
        for at in (0, half_turn):
            cell, ahead, diff, curve = state[at // half_turn]
            beyond = get((at + d + 2) % NDIR)
            diff_ahead = beyond - ahead
            curve_ahead = diff_ahead - diff
            if at == 0:
                if d < half_turn - 1:
                    f = flux(cell, diff, jnp.where(positive, curve, curve_ahead), k, u, w)
                else:
                    f = ends[1]
                put(d, cell - f + f_first)
                f_first = f
            else:
                if d < half_turn - 1:
                    f = flux(cell, diff, jnp.where(positive, curve_ahead, curve), k, u_back, w_back)
                else:
                    f = ends[0]
                put(at + d, cell + f - f_second)
                f_second = f
            state[at // half_turn] = [ahead, beyond, diff_ahead, curve_ahead]


def turn_kernel(q, tx, ty, out):
    for t in range(8):

        def put(d, value, t=t):
            out[d, t] = value

        turn_around(lambda d, t=t: q[d, t], put, tx[t], ty[t])


def gather_kernel(q, matrix, own, lhs):
    for t in range(8):
        high, low = split(q[:, t].reshape(8 * NDIR, 128))
        lhs[:, 128 * t : 128 * t + 128] = high
        lhs[:, 1024 + 128 * t : 1024 + 128 * t + 128] = low
    moved = jnp.dot(lhs[...], matrix[...], preferred_element_type=f32)
    for half in range(2):
        own[half] = moved[:, 128 * half : 128 * half + 128].reshape(NDIR, 8, 128)


def last_turn_kernel(own, static, gain, consts, early, flat0, flat1):
    for half, flat in ((0, flat0), (1, flat1)):
        point = static[half, 0]
        turning = lookup(point, consts, TAB_TURN)

        def put(d, value, half=half, flat=flat):
            flat[pl.ds(d, FREQ, stride=NDIR), :] = value * gain[d, half]

        turn_around(
            lambda d, half=half: own[half, d],
            put,
            turning * point[SLOPE_X : SLOPE_X + 1],
            turning * point[SLOPE_Y : SLOPE_Y + 1],
        )
        for low, high in ((0, 128), (128, 256), (256, 288)):
            early[128 * half : 128 * half + 128, low:high] = flat[low:high, :].T


def finish_kernel(early, static, sums, other, consts, spread, out, ready, sems):
    total = sums[...] + other[...]
    level = consts[LEVEL]
    losses = []
    for half in range(2):
        energy = total[half : half + 1]
        moment = total[2 + half : 3 + half]
        mean_level = jnp.maximum(moment, 1.0) / jnp.maximum(energy, 1.0)
        mean = energy / NCOMP
        breaking = break_coef * level * level / mean_level * (mean * mean)
        damping = static[half, 0, ICE : ICE + 1] * consts[ICE_RATE]
        losses.append(jnp.exp(-breaking - damping))
    turned = jnp.concatenate(losses, axis=0).T
    wide = jnp.dot(jnp.concatenate(split(turned), axis=1), spread[...], preferred_element_type=f32)
    for half in range(2):
        loss = wide[:, 384 * half : 384 * half + NDIR * FREQ]
        result = early[128 * half : 128 * half + 128, :] * loss
        ready[8 * half : 8 * half + 8] = result.reshape(8, 16, NDIR * FREQ)
        for i in range(4 * half, 4 * half + 4):
            mine = pl.ds(2 * i, 2)
            pltpu.make_async_copy(ready.at[mine], out.at[mine], sems.at[i]).start()
    for i in range(8):
        mine = pl.ds(2 * i, 2)
        pltpu.make_async_copy(ready.at[mine], out.at[mine], sems.at[i]).wait()


PARAMS = pltpu.CompilerParams(vmem_limit_bytes=40 * 2**20)


def call(kernel, ins, outs, scratch=(), name=None, space=pltpu.VMEM, dtype=f32, result=pltpu.VMEM):
    types = dtype if isinstance(dtype, list) else [dtype] * len(outs)
    return pl.pallas_call(
        kernel,
        out_shape=[jax.ShapeDtypeStruct(shape, kind) for shape, kind in zip(outs, types)],
        in_specs=[pl.BlockSpec(memory_space=space)] * ins,
        out_specs=[pl.BlockSpec(memory_space=result)] * len(outs),
        scratch_shapes=list(scratch),
        compiler_params=PARAMS,
        name=name,
    )


def swap(array, axis, first, closed=False):
    count = lax.axis_size(axis)
    pairs = []
    for i in range(first, count, 2):
        if i + 1 < count or closed:
            j = (i + 1) % count
            pairs += [(i, j), (j, i)]
    return lax.ppermute(array, axis, pairs)


def per_device(
    spectrum,
    sea_mask,
    ice_mask,
    depth_class,
    speed_table,
    refraction_table,
    depth_slope,
    wind_speed,
    wind_dir,
    ice_rate,
):
    tile = (8, 128)
    block = (8,) + tile
    slabs = (SLABS,) + tile
    sent = (SENT,) + tile
    inputs = [spectrum, sea_mask, ice_mask, depth_class, depth_slope, wind_speed, wind_dir]
    tables = [speed_table, refraction_table, ice_rate]
    own, speeds, turnings, ices = call(
        pack_kernel,
        10,
        [(2,) + slabs] + [x.shape for x in tables],
        [pltpu.VMEM(x.shape, x.dtype) for x in inputs]
        + [pltpu.VMEM((NDIR * FREQ, 128), f32)] * 2
        + [pltpu.VMEM((16, 128), f32), pltpu.SemaphoreType.DMA((13,))],
        name="pack",
        space=pltpu.HBM,
    )(*[pltpu.with_memory_space_constraint(x, pltpu.HBM) for x in inputs + tables])
    (to_second,) = call(functools.partial(column_kernel, True), 1, [sent], name="column_far")(own)
    cols_second = swap(to_second, "lon", 1, True)
    (to_first,) = call(functools.partial(column_kernel, False), 1, [sent], name="column_near")(own)
    cols_first = swap(to_first, "lon", 0, True)
    (edge_second,) = call(functools.partial(edge_kernel, True), 1, [sent], name="edge_far")(own)
    rows_second = swap(edge_second, "lat", 1)
    (edge_first,) = call(functools.partial(edge_kernel, False), 1, [sent], name="edge_near")(own)
    rows_first = swap(edge_first, "lat", 0)
    place, rims, shifts, gather, spread, consts = call(
        tables_kernel,
        3,
        [(1536, 1024), (512, 1024), (2, 256, 384), (2048, 256), (32, 768), (20,) + tile],
        name="tables",
        dtype=[bf16] * 5 + [f32],
    )(speeds, turnings, ices)
    (gain,) = call(growth_kernel, 2, [(NDIR, 2) + tile], name="growth")(own, consts)
    west, east = call(unpack_kernel, 5, [slabs] * 2, name="unpack")(
        cols_second, cols_first, rows_second, rows_first, consts
    )
    (rim_second,) = call(functools.partial(rim_kernel, True), 2, [slabs], name="rim_far")(west, east)
    rims_second = swap(rim_second, "lat", 1)
    (rim_first,) = call(functools.partial(rim_kernel, False), 2, [slabs], name="rim_near")(west, east)
    rims_first = swap(rim_first, "lat", 0)
    south, north = call(unpack_rows_kernel, 2, [slabs] * 2, name="unpack_rows")(rows_second, rows_first)
    (partial,) = call(
        place_kernel,
        6,
        [(SLABS,) + block],
        [pltpu.VMEM((8 * SLABS + 8, 1536), bf16)],
        name="place",
    )(own, west, east, south, north, place)
    q, taps, ky, tx, ty = call(
        rims_kernel,
        5,
        [(NDIR,) + block, (10, 2, 4) + block] + [block] * 3,
        [pltpu.VMEM((8 * NDIR, 512), bf16)],
        name="rims",
    )(partial, rims_second, rims_first, consts, rims)
    cells = [(NDIR,) + block]
    for substep in range(ITERS):
        final = substep == ITERS - 1
        q, *sums = call(
            functools.partial(sweep_kernel, final),
            5,
            cells + [tile] * final,
            [pltpu.VMEM((4, 576, 384), f32)],
            name="sweep_sums" if final else "sweep",
        )(q, taps, ky, consts, shifts)
        if not final:
            (q,) = call(turn_kernel, 3, cells, name="turn")(q, tx, ty)
    (sums,) = sums
    other = swap(sums, "band", 0)
    (last,) = call(
        gather_kernel, 2, [(2, NDIR) + tile], [pltpu.VMEM((8 * NDIR, 2048), bf16)], name="gather"
    )(q, gather)
    static = own[:, STATIC:]
    (early,) = call(
        last_turn_kernel,
        4,
        [(256, NDIR * FREQ)],
        [pltpu.VMEM((NDIR * FREQ, 128), f32)] * 2,
        name="last_turn",
    )(last, static, gain, consts)
    (out,) = call(
        finish_kernel,
        6,
        [spectrum.shape],
        [pltpu.VMEM(spectrum.shape, f32), pltpu.SemaphoreType.DMA((8,))],
        name="finish",
        result=pltpu.HBM,
    )(early, static, sums, other, consts, spread)
    return out


def solution(mesh):
    return jax.shard_map(
        per_device,
        mesh=mesh,
        in_specs=(
            P("lat", "lon", "band"),
            P("lat", "lon"),
            P("lat", "lon"),
            P("lat", "lon"),
            P(),
            P(),
            P(None, "lat", "lon"),
            P("lat", "lon"),
            P("lat", "lon"),
            P(),
        ),
        out_specs=P("lat", "lon", "band"),
        check_vma=False,
    )
```

```python
import functools
import math

import jax
import jax.numpy as jnp
import numpy as np
from jax import lax
from jax.experimental import pallas as pl
from jax.experimental.pallas import tpu as pltpu
from jax.sharding import PartitionSpec as P

NDIR = 36
NCOMP = 576
ITERS = 4
NCLASS = 8
FREQ = 8
HALO = 8
ROWS = 16
STATIC = NDIR
SLABS = NDIR + 1
SEA, DEPTH, SLOPE_X, SLOPE_Y, ICE, WIND, WDIR = range(7)

freq_ratio = 1.1
wind_gain = 0.12
break_coef = 0.05
south_edge = -30.0
band_span = 60.0

COS = [math.cos(2.0 * math.pi * d / NDIR) for d in range(NDIR)]
SIN = [math.sin(2.0 * math.pi * d / NDIR) for d in range(NDIR)]
COS_FACE = [math.cos(2.0 * math.pi * (d + 0.5) / NDIR) for d in range(NDIR)]
SIN_FACE = [math.sin(2.0 * math.pi * (d + 0.5) / NDIR) for d in range(NDIR)]

TAB_SPEED, TAB_TURN, STRETCH, LIVE, ICE_RATE, LEVEL = 0, 8, 16, 17, 18, 19

f32 = jnp.float32
bf16 = jnp.bfloat16


def lanes():
    return lax.broadcasted_iota(jnp.int32, (8, 128), 1)


def roll(x, shift):
    shift = shift % 128
    return pltpu.roll(x, shift, 1) if shift else x


def is_even(axis):
    return lax.axis_index(axis) % 2 == 0


def place_field(wide, values, static, field):
    group = lax.broadcasted_iota(jnp.int32, (16, 128), 1) // 16
    row = lax.broadcasted_iota(jnp.int32, (16, 128), 0) % 8
    wide[:, :16] = values
    moved = pltpu.roll(wide[...], 0, 1, stride=16, stride_axis=0)
    kept = jnp.where(group == row, moved, 0.0)
    for half in range(2):
        static[half, field : field + 1, :] = jnp.sum(kept[8 * half : 8 * half + 8], axis=0, keepdims=True)


def fetch(sources, landed, sems):
    copies = [pltpu.make_async_copy(src, dst, sems.at[i]) for i, (src, dst) in enumerate(zip(sources, landed))]
    for copy in copies:
        copy.start()
    return copies


def pack_kernel(*refs):
    sources, own, landed = refs[:4], refs[4], refs[5:9]
    flat0, flat1, wide, static, sems = refs[9:]
    copies = fetch(sources, landed, sems)
    wide[...] = jnp.zeros_like(wide)
    static[...] = jnp.zeros_like(static)
    for copy in copies:
        copy.wait()
    spec, sea, depth, slope = landed
    place_field(wide, sea[...].astype(f32), static, SEA)
    place_field(wide, depth[...].astype(f32), static, DEPTH)
    place_field(wide, slope[0], static, SLOPE_X)
    place_field(wide, slope[1], static, SLOPE_Y)
    own[:, STATIC] = static[...]
    grid = spec[...].reshape(256, NDIR * FREQ)
    for low, high in ((0, 128), (128, 256), (256, 288)):
        turned = grid[:, low:high].T
        flat0[low:high, :] = turned[:, :128]
        flat1[low:high, :] = turned[:, 128:]
    sea0 = static[0, SEA : SEA + 1, :]
    sea1 = static[1, SEA : SEA + 1, :]
    for d in range(NDIR):
        own[0, d] = flat0[pl.ds(d, FREQ, stride=NDIR), :] * sea0
        own[1, d] = flat1[pl.ds(d, FREQ, stride=NDIR), :] * sea1


WEST_PAIRS = [(33, 0), (34, 1), (35, 2)]
EAST_PAIRS = [(15, 18), (16, 19), (17, 20)]


def slots(pairs):
    paired = [d for pair in pairs for d in pair]
    return [d for d in range(SLABS) if d not in paired]


SENT = SLABS - 3


def column_kernel(second, own, message):
    inner = lanes() % 16
    to_east = is_even("lon") != second
    from_own0 = (inner >= 8) == to_east
    shift = jnp.where(to_east, 120, 8)

    def edge(slab):
        return jnp.where(from_own0, own[0, slab], pltpu.roll(own[1, slab], shift, 1))

    for i, (east, west) in enumerate(zip(slots(EAST_PAIRS), slots(WEST_PAIRS))):
        if east == west:
            message[i] = edge(east)
        else:
            message[i] = edge(jnp.where(to_east, east, west))
    near = (inner % 8 >= 4) == to_east
    for i, (east, west) in enumerate(zip(EAST_PAIRS, WEST_PAIRS)):
        one = edge(jnp.where(to_east, east[0], west[0]))
        two = edge(jnp.where(to_east, east[1], west[1]))
        message[SENT - 3 + i] = jnp.where(near, one, pltpu.roll(two, jnp.where(to_east, 124, 4), 1))


NORTH_PAIRS = [(24, 27), (25, 28), (26, 29)]
SOUTH_PAIRS = [(6, 9), (7, 10), (8, 11)]


def edge_kernel(second, own, message):
    to_north = is_even("lat") != second
    for i, (north, south) in enumerate(zip(slots(NORTH_PAIRS), slots(SOUTH_PAIRS))):
        message[i] = jnp.where(to_north, own[1, north], own[0, south])
    near = (lanes() >= 64) == to_north
    for i, (north, south) in enumerate(zip(NORTH_PAIRS, SOUTH_PAIRS)):
        one = jnp.where(to_north, own[1, north[0]], own[0, south[0]])
        two = jnp.where(to_north, own[1, north[1]], own[0, south[1]])
        message[SENT - 3 + i] = jnp.where(near, one, roll(two, 64))


def growth_kernel(own, local, consts, gain):
    for half in range(2):
        point = local[half]
        turn = point[WDIR : WDIR + 1]
        cos_w = jnp.cos(turn)
        sin_w = jnp.sin(turn)
        force = wind_gain * point[WIND : WIND + 1] * consts[LEVEL]
        share = own[half, STATIC, SEA : SEA + 1]
        for d in range(NDIR):
            along = jnp.maximum(COS[d] * cos_w + SIN[d] * sin_w, 0.0)
            gain[d, half] = jnp.exp(force * along) * share


def tables_kernel(*refs):
    sources, (place, rims, shifts, gather, local, consts), landed = refs[:6], refs[6:12], refs[12:18]
    wide, sems = refs[18:]
    speed_table, refraction_table, ice_rate, ice, wspeed, wdir = landed
    copies = fetch(sources, landed, sems)
    first = lax.axis_index("band") * FREQ
    sub = lax.broadcasted_iota(jnp.int32, (8, 128), 0)
    mine = lanes() == first + sub

    def column(row):
        picked = jnp.where(mine, jnp.broadcast_to(row, (8, 128)), 0.0)
        return jnp.broadcast_to(jnp.sum(picked, axis=1, keepdims=True), (8, 128))

    def widen(values):
        return jnp.concatenate([values, jnp.zeros((values.shape[0], 112), f32)], axis=1)

    consts[LEVEL] = jnp.exp(math.log(freq_ratio) * (first + sub).astype(f32))
    lat = lax.axis_index("lat")
    lats = lax.axis_size("lat")
    group = lanes() // 32
    rows = lat * ROWS - HALO + 8 * group + sub
    latitude = (south_edge + band_span * (rows.astype(f32) + 0.5) / (ROWS * lats)) * (math.pi / 180.0)
    consts[STRETCH] = 1.0 / jnp.cos(latitude)
    ghost = ((group == 0) & (lat == 0)) | ((group == 3) & (lat == lats - 1))
    consts[LIVE] = jnp.where(ghost, 0.0, 1.0)
    chunk = lax.broadcasted_iota(jnp.int32, (16, 128), 0)
    lane = lax.broadcasted_iota(jnp.int32, (16, 128), 1)
    low = chunk < 8
    targets = [
        40 + chunk,
        72 + chunk,
        jnp.where(low, 64 + chunk, 24 + chunk),
        jnp.where(low, 56 + chunk, 80 + chunk),
        8 + chunk,
        104 + chunk,
    ]
    corners = [jnp.where(low, chunk, 16 + chunk), jnp.where(low, 120 + chunk, 88 + chunk)]
    for matrix, lists in ((place, targets), (rims, corners)):
        matrix[...] = jnp.zeros_like(matrix)
        for s, target in enumerate(lists):
            stripe = (lane == target).astype(f32).astype(bf16)
            for part in range(2):
                for t in range(8):
                    row = part * 128 * len(lists) + s * 128 + 16 * t
                    matrix[row : row + 16, 128 * t : 128 * t + 128] = stripe
    row = lax.broadcasted_iota(jnp.int32, (128, 128), 0)
    col = lax.broadcasted_iota(jnp.int32, (128, 128), 1)
    for sign, taps in ((0, FORTH_TAPS), (1, BACK_TAPS)):
        for i, tap in enumerate(taps):
            moved = (row == (col + tap) % 128).astype(f32).astype(bf16)
            for part in range(2):
                shifts[sign, 128 * part : 128 * part + 128, 128 * i : 128 * i + 128] = moved
    for t in range(8):
        for half in range(2):
            from_row = 40 + 32 * half + col % 16
            moved = ((col // 16 == t) & (row == from_row)).astype(f32).astype(bf16)
            for part in range(2):
                at = part * 1024 + 128 * t
                gather[at : at + 128, 128 * half : 128 * half + 128] = moved
    local[...] = jnp.zeros_like(local)
    wide[...] = jnp.zeros_like(wide)
    for copy in copies:
        copy.wait()
    for at, table in ((TAB_SPEED, speed_table), (TAB_TURN, refraction_table)):
        padded = widen(table[...])
        for c in range(NCLASS):
            consts[at + c] = column(padded[c : c + 1])
    consts[ICE_RATE] = column(widen(ice_rate[...].reshape(1, 16)))
    place_field(wide, ice[...].astype(f32), local, ICE)
    place_field(wide, wspeed[...], local, WIND)
    place_field(wide, wdir[...], local, WDIR)


def unpack(even, first, second, pairs, out, back):
    full = slots(pairs)
    for i in range(SENT):
        got = jnp.where(even, first[i], second[i])
        if i < len(full):
            out[full[i]] = got
        else:
            pair = pairs[i - len(full)]
            out[pair[0]] = got
            out[pair[1]] = roll(got, back)


def unpack_kernel(cols_second, cols_first, rows_second, rows_first, consts, west, east):
    del rows_second, rows_first, consts
    even = is_even("lon")
    unpack(even, cols_second, cols_first, EAST_PAIRS, west, 4)
    unpack(even, cols_first, cols_second, WEST_PAIRS, east, -4)


def unpack_rows_kernel(rows_second, rows_first, south, north):
    even = is_even("lat")
    unpack(even, rows_second, rows_first, NORTH_PAIRS, south, 64)
    unpack(even, rows_first, rows_second, SOUTH_PAIRS, north, 64)


def rim_kernel(second, west, east, rim):
    west_low = (lanes() % 16 < 8) == (is_even("lat") != second)
    for slab in range(SLABS):
        rim[slab] = jnp.where(west_low, west[slab], east[slab])


def split(x):
    high = x.astype(bf16)
    return high, (x - high.astype(f32)).astype(bf16)


def fill_parts(lhs, count, s, array):
    x = jnp.concatenate([array.reshape(8 * SLABS, 128), jnp.zeros((8, 128), f32)], axis=0)
    high, low = split(x)
    lhs[:, 128 * s : 128 * s + 128] = high
    lhs[:, 128 * (count + s) : 128 * (count + s) + 128] = low


def place_kernel(own, west, east, south, north, matrix, q, lhs):
    fill_parts(lhs, 6, 0, own[0])
    fill_parts(lhs, 6, 1, own[1])
    fill_parts(lhs, 6, 2, west[...])
    fill_parts(lhs, 6, 3, east[...])
    fill_parts(lhs, 6, 4, south[...])
    fill_parts(lhs, 6, 5, north[...])
    for pair in range(4):
        moved = jnp.dot(lhs[...], matrix[:, 256 * pair : 256 * pair + 256], preferred_element_type=f32)
        for i in range(2):
            q[:, 2 * pair + i] = moved[: 8 * SLABS, 128 * i : 128 * i + 128].reshape(SLABS, 8, 128)


def lookup(point, consts, at):
    depth = jnp.broadcast_to(point[DEPTH : DEPTH + 1], (8, 128))
    value = jnp.zeros((8, 128), f32)
    for c in range(NCLASS):
        value = jnp.where(depth == float(c), consts[at + c], value)
    return value * point[SEA : SEA + 1]


def rims_kernel(partial, rims_second, rims_first, consts, matrix, q, taps, ky, tx, ty, lhs):
    even_lat = is_even("lat")
    south = jnp.where(even_lat, rims_second[...], rims_first[...])
    north = jnp.where(even_lat, rims_first[...], rims_second[...])
    for s, array in ((0, south), (1, north)):
        high, low = split(array[:NDIR].reshape(8 * NDIR, 128))
        lhs[:, 128 * s : 128 * s + 128] = high
        lhs[:, 128 * (2 + s) : 128 * (2 + s) + 128] = low
    lane = lanes()
    south, north = south[STATIC], north[STATIC]
    speed = []
    for t in range(8):
        if t % 2 == 0:
            moved = jnp.dot(lhs[...], matrix[:, 128 * t : 128 * t + 256], preferred_element_type=f32)
            for i in range(2):
                q[:, t + i] = partial[:NDIR, t + i] + moved[:, 128 * i : 128 * i + 128].reshape(NDIR, 8, 128)
        point = partial[STATIC, t]
        for low, array, shift in ((0, south, 0), (24, south, 16), (96, north, 88), (120, north, 120)):
            point = jnp.where((lane >= low) & (lane < low + 8), roll(array, shift - 16 * t), point)
        pace = lookup(point, consts, TAB_SPEED)
        turning = lookup(point, consts, TAB_TURN)
        speed.append(pace)
        tx[t] = turning * point[SLOPE_X : SLOPE_X + 1]
        ty[t] = turning * point[SLOPE_Y : SLOPE_Y + 1]
        stretch = consts[STRETCH, t : t + 1, :]
        right = 0.5 * (pace + roll(pace, -1)) * stretch
        left = 0.5 * (pace + roll(pace, 1)) * stretch
        for base in range(10):
            a1, b1, c1 = weights(COS[base] * right)
            a0, b0, c0 = weights(COS[base] * left)
            taps[base, 0, 0, t] = 1.0 - a1 + b0
            taps[base, 0, 1, t] = -b1
            taps[base, 0, 2, t] = a0 - c1
            taps[base, 0, 3, t] = c0
            taps[base, 1, 0, t] = 1.0 + b1 - a0
            taps[base, 1, 1, t] = a1 - c0
            taps[base, 1, 2, t] = -b0
            taps[base, 1, 3, t] = c1
    for t in range(8):
        ahead = speed[t + 1] if t < 7 else roll(speed[0], -32)
        ky[t] = 0.5 * (speed[t] + ahead)


def flux(q, diff, curve, k, u, w):
    return k * (q + u * (diff - w * curve))


def halves(k):
    return 0.5 - 0.5 * k, (1.0 / 3.0) + (1.0 / 3.0) * k


def weights(k):
    u, w = halves(k)
    bend = k * u * w
    return k - k * u + 2.0 * bend, k * u - bend, -bend


FORTH_TAPS = (-1, -2)
BACK_TAPS = (-1, 2)


def lon_kernel(q, taps, shifts, out):
    for sign in range(2):
        for base in range(10):
            if base == 0:
                dirs = [[0], [18]][sign]
            elif base == 9:
                dirs = [[27], [9]][sign]
            else:
                dirs = [[base, 36 - base], [18 - base, 18 + base]][sign]
            x = jnp.concatenate([q[d].reshape(64, 128) for d in dirs], axis=0)
            lhs = jnp.concatenate(split(x), axis=1)
            moved = jnp.dot(lhs, shifts[sign], preferred_element_type=f32)
            for t in range(8):
                tap = [taps[base, sign, i, t] for i in range(4)]
                for i, d in enumerate(dirs):
                    cell = q[d, t]
                    near = moved[64 * i + 8 * t : 64 * i + 8 * t + 8]
                    out[d, t] = (tap[0] * cell + tap[1] * roll(cell, -1)) + (
                        tap[2] * near[:, :128] + tap[3] * near[:, 128:]
                    )


def lat_kernel(q, ky, consts, out, sums=None):
    live = consts[LIVE]
    totals = [jnp.zeros((8, 128), f32)] * 8

    def put(d, t, value):
        out[d, t] = value
        if sums is not None:
            totals[t] = totals[t] + value

    def forth(d, ks, us, ws):
        tiles = [q[d, t] for t in range(8)]
        diff = [tiles[t + 1] - tiles[t] for t in range(7)]
        diff.append(roll(tiles[0], -32) - tiles[7])
        before = roll(diff[7], 32)
        fluxes = []
        for t in range(8):
            fluxes.append(flux(tiles[t], diff[t], diff[t] - before, ks[t], us[t], ws[t]))
            before = diff[t]
        behind = roll(fluxes[7], 32)
        for t in range(8):
            put(d, t, (tiles[t] - fluxes[t] + behind) * live)
            behind = fluxes[t]

    def back(d, ks, us, ws):
        tiles = [q[d, t] for t in range(8)]
        ahead = tiles[1:] + [roll(tiles[0], -32)]
        diff = [tiles[t] - ahead[t] for t in range(8)]
        after = diff[1:] + [roll(diff[0], -32)]
        fluxes = [flux(ahead[t], diff[t], diff[t] - after[t], ks[t], us[t], ws[t]) for t in range(8)]
        behind = roll(fluxes[7], 32)
        for t in range(8):
            put(d, t, (tiles[t] + fluxes[t] - behind) * live)
            behind = fluxes[t]

    for base in range(10):
        ks = [SIN[base] * ky[t] for t in range(8)]
        us, ws = zip(*[halves(k) for k in ks])
        if base == 0:
            north, south = [0], [18]
        elif base == 9:
            north, south = [9], [27]
        else:
            north, south = [base, 18 - base], [18 + base, 36 - base]
        for d in north:
            forth(d, ks, us, ws)
        for d in south:
            back(d, ks, us, ws)
    if sums is None:
        return
    lane = lanes()
    halves_of = [jnp.zeros((8, 128), f32)] * 2
    for t in range(8):
        moved = roll(totals[t], 16 * t - 40)
        halves_of[0] = jnp.where(lane // 16 == t, moved, halves_of[0])
        halves_of[1] = jnp.where(lane // 16 == (t + 2) % 8, moved, halves_of[1])
    halves_of[1] = roll(halves_of[1], -32)
    sums[...] = jnp.zeros((8, 128), f32)
    for half in range(2):
        sums[half : half + 1, :] = jnp.sum(halves_of[half], axis=0, keepdims=True)
        sums[2 + half : 3 + half, :] = jnp.sum(halves_of[half] * consts[LEVEL], axis=0, keepdims=True)


def turn_around(get, put, x, y):
    def factors(d):
        k = SIN_FACE[d] * x - COS_FACE[d] * y
        half, third = 0.5 * k, (1.0 / 3.0) * k
        return k, 0.5 - half, 1.0 / 3.0 + third, 0.5 + half, 1.0 / 3.0 - third

    half_turn = NDIR // 2
    k, u, w, u_back, w_back = factors(half_turn - 1)
    state = []
    ends = []
    for at in (0, half_turn):
        cell, ahead = get(at), get(at + 1)
        before, last = get((at - 1) % NDIR), get((at - 2) % NDIR)
        diff = ahead - cell
        diff1 = cell - before
        curve = diff - diff1
        curve1 = diff1 - (before - last)
        if at == 0:
            f = flux(before, diff1, jnp.where(k >= 0.0, curve, curve1), k, u_back, w_back)
        else:
            f = flux(before, diff1, jnp.where(k >= 0.0, curve1, curve), k, u, w)
        state.append([cell, ahead, diff, curve])
        ends.append(f)
    f_first, f_second = -ends[0], -ends[1]
    for d in range(half_turn):
        if d < half_turn - 1:
            k, u, w, u_back, w_back = factors(d)
            positive = k >= 0.0
        for at in (0, half_turn):
            cell, ahead, diff, curve = state[at // half_turn]
            beyond = get((at + d + 2) % NDIR)
            diff_ahead = beyond - ahead
            curve_ahead = diff_ahead - diff
            if at == 0:
                if d < half_turn - 1:
                    f = flux(cell, diff, jnp.where(positive, curve, curve_ahead), k, u, w)
                else:
                    f = ends[1]
                put(d, cell - f + f_first)
                f_first = f
            else:
                if d < half_turn - 1:
                    f = flux(cell, diff, jnp.where(positive, curve_ahead, curve), k, u_back, w_back)
                else:
                    f = ends[0]
                put(at + d, cell + f - f_second)
                f_second = f
            state[at // half_turn] = [ahead, beyond, diff_ahead, curve_ahead]


def turn_kernel(q, tx, ty, out):
    for t in range(8):

        def put(d, value, t=t):
            out[d, t] = value

        turn_around(lambda d, t=t: q[d, t], put, tx[t], ty[t])


def gather_kernel(q, matrix, own, lhs):
    for t in range(8):
        high, low = split(q[:, t].reshape(8 * NDIR, 128))
        lhs[:, 128 * t : 128 * t + 128] = high
        lhs[:, 1024 + 128 * t : 1024 + 128 * t + 128] = low
    moved = jnp.dot(lhs[...], matrix[...], preferred_element_type=f32)
    for half in range(2):
        own[half] = moved[:, 128 * half : 128 * half + 128].reshape(NDIR, 8, 128)


def last_turn_kernel(own, static, gain, consts, early):
    for half in range(2):
        point = static[half, 0]
        turning = lookup(point, consts, TAB_TURN)

        def put(d, value, half=half):
            early[half, d] = value * gain[d, half]

        turn_around(
            lambda d, half=half: own[half, d],
            put,
            turning * point[SLOPE_X : SLOPE_X + 1],
            turning * point[SLOPE_Y : SLOPE_Y + 1],
        )


def finish_kernel(early, local, sums, other, consts, out, flat0, flat1):
    total = sums[...] + other[...]
    level = consts[LEVEL]
    for half, flat in ((0, flat0), (1, flat1)):
        energy = total[half : half + 1]
        moment = total[2 + half : 3 + half]
        mean_level = jnp.maximum(moment, 1.0) / jnp.maximum(energy, 1.0)
        mean = energy / NCOMP
        breaking = break_coef * level * level / mean_level * (mean * mean)
        damping = local[half, ICE : ICE + 1] * consts[ICE_RATE]
        loss = jnp.exp(-breaking - damping)
        for d in range(NDIR):
            flat[pl.ds(d, FREQ, stride=NDIR), :] = early[half, d] * loss
        for low, high in ((0, 128), (128, 256), (256, 288)):
            out[8 * half : 8 * half + 8, :, low:high] = flat[low:high, :].T.reshape(8, 16, high - low)


PARAMS = pltpu.CompilerParams(vmem_limit_bytes=40 * 2**20)


def call(kernel, ins, outs, scratch=(), name=None, space=pltpu.VMEM, dtype=f32, result=pltpu.VMEM):
    types = dtype if isinstance(dtype, list) else [dtype] * len(outs)
    return pl.pallas_call(
        kernel,
        out_shape=[jax.ShapeDtypeStruct(shape, kind) for shape, kind in zip(outs, types)],
        in_specs=[pl.BlockSpec(memory_space=space)] * ins,
        out_specs=[pl.BlockSpec(memory_space=result)] * len(outs),
        scratch_shapes=list(scratch),
        compiler_params=PARAMS,
        name=name,
    )


def swap(array, axis, first, closed=False):
    count = lax.axis_size(axis)
    pairs = []
    for i in range(first, count, 2):
        if i + 1 < count or closed:
            j = (i + 1) % count
            pairs += [(i, j), (j, i)]
    return lax.ppermute(array, axis, pairs)


def per_device(
    spectrum,
    sea_mask,
    ice_mask,
    depth_class,
    speed_table,
    refraction_table,
    depth_slope,
    wind_speed,
    wind_dir,
    ice_rate,
):
    tile = (8, 128)
    block = (8,) + tile
    slabs = (SLABS,) + tile
    sent = (SENT,) + tile
    inputs = [spectrum, sea_mask, depth_class, depth_slope]
    (own,) = call(
        pack_kernel,
        4,
        [(2,) + slabs],
        [pltpu.VMEM(x.shape, x.dtype) for x in inputs]
        + [pltpu.VMEM((NDIR * FREQ, 128), f32)] * 2
        + [pltpu.VMEM((16, 128), f32), pltpu.VMEM((2,) + tile, f32), pltpu.SemaphoreType.DMA((4,))],
        name="pack",
        space=pltpu.HBM,
    )(*[pltpu.with_memory_space_constraint(x, pltpu.HBM) for x in inputs])
    (to_second,) = call(functools.partial(column_kernel, True), 1, [sent], name="column_far")(own)
    cols_second = swap(to_second, "lon", 1, True)
    (to_first,) = call(functools.partial(column_kernel, False), 1, [sent], name="column_near")(own)
    cols_first = swap(to_first, "lon", 0, True)
    (edge_second,) = call(functools.partial(edge_kernel, True), 1, [sent], name="edge_far")(own)
    rows_second = swap(edge_second, "lat", 1)
    (edge_first,) = call(functools.partial(edge_kernel, False), 1, [sent], name="edge_near")(own)
    rows_first = swap(edge_first, "lat", 0)
    inputs = [speed_table, refraction_table, ice_rate, ice_mask, wind_speed, wind_dir]
    place, rims, shifts, gather, local, consts = call(
        tables_kernel,
        6,
        [(1536, 1024), (512, 1024), (2, 256, 256), (2048, 256), (2,) + tile, (20,) + tile],
        [pltpu.VMEM(x.shape, x.dtype) for x in inputs]
        + [pltpu.VMEM((16, 128), f32), pltpu.SemaphoreType.DMA((6,))],
        name="tables",
        space=pltpu.HBM,
        dtype=[bf16] * 4 + [f32] * 2,
    )(*[pltpu.with_memory_space_constraint(x, pltpu.HBM) for x in inputs])
    (gain,) = call(growth_kernel, 3, [(NDIR, 2) + tile], name="growth")(own, local, consts)
    west, east = call(unpack_kernel, 5, [slabs] * 2, name="unpack")(
        cols_second, cols_first, rows_second, rows_first, consts
    )
    (rim_second,) = call(functools.partial(rim_kernel, True), 2, [slabs], name="rim_far")(west, east)
    rims_second = swap(rim_second, "lat", 1)
    (rim_first,) = call(functools.partial(rim_kernel, False), 2, [slabs], name="rim_near")(west, east)
    rims_first = swap(rim_first, "lat", 0)
    south, north = call(unpack_rows_kernel, 2, [slabs] * 2, name="unpack_rows")(rows_second, rows_first)
    (partial,) = call(
        place_kernel,
        6,
        [(SLABS,) + block],
        [pltpu.VMEM((8 * SLABS + 8, 1536), bf16)],
        name="place",
    )(own, west, east, south, north, place)
    q, taps, ky, tx, ty = call(
        rims_kernel,
        5,
        [(NDIR,) + block, (10, 2, 4) + block] + [block] * 3,
        [pltpu.VMEM((8 * NDIR, 512), bf16)],
        name="rims",
    )(partial, rims_second, rims_first, consts, rims)
    cells = [(NDIR,) + block]
    for substep in range(ITERS):
        (q,) = call(lon_kernel, 3, cells, name="lon")(q, taps, shifts)
        if substep == ITERS - 1:
            q, sums = call(lat_kernel, 3, cells + [tile], name="lat_sums")(q, ky, consts)
        else:
            (q,) = call(lat_kernel, 3, cells, name="lat")(q, ky, consts)
            (q,) = call(turn_kernel, 3, cells, name="turn")(q, tx, ty)
    other = swap(sums, "band", 0)
    (last,) = call(
        gather_kernel, 2, [(2, NDIR) + tile], [pltpu.VMEM((8 * NDIR, 2048), bf16)], name="gather"
    )(q, gather)
    static = own[:, STATIC:]
    (early,) = call(last_turn_kernel, 4, [(2, NDIR) + tile], name="last_turn")(last, static, gain, consts)
    (out,) = call(
        finish_kernel, 5, [spectrum.shape], [pltpu.VMEM((NDIR * FREQ, 128), f32)] * 2, name="finish"
    )(early, local, sums, other, consts)
    return out


def solution(mesh):
    return jax.shard_map(
        per_device,
        mesh=mesh,
        in_specs=(
            P("lat", "lon", "band"),
            P("lat", "lon"),
            P("lat", "lon"),
            P("lat", "lon"),
            P(),
            P(),
            P(None, "lat", "lon"),
            P("lat", "lon"),
            P("lat", "lon"),
            P(),
        ),
        out_specs=P("lat", "lon", "band"),
        check_vma=False,
    )
```

```python
import functools
import math

import jax
import jax.numpy as jnp
import numpy as np
from jax import lax
from jax.experimental import pallas as pl
from jax.experimental.pallas import tpu as pltpu
from jax.sharding import PartitionSpec as P

NDIR = 36
NCOMP = 576
ITERS = 4
NCLASS = 8
FREQ = 8
HALO = 8
ROWS = 16
STATIC = NDIR
SLABS = NDIR + 1
SEA, DEPTH, SLOPE_X, SLOPE_Y, ICE, WIND, WDIR = range(7)

freq_ratio = 1.1
wind_gain = 0.12
break_coef = 0.05
south_edge = -30.0
band_span = 60.0

COS = [math.cos(2.0 * math.pi * d / NDIR) for d in range(NDIR)]
SIN = [math.sin(2.0 * math.pi * d / NDIR) for d in range(NDIR)]
COS_FACE = [math.cos(2.0 * math.pi * (d + 0.5) / NDIR) for d in range(NDIR)]
SIN_FACE = [math.sin(2.0 * math.pi * (d + 0.5) / NDIR) for d in range(NDIR)]

TAB_SPEED, TAB_TURN, STRETCH, LIVE, ICE_RATE, LEVEL = 0, 8, 16, 17, 18, 19

f32 = jnp.float32
bf16 = jnp.bfloat16


def lanes():
    return lax.broadcasted_iota(jnp.int32, (8, 128), 1)


def roll(x, shift):
    shift = shift % 128
    return pltpu.roll(x, shift, 1) if shift else x


def is_even(axis):
    return lax.axis_index(axis) % 2 == 0


def place_field(wide, values, static, field):
    group = lax.broadcasted_iota(jnp.int32, (16, 128), 1) // 16
    row = lax.broadcasted_iota(jnp.int32, (16, 128), 0) % 8
    wide[:, :16] = values
    moved = pltpu.roll(wide[...], 0, 1, stride=16, stride_axis=0)
    kept = jnp.where(group == row, moved, 0.0)
    for half in range(2):
        static[half, field : field + 1, :] = jnp.sum(kept[8 * half : 8 * half + 8], axis=0, keepdims=True)


def fetch(sources, landed, sems):
    copies = [pltpu.make_async_copy(src, dst, sems.at[i]) for i, (src, dst) in enumerate(zip(sources, landed))]
    for copy in copies:
        copy.start()
    return copies


def pack_kernel(*refs):
    sources, own, landed = refs[:4], refs[4], refs[5:9]
    flat0, flat1, wide, static, sems = refs[9:]
    copies = fetch(sources, landed, sems)
    wide[...] = jnp.zeros_like(wide)
    static[...] = jnp.zeros_like(static)
    for copy in copies:
        copy.wait()
    spec, sea, depth, slope = landed
    place_field(wide, sea[...].astype(f32), static, SEA)
    place_field(wide, depth[...].astype(f32), static, DEPTH)
    place_field(wide, slope[0], static, SLOPE_X)
    place_field(wide, slope[1], static, SLOPE_Y)
    own[:, STATIC] = static[...]
    grid = spec[...].reshape(256, NDIR * FREQ)
    for low, high in ((0, 128), (128, 256), (256, 288)):
        turned = grid[:, low:high].T
        flat0[low:high, :] = turned[:, :128]
        flat1[low:high, :] = turned[:, 128:]
    sea0 = static[0, SEA : SEA + 1, :]
    sea1 = static[1, SEA : SEA + 1, :]
    for d in range(NDIR):
        own[0, d] = flat0[pl.ds(d, FREQ, stride=NDIR), :] * sea0
        own[1, d] = flat1[pl.ds(d, FREQ, stride=NDIR), :] * sea1


NEEDS = (7, 7, 6, 6, 5, 5, 4, 4, 4, 4, 4, 4, 5, 5, 6, 6, 7, 7)
PACKED = {
    0: [(12, 3, 7, 1)],
    1: [(12, 4, 7, 1)],
    2: [(15, 0, 6, 2)],
    3: [(15, 2, 6, 2)],
    4: [(12, 0, 5, 3)],
    5: [(13, 0, 5, 3)],
    6: [(9, 0, 4, 4)],
    7: [(10, 0, 4, 4)],
    8: [(11, 0, 4, 4)],
    14: [(15, 4, 6, 2)],
    16: [(13, 3, 7, 1)],
    17: [(13, 4, 7, 1)],
}
TO_WEST, TO_EAST, TO_NORTH, TO_SOUTH = 27, 9, 18, 0
SENT = 18 + 1 + len(PACKED)


def downstream(first):
    return [(first + i) % NDIR for i in range(18)]


def whole(first):
    return [d for d in range(NDIR) if d not in downstream(first)] + [STATIC]


def write_message(message, get, rising, rising_first, falling_first, place, unit):
    for i, pair in enumerate(zip(whole(rising_first), whole(falling_first))):
        message[i] = get(*pair)
    up, down = downstream(rising_first), downstream(falling_first)
    cell = jnp.where(rising, place, 7 - place)
    for i, (main, pieces) in enumerate(PACKED.items()):
        value = get(up[main], down[main])
        for other, start, to, count in pieces:
            shift = (to - start) * unit
            moved = pltpu.roll(get(up[other], down[other]), jnp.where(rising, shift, 128 - shift), 1)
            value = jnp.where((cell >= to) & (cell < to + count), moved, value)
        message[19 + i] = value


def read_message(message, out, rising, first, place, unit):
    for i, d in enumerate(whole(first)):
        out[d] = message(i)
    dirs = downstream(first)
    cell = place if rising else 7 - place
    parts = {}
    for i, (main, pieces) in enumerate(PACKED.items()):
        value = message(19 + i)
        out[dirs[main]] = value
        for other, start, to, count in pieces:
            shift = (start - to) * unit
            moved = roll(value, shift if rising else -shift)
            if other in parts:
                moved = jnp.where((cell >= start) & (cell < start + count), moved, parts[other])
            parts[other] = moved
    for other, value in parts.items():
        out[dirs[other]] = value


def column_kernel(second, own, message):
    inner = lanes() % 16
    to_east = is_even("lon") != second
    from_own0 = (inner >= 8) == to_east
    shift = jnp.where(to_east, 120, 8)

    def get(west, east):
        slab = west if west == east else jnp.where(to_east, east, west)
        return jnp.where(from_own0, own[0, slab], pltpu.roll(own[1, slab], shift, 1))

    write_message(message, get, ~to_east, TO_WEST, TO_EAST, inner % 8, 1)


def edge_kernel(second, own, message):
    to_north = is_even("lat") != second

    def get(south, north):
        return jnp.where(to_north, own[1, north], own[0, south])

    write_message(message, get, ~to_north, TO_SOUTH, TO_NORTH, lanes() // 16, 16)


def growth_kernel(own, local, consts, gain):
    for half in range(2):
        point = local[half]
        turn = point[WDIR : WDIR + 1]
        cos_w = jnp.cos(turn)
        sin_w = jnp.sin(turn)
        force = wind_gain * point[WIND : WIND + 1] * consts[LEVEL]
        share = own[half, STATIC, SEA : SEA + 1]
        for d in range(NDIR):
            along = jnp.maximum(COS[d] * cos_w + SIN[d] * sin_w, 0.0)
            gain[d, half] = jnp.exp(force * along) * share


def tables_kernel(*refs):
    sources, (place, rims, shifts, gather, local, consts), landed = refs[:6], refs[6:12], refs[12:18]
    wide, sems = refs[18:]
    speed_table, refraction_table, ice_rate, ice, wspeed, wdir = landed
    copies = fetch(sources, landed, sems)
    first = lax.axis_index("band") * FREQ
    sub = lax.broadcasted_iota(jnp.int32, (8, 128), 0)
    mine = lanes() == first + sub

    def column(row):
        picked = jnp.where(mine, jnp.broadcast_to(row, (8, 128)), 0.0)
        return jnp.broadcast_to(jnp.sum(picked, axis=1, keepdims=True), (8, 128))

    def widen(values):
        return jnp.concatenate([values, jnp.zeros((values.shape[0], 112), f32)], axis=1)

    consts[LEVEL] = jnp.exp(math.log(freq_ratio) * (first + sub).astype(f32))
    lat = lax.axis_index("lat")
    lats = lax.axis_size("lat")
    group = lanes() // 32
    rows = lat * ROWS - HALO + 8 * group + sub
    latitude = (south_edge + band_span * (rows.astype(f32) + 0.5) / (ROWS * lats)) * (math.pi / 180.0)
    consts[STRETCH] = 1.0 / jnp.cos(latitude)
    ghost = ((group == 0) & (lat == 0)) | ((group == 3) & (lat == lats - 1))
    consts[LIVE] = jnp.where(ghost, 0.0, 1.0)
    chunk = lax.broadcasted_iota(jnp.int32, (16, 128), 0)
    lane = lax.broadcasted_iota(jnp.int32, (16, 128), 1)
    low = chunk < 8
    targets = [
        40 + chunk,
        72 + chunk,
        jnp.where(low, 64 + chunk, 24 + chunk),
        jnp.where(low, 56 + chunk, 80 + chunk),
        8 + chunk,
        104 + chunk,
    ]
    corners = [jnp.where(low, chunk, 16 + chunk), jnp.where(low, 120 + chunk, 88 + chunk)]
    for matrix, lists in ((place, targets), (rims, corners)):
        matrix[...] = jnp.zeros_like(matrix)
        for s, target in enumerate(lists):
            stripe = (lane == target).astype(f32).astype(bf16)
            for part in range(2):
                for t in range(8):
                    row = part * 128 * len(lists) + s * 128 + 16 * t
                    matrix[row : row + 16, 128 * t : 128 * t + 128] = stripe
    row = lax.broadcasted_iota(jnp.int32, (128, 128), 0)
    col = lax.broadcasted_iota(jnp.int32, (128, 128), 1)
    for sign, taps in ((0, FORTH_TAPS), (1, BACK_TAPS)):
        for i, tap in enumerate(taps):
            moved = (row == (col + tap) % 128).astype(f32).astype(bf16)
            for part in range(2):
                shifts[sign, 128 * part : 128 * part + 128, 128 * i : 128 * i + 128] = moved
    for t in range(8):
        for half in range(2):
            from_row = 40 + 32 * half + col % 16
            moved = ((col // 16 == t) & (row == from_row)).astype(f32).astype(bf16)
            for part in range(2):
                at = part * 1024 + 128 * t
                gather[at : at + 128, 128 * half : 128 * half + 128] = moved
    local[...] = jnp.zeros_like(local)
    wide[...] = jnp.zeros_like(wide)
    for copy in copies:
        copy.wait()
    for at, table in ((TAB_SPEED, speed_table), (TAB_TURN, refraction_table)):
        padded = widen(table[...])
        for c in range(NCLASS):
            consts[at + c] = column(padded[c : c + 1])
    consts[ICE_RATE] = column(widen(ice_rate[...].reshape(1, 16)))
    place_field(wide, ice[...].astype(f32), local, ICE)
    place_field(wide, wspeed[...], local, WIND)
    place_field(wide, wdir[...], local, WDIR)


def unpack_kernel(cols_second, cols_first, rows_second, rows_first, consts, west, east):
    del rows_second, rows_first, consts
    even = is_even("lon")
    place = lanes() % 8
    read_message(lambda i: jnp.where(even, cols_second[i], cols_first[i]), west, False, TO_EAST, place, 1)
    read_message(lambda i: jnp.where(even, cols_first[i], cols_second[i]), east, True, TO_WEST, place, 1)


def unpack_rows_kernel(rows_second, rows_first, south, north):
    even = is_even("lat")
    place = lanes() // 16
    read_message(lambda i: jnp.where(even, rows_second[i], rows_first[i]), south, False, TO_NORTH, place, 16)
    read_message(lambda i: jnp.where(even, rows_first[i], rows_second[i]), north, True, TO_SOUTH, place, 16)


def rim_kernel(second, west, east, rim):
    west_low = (lanes() % 16 < 8) == (is_even("lat") != second)
    for slab in range(SLABS):
        rim[slab] = jnp.where(west_low, west[slab], east[slab])


def split(x):
    high = x.astype(bf16)
    return high, (x - high.astype(f32)).astype(bf16)


def fill_parts(lhs, count, s, array):
    x = jnp.concatenate([array.reshape(8 * SLABS, 128), jnp.zeros((8, 128), f32)], axis=0)
    high, low = split(x)
    lhs[:, 128 * s : 128 * s + 128] = high
    lhs[:, 128 * (count + s) : 128 * (count + s) + 128] = low


def place_kernel(own, west, east, south, north, matrix, q, lhs):
    fill_parts(lhs, 6, 0, own[0])
    fill_parts(lhs, 6, 1, own[1])
    fill_parts(lhs, 6, 2, west[...])
    fill_parts(lhs, 6, 3, east[...])
    fill_parts(lhs, 6, 4, south[...])
    fill_parts(lhs, 6, 5, north[...])
    for pair in range(4):
        moved = jnp.dot(lhs[...], matrix[:, 256 * pair : 256 * pair + 256], preferred_element_type=f32)
        for i in range(2):
            q[:, 2 * pair + i] = moved[: 8 * SLABS, 128 * i : 128 * i + 128].reshape(SLABS, 8, 128)


def lookup(point, consts, at):
    depth = jnp.broadcast_to(point[DEPTH : DEPTH + 1], (8, 128))
    value = jnp.zeros((8, 128), f32)
    for c in range(NCLASS):
        value = jnp.where(depth == float(c), consts[at + c], value)
    return value * point[SEA : SEA + 1]


def rims_kernel(partial, rims_second, rims_first, consts, matrix, q, taps, ky, tx, ty, lhs):
    even_lat = is_even("lat")
    south = jnp.where(even_lat, rims_second[...], rims_first[...])
    north = jnp.where(even_lat, rims_first[...], rims_second[...])
    for s, array in ((0, south), (1, north)):
        high, low = split(array[:NDIR].reshape(8 * NDIR, 128))
        lhs[:, 128 * s : 128 * s + 128] = high
        lhs[:, 128 * (2 + s) : 128 * (2 + s) + 128] = low
    lane = lanes()
    south, north = south[STATIC], north[STATIC]
    speed = []
    for t in range(8):
        if t % 2 == 0:
            moved = jnp.dot(lhs[...], matrix[:, 128 * t : 128 * t + 256], preferred_element_type=f32)
            for i in range(2):
                q[:, t + i] = partial[:NDIR, t + i] + moved[:, 128 * i : 128 * i + 128].reshape(NDIR, 8, 128)
        point = partial[STATIC, t]
        for low, array, shift in ((0, south, 0), (24, south, 16), (96, north, 88), (120, north, 120)):
            point = jnp.where((lane >= low) & (lane < low + 8), roll(array, shift - 16 * t), point)
        pace = lookup(point, consts, TAB_SPEED)
        turning = lookup(point, consts, TAB_TURN)
        speed.append(pace)
        tx[t] = turning * point[SLOPE_X : SLOPE_X + 1]
        ty[t] = turning * point[SLOPE_Y : SLOPE_Y + 1]
        stretch = consts[STRETCH, t : t + 1, :]
        right = 0.5 * (pace + roll(pace, -1)) * stretch
        left = 0.5 * (pace + roll(pace, 1)) * stretch
        for base in range(10):
            a1, b1, c1 = weights(COS[base] * right)
            a0, b0, c0 = weights(COS[base] * left)
            taps[base, 0, 0, t] = 1.0 - a1 + b0
            taps[base, 0, 1, t] = -b1
            taps[base, 0, 2, t] = a0 - c1
            taps[base, 0, 3, t] = c0
            taps[base, 1, 0, t] = 1.0 + b1 - a0
            taps[base, 1, 1, t] = a1 - c0
            taps[base, 1, 2, t] = -b0
            taps[base, 1, 3, t] = c1
    for t in range(8):
        ahead = speed[t + 1] if t < 7 else roll(speed[0], -32)
        ky[t] = 0.5 * (speed[t] + ahead)


def flux(q, diff, curve, k, u, w):
    return k * (q + u * (diff - w * curve))


def halves(k):
    return 0.5 - 0.5 * k, (1.0 / 3.0) + (1.0 / 3.0) * k


def weights(k):
    u, w = halves(k)
    bend = k * u * w
    return k - k * u + 2.0 * bend, k * u - bend, -bend


FORTH_TAPS = (1, -1, -2)
BACK_TAPS = (1, -1, 2)


def lon_kernel(q, taps, shifts, out):
    for sign in range(2):
        for base in range(10):
            if base == 0:
                dirs = [[0], [18]][sign]
            elif base == 9:
                dirs = [[27], [9]][sign]
            else:
                dirs = [[base, 36 - base], [18 - base, 18 + base]][sign]
            x = jnp.concatenate([q[d].reshape(64, 128) for d in dirs], axis=0)
            lhs = jnp.concatenate(split(x), axis=1)
            moved = jnp.dot(lhs, shifts[sign], preferred_element_type=f32)
            for t in range(8):
                tap = [taps[base, sign, i, t] for i in range(4)]
                for i, d in enumerate(dirs):
                    cell = q[d, t]
                    near = moved[64 * i + 8 * t : 64 * i + 8 * t + 8]
                    out[d, t] = (tap[0] * cell + tap[1] * near[:, :128]) + (
                        tap[2] * near[:, 128:256] + tap[3] * near[:, 256:]
                    )


def lat_kernel(q, ky, consts, out, sums=None):
    live = consts[LIVE]
    totals = [jnp.zeros((8, 128), f32)] * 8

    def put(d, t, value):
        out[d, t] = value
        if sums is not None:
            totals[t] = totals[t] + value

    def forth(d, ks, us, ws):
        tiles = [q[d, t] for t in range(8)]
        diff = [tiles[t + 1] - tiles[t] for t in range(7)]
        diff.append(roll(tiles[0], -32) - tiles[7])
        before = roll(diff[7], 32)
        fluxes = []
        for t in range(8):
            fluxes.append(flux(tiles[t], diff[t], diff[t] - before, ks[t], us[t], ws[t]))
            before = diff[t]
        behind = roll(fluxes[7], 32)
        for t in range(8):
            put(d, t, (tiles[t] - fluxes[t] + behind) * live)
            behind = fluxes[t]

    def back(d, ks, us, ws):
        tiles = [q[d, t] for t in range(8)]
        ahead = tiles[1:] + [roll(tiles[0], -32)]
        diff = [tiles[t] - ahead[t] for t in range(8)]
        after = diff[1:] + [roll(diff[0], -32)]
        fluxes = [flux(ahead[t], diff[t], diff[t] - after[t], ks[t], us[t], ws[t]) for t in range(8)]
        behind = roll(fluxes[7], 32)
        for t in range(8):
            put(d, t, (tiles[t] + fluxes[t] - behind) * live)
            behind = fluxes[t]

    for base in range(10):
        ks = [SIN[base] * ky[t] for t in range(8)]
        us, ws = zip(*[halves(k) for k in ks])
        if base == 0:
            north, south = [0], [18]
        elif base == 9:
            north, south = [9], [27]
        else:
            north, south = [base, 18 - base], [18 + base, 36 - base]
        for d in north:
            forth(d, ks, us, ws)
        for d in south:
            back(d, ks, us, ws)
    if sums is None:
        return
    lane = lanes()
    halves_of = [jnp.zeros((8, 128), f32)] * 2
    for t in range(8):
        moved = roll(totals[t], 16 * t - 40)
        halves_of[0] = jnp.where(lane // 16 == t, moved, halves_of[0])
        halves_of[1] = jnp.where(lane // 16 == (t + 2) % 8, moved, halves_of[1])
    halves_of[1] = roll(halves_of[1], -32)
    sums[...] = jnp.zeros((8, 128), f32)
    for half in range(2):
        sums[half : half + 1, :] = jnp.sum(halves_of[half], axis=0, keepdims=True)
        sums[2 + half : 3 + half, :] = jnp.sum(halves_of[half] * consts[LEVEL], axis=0, keepdims=True)


def turn_around(get, put, x, y):
    def factors(d):
        k = SIN_FACE[d] * x - COS_FACE[d] * y
        half, third = 0.5 * k, (1.0 / 3.0) * k
        return k, 0.5 - half, 1.0 / 3.0 + third, 0.5 + half, 1.0 / 3.0 - third

    half_turn = NDIR // 2
    k, u, w, u_back, w_back = factors(half_turn - 1)
    state = []
    ends = []
    for at in (0, half_turn):
        cell, ahead = get(at), get(at + 1)
        before, last = get((at - 1) % NDIR), get((at - 2) % NDIR)
        diff = ahead - cell
        diff1 = cell - before
        curve = diff - diff1
        curve1 = diff1 - (before - last)
        if at == 0:
            f = flux(before, diff1, jnp.where(k >= 0.0, curve, curve1), k, u_back, w_back)
        else:
            f = flux(before, diff1, jnp.where(k >= 0.0, curve1, curve), k, u, w)
        state.append([cell, ahead, diff, curve])
        ends.append(f)
    f_first, f_second = -ends[0], -ends[1]
    for d in range(half_turn):
        if d < half_turn - 1:
            k, u, w, u_back, w_back = factors(d)
            positive = k >= 0.0
        for at in (0, half_turn):
            cell, ahead, diff, curve = state[at // half_turn]
            beyond = get((at + d + 2) % NDIR)
            diff_ahead = beyond - ahead
            curve_ahead = diff_ahead - diff
            if at == 0:
                if d < half_turn - 1:
                    f = flux(cell, diff, jnp.where(positive, curve, curve_ahead), k, u, w)
                else:
                    f = ends[1]
                put(d, cell - f + f_first)
                f_first = f
            else:
                if d < half_turn - 1:
                    f = flux(cell, diff, jnp.where(positive, curve_ahead, curve), k, u_back, w_back)
                else:
                    f = ends[0]
                put(at + d, cell + f - f_second)
                f_second = f
            state[at // half_turn] = [ahead, beyond, diff_ahead, curve_ahead]


def turn_kernel(q, tx, ty, out):
    for t in range(8):

        def put(d, value, t=t):
            out[d, t] = value

        turn_around(lambda d, t=t: q[d, t], put, tx[t], ty[t])


def gather_kernel(q, matrix, own, lhs):
    for t in range(8):
        high, low = split(q[:, t].reshape(8 * NDIR, 128))
        lhs[:, 128 * t : 128 * t + 128] = high
        lhs[:, 1024 + 128 * t : 1024 + 128 * t + 128] = low
    moved = jnp.dot(lhs[...], matrix[...], preferred_element_type=f32)
    for half in range(2):
        own[half] = moved[:, 128 * half : 128 * half + 128].reshape(NDIR, 8, 128)


def last_turn_kernel(own, static, gain, consts, early):
    for half in range(2):
        point = static[half, 0]
        turning = lookup(point, consts, TAB_TURN)

        def put(d, value, half=half):
            early[half, d] = value * gain[d, half]

        turn_around(
            lambda d, half=half: own[half, d],
            put,
            turning * point[SLOPE_X : SLOPE_X + 1],
            turning * point[SLOPE_Y : SLOPE_Y + 1],
        )


def finish_kernel(early, local, sums, other, consts, out, flat0, flat1):
    total = sums[...] + other[...]
    level = consts[LEVEL]
    for half, flat in ((0, flat0), (1, flat1)):
        energy = total[half : half + 1]
        moment = total[2 + half : 3 + half]
        mean_level = jnp.maximum(moment, 1.0) / jnp.maximum(energy, 1.0)
        mean = energy / NCOMP
        breaking = break_coef * level * level / mean_level * (mean * mean)
        damping = local[half, ICE : ICE + 1] * consts[ICE_RATE]
        loss = jnp.exp(-breaking - damping)
        for d in range(NDIR):
            flat[pl.ds(d, FREQ, stride=NDIR), :] = early[half, d] * loss
        for low, high in ((0, 128), (128, 256), (256, 288)):
            out[8 * half : 8 * half + 8, :, low:high] = flat[low:high, :].T.reshape(8, 16, high - low)


PARAMS = pltpu.CompilerParams(vmem_limit_bytes=40 * 2**20)


def call(kernel, ins, outs, scratch=(), name=None, space=pltpu.VMEM, dtype=f32, result=pltpu.VMEM):
    types = dtype if isinstance(dtype, list) else [dtype] * len(outs)
    return pl.pallas_call(
        kernel,
        out_shape=[jax.ShapeDtypeStruct(shape, kind) for shape, kind in zip(outs, types)],
        in_specs=[pl.BlockSpec(memory_space=space)] * ins,
        out_specs=[pl.BlockSpec(memory_space=result)] * len(outs),
        scratch_shapes=list(scratch),
        compiler_params=PARAMS,
        name=name,
    )


def swap(array, axis, first, closed=False):
    count = lax.axis_size(axis)
    pairs = []
    for i in range(first, count, 2):
        if i + 1 < count or closed:
            j = (i + 1) % count
            pairs += [(i, j), (j, i)]
    return lax.ppermute(array, axis, pairs)


def per_device(
    spectrum,
    sea_mask,
    ice_mask,
    depth_class,
    speed_table,
    refraction_table,
    depth_slope,
    wind_speed,
    wind_dir,
    ice_rate,
):
    tile = (8, 128)
    block = (8,) + tile
    slabs = (SLABS,) + tile
    sent = (SENT,) + tile
    inputs = [spectrum, sea_mask, depth_class, depth_slope]
    (own,) = call(
        pack_kernel,
        4,
        [(2,) + slabs],
        [pltpu.VMEM(x.shape, x.dtype) for x in inputs]
        + [pltpu.VMEM((NDIR * FREQ, 128), f32)] * 2
        + [pltpu.VMEM((16, 128), f32), pltpu.VMEM((2,) + tile, f32), pltpu.SemaphoreType.DMA((4,))],
        name="pack",
        space=pltpu.HBM,
    )(*[pltpu.with_memory_space_constraint(x, pltpu.HBM) for x in inputs])
    (to_second,) = call(functools.partial(column_kernel, True), 1, [sent], name="column_far")(own)
    cols_second = swap(to_second, "lon", 1, True)
    (to_first,) = call(functools.partial(column_kernel, False), 1, [sent], name="column_near")(own)
    cols_first = swap(to_first, "lon", 0, True)
    (edge_second,) = call(functools.partial(edge_kernel, True), 1, [sent], name="edge_far")(own)
    rows_second = swap(edge_second, "lat", 1)
    (edge_first,) = call(functools.partial(edge_kernel, False), 1, [sent], name="edge_near")(own)
    rows_first = swap(edge_first, "lat", 0)
    inputs = [speed_table, refraction_table, ice_rate, ice_mask, wind_speed, wind_dir]
    place, rims, shifts, gather, local, consts = call(
        tables_kernel,
        6,
        [(1536, 1024), (512, 1024), (2, 256, 384), (2048, 256), (2,) + tile, (20,) + tile],
        [pltpu.VMEM(x.shape, x.dtype) for x in inputs]
        + [pltpu.VMEM((16, 128), f32), pltpu.SemaphoreType.DMA((6,))],
        name="tables",
        space=pltpu.HBM,
        dtype=[bf16] * 4 + [f32] * 2,
    )(*[pltpu.with_memory_space_constraint(x, pltpu.HBM) for x in inputs])
    (gain,) = call(growth_kernel, 3, [(NDIR, 2) + tile], name="growth")(own, local, consts)
    west, east = call(unpack_kernel, 5, [slabs] * 2, name="unpack")(
        cols_second, cols_first, rows_second, rows_first, consts
    )
    (rim_second,) = call(functools.partial(rim_kernel, True), 2, [slabs], name="rim_far")(west, east)
    rims_second = swap(rim_second, "lat", 1)
    (rim_first,) = call(functools.partial(rim_kernel, False), 2, [slabs], name="rim_near")(west, east)
    rims_first = swap(rim_first, "lat", 0)
    south, north = call(unpack_rows_kernel, 2, [slabs] * 2, name="unpack_rows")(rows_second, rows_first)
    (partial,) = call(
        place_kernel,
        6,
        [(SLABS,) + block],
        [pltpu.VMEM((8 * SLABS + 8, 1536), bf16)],
        name="place",
    )(own, west, east, south, north, place)
    q, taps, ky, tx, ty = call(
        rims_kernel,
        5,
        [(NDIR,) + block, (10, 2, 4) + block] + [block] * 3,
        [pltpu.VMEM((8 * NDIR, 512), bf16)],
        name="rims",
    )(partial, rims_second, rims_first, consts, rims)
    cells = [(NDIR,) + block]
    for substep in range(ITERS):
        (q,) = call(lon_kernel, 3, cells, name="lon")(q, taps, shifts)
        if substep == ITERS - 1:
            q, sums = call(lat_kernel, 3, cells + [tile], name="lat_sums")(q, ky, consts)
        else:
            (q,) = call(lat_kernel, 3, cells, name="lat")(q, ky, consts)
            (q,) = call(turn_kernel, 3, cells, name="turn")(q, tx, ty)
    other = swap(sums, "band", 0)
    (last,) = call(
        gather_kernel, 2, [(2, NDIR) + tile], [pltpu.VMEM((8 * NDIR, 2048), bf16)], name="gather"
    )(q, gather)
    static = own[:, STATIC:]
    (early,) = call(last_turn_kernel, 4, [(2, NDIR) + tile], name="last_turn")(last, static, gain, consts)
    (out,) = call(
        finish_kernel, 5, [spectrum.shape], [pltpu.VMEM((NDIR * FREQ, 128), f32)] * 2, name="finish"
    )(early, local, sums, other, consts)
    return out


def solution(mesh):
    return jax.shard_map(
        per_device,
        mesh=mesh,
        in_specs=(
            P("lat", "lon", "band"),
            P("lat", "lon"),
            P("lat", "lon"),
            P("lat", "lon"),
            P(),
            P(),
            P(None, "lat", "lon"),
            P("lat", "lon"),
            P("lat", "lon"),
            P(),
        ),
        out_specs=P("lat", "lon", "band"),
        check_vma=False,
    )
```

```python
import functools
import math

import jax
import jax.numpy as jnp
import numpy as np
from jax import lax
from jax.experimental import pallas as pl
from jax.experimental.pallas import tpu as pltpu
from jax.sharding import PartitionSpec as P

NDIR = 36
NCOMP = 576
ITERS = 4
NCLASS = 8
FREQ = 8
HALO = 8
ROWS = 16
STATIC = NDIR
SLABS = NDIR + 1
SEA, DEPTH, SLOPE_X, SLOPE_Y, ICE, WIND, WDIR = range(7)

freq_ratio = 1.1
wind_gain = 0.12
break_coef = 0.05
south_edge = -30.0
band_span = 60.0

COS = [math.cos(2.0 * math.pi * d / NDIR) for d in range(NDIR)]
SIN = [math.sin(2.0 * math.pi * d / NDIR) for d in range(NDIR)]
COS_FACE = [math.cos(2.0 * math.pi * (d + 0.5) / NDIR) for d in range(NDIR)]
SIN_FACE = [math.sin(2.0 * math.pi * (d + 0.5) / NDIR) for d in range(NDIR)]

TAB_SPEED, TAB_TURN, STRETCH, LIVE, ICE_RATE, LEVEL = 0, 8, 16, 17, 18, 19

f32 = jnp.float32
bf16 = jnp.bfloat16


def lanes():
    return lax.broadcasted_iota(jnp.int32, (8, 128), 1)


def roll(x, shift):
    shift = shift % 128
    return pltpu.roll(x, shift, 1) if shift else x


def is_even(axis):
    return lax.axis_index(axis) % 2 == 0


def place_field(wide, values, static, field):
    group = lax.broadcasted_iota(jnp.int32, (16, 128), 1) // 16
    row = lax.broadcasted_iota(jnp.int32, (16, 128), 0) % 8
    wide[:, :16] = values
    moved = pltpu.roll(wide[...], 0, 1, stride=16, stride_axis=0)
    kept = jnp.where(group == row, moved, 0.0)
    for half in range(2):
        static[half, field : field + 1, :] = jnp.sum(kept[8 * half : 8 * half + 8], axis=0, keepdims=True)


def fetch(sources, landed, sems):
    copies = [pltpu.make_async_copy(src, dst, sems.at[i]) for i, (src, dst) in enumerate(zip(sources, landed))]
    for copy in copies:
        copy.start()
    return copies


def pack_kernel(*refs):
    sources, own, landed = refs[:4], refs[4], refs[5:9]
    flat0, flat1, wide, static, sems = refs[9:]
    copies = fetch(sources, landed, sems)
    wide[...] = jnp.zeros_like(wide)
    static[...] = jnp.zeros_like(static)
    for copy in copies:
        copy.wait()
    spec, sea, depth, slope = landed
    place_field(wide, sea[...].astype(f32), static, SEA)
    place_field(wide, depth[...].astype(f32), static, DEPTH)
    place_field(wide, slope[0], static, SLOPE_X)
    place_field(wide, slope[1], static, SLOPE_Y)
    own[:, STATIC] = static[...]
    grid = spec[...].reshape(256, NDIR * FREQ)
    for low, high in ((0, 128), (128, 256), (256, 288)):
        turned = grid[:, low:high].T
        flat0[low:high, :] = turned[:, :128]
        flat1[low:high, :] = turned[:, 128:]
    sea0 = static[0, SEA : SEA + 1, :]
    sea1 = static[1, SEA : SEA + 1, :]
    for d in range(NDIR):
        own[0, d] = flat0[pl.ds(d, FREQ, stride=NDIR), :] * sea0
        own[1, d] = flat1[pl.ds(d, FREQ, stride=NDIR), :] * sea1


NEEDS = (7, 7, 6, 6, 5, 5, 4, 4, 4, 4, 4, 4, 5, 5, 6, 6, 7, 7)
PACKED = {
    0: [(12, 3, 7, 1)],
    1: [(12, 4, 7, 1)],
    2: [(15, 0, 6, 2)],
    3: [(15, 2, 6, 2)],
    4: [(12, 0, 5, 3)],
    5: [(13, 0, 5, 3)],
    6: [(9, 0, 4, 4)],
    7: [(10, 0, 4, 4)],
    8: [(11, 0, 4, 4)],
    14: [(15, 4, 6, 2)],
    16: [(13, 3, 7, 1)],
    17: [(13, 4, 7, 1)],
}
TO_WEST, TO_EAST, TO_NORTH, TO_SOUTH = 27, 9, 18, 0
SENT = 18 + 1 + len(PACKED)


def downstream(first):
    return [(first + i) % NDIR for i in range(18)]


def whole(first):
    return [d for d in range(NDIR) if d not in downstream(first)] + [STATIC]


def write_message(message, get, rising, rising_first, falling_first, place, unit):
    for i, pair in enumerate(zip(whole(rising_first), whole(falling_first))):
        message[i] = get(*pair)
    up, down = downstream(rising_first), downstream(falling_first)
    cell = jnp.where(rising, place, 7 - place)
    for i, (main, pieces) in enumerate(PACKED.items()):
        value = get(up[main], down[main])
        for other, start, to, count in pieces:
            shift = (to - start) * unit
            moved = pltpu.roll(get(up[other], down[other]), jnp.where(rising, shift, 128 - shift), 1)
            value = jnp.where((cell >= to) & (cell < to + count), moved, value)
        message[19 + i] = value


def read_message(message, out, rising, first, place, unit):
    for i, d in enumerate(whole(first)):
        out[d] = message(i)
    dirs = downstream(first)
    cell = place if rising else 7 - place
    parts = {}
    for i, (main, pieces) in enumerate(PACKED.items()):
        value = message(19 + i)
        out[dirs[main]] = value
        for other, start, to, count in pieces:
            shift = (start - to) * unit
            moved = roll(value, shift if rising else -shift)
            if other in parts:
                moved = jnp.where((cell >= start) & (cell < start + count), moved, parts[other])
            parts[other] = moved
    for other, value in parts.items():
        out[dirs[other]] = value


def column_kernel(second, own, message):
    inner = lanes() % 16
    to_east = is_even("lon") != second
    from_own0 = (inner >= 8) == to_east
    shift = jnp.where(to_east, 120, 8)

    def get(west, east):
        slab = west if west == east else jnp.where(to_east, east, west)
        return jnp.where(from_own0, own[0, slab], pltpu.roll(own[1, slab], shift, 1))

    write_message(message, get, ~to_east, TO_WEST, TO_EAST, inner % 8, 1)


def edge_kernel(second, own, message):
    to_north = is_even("lat") != second

    def get(south, north):
        return jnp.where(to_north, own[1, north], own[0, south])

    write_message(message, get, ~to_north, TO_SOUTH, TO_NORTH, lanes() // 16, 16)


def growth_kernel(own, local, consts, gain):
    for half in range(2):
        point = local[half]
        turn = point[WDIR : WDIR + 1]
        cos_w = jnp.cos(turn)
        sin_w = jnp.sin(turn)
        force = wind_gain * point[WIND : WIND + 1] * consts[LEVEL]
        share = own[half, STATIC, SEA : SEA + 1]
        for d in range(NDIR):
            along = jnp.maximum(COS[d] * cos_w + SIN[d] * sin_w, 0.0)
            gain[d, half] = jnp.exp(force * along) * share


def tables_kernel(*refs):
    sources, (place, rims, shifts, gather, local, consts), landed = refs[:6], refs[6:12], refs[12:18]
    wide, sems = refs[18:]
    speed_table, refraction_table, ice_rate, ice, wspeed, wdir = landed
    copies = fetch(sources, landed, sems)
    first = lax.axis_index("band") * FREQ
    sub = lax.broadcasted_iota(jnp.int32, (8, 128), 0)
    mine = lanes() == first + sub

    def column(row):
        picked = jnp.where(mine, jnp.broadcast_to(row, (8, 128)), 0.0)
        return jnp.broadcast_to(jnp.sum(picked, axis=1, keepdims=True), (8, 128))

    def widen(values):
        return jnp.concatenate([values, jnp.zeros((values.shape[0], 112), f32)], axis=1)

    consts[LEVEL] = jnp.exp(math.log(freq_ratio) * (first + sub).astype(f32))
    lat = lax.axis_index("lat")
    lats = lax.axis_size("lat")
    group = lanes() // 32
    rows = lat * ROWS - HALO + 8 * group + sub
    latitude = (south_edge + band_span * (rows.astype(f32) + 0.5) / (ROWS * lats)) * (math.pi / 180.0)
    consts[STRETCH] = 1.0 / jnp.cos(latitude)
    ghost = ((group == 0) & (lat == 0)) | ((group == 3) & (lat == lats - 1))
    consts[LIVE] = jnp.where(ghost, 0.0, 1.0)
    chunk = lax.broadcasted_iota(jnp.int32, (16, 128), 0)
    lane = lax.broadcasted_iota(jnp.int32, (16, 128), 1)
    low = chunk < 8
    targets = [
        40 + chunk,
        72 + chunk,
        jnp.where(low, 64 + chunk, 24 + chunk),
        jnp.where(low, 56 + chunk, 80 + chunk),
        8 + chunk,
        104 + chunk,
    ]
    corners = [jnp.where(low, chunk, 16 + chunk), jnp.where(low, 120 + chunk, 88 + chunk)]
    for matrix, lists in ((place, targets), (rims, corners)):
        matrix[...] = jnp.zeros_like(matrix)
        for s, target in enumerate(lists):
            stripe = (lane == target).astype(f32).astype(bf16)
            for part in range(2):
                for t in range(8):
                    row = part * 128 * len(lists) + s * 128 + 16 * t
                    matrix[row : row + 16, 128 * t : 128 * t + 128] = stripe
    row = lax.broadcasted_iota(jnp.int32, (128, 128), 0)
    col = lax.broadcasted_iota(jnp.int32, (128, 128), 1)
    for sign, taps in ((0, FORTH_TAPS), (1, BACK_TAPS)):
        for i, tap in enumerate(taps):
            moved = (row == (col + tap) % 128).astype(f32).astype(bf16)
            for part in range(2):
                shifts[sign, 128 * part : 128 * part + 128, 128 * i : 128 * i + 128] = moved
    for t in range(8):
        for half in range(2):
            from_row = 40 + 32 * half + col % 16
            moved = ((col // 16 == t) & (row == from_row)).astype(f32).astype(bf16)
            for part in range(2):
                at = part * 1024 + 128 * t
                gather[at : at + 128, 128 * half : 128 * half + 128] = moved
    local[...] = jnp.zeros_like(local)
    wide[...] = jnp.zeros_like(wide)
    for copy in copies:
        copy.wait()
    for at, table in ((TAB_SPEED, speed_table), (TAB_TURN, refraction_table)):
        padded = widen(table[...])
        for c in range(NCLASS):
            consts[at + c] = column(padded[c : c + 1])
    consts[ICE_RATE] = column(widen(ice_rate[...].reshape(1, 16)))
    place_field(wide, ice[...].astype(f32), local, ICE)
    place_field(wide, wspeed[...], local, WIND)
    place_field(wide, wdir[...], local, WDIR)


def unpack_kernel(cols_second, cols_first, consts, west, east):
    del consts
    even = is_even("lon")
    place = lanes() % 8
    read_message(lambda i: jnp.where(even, cols_second[i], cols_first[i]), west, False, TO_EAST, place, 1)
    read_message(lambda i: jnp.where(even, cols_first[i], cols_second[i]), east, True, TO_WEST, place, 1)


def unpack_rows_kernel(rows_second, rows_first, south, north):
    even = is_even("lat")
    place = lanes() // 16
    read_message(lambda i: jnp.where(even, rows_second[i], rows_first[i]), south, False, TO_NORTH, place, 16)
    read_message(lambda i: jnp.where(even, rows_first[i], rows_second[i]), north, True, TO_SOUTH, place, 16)


def rim_kernel(second, west, east, *refs):
    rim = refs[-1]
    west_low = (lanes() % 16 < 8) == (is_even("lat") != second)
    for slab in range(SLABS):
        rim[slab] = jnp.where(west_low, west[slab], east[slab])


def split(x):
    high = x.astype(bf16)
    return high, (x - high.astype(f32)).astype(bf16)


def fill_parts(lhs, count, s, array):
    x = jnp.concatenate([array.reshape(8 * SLABS, 128), jnp.zeros((8, 128), f32)], axis=0)
    high, low = split(x)
    lhs[:, 128 * s : 128 * s + 128] = high
    lhs[:, 128 * (count + s) : 128 * (count + s) + 128] = low


def place_kernel(own, west, east, south, north, matrix, q, lhs):
    fill_parts(lhs, 6, 0, own[0])
    fill_parts(lhs, 6, 1, own[1])
    fill_parts(lhs, 6, 2, west[...])
    fill_parts(lhs, 6, 3, east[...])
    fill_parts(lhs, 6, 4, south[...])
    fill_parts(lhs, 6, 5, north[...])
    for pair in range(4):
        moved = jnp.dot(lhs[...], matrix[:, 256 * pair : 256 * pair + 256], preferred_element_type=f32)
        for i in range(2):
            q[:, 2 * pair + i] = moved[: 8 * SLABS, 128 * i : 128 * i + 128].reshape(SLABS, 8, 128)


def lookup(point, consts, at):
    depth = jnp.broadcast_to(point[DEPTH : DEPTH + 1], (8, 128))
    value = jnp.zeros((8, 128), f32)
    for c in range(NCLASS):
        value = jnp.where(depth == float(c), consts[at + c], value)
    return value * point[SEA : SEA + 1]


def rims_kernel(partial, rims_second, rims_first, consts, matrix, q, taps, ky, tx, ty, lhs):
    even_lat = is_even("lat")
    south = jnp.where(even_lat, rims_second[...], rims_first[...])
    north = jnp.where(even_lat, rims_first[...], rims_second[...])
    for s, array in ((0, south), (1, north)):
        high, low = split(array[:NDIR].reshape(8 * NDIR, 128))
        lhs[:, 128 * s : 128 * s + 128] = high
        lhs[:, 128 * (2 + s) : 128 * (2 + s) + 128] = low
    lane = lanes()
    south, north = south[STATIC], north[STATIC]
    speed = []
    for t in range(8):
        if t % 2 == 0:
            moved = jnp.dot(lhs[...], matrix[:, 128 * t : 128 * t + 256], preferred_element_type=f32)
            for i in range(2):
                q[:, t + i] = partial[:NDIR, t + i] + moved[:, 128 * i : 128 * i + 128].reshape(NDIR, 8, 128)
        point = partial[STATIC, t]
        for low, array, shift in ((0, south, 0), (24, south, 16), (96, north, 88), (120, north, 120)):
            point = jnp.where((lane >= low) & (lane < low + 8), roll(array, shift - 16 * t), point)
        pace = lookup(point, consts, TAB_SPEED)
        turning = lookup(point, consts, TAB_TURN)
        speed.append(pace)
        tx[t] = turning * point[SLOPE_X : SLOPE_X + 1]
        ty[t] = turning * point[SLOPE_Y : SLOPE_Y + 1]
        stretch = consts[STRETCH, t : t + 1, :]
        right = 0.5 * (pace + roll(pace, -1)) * stretch
        left = 0.5 * (pace + roll(pace, 1)) * stretch
        for base in range(10):
            a1, b1, c1 = weights(COS[base] * right)
            a0, b0, c0 = weights(COS[base] * left)
            taps[base, 0, 0, t] = 1.0 - a1 + b0
            taps[base, 0, 1, t] = -b1
            taps[base, 0, 2, t] = a0 - c1
            taps[base, 0, 3, t] = c0
            taps[base, 1, 0, t] = 1.0 + b1 - a0
            taps[base, 1, 1, t] = a1 - c0
            taps[base, 1, 2, t] = -b0
            taps[base, 1, 3, t] = c1
    for t in range(8):
        ahead = speed[t + 1] if t < 7 else roll(speed[0], -32)
        ky[t] = 0.5 * (speed[t] + ahead)


def flux(q, diff, curve, k, u, w):
    return k * (q + u * (diff - w * curve))


def halves(k):
    return 0.5 - 0.5 * k, (1.0 / 3.0) + (1.0 / 3.0) * k


def weights(k):
    u, w = halves(k)
    bend = k * u * w
    return k - k * u + 2.0 * bend, k * u - bend, -bend


FORTH_TAPS = (-1, -2)
BACK_TAPS = (-1, 2)


def lon_kernel(q, taps, shifts, out):
    for sign in range(2):
        for base in range(10):
            if base == 0:
                dirs = [[0], [18]][sign]
            elif base == 9:
                dirs = [[27], [9]][sign]
            else:
                dirs = [[base, 36 - base], [18 - base, 18 + base]][sign]
            x = jnp.concatenate([q[d].reshape(64, 128) for d in dirs], axis=0)
            lhs = jnp.concatenate(split(x), axis=1)
            moved = jnp.dot(lhs, shifts[sign], preferred_element_type=f32)
            for t in range(8):
                tap = [taps[base, sign, i, t] for i in range(4)]
                for i, d in enumerate(dirs):
                    cell = q[d, t]
                    near = moved[64 * i + 8 * t : 64 * i + 8 * t + 8]
                    out[d, t] = (tap[0] * cell + tap[1] * roll(cell, -1)) + (
                        tap[2] * near[:, :128] + tap[3] * near[:, 128:]
                    )


def lat_kernel(q, ky, consts, out, sums=None):
    live = consts[LIVE]
    totals = [jnp.zeros((8, 128), f32)] * 8

    def put(d, t, value):
        out[d, t] = value
        if sums is not None:
            totals[t] = totals[t] + value

    def forth(d, ks, us, ws):
        tiles = [q[d, t] for t in range(8)]
        diff = [tiles[t + 1] - tiles[t] for t in range(7)]
        diff.append(roll(tiles[0], -32) - tiles[7])
        before = roll(diff[7], 32)
        fluxes = []
        for t in range(8):
            fluxes.append(flux(tiles[t], diff[t], diff[t] - before, ks[t], us[t], ws[t]))
            before = diff[t]
        behind = roll(fluxes[7], 32)
        for t in range(8):
            put(d, t, (tiles[t] - fluxes[t] + behind) * live)
            behind = fluxes[t]

    def back(d, ks, us, ws):
        tiles = [q[d, t] for t in range(8)]
        ahead = tiles[1:] + [roll(tiles[0], -32)]
        diff = [tiles[t] - ahead[t] for t in range(8)]
        after = diff[1:] + [roll(diff[0], -32)]
        fluxes = [flux(ahead[t], diff[t], diff[t] - after[t], ks[t], us[t], ws[t]) for t in range(8)]
        behind = roll(fluxes[7], 32)
        for t in range(8):
            put(d, t, (tiles[t] + fluxes[t] - behind) * live)
            behind = fluxes[t]

    for base in range(10):
        ks = [SIN[base] * ky[t] for t in range(8)]
        us, ws = zip(*[halves(k) for k in ks])
        if base == 0:
            north, south = [0], [18]
        elif base == 9:
            north, south = [9], [27]
        else:
            north, south = [base, 18 - base], [18 + base, 36 - base]
        for d in north:
            forth(d, ks, us, ws)
        for d in south:
            back(d, ks, us, ws)
    if sums is None:
        return
    lane = lanes()
    halves_of = [jnp.zeros((8, 128), f32)] * 2
    for t in range(8):
        moved = roll(totals[t], 16 * t - 40)
        halves_of[0] = jnp.where(lane // 16 == t, moved, halves_of[0])
        halves_of[1] = jnp.where(lane // 16 == (t + 2) % 8, moved, halves_of[1])
    halves_of[1] = roll(halves_of[1], -32)
    sums[...] = jnp.zeros((8, 128), f32)
    for half in range(2):
        sums[half : half + 1, :] = jnp.sum(halves_of[half], axis=0, keepdims=True)
        sums[2 + half : 3 + half, :] = jnp.sum(halves_of[half] * consts[LEVEL], axis=0, keepdims=True)


def turn_around(get, put, x, y):
    def factors(d):
        k = SIN_FACE[d] * x - COS_FACE[d] * y
        half, third = 0.5 * k, (1.0 / 3.0) * k
        return k, 0.5 - half, 1.0 / 3.0 + third, 0.5 + half, 1.0 / 3.0 - third

    half_turn = NDIR // 2
    k, u, w, u_back, w_back = factors(half_turn - 1)
    state = []
    ends = []
    for at in (0, half_turn):
        cell, ahead = get(at), get(at + 1)
        before, last = get((at - 1) % NDIR), get((at - 2) % NDIR)
        diff = ahead - cell
        diff1 = cell - before
        curve = diff - diff1
        curve1 = diff1 - (before - last)
        if at == 0:
            f = flux(before, diff1, jnp.where(k >= 0.0, curve, curve1), k, u_back, w_back)
        else:
            f = flux(before, diff1, jnp.where(k >= 0.0, curve1, curve), k, u, w)
        state.append([cell, ahead, diff, curve])
        ends.append(f)
    f_first, f_second = -ends[0], -ends[1]
    for d in range(half_turn):
        if d < half_turn - 1:
            k, u, w, u_back, w_back = factors(d)
            positive = k >= 0.0
        for at in (0, half_turn):
            cell, ahead, diff, curve = state[at // half_turn]
            beyond = get((at + d + 2) % NDIR)
            diff_ahead = beyond - ahead
            curve_ahead = diff_ahead - diff
            if at == 0:
                if d < half_turn - 1:
                    f = flux(cell, diff, jnp.where(positive, curve, curve_ahead), k, u, w)
                else:
                    f = ends[1]
                put(d, cell - f + f_first)
                f_first = f
            else:
                if d < half_turn - 1:
                    f = flux(cell, diff, jnp.where(positive, curve_ahead, curve), k, u_back, w_back)
                else:
                    f = ends[0]
                put(at + d, cell + f - f_second)
                f_second = f
            state[at // half_turn] = [ahead, beyond, diff_ahead, curve_ahead]


def turn_kernel(q, tx, ty, out):
    for t in range(8):

        def put(d, value, t=t):
            out[d, t] = value

        turn_around(lambda d, t=t: q[d, t], put, tx[t], ty[t])


def gather_kernel(q, matrix, own, lhs):
    for t in range(8):
        high, low = split(q[:, t].reshape(8 * NDIR, 128))
        lhs[:, 128 * t : 128 * t + 128] = high
        lhs[:, 1024 + 128 * t : 1024 + 128 * t + 128] = low
    moved = jnp.dot(lhs[...], matrix[...], preferred_element_type=f32)
    for half in range(2):
        own[half] = moved[:, 128 * half : 128 * half + 128].reshape(NDIR, 8, 128)


def last_turn_kernel(own, static, gain, consts, early):
    for half in range(2):
        point = static[half, 0]
        turning = lookup(point, consts, TAB_TURN)

        def put(d, value, half=half):
            early[half, d] = value * gain[d, half]

        turn_around(
            lambda d, half=half: own[half, d],
            put,
            turning * point[SLOPE_X : SLOPE_X + 1],
            turning * point[SLOPE_Y : SLOPE_Y + 1],
        )


def finish_kernel(early, local, sums, other, consts, out, flat0, flat1):
    total = sums[...] + other[...]
    level = consts[LEVEL]
    for half, flat in ((0, flat0), (1, flat1)):
        energy = total[half : half + 1]
        moment = total[2 + half : 3 + half]
        mean_level = jnp.maximum(moment, 1.0) / jnp.maximum(energy, 1.0)
        mean = energy / NCOMP
        breaking = break_coef * level * level / mean_level * (mean * mean)
        damping = local[half, ICE : ICE + 1] * consts[ICE_RATE]
        loss = jnp.exp(-breaking - damping)
        for d in range(NDIR):
            flat[pl.ds(d, FREQ, stride=NDIR), :] = early[half, d] * loss
        for low, high in ((0, 128), (128, 256), (256, 288)):
            out[8 * half : 8 * half + 8, :, low:high] = flat[low:high, :].T.reshape(8, 16, high - low)


PARAMS = pltpu.CompilerParams(vmem_limit_bytes=40 * 2**20)


def call(kernel, ins, outs, scratch=(), name=None, space=pltpu.VMEM, dtype=f32, result=pltpu.VMEM):
    types = dtype if isinstance(dtype, list) else [dtype] * len(outs)
    return pl.pallas_call(
        kernel,
        out_shape=[jax.ShapeDtypeStruct(shape, kind) for shape, kind in zip(outs, types)],
        in_specs=[pl.BlockSpec(memory_space=space)] * ins,
        out_specs=[pl.BlockSpec(memory_space=result)] * len(outs),
        scratch_shapes=list(scratch),
        compiler_params=PARAMS,
        name=name,
    )


def swap(array, axis, first, closed=False):
    count = lax.axis_size(axis)
    pairs = []
    for i in range(first, count, 2):
        if i + 1 < count or closed:
            j = (i + 1) % count
            pairs += [(i, j), (j, i)]
    return lax.ppermute(array, axis, pairs)


def per_device(
    spectrum,
    sea_mask,
    ice_mask,
    depth_class,
    speed_table,
    refraction_table,
    depth_slope,
    wind_speed,
    wind_dir,
    ice_rate,
):
    tile = (8, 128)
    block = (8,) + tile
    slabs = (SLABS,) + tile
    sent = (SENT,) + tile
    inputs = [spectrum, sea_mask, depth_class, depth_slope]
    (own,) = call(
        pack_kernel,
        4,
        [(2,) + slabs],
        [pltpu.VMEM(x.shape, x.dtype) for x in inputs]
        + [pltpu.VMEM((NDIR * FREQ, 128), f32)] * 2
        + [pltpu.VMEM((16, 128), f32), pltpu.VMEM((2,) + tile, f32), pltpu.SemaphoreType.DMA((4,))],
        name="pack",
        space=pltpu.HBM,
    )(*[pltpu.with_memory_space_constraint(x, pltpu.HBM) for x in inputs])
    (to_second,) = call(functools.partial(column_kernel, True), 1, [sent], name="column_far")(own)
    cols_second = swap(to_second, "lon", 1, True)
    (to_first,) = call(functools.partial(column_kernel, False), 1, [sent], name="column_near")(own)
    cols_first = swap(to_first, "lon", 0, True)
    (edge_second,) = call(functools.partial(edge_kernel, True), 1, [sent], name="edge_far")(own)
    rows_second = swap(edge_second, "lat", 1)
    (edge_first,) = call(functools.partial(edge_kernel, False), 1, [sent], name="edge_near")(own)
    rows_first = swap(edge_first, "lat", 0)
    inputs = [speed_table, refraction_table, ice_rate, ice_mask, wind_speed, wind_dir]
    place, rims, shifts, gather, local, consts = call(
        tables_kernel,
        6,
        [(1536, 1024), (512, 1024), (2, 256, 256), (2048, 256), (2,) + tile, (20,) + tile],
        [pltpu.VMEM(x.shape, x.dtype) for x in inputs]
        + [pltpu.VMEM((16, 128), f32), pltpu.SemaphoreType.DMA((6,))],
        name="tables",
        space=pltpu.HBM,
        dtype=[bf16] * 4 + [f32] * 2,
    )(*[pltpu.with_memory_space_constraint(x, pltpu.HBM) for x in inputs])
    (gain,) = call(growth_kernel, 3, [(NDIR, 2) + tile], name="growth")(own, local, consts)
    west, east = call(unpack_kernel, 3, [slabs] * 2, name="unpack")(cols_second, cols_first, consts)
    (rim_second,) = call(functools.partial(rim_kernel, True), 2, [slabs], name="rim_far")(west, east)
    rims_second = swap(rim_second, "lat", 1)
    (rim_first,) = call(functools.partial(rim_kernel, False), 4, [slabs], name="rim_near")(
        west, east, rows_second, rows_first
    )
    rims_first = swap(rim_first, "lat", 0)
    south, north = call(unpack_rows_kernel, 2, [slabs] * 2, name="unpack_rows")(rows_second, rows_first)
    (partial,) = call(
        place_kernel,
        6,
        [(SLABS,) + block],
        [pltpu.VMEM((8 * SLABS + 8, 1536), bf16)],
        name="place",
    )(own, west, east, south, north, place)
    q, taps, ky, tx, ty = call(
        rims_kernel,
        5,
        [(NDIR,) + block, (10, 2, 4) + block] + [block] * 3,
        [pltpu.VMEM((8 * NDIR, 512), bf16)],
        name="rims",
    )(partial, rims_second, rims_first, consts, rims)
    cells = [(NDIR,) + block]
    for substep in range(ITERS):
        (q,) = call(lon_kernel, 3, cells, name="lon")(q, taps, shifts)
        if substep == ITERS - 1:
            q, sums = call(lat_kernel, 3, cells + [tile], name="lat_sums")(q, ky, consts)
        else:
            (q,) = call(lat_kernel, 3, cells, name="lat")(q, ky, consts)
            (q,) = call(turn_kernel, 3, cells, name="turn")(q, tx, ty)
    other = swap(sums, "band", 0)
    (last,) = call(
        gather_kernel, 2, [(2, NDIR) + tile], [pltpu.VMEM((8 * NDIR, 2048), bf16)], name="gather"
    )(q, gather)
    static = own[:, STATIC:]
    (early,) = call(last_turn_kernel, 4, [(2, NDIR) + tile], name="last_turn")(last, static, gain, consts)
    (out,) = call(
        finish_kernel, 5, [spectrum.shape], [pltpu.VMEM((NDIR * FREQ, 128), f32)] * 2, name="finish"
    )(early, local, sums, other, consts)
    return out


def solution(mesh):
    return jax.shard_map(
        per_device,
        mesh=mesh,
        in_specs=(
            P("lat", "lon", "band"),
            P("lat", "lon"),
            P("lat", "lon"),
            P("lat", "lon"),
            P(),
            P(),
            P(None, "lat", "lon"),
            P("lat", "lon"),
            P("lat", "lon"),
            P(),
        ),
        out_specs=P("lat", "lon", "band"),
        check_vma=False,
    )
```

```python
import functools
import math

import jax
import jax.numpy as jnp
import numpy as np
from jax import lax
from jax.experimental import pallas as pl
from jax.experimental.pallas import tpu as pltpu
from jax.sharding import PartitionSpec as P

NDIR = 36
NCOMP = 576
ITERS = 4
NCLASS = 8
FREQ = 8
HALO = 8
ROWS = 16
STATIC = NDIR
SLABS = NDIR + 1
SEA, DEPTH, SLOPE_X, SLOPE_Y, ICE, WIND, WDIR = range(7)

freq_ratio = 1.1
wind_gain = 0.12
break_coef = 0.05
south_edge = -30.0
band_span = 60.0

COS = [math.cos(2.0 * math.pi * d / NDIR) for d in range(NDIR)]
SIN = [math.sin(2.0 * math.pi * d / NDIR) for d in range(NDIR)]
COS_FACE = [math.cos(2.0 * math.pi * (d + 0.5) / NDIR) for d in range(NDIR)]
SIN_FACE = [math.sin(2.0 * math.pi * (d + 0.5) / NDIR) for d in range(NDIR)]

TAB_SPEED, TAB_TURN, STRETCH, LIVE, ICE_RATE, LEVEL = 0, 8, 16, 17, 18, 19

f32 = jnp.float32
bf16 = jnp.bfloat16


def lanes():
    return lax.broadcasted_iota(jnp.int32, (8, 128), 1)


def roll(x, shift):
    shift = shift % 128
    return pltpu.roll(x, shift, 1) if shift else x


def is_even(axis):
    return lax.axis_index(axis) % 2 == 0


def place_field(wide, values, static, field):
    group = lax.broadcasted_iota(jnp.int32, (16, 128), 1) // 16
    row = lax.broadcasted_iota(jnp.int32, (16, 128), 0) % 8
    wide[:, :16] = values
    moved = pltpu.roll(wide[...], 0, 1, stride=16, stride_axis=0)
    kept = jnp.where(group == row, moved, 0.0)
    for half in range(2):
        static[half, field : field + 1, :] = jnp.sum(kept[8 * half : 8 * half + 8], axis=0, keepdims=True)


def fetch(sources, landed, sems):
    copies = [pltpu.make_async_copy(src, dst, sems.at[i]) for i, (src, dst) in enumerate(zip(sources, landed))]
    for copy in copies:
        copy.start()
    return copies


def pack_kernel(*refs):
    sources, own, landed = refs[:4], refs[4], refs[5:9]
    flat0, flat1, wide, static, sems = refs[9:]
    copies = fetch(sources, landed, sems)
    wide[...] = jnp.zeros_like(wide)
    static[...] = jnp.zeros_like(static)
    for copy in copies:
        copy.wait()
    spec, sea, depth, slope = landed
    place_field(wide, sea[...].astype(f32), static, SEA)
    place_field(wide, depth[...].astype(f32), static, DEPTH)
    place_field(wide, slope[0], static, SLOPE_X)
    place_field(wide, slope[1], static, SLOPE_Y)
    own[:, STATIC] = static[...]
    grid = spec[...].reshape(256, NDIR * FREQ)
    for low, high in ((0, 128), (128, 256), (256, 288)):
        turned = grid[:, low:high].T
        flat0[low:high, :] = turned[:, :128]
        flat1[low:high, :] = turned[:, 128:]
    sea0 = static[0, SEA : SEA + 1, :]
    sea1 = static[1, SEA : SEA + 1, :]
    for d in range(NDIR):
        own[0, d] = flat0[pl.ds(d, FREQ, stride=NDIR), :] * sea0
        own[1, d] = flat1[pl.ds(d, FREQ, stride=NDIR), :] * sea1


NEEDS = (7, 7, 6, 6, 5, 5, 4, 4, 4, 4, 4, 4, 5, 5, 6, 6, 7, 7)
PACKED = {
    0: [(12, 3, 7, 1)],
    1: [(12, 4, 7, 1)],
    2: [(15, 0, 6, 2)],
    3: [(15, 2, 6, 2)],
    4: [(12, 0, 5, 3)],
    5: [(13, 0, 5, 3)],
    6: [(9, 0, 4, 4)],
    7: [(10, 0, 4, 4)],
    8: [(11, 0, 4, 4)],
    14: [(15, 4, 6, 2)],
    16: [(13, 3, 7, 1)],
    17: [(13, 4, 7, 1)],
}
TO_WEST, TO_EAST, TO_NORTH, TO_SOUTH = 27, 9, 18, 0
SENT = 18 + 1 + len(PACKED)


def downstream(first):
    return [(first + i) % NDIR for i in range(18)]


def whole(first):
    return [d for d in range(NDIR) if d not in downstream(first)] + [STATIC]


def write_message(message, get, rising, rising_first, falling_first, place, unit):
    for i, pair in enumerate(zip(whole(rising_first), whole(falling_first))):
        message[i] = get(*pair)
    up, down = downstream(rising_first), downstream(falling_first)
    cell = jnp.where(rising, place, 7 - place)
    for i, (main, pieces) in enumerate(PACKED.items()):
        value = get(up[main], down[main])
        for other, start, to, count in pieces:
            shift = (to - start) * unit
            moved = pltpu.roll(get(up[other], down[other]), jnp.where(rising, shift, 128 - shift), 1)
            value = jnp.where((cell >= to) & (cell < to + count), moved, value)
        message[19 + i] = value


def read_message(message, out, rising, first, place, unit):
    for i, d in enumerate(whole(first)):
        out[d] = message(i)
    dirs = downstream(first)
    cell = place if rising else 7 - place
    parts = {}
    for i, (main, pieces) in enumerate(PACKED.items()):
        value = message(19 + i)
        out[dirs[main]] = value
        for other, start, to, count in pieces:
            shift = (start - to) * unit
            moved = roll(value, shift if rising else -shift)
            if other in parts:
                moved = jnp.where((cell >= start) & (cell < start + count), moved, parts[other])
            parts[other] = moved
    for other, value in parts.items():
        out[dirs[other]] = value


def column_kernel(second, own, message):
    inner = lanes() % 16
    to_east = is_even("lon") != second
    from_own0 = (inner >= 8) == to_east
    shift = jnp.where(to_east, 120, 8)

    def get(west, east):
        slab = west if west == east else jnp.where(to_east, east, west)
        return jnp.where(from_own0, own[0, slab], pltpu.roll(own[1, slab], shift, 1))

    write_message(message, get, ~to_east, TO_WEST, TO_EAST, inner % 8, 1)


def edge_kernel(second, own, message):
    to_north = is_even("lat") != second

    def get(south, north):
        return jnp.where(to_north, own[1, north], own[0, south])

    write_message(message, get, ~to_north, TO_SOUTH, TO_NORTH, lanes() // 16, 16)


def growth_kernel(own, local, consts, gain):
    for half in range(2):
        point = local[half]
        turn = point[WDIR : WDIR + 1]
        cos_w = jnp.cos(turn)
        sin_w = jnp.sin(turn)
        force = wind_gain * point[WIND : WIND + 1] * consts[LEVEL]
        share = own[half, STATIC, SEA : SEA + 1]
        for d in range(NDIR):
            along = jnp.maximum(COS[d] * cos_w + SIN[d] * sin_w, 0.0)
            gain[d, half] = jnp.exp(force * along) * share


def tables_kernel(*refs):
    sources, (place, rims, shifts, gather, local, consts), landed = refs[:6], refs[6:12], refs[12:18]
    wide, sems = refs[18:]
    speed_table, refraction_table, ice_rate, ice, wspeed, wdir = landed
    copies = fetch(sources, landed, sems)
    first = lax.axis_index("band") * FREQ
    sub = lax.broadcasted_iota(jnp.int32, (8, 128), 0)
    mine = lanes() == first + sub

    def column(row):
        picked = jnp.where(mine, jnp.broadcast_to(row, (8, 128)), 0.0)
        return jnp.broadcast_to(jnp.sum(picked, axis=1, keepdims=True), (8, 128))

    def widen(values):
        return jnp.concatenate([values, jnp.zeros((values.shape[0], 112), f32)], axis=1)

    consts[LEVEL] = jnp.exp(math.log(freq_ratio) * (first + sub).astype(f32))
    lat = lax.axis_index("lat")
    lats = lax.axis_size("lat")
    group = lanes() // 32
    rows = lat * ROWS - HALO + 8 * group + sub
    latitude = (south_edge + band_span * (rows.astype(f32) + 0.5) / (ROWS * lats)) * (math.pi / 180.0)
    consts[STRETCH] = 1.0 / jnp.cos(latitude)
    ghost = ((group == 0) & (lat == 0)) | ((group == 3) & (lat == lats - 1))
    consts[LIVE] = jnp.where(ghost, 0.0, 1.0)
    chunk = lax.broadcasted_iota(jnp.int32, (16, 128), 0)
    lane = lax.broadcasted_iota(jnp.int32, (16, 128), 1)
    low = chunk < 8
    targets = [
        40 + chunk,
        72 + chunk,
        jnp.where(low, 64 + chunk, 24 + chunk),
        jnp.where(low, 56 + chunk, 80 + chunk),
        8 + chunk,
        104 + chunk,
    ]
    corners = [jnp.where(low, chunk, 16 + chunk), jnp.where(low, 120 + chunk, 88 + chunk)]
    for matrix, lists in ((place, targets), (rims, corners)):
        matrix[...] = jnp.zeros_like(matrix)
        for s, target in enumerate(lists):
            stripe = (lane == target).astype(f32).astype(bf16)
            for part in range(2):
                for t in range(8):
                    row = part * 128 * len(lists) + s * 128 + 16 * t
                    matrix[row : row + 16, 128 * t : 128 * t + 128] = stripe
    row = lax.broadcasted_iota(jnp.int32, (128, 128), 0)
    col = lax.broadcasted_iota(jnp.int32, (128, 128), 1)
    for sign, taps in ((0, FORTH_TAPS), (1, BACK_TAPS)):
        for i, tap in enumerate(taps):
            moved = (row == (col + tap) % 128).astype(f32).astype(bf16)
            for part in range(2):
                shifts[sign, 128 * part : 128 * part + 128, 128 * i : 128 * i + 128] = moved
    for t in range(8):
        for half in range(2):
            from_row = 40 + 32 * half + col % 16
            moved = ((col // 16 == t) & (row == from_row)).astype(f32).astype(bf16)
            for part in range(2):
                at = part * 1024 + 128 * t
                gather[at : at + 128, 128 * half : 128 * half + 128] = moved
    local[...] = jnp.zeros_like(local)
    wide[...] = jnp.zeros_like(wide)
    for copy in copies:
        copy.wait()
    for at, table in ((TAB_SPEED, speed_table), (TAB_TURN, refraction_table)):
        padded = widen(table[...])
        for c in range(NCLASS):
            consts[at + c] = column(padded[c : c + 1])
    consts[ICE_RATE] = column(widen(ice_rate[...].reshape(1, 16)))
    place_field(wide, ice[...].astype(f32), local, ICE)
    place_field(wide, wspeed[...], local, WIND)
    place_field(wide, wdir[...], local, WDIR)


def unpack_kernel(cols_first, cols_second, consts, west, east):
    del consts
    even = is_even("lon")
    place = lanes() % 8
    read_message(lambda i: jnp.where(even, cols_second[i], cols_first[i]), west, False, TO_EAST, place, 1)
    read_message(lambda i: jnp.where(even, cols_first[i], cols_second[i]), east, True, TO_WEST, place, 1)


def unpack_rows_kernel(rows_second, rows_first, south, north):
    even = is_even("lat")
    place = lanes() // 16
    read_message(lambda i: jnp.where(even, rows_second[i], rows_first[i]), south, False, TO_NORTH, place, 16)
    read_message(lambda i: jnp.where(even, rows_first[i], rows_second[i]), north, True, TO_SOUTH, place, 16)


def rim_kernel(second, west, east, *refs):
    rim = refs[-1]
    west_low = (lanes() % 16 < 8) == (is_even("lat") != second)
    for slab in range(SLABS):
        rim[slab] = jnp.where(west_low, west[slab], east[slab])


def split(x):
    high = x.astype(bf16)
    return high, (x - high.astype(f32)).astype(bf16)


def fill_parts(lhs, count, s, array):
    x = jnp.concatenate([array.reshape(8 * SLABS, 128), jnp.zeros((8, 128), f32)], axis=0)
    high, low = split(x)
    lhs[:, 128 * s : 128 * s + 128] = high
    lhs[:, 128 * (count + s) : 128 * (count + s) + 128] = low


def place_kernel(own, west, east, south, north, matrix, q, lhs):
    fill_parts(lhs, 6, 0, own[0])
    fill_parts(lhs, 6, 1, own[1])
    fill_parts(lhs, 6, 2, west[...])
    fill_parts(lhs, 6, 3, east[...])
    fill_parts(lhs, 6, 4, south[...])
    fill_parts(lhs, 6, 5, north[...])
    for pair in range(4):
        moved = jnp.dot(lhs[...], matrix[:, 256 * pair : 256 * pair + 256], preferred_element_type=f32)
        for i in range(2):
            q[:, 2 * pair + i] = moved[: 8 * SLABS, 128 * i : 128 * i + 128].reshape(SLABS, 8, 128)


def lookup(point, consts, at):
    depth = jnp.broadcast_to(point[DEPTH : DEPTH + 1], (8, 128))
    value = jnp.zeros((8, 128), f32)
    for c in range(NCLASS):
        value = jnp.where(depth == float(c), consts[at + c], value)
    return value * point[SEA : SEA + 1]


def rims_kernel(partial, rims_second, rims_first, consts, matrix, q, kx, ky, tx, ty, lhs):
    even_lat = is_even("lat")
    south = jnp.where(even_lat, rims_second[...], rims_first[...])
    north = jnp.where(even_lat, rims_first[...], rims_second[...])
    for s, array in ((0, south), (1, north)):
        high, low = split(array[:NDIR].reshape(8 * NDIR, 128))
        lhs[:, 128 * s : 128 * s + 128] = high
        lhs[:, 128 * (2 + s) : 128 * (2 + s) + 128] = low
    lane = lanes()
    south, north = south[STATIC], north[STATIC]
    speed = []
    for t in range(8):
        if t % 2 == 0:
            moved = jnp.dot(lhs[...], matrix[:, 128 * t : 128 * t + 256], preferred_element_type=f32)
            for i in range(2):
                q[:, t + i] = partial[:NDIR, t + i] + moved[:, 128 * i : 128 * i + 128].reshape(NDIR, 8, 128)
        point = partial[STATIC, t]
        for low, array, shift in ((0, south, 0), (24, south, 16), (96, north, 88), (120, north, 120)):
            point = jnp.where((lane >= low) & (lane < low + 8), roll(array, shift - 16 * t), point)
        pace = lookup(point, consts, TAB_SPEED)
        turning = lookup(point, consts, TAB_TURN)
        speed.append(pace)
        tx[t] = turning * point[SLOPE_X : SLOPE_X + 1]
        ty[t] = turning * point[SLOPE_Y : SLOPE_Y + 1]
        stretch = consts[STRETCH, t : t + 1, :]
        kx[0, t] = 0.5 * (pace + roll(pace, -1)) * stretch
        kx[1, t] = 0.5 * (pace + roll(pace, 1)) * stretch
    for t in range(8):
        ahead = speed[t + 1] if t < 7 else roll(speed[0], -32)
        ky[t] = 0.5 * (speed[t] + ahead)


def flux(q, diff, curve, k, u, w):
    return k * (q + u * (diff - w * curve))


def halves(k):
    return 0.5 - 0.5 * k, (1.0 / 3.0) + (1.0 / 3.0) * k


def weights(k):
    u, w = halves(k)
    bend = k * u * w
    return k - k * u + 2.0 * bend, k * u - bend, -bend


FORTH_TAPS = (-1, -2)
BACK_TAPS = (-1, 2)


def lon_dirs(sign, base):
    if base == 0:
        return [[0], [18]][sign]
    if base == 9:
        return [[27], [9]][sign]
    return [[base, 36 - base], [18 - base, 18 + base]][sign]


def lon_pair(q, shifts, out, sign, base, tap_of):
    dirs = lon_dirs(sign, base)
    x = jnp.concatenate([q[d].reshape(64, 128) for d in dirs], axis=0)
    lhs = jnp.concatenate(split(x), axis=1)
    moved = jnp.dot(lhs, shifts[sign], preferred_element_type=f32)
    for t in range(8):
        tap = tap_of(t)
        for i, d in enumerate(dirs):
            cell = q[d, t]
            near = moved[64 * i + 8 * t : 64 * i + 8 * t + 8]
            out[d, t] = (tap[0] * cell + tap[1] * roll(cell, -1)) + (
                tap[2] * near[:, :128] + tap[3] * near[:, 128:]
            )


def first_lon_kernel(q, kx, shifts, out, taps):
    for base in range(10):
        for t in range(8):
            a1, b1, c1 = weights(COS[base] * kx[0, t])
            a0, b0, c0 = weights(COS[base] * kx[1, t])
            for sign, tap in enumerate(
                ((1.0 - a1 + b0, -b1, a0 - c1, c0), (1.0 + b1 - a0, a1 - c0, -b0, c1))
            ):
                for i in range(4):
                    taps[base, sign, i, t] = tap[i]
        for sign in range(2):
            lon_pair(q, shifts, out, sign, base, lambda t: [taps[base, sign, i, t] for i in range(4)])


def lon_kernel(q, taps, shifts, out):
    for sign in range(2):
        for base in range(10):
            lon_pair(q, shifts, out, sign, base, lambda t: [taps[base, sign, i, t] for i in range(4)])


def lat_kernel(q, ky, consts, out, sums=None):
    live = consts[LIVE]
    totals = [jnp.zeros((8, 128), f32)] * 8

    def put(d, t, value):
        out[d, t] = value
        if sums is not None:
            totals[t] = totals[t] + value

    def forth(d, ks, us, ws):
        tiles = [q[d, t] for t in range(8)]
        diff = [tiles[t + 1] - tiles[t] for t in range(7)]
        diff.append(roll(tiles[0], -32) - tiles[7])
        before = roll(diff[7], 32)
        fluxes = []
        for t in range(8):
            fluxes.append(flux(tiles[t], diff[t], diff[t] - before, ks[t], us[t], ws[t]))
            before = diff[t]
        behind = roll(fluxes[7], 32)
        for t in range(8):
            put(d, t, (tiles[t] - fluxes[t] + behind) * live)
            behind = fluxes[t]

    def back(d, ks, us, ws):
        tiles = [q[d, t] for t in range(8)]
        ahead = tiles[1:] + [roll(tiles[0], -32)]
        diff = [tiles[t] - ahead[t] for t in range(8)]
        after = diff[1:] + [roll(diff[0], -32)]
        fluxes = [flux(ahead[t], diff[t], diff[t] - after[t], ks[t], us[t], ws[t]) for t in range(8)]
        behind = roll(fluxes[7], 32)
        for t in range(8):
            put(d, t, (tiles[t] + fluxes[t] - behind) * live)
            behind = fluxes[t]

    for base in range(10):
        ks = [SIN[base] * ky[t] for t in range(8)]
        us, ws = zip(*[halves(k) for k in ks])
        if base == 0:
            north, south = [0], [18]
        elif base == 9:
            north, south = [9], [27]
        else:
            north, south = [base, 18 - base], [18 + base, 36 - base]
        for d in north:
            forth(d, ks, us, ws)
        for d in south:
            back(d, ks, us, ws)
    if sums is None:
        return
    lane = lanes()
    halves_of = [jnp.zeros((8, 128), f32)] * 2
    for t in range(8):
        moved = roll(totals[t], 16 * t - 40)
        halves_of[0] = jnp.where(lane // 16 == t, moved, halves_of[0])
        halves_of[1] = jnp.where(lane // 16 == (t + 2) % 8, moved, halves_of[1])
    halves_of[1] = roll(halves_of[1], -32)
    sums[...] = jnp.zeros((8, 128), f32)
    for half in range(2):
        sums[half : half + 1, :] = jnp.sum(halves_of[half], axis=0, keepdims=True)
        sums[2 + half : 3 + half, :] = jnp.sum(halves_of[half] * consts[LEVEL], axis=0, keepdims=True)


def turn_around(get, put, x, y):
    def factors(d):
        k = SIN_FACE[d] * x - COS_FACE[d] * y
        return (k, *halves(k))

    def opposite(cell, diff, curve, k, u, w):
        return k * (cell + w * (1.5 * diff - u * curve))

    half_turn = NDIR // 2
    k, u, w = factors(half_turn - 1)
    state = []
    ends = []
    for at in (0, half_turn):
        cell, ahead = get(at), get(at + 1)
        before, last = get((at - 1) % NDIR), get((at - 2) % NDIR)
        diff = ahead - cell
        diff1 = cell - before
        curve = diff - diff1
        curve1 = diff1 - (before - last)
        if at == 0:
            f = opposite(before, diff1, jnp.where(k >= 0.0, curve, curve1), k, u, w)
        else:
            f = flux(before, diff1, jnp.where(k >= 0.0, curve1, curve), k, u, w)
        state.append([cell, ahead, diff, curve])
        ends.append(f)
    f_first, f_second = -ends[0], -ends[1]
    for d in range(half_turn):
        if d < half_turn - 1:
            k, u, w = factors(d)
            positive = k >= 0.0
        for at in (0, half_turn):
            cell, ahead, diff, curve = state[at // half_turn]
            beyond = get((at + d + 2) % NDIR)
            diff_ahead = beyond - ahead
            curve_ahead = diff_ahead - diff
            if at == 0:
                if d < half_turn - 1:
                    f = flux(cell, diff, jnp.where(positive, curve, curve_ahead), k, u, w)
                else:
                    f = ends[1]
                put(d, cell - f + f_first)
                f_first = f
            else:
                if d < half_turn - 1:
                    f = opposite(cell, diff, jnp.where(positive, curve_ahead, curve), k, u, w)
                else:
                    f = ends[0]
                put(at + d, cell + f - f_second)
                f_second = f
            state[at // half_turn] = [ahead, beyond, diff_ahead, curve_ahead]


def turn_kernel(q, tx, ty, out):
    for t in range(8):

        def put(d, value, t=t):
            out[d, t] = value

        turn_around(lambda d, t=t: q[d, t], put, tx[t], ty[t])


def gather_kernel(q, matrix, own, lhs):
    for t in range(8):
        high, low = split(q[:, t].reshape(8 * NDIR, 128))
        lhs[:, 128 * t : 128 * t + 128] = high
        lhs[:, 1024 + 128 * t : 1024 + 128 * t + 128] = low
    moved = jnp.dot(lhs[...], matrix[...], preferred_element_type=f32)
    for half in range(2):
        own[half] = moved[:, 128 * half : 128 * half + 128].reshape(NDIR, 8, 128)


def last_turn_kernel(own, static, gain, consts, early):
    for half in range(2):
        point = static[half, 0]
        turning = lookup(point, consts, TAB_TURN)

        def put(d, value, half=half):
            early[half, d] = value * gain[d, half]

        turn_around(
            lambda d, half=half: own[half, d],
            put,
            turning * point[SLOPE_X : SLOPE_X + 1],
            turning * point[SLOPE_Y : SLOPE_Y + 1],
        )


def finish_kernel(early, local, sums, other, consts, out, flat0, flat1):
    total = sums[...] + other[...]
    level = consts[LEVEL]
    for half, flat in ((0, flat0), (1, flat1)):
        energy = total[half : half + 1]
        moment = total[2 + half : 3 + half]
        mean_level = jnp.maximum(moment, 1.0) / jnp.maximum(energy, 1.0)
        mean = energy / NCOMP
        breaking = break_coef * level * level / mean_level * (mean * mean)
        damping = local[half, ICE : ICE + 1] * consts[ICE_RATE]
        loss = jnp.exp(-breaking - damping)
        for d in range(NDIR):
            flat[pl.ds(d, FREQ, stride=NDIR), :] = early[half, d] * loss
        for low, high in ((0, 128), (128, 256), (256, 288)):
            out[8 * half : 8 * half + 8, :, low:high] = flat[low:high, :].T.reshape(8, 16, high - low)


PARAMS = pltpu.CompilerParams(vmem_limit_bytes=40 * 2**20)


def call(kernel, ins, outs, scratch=(), name=None, space=pltpu.VMEM, dtype=f32, result=pltpu.VMEM):
    types = dtype if isinstance(dtype, list) else [dtype] * len(outs)
    return pl.pallas_call(
        kernel,
        out_shape=[jax.ShapeDtypeStruct(shape, kind) for shape, kind in zip(outs, types)],
        in_specs=[pl.BlockSpec(memory_space=space)] * ins,
        out_specs=[pl.BlockSpec(memory_space=result)] * len(outs),
        scratch_shapes=list(scratch),
        compiler_params=PARAMS,
        name=name,
    )


def swap(array, axis, first, closed=False):
    count = lax.axis_size(axis)
    pairs = []
    for i in range(first, count, 2):
        if i + 1 < count or closed:
            j = (i + 1) % count
            pairs += [(i, j), (j, i)]
    return lax.ppermute(array, axis, pairs)


def per_device(
    spectrum,
    sea_mask,
    ice_mask,
    depth_class,
    speed_table,
    refraction_table,
    depth_slope,
    wind_speed,
    wind_dir,
    ice_rate,
):
    tile = (8, 128)
    block = (8,) + tile
    slabs = (SLABS,) + tile
    sent = (SENT,) + tile
    inputs = [spectrum, sea_mask, depth_class, depth_slope]
    (own,) = call(
        pack_kernel,
        4,
        [(2,) + slabs],
        [pltpu.VMEM(x.shape, x.dtype) for x in inputs]
        + [pltpu.VMEM((NDIR * FREQ, 128), f32)] * 2
        + [pltpu.VMEM((16, 128), f32), pltpu.VMEM((2,) + tile, f32), pltpu.SemaphoreType.DMA((4,))],
        name="pack",
        space=pltpu.HBM,
    )(*[pltpu.with_memory_space_constraint(x, pltpu.HBM) for x in inputs])
    (to_first,) = call(functools.partial(column_kernel, False), 1, [sent], name="column_near")(own)
    cols_first = swap(to_first, "lon", 0, True)
    (to_second,) = call(functools.partial(column_kernel, True), 1, [sent], name="column_far")(own)
    cols_second = swap(to_second, "lon", 1, True)
    (edge_second,) = call(functools.partial(edge_kernel, True), 1, [sent], name="edge_far")(own)
    rows_second = swap(edge_second, "lat", 1)
    (edge_first,) = call(functools.partial(edge_kernel, False), 1, [sent], name="edge_near")(own)
    rows_first = swap(edge_first, "lat", 0)
    inputs = [speed_table, refraction_table, ice_rate, ice_mask, wind_speed, wind_dir]
    place, rims, shifts, gather, local, consts = call(
        tables_kernel,
        6,
        [(1536, 1024), (512, 1024), (2, 256, 256), (2048, 256), (2,) + tile, (20,) + tile],
        [pltpu.VMEM(x.shape, x.dtype) for x in inputs]
        + [pltpu.VMEM((16, 128), f32), pltpu.SemaphoreType.DMA((6,))],
        name="tables",
        space=pltpu.HBM,
        dtype=[bf16] * 4 + [f32] * 2,
    )(*[pltpu.with_memory_space_constraint(x, pltpu.HBM) for x in inputs])
    (gain,) = call(growth_kernel, 3, [(NDIR, 2) + tile], name="growth")(own, local, consts)
    west, east = call(unpack_kernel, 3, [slabs] * 2, name="unpack")(cols_first, cols_second, consts)
    (rim_second,) = call(functools.partial(rim_kernel, True), 2, [slabs], name="rim_far")(west, east)
    rims_second = swap(rim_second, "lat", 1)
    (rim_first,) = call(functools.partial(rim_kernel, False), 5, [slabs], name="rim_near")(
        west, east, rows_second, rows_first, rim_second
    )
    rims_first = swap(rim_first, "lat", 0)
    south, north = call(unpack_rows_kernel, 2, [slabs] * 2, name="unpack_rows")(rows_second, rows_first)
    (partial,) = call(
        place_kernel,
        6,
        [(SLABS,) + block],
        [pltpu.VMEM((8 * SLABS + 8, 1536), bf16)],
        name="place",
    )(own, west, east, south, north, place)
    q, kx, ky, tx, ty = call(
        rims_kernel,
        5,
        [(NDIR,) + block, (2,) + block] + [block] * 3,
        [pltpu.VMEM((8 * NDIR, 512), bf16)],
        name="rims",
    )(partial, rims_second, rims_first, consts, rims)
    cells = [(NDIR,) + block]
    for substep in range(ITERS):
        if substep == 0:
            q, taps = call(first_lon_kernel, 3, cells + [(10, 2, 4) + block], name="first_lon")(q, kx, shifts)
        else:
            (q,) = call(lon_kernel, 3, cells, name="lon")(q, taps, shifts)
        if substep == ITERS - 1:
            q, sums = call(lat_kernel, 3, cells + [tile], name="lat_sums")(q, ky, consts)
        else:
            (q,) = call(lat_kernel, 3, cells, name="lat")(q, ky, consts)
            (q,) = call(turn_kernel, 3, cells, name="turn")(q, tx, ty)
    other = swap(sums, "band", 0)
    (last,) = call(
        gather_kernel, 2, [(2, NDIR) + tile], [pltpu.VMEM((8 * NDIR, 2048), bf16)], name="gather"
    )(q, gather)
    static = own[:, STATIC:]
    (early,) = call(last_turn_kernel, 4, [(2, NDIR) + tile], name="last_turn")(last, static, gain, consts)
    (out,) = call(
        finish_kernel, 5, [spectrum.shape], [pltpu.VMEM((NDIR * FREQ, 128), f32)] * 2, name="finish"
    )(early, local, sums, other, consts)
    return out


def solution(mesh):
    return jax.shard_map(
        per_device,
        mesh=mesh,
        in_specs=(
            P("lat", "lon", "band"),
            P("lat", "lon"),
            P("lat", "lon"),
            P("lat", "lon"),
            P(),
            P(),
            P(None, "lat", "lon"),
            P("lat", "lon"),
            P("lat", "lon"),
            P(),
        ),
        out_specs=P("lat", "lon", "band"),
        check_vma=False,
    )
```

```python
import functools
import math

import jax
import jax.numpy as jnp
import numpy as np
from jax import lax
from jax.experimental import pallas as pl
from jax.experimental.pallas import tpu as pltpu
from jax.sharding import PartitionSpec as P

NDIR = 36
NCOMP = 576
ITERS = 4
NCLASS = 8
FREQ = 8
HALO = 8
ROWS = 16
STATIC = NDIR
SLABS = NDIR + 1
SEA, DEPTH, SLOPE_X, SLOPE_Y, ICE, WIND, WDIR = range(7)

freq_ratio = 1.1
wind_gain = 0.12
break_coef = 0.05
south_edge = -30.0
band_span = 60.0

COS = [math.cos(2.0 * math.pi * d / NDIR) for d in range(NDIR)]
SIN = [math.sin(2.0 * math.pi * d / NDIR) for d in range(NDIR)]
COS_FACE = [math.cos(2.0 * math.pi * (d + 0.5) / NDIR) for d in range(NDIR)]
SIN_FACE = [math.sin(2.0 * math.pi * (d + 0.5) / NDIR) for d in range(NDIR)]

TAB_SPEED, TAB_TURN, STRETCH, LIVE, ICE_RATE, LEVEL = 0, 8, 16, 17, 18, 19

f32 = jnp.float32
bf16 = jnp.bfloat16


def lanes():
    return lax.broadcasted_iota(jnp.int32, (8, 128), 1)


def roll(x, shift):
    shift = shift % 128
    return pltpu.roll(x, shift, 1) if shift else x


def is_even(axis):
    return lax.axis_index(axis) % 2 == 0


def place_field(wide, values, static, field):
    group = lax.broadcasted_iota(jnp.int32, (16, 128), 1) // 16
    row = lax.broadcasted_iota(jnp.int32, (16, 128), 0) % 8
    wide[:, :16] = values
    moved = pltpu.roll(wide[...], 0, 1, stride=16, stride_axis=0)
    kept = jnp.where(group == row, moved, 0.0)
    for half in range(2):
        static[half, field : field + 1, :] = jnp.sum(kept[8 * half : 8 * half + 8], axis=0, keepdims=True)


def fetch(sources, landed, sems):
    copies = [pltpu.make_async_copy(src, dst, sems.at[i]) for i, (src, dst) in enumerate(zip(sources, landed))]
    for copy in copies:
        copy.start()
    return copies


def pack_kernel(*refs):
    sources, own, landed = refs[:4], refs[4], refs[5:9]
    flat0, flat1, wide, static, sems = refs[9:]
    copies = fetch(sources, landed, sems)
    wide[...] = jnp.zeros_like(wide)
    static[...] = jnp.zeros_like(static)
    for copy in copies:
        copy.wait()
    spec, sea, depth, slope = landed
    place_field(wide, sea[...].astype(f32), static, SEA)
    place_field(wide, depth[...].astype(f32), static, DEPTH)
    place_field(wide, slope[0], static, SLOPE_X)
    place_field(wide, slope[1], static, SLOPE_Y)
    own[:, STATIC] = static[...]
    grid = spec[...].reshape(256, NDIR * FREQ)
    for low, high in ((0, 128), (128, 256), (256, 288)):
        turned = grid[:, low:high].T
        flat0[low:high, :] = turned[:, :128]
        flat1[low:high, :] = turned[:, 128:]
    sea0 = static[0, SEA : SEA + 1, :]
    sea1 = static[1, SEA : SEA + 1, :]
    for d in range(NDIR):
        own[0, d] = flat0[pl.ds(d, FREQ, stride=NDIR), :] * sea0
        own[1, d] = flat1[pl.ds(d, FREQ, stride=NDIR), :] * sea1


NEEDS = (7, 7, 6, 6, 5, 5, 4, 4, 4, 4, 4, 4, 5, 5, 6, 6, 7, 7)
PACKED = {
    0: [(12, 3, 7, 1)],
    1: [(12, 4, 7, 1)],
    2: [(15, 0, 6, 2)],
    3: [(15, 2, 6, 2)],
    4: [(12, 0, 5, 3)],
    5: [(13, 0, 5, 3)],
    6: [(9, 0, 4, 4)],
    7: [(10, 0, 4, 4)],
    8: [(11, 0, 4, 4)],
    14: [(15, 4, 6, 2)],
    16: [(13, 3, 7, 1)],
    17: [(13, 4, 7, 1)],
}
TO_WEST, TO_EAST, TO_NORTH, TO_SOUTH = 27, 9, 18, 0
SENT = 18 + 1 + len(PACKED)


def downstream(first):
    return [(first + i) % NDIR for i in range(18)]


def whole(first):
    return [d for d in range(NDIR) if d not in downstream(first)] + [STATIC]


def write_message(message, get, rising, rising_first, falling_first, place, unit):
    for i, pair in enumerate(zip(whole(rising_first), whole(falling_first))):
        message[i] = get(*pair)
    up, down = downstream(rising_first), downstream(falling_first)
    cell = jnp.where(rising, place, 7 - place)
    for i, (main, pieces) in enumerate(PACKED.items()):
        value = get(up[main], down[main])
        for other, start, to, count in pieces:
            shift = (to - start) * unit
            moved = pltpu.roll(get(up[other], down[other]), jnp.where(rising, shift, 128 - shift), 1)
            value = jnp.where((cell >= to) & (cell < to + count), moved, value)
        message[19 + i] = value


def read_message(message, out, rising, first, place, unit):
    for i, d in enumerate(whole(first)):
        out[d] = message(i)
    dirs = downstream(first)
    cell = place if rising else 7 - place
    parts = {}
    for i, (main, pieces) in enumerate(PACKED.items()):
        value = message(19 + i)
        out[dirs[main]] = value
        for other, start, to, count in pieces:
            shift = (start - to) * unit
            moved = roll(value, shift if rising else -shift)
            if other in parts:
                moved = jnp.where((cell >= start) & (cell < start + count), moved, parts[other])
            parts[other] = moved
    for other, value in parts.items():
        out[dirs[other]] = value


def column_kernel(second, own, message):
    inner = lanes() % 16
    to_east = is_even("lon") != second
    from_own0 = (inner >= 8) == to_east
    shift = jnp.where(to_east, 120, 8)

    def get(west, east):
        slab = west if west == east else jnp.where(to_east, east, west)
        return jnp.where(from_own0, own[0, slab], pltpu.roll(own[1, slab], shift, 1))

    write_message(message, get, ~to_east, TO_WEST, TO_EAST, inner % 8, 1)


def edge_kernel(second, own, message):
    to_north = is_even("lat") != second

    def get(south, north):
        return jnp.where(to_north, own[1, north], own[0, south])

    write_message(message, get, ~to_north, TO_SOUTH, TO_NORTH, lanes() // 16, 16)


def growth_kernel(own, local, consts, gain):
    for half in range(2):
        point = local[half]
        turn = point[WDIR : WDIR + 1]
        cos_w = jnp.cos(turn)
        sin_w = jnp.sin(turn)
        force = wind_gain * point[WIND : WIND + 1] * consts[LEVEL]
        share = own[half, STATIC, SEA : SEA + 1]
        for d in range(NDIR):
            along = jnp.maximum(COS[d] * cos_w + SIN[d] * sin_w, 0.0)
            gain[d, half] = jnp.exp(force * along) * share


def tables_kernel(*refs):
    sources, (place, rims, shifts, gather, local, consts), landed = refs[:6], refs[6:12], refs[12:18]
    wide, sems = refs[18:]
    speed_table, refraction_table, ice_rate, ice, wspeed, wdir = landed
    copies = fetch(sources, landed, sems)
    first = lax.axis_index("band") * FREQ
    sub = lax.broadcasted_iota(jnp.int32, (8, 128), 0)
    mine = lanes() == first + sub

    def column(row):
        picked = jnp.where(mine, jnp.broadcast_to(row, (8, 128)), 0.0)
        return jnp.broadcast_to(jnp.sum(picked, axis=1, keepdims=True), (8, 128))

    def widen(values):
        return jnp.concatenate([values, jnp.zeros((values.shape[0], 112), f32)], axis=1)

    consts[LEVEL] = jnp.exp(math.log(freq_ratio) * (first + sub).astype(f32))
    lat = lax.axis_index("lat")
    lats = lax.axis_size("lat")
    group = lanes() // 32
    rows = lat * ROWS - HALO + 8 * group + sub
    latitude = (south_edge + band_span * (rows.astype(f32) + 0.5) / (ROWS * lats)) * (math.pi / 180.0)
    consts[STRETCH] = 1.0 / jnp.cos(latitude)
    ghost = ((group == 0) & (lat == 0)) | ((group == 3) & (lat == lats - 1))
    consts[LIVE] = jnp.where(ghost, 0.0, 1.0)
    chunk = lax.broadcasted_iota(jnp.int32, (16, 128), 0)
    lane = lax.broadcasted_iota(jnp.int32, (16, 128), 1)
    low = chunk < 8
    targets = [
        40 + chunk,
        72 + chunk,
        jnp.where(low, 64 + chunk, 24 + chunk),
        jnp.where(low, 56 + chunk, 80 + chunk),
        8 + chunk,
        104 + chunk,
    ]
    corners = [jnp.where(low, chunk, 16 + chunk), jnp.where(low, 120 + chunk, 88 + chunk)]
    for matrix, lists in ((place, targets), (rims, corners)):
        matrix[...] = jnp.zeros_like(matrix)
        for s, target in enumerate(lists):
            stripe = (lane == target).astype(f32).astype(bf16)
            for part in range(2):
                for t in range(8):
                    row = part * 128 * len(lists) + s * 128 + 16 * t
                    matrix[row : row + 16, 128 * t : 128 * t + 128] = stripe
    row = lax.broadcasted_iota(jnp.int32, (128, 128), 0)
    col = lax.broadcasted_iota(jnp.int32, (128, 128), 1)
    for sign, taps in ((0, FORTH_TAPS), (1, BACK_TAPS)):
        for i, tap in enumerate(taps):
            moved = (row == (col + tap) % 128).astype(f32).astype(bf16)
            for part in range(2):
                shifts[sign, 128 * part : 128 * part + 128, 128 * i : 128 * i + 128] = moved
    for t in range(8):
        for half in range(2):
            from_row = 40 + 32 * half + col % 16
            moved = ((col // 16 == t) & (row == from_row)).astype(f32).astype(bf16)
            for part in range(2):
                at = part * 1024 + 128 * t
                gather[at : at + 128, 128 * half : 128 * half + 128] = moved
    local[...] = jnp.zeros_like(local)
    wide[...] = jnp.zeros_like(wide)
    for copy in copies:
        copy.wait()
    for at, table in ((TAB_SPEED, speed_table), (TAB_TURN, refraction_table)):
        padded = widen(table[...])
        for c in range(NCLASS):
            consts[at + c] = column(padded[c : c + 1])
    consts[ICE_RATE] = column(widen(ice_rate[...].reshape(1, 16)))
    place_field(wide, ice[...].astype(f32), local, ICE)
    place_field(wide, wspeed[...], local, WIND)
    place_field(wide, wdir[...], local, WDIR)


def unpack_kernel(cols_first, cols_second, consts, west, east):
    del consts
    even = is_even("lon")
    place = lanes() % 8
    read_message(lambda i: jnp.where(even, cols_second[i], cols_first[i]), west, False, TO_EAST, place, 1)
    read_message(lambda i: jnp.where(even, cols_first[i], cols_second[i]), east, True, TO_WEST, place, 1)


def unpack_rows_kernel(rows_second, rows_first, south, north):
    even = is_even("lat")
    place = lanes() // 16
    read_message(lambda i: jnp.where(even, rows_second[i], rows_first[i]), south, False, TO_NORTH, place, 16)
    read_message(lambda i: jnp.where(even, rows_first[i], rows_second[i]), north, True, TO_SOUTH, place, 16)


def rim_kernel(second, west, east, *refs):
    to_north = is_even("lat") != second
    west_low = (lanes() % 16 < 8) == to_north

    def get(south, north):
        slab = south if south == north else jnp.where(to_north, north, south)
        return jnp.where(west_low, west[slab], east[slab])

    write_message(refs[-1], get, ~to_north, TO_SOUTH, TO_NORTH, lanes() // 16, 16)
    if second:
        refs[-1][SENT] = jnp.zeros((8, 128), f32)


def split(x):
    high = x.astype(bf16)
    return high, (x - high.astype(f32)).astype(bf16)


def fill_parts(lhs, count, s, array):
    x = jnp.concatenate([array.reshape(8 * SLABS, 128), jnp.zeros((8, 128), f32)], axis=0)
    high, low = split(x)
    lhs[:, 128 * s : 128 * s + 128] = high
    lhs[:, 128 * (count + s) : 128 * (count + s) + 128] = low


def place_kernel(own, west, east, south, north, matrix, q, lhs):
    fill_parts(lhs, 6, 0, own[0])
    fill_parts(lhs, 6, 1, own[1])
    fill_parts(lhs, 6, 2, west[...])
    fill_parts(lhs, 6, 3, east[...])
    fill_parts(lhs, 6, 4, south[...])
    fill_parts(lhs, 6, 5, north[...])
    for pair in range(4):
        moved = jnp.dot(lhs[...], matrix[:, 256 * pair : 256 * pair + 256], preferred_element_type=f32)
        for i in range(2):
            q[:, 2 * pair + i] = moved[: 8 * SLABS, 128 * i : 128 * i + 128].reshape(SLABS, 8, 128)


def lookup(point, consts, at):
    depth = jnp.broadcast_to(point[DEPTH : DEPTH + 1], (8, 128))
    value = jnp.zeros((8, 128), f32)
    for c in range(NCLASS):
        value = jnp.where(depth == float(c), consts[at + c], value)
    return value * point[SEA : SEA + 1]


def rims_kernel(partial, rims_second, rims_first, consts, matrix, q, kx, ky, tx, ty, lhs, south, north):
    even_lat = is_even("lat")
    place = lanes() // 16
    read_message(lambda i: jnp.where(even_lat, rims_second[i], rims_first[i]), south, False, TO_NORTH, place, 16)
    read_message(lambda i: jnp.where(even_lat, rims_first[i], rims_second[i]), north, True, TO_SOUTH, place, 16)
    for s, array in ((0, south), (1, north)):
        high, low = split(array[:NDIR].reshape(8 * NDIR, 128))
        lhs[:, 128 * s : 128 * s + 128] = high
        lhs[:, 128 * (2 + s) : 128 * (2 + s) + 128] = low
    lane = lanes()
    south, north = south[STATIC], north[STATIC]
    speed = []
    for t in range(8):
        if t % 2 == 0:
            moved = jnp.dot(lhs[...], matrix[:, 128 * t : 128 * t + 256], preferred_element_type=f32)
            for i in range(2):
                q[:, t + i] = partial[:NDIR, t + i] + moved[:, 128 * i : 128 * i + 128].reshape(NDIR, 8, 128)
        point = partial[STATIC, t]
        for low, array, shift in ((0, south, 0), (24, south, 16), (96, north, 88), (120, north, 120)):
            point = jnp.where((lane >= low) & (lane < low + 8), roll(array, shift - 16 * t), point)
        pace = lookup(point, consts, TAB_SPEED)
        turning = lookup(point, consts, TAB_TURN)
        speed.append(pace)
        tx[t] = turning * point[SLOPE_X : SLOPE_X + 1]
        ty[t] = turning * point[SLOPE_Y : SLOPE_Y + 1]
        stretch = consts[STRETCH, t : t + 1, :]
        kx[0, t] = 0.5 * (pace + roll(pace, -1)) * stretch
        kx[1, t] = 0.5 * (pace + roll(pace, 1)) * stretch
    for t in range(8):
        ahead = speed[t + 1] if t < 7 else roll(speed[0], -32)
        ky[t] = 0.5 * (speed[t] + ahead)


def flux(q, diff, curve, k, u, w):
    return k * (q + u * (diff - w * curve))


def halves(k):
    return 0.5 - 0.5 * k, (1.0 / 3.0) + (1.0 / 3.0) * k


def weights(k):
    u, w = halves(k)
    bend = k * u * w
    return k - k * u + 2.0 * bend, k * u - bend, -bend


FORTH_TAPS = (-1, -2)
BACK_TAPS = (-1, 2)


def lon_dirs(sign, base):
    if base == 0:
        return [[0], [18]][sign]
    if base == 9:
        return [[27], [9]][sign]
    return [[base, 36 - base], [18 - base, 18 + base]][sign]


def lon_products(q, shifts, sign, base):
    x = jnp.concatenate([q[d].reshape(64, 128) for d in lon_dirs(sign, base)], axis=0)
    lhs = jnp.concatenate(split(x), axis=1)
    return jnp.dot(lhs, shifts[sign], preferred_element_type=f32)


def lon_stages(q, taps, shifts, out, order, before):
    ahead = lon_products(q, shifts, *order[0])
    for step, (sign, base) in enumerate(order):
        moved = ahead
        if step + 1 < len(order):
            ahead = lon_products(q, shifts, *order[step + 1])
        before(step)
        for t in range(8):
            tap = [taps[base, sign, i, t] for i in range(4)]
            for i, d in enumerate(lon_dirs(sign, base)):
                cell = q[d, t]
                near = moved[64 * i + 8 * t : 64 * i + 8 * t + 8]
                out[d, t] = (tap[0] * cell + tap[1] * roll(cell, -1)) + (
                    tap[2] * near[:, :128] + tap[3] * near[:, 128:]
                )


def first_lon_kernel(q, kx, shifts, out, taps):
    def prepare(base, tiles):
        for t in tiles:
            a1, b1, c1 = weights(COS[base] * kx[0, t])
            a0, b0, c0 = weights(COS[base] * kx[1, t])
            for sign, tap in enumerate(
                ((1.0 - a1 + b0, -b1, a0 - c1, c0), (1.0 + b1 - a0, a1 - c0, -b0, c1))
            ):
                for i in range(4):
                    taps[base, sign, i, t] = tap[i]

    def before(step):
        if step // 2 < 9:
            prepare(step // 2 + 1, range(4 * (step % 2), 4 * (step % 2) + 4))

    prepare(0, range(8))
    lon_stages(q, taps, shifts, out, [(sign, base) for base in range(10) for sign in range(2)], before)


def lon_kernel(q, taps, shifts, out):
    order = [(sign, base) for sign in range(2) for base in range(10)]
    lon_stages(q, taps, shifts, out, order, lambda step: None)


def lat_kernel(q, ky, consts, out, sums=None):
    live = consts[LIVE]
    totals = [jnp.zeros((8, 128), f32)] * 8

    def put(d, t, value):
        out[d, t] = value
        if sums is not None:
            totals[t] = totals[t] + value

    def forth(d, ks, us, ws):
        tiles = [q[d, t] for t in range(8)]
        diff = [tiles[t + 1] - tiles[t] for t in range(7)]
        diff.append(roll(tiles[0], -32) - tiles[7])
        before = roll(diff[7], 32)
        fluxes = []
        for t in range(8):
            fluxes.append(flux(tiles[t], diff[t], diff[t] - before, ks[t], us[t], ws[t]))
            before = diff[t]
        behind = roll(fluxes[7], 32)
        for t in range(8):
            put(d, t, (tiles[t] - fluxes[t] + behind) * live)
            behind = fluxes[t]

    def back(d, ks, us, ws):
        tiles = [q[d, t] for t in range(8)]
        ahead = tiles[1:] + [roll(tiles[0], -32)]
        diff = [tiles[t] - ahead[t] for t in range(8)]
        after = diff[1:] + [roll(diff[0], -32)]
        fluxes = [flux(ahead[t], diff[t], diff[t] - after[t], ks[t], us[t], ws[t]) for t in range(8)]
        behind = roll(fluxes[7], 32)
        for t in range(8):
            put(d, t, (tiles[t] + fluxes[t] - behind) * live)
            behind = fluxes[t]

    for base in range(10):
        ks = [SIN[base] * ky[t] for t in range(8)]
        us, ws = zip(*[halves(k) for k in ks])
        if base == 0:
            north, south = [0], [18]
        elif base == 9:
            north, south = [9], [27]
        else:
            north, south = [base, 18 - base], [18 + base, 36 - base]
        for d in north:
            forth(d, ks, us, ws)
        for d in south:
            back(d, ks, us, ws)
    if sums is None:
        return
    lane = lanes()
    halves_of = [jnp.zeros((8, 128), f32)] * 2
    for t in range(8):
        moved = roll(totals[t], 16 * t - 40)
        halves_of[0] = jnp.where(lane // 16 == t, moved, halves_of[0])
        halves_of[1] = jnp.where(lane // 16 == (t + 2) % 8, moved, halves_of[1])
    halves_of[1] = roll(halves_of[1], -32)
    sums[...] = jnp.zeros((8, 128), f32)
    for half in range(2):
        sums[half : half + 1, :] = jnp.sum(halves_of[half], axis=0, keepdims=True)
        sums[2 + half : 3 + half, :] = jnp.sum(halves_of[half] * consts[LEVEL], axis=0, keepdims=True)


def turn_around(get, put, x, y):
    def factors(d):
        k = SIN_FACE[d] * x - COS_FACE[d] * y
        return (k, *halves(k))

    def opposite(cell, diff, curve, k, u, w):
        return k * (cell + w * (1.5 * diff - u * curve))

    half_turn = NDIR // 2
    k, u, w = factors(half_turn - 1)
    state = []
    ends = []
    for at in (0, half_turn):
        cell, ahead = get(at), get(at + 1)
        before, last = get((at - 1) % NDIR), get((at - 2) % NDIR)
        diff = ahead - cell
        diff1 = cell - before
        curve = diff - diff1
        curve1 = diff1 - (before - last)
        if at == 0:
            f = opposite(before, diff1, jnp.where(k >= 0.0, curve, curve1), k, u, w)
        else:
            f = flux(before, diff1, jnp.where(k >= 0.0, curve1, curve), k, u, w)
        state.append([cell, ahead, diff, curve])
        ends.append(f)
    f_first, f_second = -ends[0], -ends[1]
    for d in range(half_turn):
        if d < half_turn - 1:
            k, u, w = factors(d)
            positive = k >= 0.0
        for at in (0, half_turn):
            cell, ahead, diff, curve = state[at // half_turn]
            beyond = get((at + d + 2) % NDIR)
            diff_ahead = beyond - ahead
            curve_ahead = diff_ahead - diff
            if at == 0:
                if d < half_turn - 1:
                    f = flux(cell, diff, jnp.where(positive, curve, curve_ahead), k, u, w)
                else:
                    f = ends[1]
                put(d, cell - f + f_first)
                f_first = f
            else:
                if d < half_turn - 1:
                    f = opposite(cell, diff, jnp.where(positive, curve_ahead, curve), k, u, w)
                else:
                    f = ends[0]
                put(at + d, cell + f - f_second)
                f_second = f
            state[at // half_turn] = [ahead, beyond, diff_ahead, curve_ahead]


def turn_kernel(q, tx, ty, out):
    for t in range(8):

        def put(d, value, t=t):
            out[d, t] = value

        turn_around(lambda d, t=t: q[d, t], put, tx[t], ty[t])


def gather_kernel(q, matrix, own, lhs):
    for t in range(8):
        high, low = split(q[:, t].reshape(8 * NDIR, 128))
        lhs[:, 128 * t : 128 * t + 128] = high
        lhs[:, 1024 + 128 * t : 1024 + 128 * t + 128] = low
    moved = jnp.dot(lhs[...], matrix[...], preferred_element_type=f32)
    for half in range(2):
        own[half] = moved[:, 128 * half : 128 * half + 128].reshape(NDIR, 8, 128)


def last_turn_kernel(own, static, gain, consts, early):
    for half in range(2):
        point = static[half, 0]
        turning = lookup(point, consts, TAB_TURN)

        def put(d, value, half=half):
            early[half, d] = value * gain[d, half]

        turn_around(
            lambda d, half=half: own[half, d],
            put,
            turning * point[SLOPE_X : SLOPE_X + 1],
            turning * point[SLOPE_Y : SLOPE_Y + 1],
        )


def finish_kernel(early, local, sums, other, consts, out, flat0, flat1):
    total = sums[...] + other[...]
    level = consts[LEVEL]
    for half, flat in ((0, flat0), (1, flat1)):
        energy = total[half : half + 1]
        moment = total[2 + half : 3 + half]
        mean_level = jnp.maximum(moment, 1.0) / jnp.maximum(energy, 1.0)
        mean = energy / NCOMP
        breaking = break_coef * level * level / mean_level * (mean * mean)
        damping = local[half, ICE : ICE + 1] * consts[ICE_RATE]
        loss = jnp.exp(-breaking - damping)
        for d in range(NDIR):
            flat[pl.ds(d, FREQ, stride=NDIR), :] = early[half, d] * loss
        for low, high in ((0, 128), (128, 256), (256, 288)):
            out[8 * half : 8 * half + 8, :, low:high] = flat[low:high, :].T.reshape(8, 16, high - low)


PARAMS = pltpu.CompilerParams(vmem_limit_bytes=40 * 2**20)


def call(kernel, ins, outs, scratch=(), name=None, space=pltpu.VMEM, dtype=f32, result=pltpu.VMEM):
    types = dtype if isinstance(dtype, list) else [dtype] * len(outs)
    return pl.pallas_call(
        kernel,
        out_shape=[jax.ShapeDtypeStruct(shape, kind) for shape, kind in zip(outs, types)],
        in_specs=[pl.BlockSpec(memory_space=space)] * ins,
        out_specs=[pl.BlockSpec(memory_space=result)] * len(outs),
        scratch_shapes=list(scratch),
        compiler_params=PARAMS,
        name=name,
    )


def swap(array, axis, first, closed=False):
    count = lax.axis_size(axis)
    pairs = []
    for i in range(first, count, 2):
        if i + 1 < count or closed:
            j = (i + 1) % count
            pairs += [(i, j), (j, i)]
    return lax.ppermute(array, axis, pairs)


def per_device(
    spectrum,
    sea_mask,
    ice_mask,
    depth_class,
    speed_table,
    refraction_table,
    depth_slope,
    wind_speed,
    wind_dir,
    ice_rate,
):
    tile = (8, 128)
    block = (8,) + tile
    slabs = (SLABS,) + tile
    sent = (SENT,) + tile
    inputs = [spectrum, sea_mask, depth_class, depth_slope]
    (own,) = call(
        pack_kernel,
        4,
        [(2,) + slabs],
        [pltpu.VMEM(x.shape, x.dtype) for x in inputs]
        + [pltpu.VMEM((NDIR * FREQ, 128), f32)] * 2
        + [pltpu.VMEM((16, 128), f32), pltpu.VMEM((2,) + tile, f32), pltpu.SemaphoreType.DMA((4,))],
        name="pack",
        space=pltpu.HBM,
    )(*[pltpu.with_memory_space_constraint(x, pltpu.HBM) for x in inputs])
    (to_first,) = call(functools.partial(column_kernel, False), 1, [sent], name="column_near")(own)
    cols_first = swap(to_first, "lon", 0, True)
    (to_second,) = call(functools.partial(column_kernel, True), 1, [sent], name="column_far")(own)
    cols_second = swap(to_second, "lon", 1, True)
    (edge_second,) = call(functools.partial(edge_kernel, True), 1, [sent], name="edge_far")(own)
    rows_second = swap(edge_second, "lat", 1)
    (edge_first,) = call(functools.partial(edge_kernel, False), 1, [sent], name="edge_near")(own)
    rows_first = swap(edge_first, "lat", 0)
    inputs = [speed_table, refraction_table, ice_rate, ice_mask, wind_speed, wind_dir]
    place, rims, shifts, gather, local, consts = call(
        tables_kernel,
        6,
        [(1536, 1024), (512, 1024), (2, 256, 256), (2048, 256), (2,) + tile, (20,) + tile],
        [pltpu.VMEM(x.shape, x.dtype) for x in inputs]
        + [pltpu.VMEM((16, 128), f32), pltpu.SemaphoreType.DMA((6,))],
        name="tables",
        space=pltpu.HBM,
        dtype=[bf16] * 4 + [f32] * 2,
    )(*[pltpu.with_memory_space_constraint(x, pltpu.HBM) for x in inputs])
    (gain,) = call(growth_kernel, 3, [(NDIR, 2) + tile], name="growth")(own, local, consts)
    west, east = call(unpack_kernel, 3, [slabs] * 2, name="unpack")(cols_first, cols_second, consts)
    (rim_second,) = call(functools.partial(rim_kernel, True), 2, [(SENT + 1,) + tile], name="rim_far")(west, east)
    rims_second = swap(rim_second, "lat", 1)
    (rim_first,) = call(functools.partial(rim_kernel, False), 5, [sent], name="rim_near")(
        west, east, rows_second, rows_first, rim_second
    )
    rims_first = swap(rim_first, "lat", 0)
    south, north = call(unpack_rows_kernel, 2, [slabs] * 2, name="unpack_rows")(rows_second, rows_first)
    (partial,) = call(
        place_kernel,
        6,
        [(SLABS,) + block],
        [pltpu.VMEM((8 * SLABS + 8, 1536), bf16)],
        name="place",
    )(own, west, east, south, north, place)
    q, kx, ky, tx, ty = call(
        rims_kernel,
        5,
        [(NDIR,) + block, (2,) + block] + [block] * 3,
        [pltpu.VMEM((8 * NDIR, 512), bf16)] + [pltpu.VMEM(slabs, f32)] * 2,
        name="rims",
    )(partial, rims_second, rims_first, consts, rims)
    cells = [(NDIR,) + block]
    for substep in range(ITERS):
        if substep == 0:
            q, taps = call(first_lon_kernel, 3, cells + [(10, 2, 4) + block], name="first_lon")(q, kx, shifts)
        else:
            (q,) = call(lon_kernel, 3, cells, name="lon")(q, taps, shifts)
        if substep == ITERS - 1:
            q, sums = call(lat_kernel, 3, cells + [tile], name="lat_sums")(q, ky, consts)
        else:
            (q,) = call(lat_kernel, 3, cells, name="lat")(q, ky, consts)
            (q,) = call(turn_kernel, 3, cells, name="turn")(q, tx, ty)
    other = swap(sums, "band", 0)
    (last,) = call(
        gather_kernel, 2, [(2, NDIR) + tile], [pltpu.VMEM((8 * NDIR, 2048), bf16)], name="gather"
    )(q, gather)
    static = own[:, STATIC:]
    (early,) = call(last_turn_kernel, 4, [(2, NDIR) + tile], name="last_turn")(last, static, gain, consts)
    (out,) = call(
        finish_kernel, 5, [spectrum.shape], [pltpu.VMEM((NDIR * FREQ, 128), f32)] * 2, name="finish"
    )(early, local, sums, other, consts)
    return out


def solution(mesh):
    return jax.shard_map(
        per_device,
        mesh=mesh,
        in_specs=(
            P("lat", "lon", "band"),
            P("lat", "lon"),
            P("lat", "lon"),
            P("lat", "lon"),
            P(),
            P(),
            P(None, "lat", "lon"),
            P("lat", "lon"),
            P("lat", "lon"),
            P(),
        ),
        out_specs=P("lat", "lon", "band"),
        check_vma=False,
    )
```

```python
import functools
import math

import jax
import jax.numpy as jnp
import numpy as np
from jax import lax
from jax.experimental import pallas as pl
from jax.experimental.pallas import tpu as pltpu
from jax.sharding import PartitionSpec as P

NDIR = 36
NCOMP = 576
ITERS = 4
NCLASS = 8
FREQ = 8
HALO = 8
ROWS = 16
STATIC = NDIR
SLABS = NDIR + 1
SEA, DEPTH, SLOPE_X, SLOPE_Y, ICE, WIND, WDIR = range(7)

freq_ratio = 1.1
wind_gain = 0.12
break_coef = 0.05
south_edge = -30.0
band_span = 60.0

COS = [math.cos(2.0 * math.pi * d / NDIR) for d in range(NDIR)]
SIN = [math.sin(2.0 * math.pi * d / NDIR) for d in range(NDIR)]
COS_FACE = [math.cos(2.0 * math.pi * (d + 0.5) / NDIR) for d in range(NDIR)]
SIN_FACE = [math.sin(2.0 * math.pi * (d + 0.5) / NDIR) for d in range(NDIR)]

TAB_SPEED, TAB_TURN, STRETCH, LIVE, ICE_RATE, LEVEL = 0, 8, 16, 17, 18, 19

f32 = jnp.float32
bf16 = jnp.bfloat16


def lanes():
    return lax.broadcasted_iota(jnp.int32, (8, 128), 1)


def roll(x, shift):
    shift = shift % 128
    return pltpu.roll(x, shift, 1) if shift else x


def is_even(axis):
    return lax.axis_index(axis) % 2 == 0


def place_field(wide, values, static, field):
    group = lax.broadcasted_iota(jnp.int32, (16, 128), 1) // 16
    row = lax.broadcasted_iota(jnp.int32, (16, 128), 0) % 8
    wide[:, :16] = values
    moved = pltpu.roll(wide[...], 0, 1, stride=16, stride_axis=0)
    kept = jnp.where(group == row, moved, 0.0)
    for half in range(2):
        static[half, field : field + 1, :] = jnp.sum(kept[8 * half : 8 * half + 8], axis=0, keepdims=True)


def fetch(sources, landed, sems):
    copies = [pltpu.make_async_copy(src, dst, sems.at[i]) for i, (src, dst) in enumerate(zip(sources, landed))]
    for copy in copies:
        copy.start()
    return copies


def pack_kernel(*refs):
    sources, own, landed = refs[:4], refs[4], refs[5:9]
    flat0, flat1, wide, static, sems = refs[9:]
    copies = fetch(sources, landed, sems)
    wide[...] = jnp.zeros_like(wide)
    static[...] = jnp.zeros_like(static)
    for copy in copies:
        copy.wait()
    spec, sea, depth, slope = landed
    place_field(wide, sea[...].astype(f32), static, SEA)
    place_field(wide, depth[...].astype(f32), static, DEPTH)
    place_field(wide, slope[0], static, SLOPE_X)
    place_field(wide, slope[1], static, SLOPE_Y)
    own[:, STATIC] = static[...]
    grid = spec[...].reshape(256, NDIR * FREQ)
    for low, high in ((0, 128), (128, 256), (256, 288)):
        turned = grid[:, low:high].T
        flat0[low:high, :] = turned[:, :128]
        flat1[low:high, :] = turned[:, 128:]
    sea0 = static[0, SEA : SEA + 1, :]
    sea1 = static[1, SEA : SEA + 1, :]
    for d in range(NDIR):
        own[0, d] = flat0[pl.ds(d, FREQ, stride=NDIR), :] * sea0
        own[1, d] = flat1[pl.ds(d, FREQ, stride=NDIR), :] * sea1


NEEDS = (7, 7, 6, 6, 5, 5, 4, 4, 4, 4, 4, 4, 5, 5, 6, 6, 7, 7)
PACKED = {
    0: [(12, 3, 7, 1)],
    1: [(12, 4, 7, 1)],
    2: [(15, 0, 6, 2)],
    3: [(15, 2, 6, 2)],
    4: [(12, 0, 5, 3)],
    5: [(13, 0, 5, 3)],
    6: [(9, 0, 4, 4)],
    7: [(10, 0, 4, 4)],
    8: [(11, 0, 4, 4)],
    14: [(15, 4, 6, 2)],
    16: [(13, 3, 7, 1)],
    17: [(13, 4, 7, 1)],
}
TO_WEST, TO_EAST, TO_NORTH, TO_SOUTH = 27, 9, 18, 0
SENT = 18 + 1 + len(PACKED)


def downstream(first):
    return [(first + i) % NDIR for i in range(18)]


def whole(first):
    return [d for d in range(NDIR) if d not in downstream(first)] + [STATIC]


def write_message(message, get, rising, rising_first, falling_first, place, unit):
    for i, pair in enumerate(zip(whole(rising_first), whole(falling_first))):
        message[i] = get(*pair)
    up, down = downstream(rising_first), downstream(falling_first)
    cell = jnp.where(rising, place, 7 - place)
    for i, (main, pieces) in enumerate(PACKED.items()):
        value = get(up[main], down[main])
        for other, start, to, count in pieces:
            shift = (to - start) * unit
            moved = pltpu.roll(get(up[other], down[other]), jnp.where(rising, shift, 128 - shift), 1)
            value = jnp.where((cell >= to) & (cell < to + count), moved, value)
        message[19 + i] = value


def read_message(message, out, rising, first, place, unit):
    for i, d in enumerate(whole(first)):
        out[d] = message(i)
    dirs = downstream(first)
    cell = place if rising else 7 - place
    parts = {}
    for i, (main, pieces) in enumerate(PACKED.items()):
        value = message(19 + i)
        out[dirs[main]] = value
        for other, start, to, count in pieces:
            shift = (start - to) * unit
            moved = roll(value, shift if rising else -shift)
            if other in parts:
                moved = jnp.where((cell >= start) & (cell < start + count), moved, parts[other])
            parts[other] = moved
    for other, value in parts.items():
        out[dirs[other]] = value


def column_kernel(second, own, message):
    inner = lanes() % 16
    to_east = is_even("lon") != second
    from_own0 = (inner >= 8) == to_east
    shift = jnp.where(to_east, 120, 8)

    def get(west, east):
        slab = west if west == east else jnp.where(to_east, east, west)
        return jnp.where(from_own0, own[0, slab], pltpu.roll(own[1, slab], shift, 1))

    write_message(message, get, ~to_east, TO_WEST, TO_EAST, inner % 8, 1)


def edge_kernel(second, own, message):
    to_north = is_even("lat") != second

    def get(south, north):
        return jnp.where(to_north, own[1, north], own[0, south])

    write_message(message, get, ~to_north, TO_SOUTH, TO_NORTH, lanes() // 16, 16)


def growth_kernel(own, local, consts, gain):
    for half in range(2):
        point = local[half]
        turn = point[WDIR : WDIR + 1]
        cos_w = jnp.cos(turn)
        sin_w = jnp.sin(turn)
        force = wind_gain * point[WIND : WIND + 1] * consts[LEVEL]
        share = own[half, STATIC, SEA : SEA + 1]
        for d in range(NDIR):
            along = jnp.maximum(COS[d] * cos_w + SIN[d] * sin_w, 0.0)
            gain[d, half] = jnp.exp(force * along) * share


def tables_kernel(*refs):
    sources, (place, rims, shifts, gather, local, consts), landed = refs[:6], refs[6:12], refs[12:18]
    wide, sems = refs[18:]
    speed_table, refraction_table, ice_rate, ice, wspeed, wdir = landed
    copies = fetch(sources, landed, sems)
    first = lax.axis_index("band") * FREQ
    sub = lax.broadcasted_iota(jnp.int32, (8, 128), 0)
    mine = lanes() == first + sub

    def column(row):
        picked = jnp.where(mine, jnp.broadcast_to(row, (8, 128)), 0.0)
        return jnp.broadcast_to(jnp.sum(picked, axis=1, keepdims=True), (8, 128))

    def widen(values):
        return jnp.concatenate([values, jnp.zeros((values.shape[0], 112), f32)], axis=1)

    consts[LEVEL] = jnp.exp(math.log(freq_ratio) * (first + sub).astype(f32))
    lat = lax.axis_index("lat")
    lats = lax.axis_size("lat")
    group = lanes() // 32
    rows = lat * ROWS - HALO + 8 * group + sub
    latitude = (south_edge + band_span * (rows.astype(f32) + 0.5) / (ROWS * lats)) * (math.pi / 180.0)
    consts[STRETCH] = 1.0 / jnp.cos(latitude)
    ghost = ((group == 0) & (lat == 0)) | ((group == 3) & (lat == lats - 1))
    consts[LIVE] = jnp.where(ghost, 0.0, 1.0)
    chunk = lax.broadcasted_iota(jnp.int32, (16, 128), 0)
    lane = lax.broadcasted_iota(jnp.int32, (16, 128), 1)
    low = chunk < 8
    targets = [
        40 + chunk,
        72 + chunk,
        jnp.where(low, 64 + chunk, 24 + chunk),
        jnp.where(low, 56 + chunk, 80 + chunk),
        8 + chunk,
        104 + chunk,
    ]
    corners = [jnp.where(low, chunk, 16 + chunk), jnp.where(low, 120 + chunk, 88 + chunk)]
    for matrix, lists in ((place, targets), (rims, corners)):
        matrix[...] = jnp.zeros_like(matrix)
        for s, target in enumerate(lists):
            stripe = (lane == target).astype(f32).astype(bf16)
            for part in range(2):
                for t in range(8):
                    row = part * 128 * len(lists) + s * 128 + 16 * t
                    matrix[row : row + 16, 128 * t : 128 * t + 128] = stripe
    row = lax.broadcasted_iota(jnp.int32, (128, 128), 0)
    col = lax.broadcasted_iota(jnp.int32, (128, 128), 1)
    for sign, taps in ((0, FORTH_TAPS), (1, BACK_TAPS)):
        for i, tap in enumerate(taps):
            moved = (row == (col + tap) % 128).astype(f32).astype(bf16)
            for part in range(2):
                shifts[sign, 128 * part : 128 * part + 128, 128 * i : 128 * i + 128] = moved
    for t in range(8):
        for half in range(2):
            from_row = 40 + 32 * half + col % 16
            moved = ((col // 16 == t) & (row == from_row)).astype(f32).astype(bf16)
            for part in range(2):
                at = part * 1024 + 128 * t
                gather[at : at + 128, 128 * half : 128 * half + 128] = moved
    local[...] = jnp.zeros_like(local)
    wide[...] = jnp.zeros_like(wide)
    for copy in copies:
        copy.wait()
    for at, table in ((TAB_SPEED, speed_table), (TAB_TURN, refraction_table)):
        padded = widen(table[...])
        for c in range(NCLASS):
            consts[at + c] = column(padded[c : c + 1])
    consts[ICE_RATE] = column(widen(ice_rate[...].reshape(1, 16)))
    place_field(wide, ice[...].astype(f32), local, ICE)
    place_field(wide, wspeed[...], local, WIND)
    place_field(wide, wdir[...], local, WDIR)


def read_columns(cols_first, cols_second, west, east):
    even = is_even("lon")
    place = lanes() % 8
    read_message(lambda i: jnp.where(even, cols_second[i], cols_first[i]), west, False, TO_EAST, place, 1)
    read_message(lambda i: jnp.where(even, cols_first[i], cols_second[i]), east, True, TO_WEST, place, 1)


def unpack_kernel(cols_first, cols_second, west, east):
    read_columns(cols_first, cols_second, west, east)


def unpack_rows_kernel(rows_second, rows_first, south, north):
    even = is_even("lat")
    place = lanes() // 16
    read_message(lambda i: jnp.where(even, rows_second[i], rows_first[i]), south, False, TO_NORTH, place, 16)
    read_message(lambda i: jnp.where(even, rows_first[i], rows_second[i]), north, True, TO_SOUTH, place, 16)


def write_rim(second, west, east, message):
    to_north = is_even("lat") != second
    west_low = (lanes() % 16 < 8) == to_north

    def pick(side, south, north):
        return side[south] if south == north else jnp.where(to_north, side[north], side[south])

    def get(south, north):
        return jnp.where(west_low, pick(west, south, north), pick(east, south, north))

    write_message(message, get, ~to_north, TO_SOUTH, TO_NORTH, lanes() // 16, 16)


def far_rim_kernel(cols_first, cols_second, consts, message):
    del consts
    west, east = {}, {}
    read_columns(cols_first, cols_second, west, east)
    write_rim(True, west, east, message)
    message[SENT] = jnp.zeros((8, 128), f32)


def near_rim_kernel(west, east, rows_second, rows_first, far, message):
    del rows_second, rows_first, far
    write_rim(False, west, east, message)


def split(x):
    high = x.astype(bf16)
    return high, (x - high.astype(f32)).astype(bf16)


def fill_parts(lhs, count, s, array):
    x = jnp.concatenate([array.reshape(8 * SLABS, 128), jnp.zeros((8, 128), f32)], axis=0)
    high, low = split(x)
    lhs[:, 128 * s : 128 * s + 128] = high
    lhs[:, 128 * (count + s) : 128 * (count + s) + 128] = low


def place_kernel(own, west, east, south, north, matrix, q, lhs):
    fill_parts(lhs, 6, 0, own[0])
    fill_parts(lhs, 6, 1, own[1])
    fill_parts(lhs, 6, 2, west[...])
    fill_parts(lhs, 6, 3, east[...])
    fill_parts(lhs, 6, 4, south[...])
    fill_parts(lhs, 6, 5, north[...])
    for pair in range(4):
        moved = jnp.dot(lhs[...], matrix[:, 256 * pair : 256 * pair + 256], preferred_element_type=f32)
        for i in range(2):
            q[:, 2 * pair + i] = moved[: 8 * SLABS, 128 * i : 128 * i + 128].reshape(SLABS, 8, 128)


def lookup(point, consts, at):
    depth = jnp.broadcast_to(point[DEPTH : DEPTH + 1], (8, 128))
    value = jnp.zeros((8, 128), f32)
    for c in range(NCLASS):
        value = jnp.where(depth == float(c), consts[at + c], value)
    return value * point[SEA : SEA + 1]


def rims_kernel(partial, rims_second, rims_first, consts, matrix, q, taps, ky, tx, ty, lhs, south, north):
    even_lat = is_even("lat")
    place = lanes() // 16
    read_message(lambda i: jnp.where(even_lat, rims_second[i], rims_first[i]), south, False, TO_NORTH, place, 16)
    read_message(lambda i: jnp.where(even_lat, rims_first[i], rims_second[i]), north, True, TO_SOUTH, place, 16)
    for s, array in ((0, south), (1, north)):
        high, low = split(array[:NDIR].reshape(8 * NDIR, 128))
        lhs[:, 128 * s : 128 * s + 128] = high
        lhs[:, 128 * (2 + s) : 128 * (2 + s) + 128] = low
    lane = lanes()
    south, north = south[STATIC], north[STATIC]
    speed = []
    for t in range(8):
        if t % 2 == 0:
            moved = jnp.dot(lhs[...], matrix[:, 128 * t : 128 * t + 256], preferred_element_type=f32)
            for i in range(2):
                q[:, t + i] = partial[:NDIR, t + i] + moved[:, 128 * i : 128 * i + 128].reshape(NDIR, 8, 128)
        point = partial[STATIC, t]
        for low, array, shift in ((0, south, 0), (24, south, 16), (96, north, 88), (120, north, 120)):
            point = jnp.where((lane >= low) & (lane < low + 8), roll(array, shift - 16 * t), point)
        pace = lookup(point, consts, TAB_SPEED)
        turning = lookup(point, consts, TAB_TURN)
        speed.append(pace)
        tx[t] = turning * point[SLOPE_X : SLOPE_X + 1]
        ty[t] = turning * point[SLOPE_Y : SLOPE_Y + 1]
        stretch = consts[STRETCH, t : t + 1, :]
        right = powers(0.5 * (pace + roll(pace, -1)) * stretch)
        left = powers(0.5 * (pace + roll(pace, 1)) * stretch)
        for base in range(10):
            a1, b1, c1 = weights(COS[base], right)
            a0, b0, c0 = weights(COS[base], left)
            for sign, tap in enumerate(((1.0 - a1 + b0, b1, a0 + c1, c0), (1.0 + b1 - a0, a1 + c0, b0, c1))):
                for i in range(4):
                    taps[base, sign, i, t] = tap[i]
    for t in range(8):
        ahead = speed[t + 1] if t < 7 else roll(speed[0], -32)
        ky[t] = 0.5 * (speed[t] + ahead)


def flux(q, diff, curve, k, u, w):
    return k * (q + u * (diff - w * curve))


def halves(k):
    return 0.5 - 0.5 * k, (1.0 / 3.0) + (1.0 / 3.0) * k


def powers(face):
    square = face * face
    return (1.0 / 6.0) * face, 0.5 * square, (1.0 / 6.0) * (square * face)


def weights(cos_d, face_powers):
    p, s, c = face_powers
    bend = cos_d * p - cos_d**3 * c
    rest = cos_d**2 * s - cos_d**3 * c
    return (5.0 * cos_d * p - cos_d**3 * c) + rest, 2.0 * cos_d * p - rest, bend


FORTH_TAPS = (-1, -2)
BACK_TAPS = (-1, 2)


def lon_dirs(sign, base):
    if base == 0:
        return [[0], [18]][sign]
    if base == 9:
        return [[27], [9]][sign]
    return [[base, 36 - base], [18 - base, 18 + base]][sign]


def lon_kernel(q, taps, shifts, out):
    for sign in range(2):
        for base in range(10):
            dirs = lon_dirs(sign, base)
            x = jnp.concatenate([q[d].reshape(64, 128) for d in dirs], axis=0)
            lhs = jnp.concatenate(split(x), axis=1)
            moved = jnp.dot(lhs, shifts[sign], preferred_element_type=f32)
            for t in range(8):
                tap = [taps[base, sign, i, t] for i in range(4)]
                for i, d in enumerate(dirs):
                    cell = q[d, t]
                    ahead = roll(cell, -1)
                    near = moved[64 * i + 8 * t : 64 * i + 8 * t + 8]
                    behind, beyond = near[:, :128], near[:, 128:]
                    if sign == 0:
                        out[d, t] = (tap[0] * cell - tap[1] * ahead) + (tap[2] * behind - tap[3] * beyond)
                    else:
                        out[d, t] = (tap[0] * cell + tap[1] * ahead) - (tap[2] * behind + tap[3] * beyond)


def lat_kernel(q, ky, consts, out, sums=None):
    live = consts[LIVE]
    totals = [jnp.zeros((8, 128), f32)] * 8

    def put(d, t, value):
        out[d, t] = value
        if sums is not None:
            totals[t] = totals[t] + value

    def forth(d, ks, us, ws):
        tiles = [q[d, t] for t in range(8)]
        diff = [tiles[t + 1] - tiles[t] for t in range(7)]
        diff.append(roll(tiles[0], -32) - tiles[7])
        before = roll(diff[7], 32)
        fluxes = []
        for t in range(8):
            fluxes.append(flux(tiles[t], diff[t], diff[t] - before, ks[t], us[t], ws[t]))
            before = diff[t]
        behind = roll(fluxes[7], 32)
        for t in range(8):
            put(d, t, (tiles[t] - fluxes[t] + behind) * live)
            behind = fluxes[t]

    def back(d, ks, us, ws):
        tiles = [q[d, t] for t in range(8)]
        ahead = tiles[1:] + [roll(tiles[0], -32)]
        diff = [tiles[t] - ahead[t] for t in range(8)]
        after = diff[1:] + [roll(diff[0], -32)]
        fluxes = [flux(ahead[t], diff[t], diff[t] - after[t], ks[t], us[t], ws[t]) for t in range(8)]
        behind = roll(fluxes[7], 32)
        for t in range(8):
            put(d, t, (tiles[t] + fluxes[t] - behind) * live)
            behind = fluxes[t]

    for base in range(10):
        ks = [SIN[base] * ky[t] for t in range(8)]
        us, ws = zip(*[halves(k) for k in ks])
        if base == 0:
            north, south = [0], [18]
        elif base == 9:
            north, south = [9], [27]
        else:
            north, south = [base, 18 - base], [18 + base, 36 - base]
        for d in north:
            forth(d, ks, us, ws)
        for d in south:
            back(d, ks, us, ws)
    if sums is None:
        return
    lane = lanes()
    halves_of = [jnp.zeros((8, 128), f32)] * 2
    for t in range(8):
        moved = roll(totals[t], 16 * t - 40)
        halves_of[0] = jnp.where(lane // 16 == t, moved, halves_of[0])
        halves_of[1] = jnp.where(lane // 16 == (t + 2) % 8, moved, halves_of[1])
    halves_of[1] = roll(halves_of[1], -32)
    sums[...] = jnp.zeros((8, 128), f32)
    for half in range(2):
        sums[half : half + 1, :] = jnp.sum(halves_of[half], axis=0, keepdims=True)
        sums[2 + half : 3 + half, :] = jnp.sum(halves_of[half] * consts[LEVEL], axis=0, keepdims=True)


def turn_around(get, put, x, y):
    def factors(d):
        k = SIN_FACE[d] * x - COS_FACE[d] * y
        return (k, *halves(k))

    def opposite(cell, diff, curve, k, u, w):
        return k * (cell + w * (1.5 * diff - u * curve))

    half_turn = NDIR // 2
    k, u, w = factors(half_turn - 1)
    state = []
    ends = []
    for at in (0, half_turn):
        cell, ahead = get(at), get(at + 1)
        before, last = get((at - 1) % NDIR), get((at - 2) % NDIR)
        diff = ahead - cell
        diff1 = cell - before
        curve = diff - diff1
        curve1 = diff1 - (before - last)
        if at == 0:
            f = opposite(before, diff1, jnp.where(k >= 0.0, curve, curve1), k, u, w)
        else:
            f = flux(before, diff1, jnp.where(k >= 0.0, curve1, curve), k, u, w)
        state.append([cell, ahead, diff, curve])
        ends.append(f)
    f_first, f_second = -ends[0], -ends[1]
    for d in range(half_turn):
        if d < half_turn - 1:
            k, u, w = factors(d)
            positive = k >= 0.0
        for at in (0, half_turn):
            cell, ahead, diff, curve = state[at // half_turn]
            beyond = get((at + d + 2) % NDIR)
            diff_ahead = beyond - ahead
            curve_ahead = diff_ahead - diff
            if at == 0:
                if d < half_turn - 1:
                    f = flux(cell, diff, jnp.where(positive, curve, curve_ahead), k, u, w)
                else:
                    f = ends[1]
                put(d, cell - f + f_first)
                f_first = f
            else:
                if d < half_turn - 1:
                    f = opposite(cell, diff, jnp.where(positive, curve_ahead, curve), k, u, w)
                else:
                    f = ends[0]
                put(at + d, cell + f - f_second)
                f_second = f
            state[at // half_turn] = [ahead, beyond, diff_ahead, curve_ahead]


def turn_kernel(q, tx, ty, out):
    for t in range(8):

        def put(d, value, t=t):
            out[d, t] = value

        turn_around(lambda d, t=t: q[d, t], put, tx[t], ty[t])


def gather_kernel(q, matrix, own, lhs):
    for t in range(8):
        high, low = split(q[:, t].reshape(8 * NDIR, 128))
        lhs[:, 128 * t : 128 * t + 128] = high
        lhs[:, 1024 + 128 * t : 1024 + 128 * t + 128] = low
    moved = jnp.dot(lhs[...], matrix[...], preferred_element_type=f32)
    for half in range(2):
        own[half] = moved[:, 128 * half : 128 * half + 128].reshape(NDIR, 8, 128)


def last_turn_kernel(own, static, gain, consts, early):
    for half in range(2):
        point = static[half, 0]
        turning = lookup(point, consts, TAB_TURN)

        def put(d, value, half=half):
            early[half, d] = value * gain[d, half]

        turn_around(
            lambda d, half=half: own[half, d],
            put,
            turning * point[SLOPE_X : SLOPE_X + 1],
            turning * point[SLOPE_Y : SLOPE_Y + 1],
        )


def finish_kernel(early, local, sums, other, consts, out, flat0, flat1):
    total = sums[...] + other[...]
    level = consts[LEVEL]
    for half, flat in ((0, flat0), (1, flat1)):
        energy = total[half : half + 1]
        moment = total[2 + half : 3 + half]
        mean_level = jnp.maximum(moment, 1.0) / jnp.maximum(energy, 1.0)
        mean = energy / NCOMP
        breaking = break_coef * level * level / mean_level * (mean * mean)
        damping = local[half, ICE : ICE + 1] * consts[ICE_RATE]
        loss = jnp.exp(-breaking - damping)
        for d in range(NDIR):
            flat[pl.ds(d, FREQ, stride=NDIR), :] = early[half, d] * loss
        for low, high in ((0, 128), (128, 256), (256, 288)):
            out[8 * half : 8 * half + 8, :, low:high] = flat[low:high, :].T.reshape(8, 16, high - low)


PARAMS = pltpu.CompilerParams(vmem_limit_bytes=40 * 2**20)


def call(kernel, ins, outs, scratch=(), name=None, space=pltpu.VMEM, dtype=f32, result=pltpu.VMEM):
    types = dtype if isinstance(dtype, list) else [dtype] * len(outs)
    return pl.pallas_call(
        kernel,
        out_shape=[jax.ShapeDtypeStruct(shape, kind) for shape, kind in zip(outs, types)],
        in_specs=[pl.BlockSpec(memory_space=space)] * ins,
        out_specs=[pl.BlockSpec(memory_space=result)] * len(outs),
        scratch_shapes=list(scratch),
        compiler_params=PARAMS,
        name=name,
    )


def swap(array, axis, first, closed=False):
    count = lax.axis_size(axis)
    pairs = []
    for i in range(first, count, 2):
        if i + 1 < count or closed:
            j = (i + 1) % count
            pairs += [(i, j), (j, i)]
    return lax.ppermute(array, axis, pairs)


def per_device(
    spectrum,
    sea_mask,
    ice_mask,
    depth_class,
    speed_table,
    refraction_table,
    depth_slope,
    wind_speed,
    wind_dir,
    ice_rate,
):
    tile = (8, 128)
    block = (8,) + tile
    slabs = (SLABS,) + tile
    sent = (SENT,) + tile
    inputs = [spectrum, sea_mask, depth_class, depth_slope]
    (own,) = call(
        pack_kernel,
        4,
        [(2,) + slabs],
        [pltpu.VMEM(x.shape, x.dtype) for x in inputs]
        + [pltpu.VMEM((NDIR * FREQ, 128), f32)] * 2
        + [pltpu.VMEM((16, 128), f32), pltpu.VMEM((2,) + tile, f32), pltpu.SemaphoreType.DMA((4,))],
        name="pack",
        space=pltpu.HBM,
    )(*[pltpu.with_memory_space_constraint(x, pltpu.HBM) for x in inputs])
    (to_first,) = call(functools.partial(column_kernel, False), 1, [sent], name="column_near")(own)
    cols_first = swap(to_first, "lon", 0, True)
    (to_second,) = call(functools.partial(column_kernel, True), 1, [sent], name="column_far")(own)
    cols_second = swap(to_second, "lon", 1, True)
    (edge_second,) = call(functools.partial(edge_kernel, True), 1, [sent], name="edge_far")(own)
    rows_second = swap(edge_second, "lat", 1)
    (edge_first,) = call(functools.partial(edge_kernel, False), 1, [sent], name="edge_near")(own)
    rows_first = swap(edge_first, "lat", 0)
    inputs = [speed_table, refraction_table, ice_rate, ice_mask, wind_speed, wind_dir]
    place, rims, shifts, gather, local, consts = call(
        tables_kernel,
        6,
        [(1536, 1024), (512, 1024), (2, 256, 256), (2048, 256), (2,) + tile, (20,) + tile],
        [pltpu.VMEM(x.shape, x.dtype) for x in inputs]
        + [pltpu.VMEM((16, 128), f32), pltpu.SemaphoreType.DMA((6,))],
        name="tables",
        space=pltpu.HBM,
        dtype=[bf16] * 4 + [f32] * 2,
    )(*[pltpu.with_memory_space_constraint(x, pltpu.HBM) for x in inputs])
    (gain,) = call(growth_kernel, 3, [(NDIR, 2) + tile], name="growth")(own, local, consts)
    (rim_second,) = call(far_rim_kernel, 3, [(SENT + 1,) + tile], name="rim_far")(cols_first, cols_second, consts)
    rims_second = swap(rim_second, "lat", 1)
    west, east = call(unpack_kernel, 2, [slabs] * 2, name="unpack")(cols_first, cols_second)
    (rim_first,) = call(near_rim_kernel, 5, [sent], name="rim_near")(
        west, east, rows_second, rows_first, rim_second
    )
    rims_first = swap(rim_first, "lat", 0)
    south, north = call(unpack_rows_kernel, 2, [slabs] * 2, name="unpack_rows")(rows_second, rows_first)
    (partial,) = call(
        place_kernel,
        6,
        [(SLABS,) + block],
        [pltpu.VMEM((8 * SLABS + 8, 1536), bf16)],
        name="place",
    )(own, west, east, south, north, place)
    q, taps, ky, tx, ty = call(
        rims_kernel,
        5,
        [(NDIR,) + block, (10, 2, 4) + block] + [block] * 3,
        [pltpu.VMEM((8 * NDIR, 512), bf16)] + [pltpu.VMEM(slabs, f32)] * 2,
        name="rims",
    )(partial, rims_second, rims_first, consts, rims)
    cells = [(NDIR,) + block]
    for substep in range(ITERS):
        (q,) = call(lon_kernel, 3, cells, name="lon")(q, taps, shifts)
        if substep == ITERS - 1:
            q, sums = call(lat_kernel, 3, cells + [tile], name="lat_sums")(q, ky, consts)
        else:
            (q,) = call(lat_kernel, 3, cells, name="lat")(q, ky, consts)
            (q,) = call(turn_kernel, 3, cells, name="turn")(q, tx, ty)
    other = swap(sums, "band", 0)
    (last,) = call(
        gather_kernel, 2, [(2, NDIR) + tile], [pltpu.VMEM((8 * NDIR, 2048), bf16)], name="gather"
    )(q, gather)
    static = own[:, STATIC:]
    (early,) = call(last_turn_kernel, 4, [(2, NDIR) + tile], name="last_turn")(last, static, gain, consts)
    (out,) = call(
        finish_kernel, 5, [spectrum.shape], [pltpu.VMEM((NDIR * FREQ, 128), f32)] * 2, name="finish"
    )(early, local, sums, other, consts)
    return out


def solution(mesh):
    return jax.shard_map(
        per_device,
        mesh=mesh,
        in_specs=(
            P("lat", "lon", "band"),
            P("lat", "lon"),
            P("lat", "lon"),
            P("lat", "lon"),
            P(),
            P(),
            P(None, "lat", "lon"),
            P("lat", "lon"),
            P("lat", "lon"),
            P(),
        ),
        out_specs=P("lat", "lon", "band"),
        check_vma=False,
    )
```

```python
import functools
import math

import jax
import jax.numpy as jnp
import numpy as np
from jax import lax
from jax.experimental import pallas as pl
from jax.experimental.pallas import tpu as pltpu
from jax.sharding import PartitionSpec as P

NDIR = 36
NCOMP = 576
ITERS = 4
NCLASS = 8
FREQ = 8
HALO = 8
ROWS = 16
STATIC = NDIR
SLABS = NDIR + 1
SEA, DEPTH, SLOPE_X, SLOPE_Y, ICE, WIND, WDIR = range(7)

freq_ratio = 1.1
wind_gain = 0.12
break_coef = 0.05
south_edge = -30.0
band_span = 60.0

COS = [math.cos(2.0 * math.pi * d / NDIR) for d in range(NDIR)]
SIN = [math.sin(2.0 * math.pi * d / NDIR) for d in range(NDIR)]
COS_FACE = [math.cos(2.0 * math.pi * (d + 0.5) / NDIR) for d in range(NDIR)]
SIN_FACE = [math.sin(2.0 * math.pi * (d + 0.5) / NDIR) for d in range(NDIR)]

TAB_SPEED, TAB_TURN, STRETCH, LIVE, ICE_RATE, LEVEL = 0, 8, 16, 17, 18, 19

f32 = jnp.float32
bf16 = jnp.bfloat16


def lanes():
    return lax.broadcasted_iota(jnp.int32, (8, 128), 1)


def roll(x, shift):
    shift = shift % 128
    return pltpu.roll(x, shift, 1) if shift else x


def is_even(axis):
    return lax.axis_index(axis) % 2 == 0


def place_field(wide, values, static, field):
    group = lax.broadcasted_iota(jnp.int32, (16, 128), 1) // 16
    row = lax.broadcasted_iota(jnp.int32, (16, 128), 0) % 8
    wide[:, :16] = values
    moved = pltpu.roll(wide[...], 0, 1, stride=16, stride_axis=0)
    kept = jnp.where(group == row, moved, 0.0)
    for half in range(2):
        static[half, field : field + 1, :] = jnp.sum(kept[8 * half : 8 * half + 8], axis=0, keepdims=True)


def fetch(sources, landed, sems):
    copies = [pltpu.make_async_copy(src, dst, sems.at[i]) for i, (src, dst) in enumerate(zip(sources, landed))]
    for copy in copies:
        copy.start()
    return copies


def pack_kernel(*refs):
    sources, own, landed = refs[:4], refs[4], refs[5:9]
    flat0, flat1, wide, static, sems = refs[9:]
    copies = fetch(sources, landed, sems)
    wide[...] = jnp.zeros_like(wide)
    static[...] = jnp.zeros_like(static)
    for copy in copies[1:]:
        copy.wait()
    spec, sea, depth, slope = landed
    place_field(wide, sea[...].astype(f32), static, SEA)
    place_field(wide, depth[...].astype(f32), static, DEPTH)
    place_field(wide, slope[0], static, SLOPE_X)
    place_field(wide, slope[1], static, SLOPE_Y)
    own[:, STATIC] = static[...]
    copies[0].wait()
    grid = spec[...].reshape(256, NDIR * FREQ)
    for low, high in ((0, 128), (128, 256), (256, 288)):
        turned = grid[:, low:high].T
        flat0[low:high, :] = turned[:, :128]
        flat1[low:high, :] = turned[:, 128:]
    sea0 = static[0, SEA : SEA + 1, :]
    sea1 = static[1, SEA : SEA + 1, :]
    for d in range(NDIR):
        own[0, d] = flat0[pl.ds(d, FREQ, stride=NDIR), :] * sea0
        own[1, d] = flat1[pl.ds(d, FREQ, stride=NDIR), :] * sea1


NEEDS = (7, 7, 6, 6, 5, 5, 4, 4, 4, 4, 4, 4, 5, 5, 6, 6, 7, 7)
PACKED = {
    0: [(12, 3, 7, 1)],
    1: [(12, 4, 7, 1)],
    2: [(15, 0, 6, 2)],
    3: [(15, 2, 6, 2)],
    4: [(12, 0, 5, 3)],
    5: [(13, 0, 5, 3)],
    6: [(9, 0, 4, 4)],
    7: [(10, 0, 4, 4)],
    8: [(11, 0, 4, 4)],
    14: [(15, 4, 6, 2)],
    16: [(13, 3, 7, 1)],
    17: [(13, 4, 7, 1)],
}
TO_WEST, TO_EAST, TO_NORTH, TO_SOUTH = 27, 9, 18, 0
SENT = 18 + 1 + len(PACKED)


def downstream(first):
    return [(first + i) % NDIR for i in range(18)]


def whole(first):
    return [d for d in range(NDIR) if d not in downstream(first)] + [STATIC]


def write_message(message, get, rising, rising_first, falling_first, place, unit):
    for i, pair in enumerate(zip(whole(rising_first), whole(falling_first))):
        message[i] = get(*pair)
    up, down = downstream(rising_first), downstream(falling_first)
    cell = jnp.where(rising, place, 7 - place)
    for i, (main, pieces) in enumerate(PACKED.items()):
        value = get(up[main], down[main])
        for other, start, to, count in pieces:
            shift = (to - start) * unit
            moved = pltpu.roll(get(up[other], down[other]), jnp.where(rising, shift, 128 - shift), 1)
            value = jnp.where((cell >= to) & (cell < to + count), moved, value)
        message[19 + i] = value


def read_message(message, out, rising, first, place, unit):
    for i, d in enumerate(whole(first)):
        out[d] = message(i)
    dirs = downstream(first)
    cell = place if rising else 7 - place
    parts = {}
    for i, (main, pieces) in enumerate(PACKED.items()):
        value = message(19 + i)
        out[dirs[main]] = value
        for other, start, to, count in pieces:
            shift = (start - to) * unit
            moved = roll(value, shift if rising else -shift)
            if other in parts:
                moved = jnp.where((cell >= start) & (cell < start + count), moved, parts[other])
            parts[other] = moved
    for other, value in parts.items():
        out[dirs[other]] = value


def column_kernel(second, own, message):
    inner = lanes() % 16
    to_east = is_even("lon") != second
    from_own0 = (inner >= 8) == to_east
    shift = jnp.where(to_east, 120, 8)

    def get(west, east):
        slab = west if west == east else jnp.where(to_east, east, west)
        return jnp.where(from_own0, own[0, slab], pltpu.roll(own[1, slab], shift, 1))

    write_message(message, get, ~to_east, TO_WEST, TO_EAST, inner % 8, 1)


def edge_kernel(second, own, message):
    to_north = is_even("lat") != second

    def get(south, north):
        return jnp.where(to_north, own[1, north], own[0, south])

    write_message(message, get, ~to_north, TO_SOUTH, TO_NORTH, lanes() // 16, 16)


def growth_kernel(own, local, consts, gain):
    for half in range(2):
        point = local[half]
        turn = point[WDIR : WDIR + 1]
        cos_w = jnp.cos(turn)
        sin_w = jnp.sin(turn)
        force = wind_gain * point[WIND : WIND + 1] * consts[LEVEL]
        share = own[half, STATIC, SEA : SEA + 1]
        for d in range(NDIR):
            along = jnp.maximum(COS[d] * cos_w + SIN[d] * sin_w, 0.0)
            gain[d, half] = jnp.exp(force * along) * share


def tables_kernel(*refs):
    sources, (place, rims, shifts, gather, local, consts), landed = refs[:6], refs[6:12], refs[12:18]
    wide, sems = refs[18:]
    speed_table, refraction_table, ice_rate, ice, wspeed, wdir = landed
    copies = fetch(sources, landed, sems)
    first = lax.axis_index("band") * FREQ
    sub = lax.broadcasted_iota(jnp.int32, (8, 128), 0)
    mine = lanes() == first + sub

    def column(row):
        picked = jnp.where(mine, jnp.broadcast_to(row, (8, 128)), 0.0)
        return jnp.broadcast_to(jnp.sum(picked, axis=1, keepdims=True), (8, 128))

    def widen(values):
        return jnp.concatenate([values, jnp.zeros((values.shape[0], 112), f32)], axis=1)

    consts[LEVEL] = jnp.exp(math.log(freq_ratio) * (first + sub).astype(f32))
    lat = lax.axis_index("lat")
    lats = lax.axis_size("lat")
    group = lanes() // 32
    rows = lat * ROWS - HALO + 8 * group + sub
    latitude = (south_edge + band_span * (rows.astype(f32) + 0.5) / (ROWS * lats)) * (math.pi / 180.0)
    consts[STRETCH] = 1.0 / jnp.cos(latitude)
    ghost = ((group == 0) & (lat == 0)) | ((group == 3) & (lat == lats - 1))
    consts[LIVE] = jnp.where(ghost, 0.0, 1.0)
    chunk = lax.broadcasted_iota(jnp.int32, (16, 128), 0)
    lane = lax.broadcasted_iota(jnp.int32, (16, 128), 1)
    low = chunk < 8
    targets = [
        40 + chunk,
        72 + chunk,
        jnp.where(low, 64 + chunk, 24 + chunk),
        jnp.where(low, 56 + chunk, 80 + chunk),
        8 + chunk,
        104 + chunk,
    ]
    corners = [jnp.where(low, chunk, 16 + chunk), jnp.where(low, 120 + chunk, 88 + chunk)]
    for matrix, lists in ((place, targets), (rims, corners)):
        matrix[...] = jnp.zeros_like(matrix)
        for s, target in enumerate(lists):
            stripe = (lane == target).astype(f32).astype(bf16)
            for part in range(2):
                for t in range(8):
                    row = part * 128 * len(lists) + s * 128 + 16 * t
                    matrix[row : row + 16, 128 * t : 128 * t + 128] = stripe
    row = lax.broadcasted_iota(jnp.int32, (128, 128), 0)
    col = lax.broadcasted_iota(jnp.int32, (128, 128), 1)
    for sign, taps in ((0, FORTH_TAPS), (1, BACK_TAPS)):
        for i, tap in enumerate(taps):
            moved = (row == (col + tap) % 128).astype(f32).astype(bf16)
            for part in range(2):
                shifts[sign, 128 * part : 128 * part + 128, 128 * i : 128 * i + 128] = moved
    for t in range(8):
        for half in range(2):
            from_row = 40 + 32 * half + col % 16
            moved = ((col // 16 == t) & (row == from_row)).astype(f32).astype(bf16)
            for part in range(2):
                at = part * 1024 + 128 * t
                gather[at : at + 128, 128 * half : 128 * half + 128] = moved
    local[...] = jnp.zeros_like(local)
    wide[...] = jnp.zeros_like(wide)
    for copy in copies:
        copy.wait()
    for at, table in ((TAB_SPEED, speed_table), (TAB_TURN, refraction_table)):
        padded = widen(table[...])
        for c in range(NCLASS):
            consts[at + c] = column(padded[c : c + 1])
    consts[ICE_RATE] = column(widen(ice_rate[...].reshape(1, 16)))
    place_field(wide, ice[...].astype(f32), local, ICE)
    place_field(wide, wspeed[...], local, WIND)
    place_field(wide, wdir[...], local, WDIR)


def unpack_kernel(cols_first, cols_second, consts, west, east):
    del consts
    even = is_even("lon")
    place = lanes() % 8
    read_message(lambda i: jnp.where(even, cols_second[i], cols_first[i]), west, False, TO_EAST, place, 1)
    read_message(lambda i: jnp.where(even, cols_first[i], cols_second[i]), east, True, TO_WEST, place, 1)


def unpack_rows_kernel(rows_second, rows_first, south, north):
    even = is_even("lat")
    place = lanes() // 16
    read_message(lambda i: jnp.where(even, rows_second[i], rows_first[i]), south, False, TO_NORTH, place, 16)
    read_message(lambda i: jnp.where(even, rows_first[i], rows_second[i]), north, True, TO_SOUTH, place, 16)


def rim_kernel(second, west, east, *refs):
    to_north = is_even("lat") != second
    west_low = (lanes() % 16 < 8) == to_north

    def get(south, north):
        slab = south if south == north else jnp.where(to_north, north, south)
        return jnp.where(west_low, west[slab], east[slab])

    write_message(refs[-1], get, ~to_north, TO_SOUTH, TO_NORTH, lanes() // 16, 16)
    if second:
        refs[-1][SENT] = jnp.zeros((8, 128), f32)


def split(x):
    high = x.astype(bf16)
    return high, (x - high.astype(f32)).astype(bf16)


def fill_parts(lhs, count, s, array):
    x = jnp.concatenate([array.reshape(8 * SLABS, 128), jnp.zeros((8, 128), f32)], axis=0)
    high, low = split(x)
    lhs[:, 128 * s : 128 * s + 128] = high
    lhs[:, 128 * (count + s) : 128 * (count + s) + 128] = low


def place_kernel(own, west, east, south, north, matrix, q, lhs):
    fill_parts(lhs, 6, 0, own[0])
    fill_parts(lhs, 6, 1, own[1])
    fill_parts(lhs, 6, 2, west[...])
    fill_parts(lhs, 6, 3, east[...])
    fill_parts(lhs, 6, 4, south[...])
    fill_parts(lhs, 6, 5, north[...])
    for pair in range(4):
        moved = jnp.dot(lhs[...], matrix[:, 256 * pair : 256 * pair + 256], preferred_element_type=f32)
        for i in range(2):
            q[:, 2 * pair + i] = moved[: 8 * SLABS, 128 * i : 128 * i + 128].reshape(SLABS, 8, 128)


def lookup(point, consts, at):
    depth = jnp.broadcast_to(point[DEPTH : DEPTH + 1], (8, 128))
    value = jnp.zeros((8, 128), f32)
    for c in range(NCLASS):
        value = jnp.where(depth == float(c), consts[at + c], value)
    return value * point[SEA : SEA + 1]


def rims_kernel(partial, rims_second, rims_first, consts, matrix, q, kx, ky, tx, ty, lhs, south, north):
    even_lat = is_even("lat")
    place = lanes() // 16
    read_message(lambda i: jnp.where(even_lat, rims_second[i], rims_first[i]), south, False, TO_NORTH, place, 16)
    read_message(lambda i: jnp.where(even_lat, rims_first[i], rims_second[i]), north, True, TO_SOUTH, place, 16)
    for s, array in ((0, south), (1, north)):
        high, low = split(array[:NDIR].reshape(8 * NDIR, 128))
        lhs[:, 128 * s : 128 * s + 128] = high
        lhs[:, 128 * (2 + s) : 128 * (2 + s) + 128] = low
    lane = lanes()
    south, north = south[STATIC], north[STATIC]
    speed = []
    for t in range(8):
        if t % 2 == 0:
            moved = jnp.dot(lhs[...], matrix[:, 128 * t : 128 * t + 256], preferred_element_type=f32)
            for i in range(2):
                q[:, t + i] = partial[:NDIR, t + i] + moved[:, 128 * i : 128 * i + 128].reshape(NDIR, 8, 128)
        point = partial[STATIC, t]
        for low, array, shift in ((0, south, 0), (24, south, 16), (96, north, 88), (120, north, 120)):
            point = jnp.where((lane >= low) & (lane < low + 8), roll(array, shift - 16 * t), point)
        pace = lookup(point, consts, TAB_SPEED)
        turning = lookup(point, consts, TAB_TURN)
        speed.append(pace)
        tx[t] = turning * point[SLOPE_X : SLOPE_X + 1]
        ty[t] = turning * point[SLOPE_Y : SLOPE_Y + 1]
        stretch = consts[STRETCH, t : t + 1, :]
        kx[0, t] = 0.5 * (pace + roll(pace, -1)) * stretch
        kx[1, t] = 0.5 * (pace + roll(pace, 1)) * stretch
    for t in range(8):
        ahead = speed[t + 1] if t < 7 else roll(speed[0], -32)
        ky[t] = 0.5 * (speed[t] + ahead)


def flux(q, diff, curve, k, u, w):
    return k * (q + u * (diff - w * curve))


def halves(k):
    return 0.5 - 0.5 * k, (1.0 / 3.0) + (1.0 / 3.0) * k


def weights(k):
    u, w = halves(k)
    bend = k * u * w
    return k - k * u + 2.0 * bend, k * u - bend, -bend


FORTH_TAPS = (-1, -2)
BACK_TAPS = (-1, 2)


def lon_dirs(sign, base):
    if base == 0:
        return [[0], [18]][sign]
    if base == 9:
        return [[27], [9]][sign]
    return [[base, 36 - base], [18 - base, 18 + base]][sign]


def lon_products(q, shifts, sign, base):
    x = jnp.concatenate([q[d].reshape(64, 128) for d in lon_dirs(sign, base)], axis=0)
    lhs = jnp.concatenate(split(x), axis=1)
    return jnp.dot(lhs, shifts[sign], preferred_element_type=f32)


def lon_stages(q, taps, shifts, out, order, before):
    ahead = lon_products(q, shifts, *order[0])
    for step, (sign, base) in enumerate(order):
        moved = ahead
        if step + 1 < len(order):
            ahead = lon_products(q, shifts, *order[step + 1])
        before(step)
        for t in range(8):
            tap = [taps[base, sign, i, t] for i in range(4)]
            for i, d in enumerate(lon_dirs(sign, base)):
                cell = q[d, t]
                near = moved[64 * i + 8 * t : 64 * i + 8 * t + 8]
                out[d, t] = (tap[0] * cell + tap[1] * roll(cell, -1)) + (
                    tap[2] * near[:, :128] + tap[3] * near[:, 128:]
                )


def first_lon_kernel(q, kx, shifts, out, taps):
    def prepare(base, tiles):
        for t in tiles:
            a1, b1, c1 = weights(COS[base] * kx[0, t])
            a0, b0, c0 = weights(COS[base] * kx[1, t])
            for sign, tap in enumerate(
                ((1.0 - a1 + b0, -b1, a0 - c1, c0), (1.0 + b1 - a0, a1 - c0, -b0, c1))
            ):
                for i in range(4):
                    taps[base, sign, i, t] = tap[i]

    def before(step):
        if step // 2 < 9:
            prepare(step // 2 + 1, range(4 * (step % 2), 4 * (step % 2) + 4))

    prepare(0, range(8))
    lon_stages(q, taps, shifts, out, [(sign, base) for base in range(10) for sign in range(2)], before)


def lon_kernel(q, taps, shifts, out):
    order = [(sign, base) for sign in range(2) for base in range(10)]
    lon_stages(q, taps, shifts, out, order, lambda step: None)


def lat_kernel(q, ky, consts, out, sums=None):
    live = consts[LIVE]
    totals = [jnp.zeros((8, 128), f32)] * 8

    def put(d, t, value):
        out[d, t] = value
        if sums is not None:
            totals[t] = totals[t] + value

    def forth(d, ks, us, ws):
        tiles = [q[d, t] for t in range(8)]
        diff = [tiles[t + 1] - tiles[t] for t in range(7)]
        diff.append(roll(tiles[0], -32) - tiles[7])
        before = roll(diff[7], 32)
        fluxes = []
        for t in range(8):
            fluxes.append(flux(tiles[t], diff[t], diff[t] - before, ks[t], us[t], ws[t]))
            before = diff[t]
        behind = roll(fluxes[7], 32)
        for t in range(8):
            put(d, t, (tiles[t] - fluxes[t] + behind) * live)
            behind = fluxes[t]

    def back(d, ks, us, ws):
        tiles = [q[d, t] for t in range(8)]
        ahead = tiles[1:] + [roll(tiles[0], -32)]
        diff = [tiles[t] - ahead[t] for t in range(8)]
        after = diff[1:] + [roll(diff[0], -32)]
        fluxes = [flux(ahead[t], diff[t], diff[t] - after[t], ks[t], us[t], ws[t]) for t in range(8)]
        behind = roll(fluxes[7], 32)
        for t in range(8):
            put(d, t, (tiles[t] + fluxes[t] - behind) * live)
            behind = fluxes[t]

    for base in range(10):
        ks = [SIN[base] * ky[t] for t in range(8)]
        us, ws = zip(*[halves(k) for k in ks])
        if base == 0:
            north, south = [0], [18]
        elif base == 9:
            north, south = [9], [27]
        else:
            north, south = [base, 18 - base], [18 + base, 36 - base]
        for d in north:
            forth(d, ks, us, ws)
        for d in south:
            back(d, ks, us, ws)
    if sums is None:
        return
    lane = lanes()
    halves_of = [jnp.zeros((8, 128), f32)] * 2
    for t in range(8):
        moved = roll(totals[t], 16 * t - 40)
        halves_of[0] = jnp.where(lane // 16 == t, moved, halves_of[0])
        halves_of[1] = jnp.where(lane // 16 == (t + 2) % 8, moved, halves_of[1])
    halves_of[1] = roll(halves_of[1], -32)
    sums[...] = jnp.zeros((8, 128), f32)
    for half in range(2):
        sums[half : half + 1, :] = jnp.sum(halves_of[half], axis=0, keepdims=True)
        sums[2 + half : 3 + half, :] = jnp.sum(halves_of[half] * consts[LEVEL], axis=0, keepdims=True)


def turn_around(get, put, x, y):
    def factors(d):
        k = SIN_FACE[d] * x - COS_FACE[d] * y
        return (k, *halves(k))

    def opposite(cell, diff, curve, k, u, w):
        return k * (cell + w * (1.5 * diff - u * curve))

    half_turn = NDIR // 2
    k, u, w = factors(half_turn - 1)
    state = []
    ends = []
    for at in (0, half_turn):
        cell, ahead = get(at), get(at + 1)
        before, last = get((at - 1) % NDIR), get((at - 2) % NDIR)
        diff = ahead - cell
        diff1 = cell - before
        curve = diff - diff1
        curve1 = diff1 - (before - last)
        if at == 0:
            f = opposite(before, diff1, jnp.where(k >= 0.0, curve, curve1), k, u, w)
        else:
            f = flux(before, diff1, jnp.where(k >= 0.0, curve1, curve), k, u, w)
        state.append([cell, ahead, diff, curve])
        ends.append(f)
    f_first, f_second = -ends[0], -ends[1]
    for d in range(half_turn):
        if d < half_turn - 1:
            k, u, w = factors(d)
            positive = k >= 0.0
        for at in (0, half_turn):
            cell, ahead, diff, curve = state[at // half_turn]
            beyond = get((at + d + 2) % NDIR)
            diff_ahead = beyond - ahead
            curve_ahead = diff_ahead - diff
            if at == 0:
                if d < half_turn - 1:
                    f = flux(cell, diff, jnp.where(positive, curve, curve_ahead), k, u, w)
                else:
                    f = ends[1]
                put(d, cell - f + f_first)
                f_first = f
            else:
                if d < half_turn - 1:
                    f = opposite(cell, diff, jnp.where(positive, curve_ahead, curve), k, u, w)
                else:
                    f = ends[0]
                put(at + d, cell + f - f_second)
                f_second = f
            state[at // half_turn] = [ahead, beyond, diff_ahead, curve_ahead]


def turn_kernel(q, tx, ty, out):
    for t in range(8):

        def put(d, value, t=t):
            out[d, t] = value

        turn_around(lambda d, t=t: q[d, t], put, tx[t], ty[t])


def gather_kernel(q, matrix, own, lhs):
    for t in range(8):
        high, low = split(q[:, t].reshape(8 * NDIR, 128))
        lhs[:, 128 * t : 128 * t + 128] = high
        lhs[:, 1024 + 128 * t : 1024 + 128 * t + 128] = low
    moved = jnp.dot(lhs[...], matrix[...], preferred_element_type=f32)
    for half in range(2):
        own[half] = moved[:, 128 * half : 128 * half + 128].reshape(NDIR, 8, 128)


def last_turn_kernel(own, static, gain, consts, early):
    for half in range(2):
        point = static[half, 0]
        turning = lookup(point, consts, TAB_TURN)

        def put(d, value, half=half):
            early[half, d] = value * gain[d, half]

        turn_around(
            lambda d, half=half: own[half, d],
            put,
            turning * point[SLOPE_X : SLOPE_X + 1],
            turning * point[SLOPE_Y : SLOPE_Y + 1],
        )


def finish_kernel(early, local, sums, other, consts, out, flat0, flat1):
    total = sums[...] + other[...]
    level = consts[LEVEL]
    for half, flat in ((0, flat0), (1, flat1)):
        energy = total[half : half + 1]
        moment = total[2 + half : 3 + half]
        mean_level = jnp.maximum(moment, 1.0) / jnp.maximum(energy, 1.0)
        mean = energy / NCOMP
        breaking = break_coef * level * level / mean_level * (mean * mean)
        damping = local[half, ICE : ICE + 1] * consts[ICE_RATE]
        loss = jnp.exp(-breaking - damping)
        for d in range(NDIR):
            flat[pl.ds(d, FREQ, stride=NDIR), :] = early[half, d] * loss
        for low, high in ((0, 128), (128, 256), (256, 288)):
            out[8 * half : 8 * half + 8, :, low:high] = flat[low:high, :].T.reshape(8, 16, high - low)


PARAMS = pltpu.CompilerParams(vmem_limit_bytes=40 * 2**20)


def call(kernel, ins, outs, scratch=(), name=None, space=pltpu.VMEM, dtype=f32, result=pltpu.VMEM):
    types = dtype if isinstance(dtype, list) else [dtype] * len(outs)
    return pl.pallas_call(
        kernel,
        out_shape=[jax.ShapeDtypeStruct(shape, kind) for shape, kind in zip(outs, types)],
        in_specs=[pl.BlockSpec(memory_space=space)] * ins,
        out_specs=[pl.BlockSpec(memory_space=result)] * len(outs),
        scratch_shapes=list(scratch),
        compiler_params=PARAMS,
        name=name,
    )


def swap(array, axis, first, closed=False):
    count = lax.axis_size(axis)
    pairs = []
    for i in range(first, count, 2):
        if i + 1 < count or closed:
            j = (i + 1) % count
            pairs += [(i, j), (j, i)]
    return lax.ppermute(array, axis, pairs)


def per_device(
    spectrum,
    sea_mask,
    ice_mask,
    depth_class,
    speed_table,
    refraction_table,
    depth_slope,
    wind_speed,
    wind_dir,
    ice_rate,
):
    tile = (8, 128)
    block = (8,) + tile
    slabs = (SLABS,) + tile
    sent = (SENT,) + tile
    inputs = [spectrum, sea_mask, depth_class, depth_slope]
    (own,) = call(
        pack_kernel,
        4,
        [(2,) + slabs],
        [pltpu.VMEM(x.shape, x.dtype) for x in inputs]
        + [pltpu.VMEM((NDIR * FREQ, 128), f32)] * 2
        + [pltpu.VMEM((16, 128), f32), pltpu.VMEM((2,) + tile, f32), pltpu.SemaphoreType.DMA((4,))],
        name="pack",
        space=pltpu.HBM,
    )(*[pltpu.with_memory_space_constraint(x, pltpu.HBM) for x in inputs])
    (to_first,) = call(functools.partial(column_kernel, False), 1, [sent], name="column_near")(own)
    cols_first = swap(to_first, "lon", 0, True)
    (to_second,) = call(functools.partial(column_kernel, True), 1, [sent], name="column_far")(own)
    cols_second = swap(to_second, "lon", 1, True)
    (edge_second,) = call(functools.partial(edge_kernel, True), 1, [sent], name="edge_far")(own)
    rows_second = swap(edge_second, "lat", 1)
    (edge_first,) = call(functools.partial(edge_kernel, False), 1, [sent], name="edge_near")(own)
    rows_first = swap(edge_first, "lat", 0)
    inputs = [speed_table, refraction_table, ice_rate, ice_mask, wind_speed, wind_dir]
    place, rims, shifts, gather, local, consts = call(
        tables_kernel,
        6,
        [(1536, 1024), (512, 1024), (2, 256, 256), (2048, 256), (2,) + tile, (20,) + tile],
        [pltpu.VMEM(x.shape, x.dtype) for x in inputs]
        + [pltpu.VMEM((16, 128), f32), pltpu.SemaphoreType.DMA((6,))],
        name="tables",
        space=pltpu.HBM,
        dtype=[bf16] * 4 + [f32] * 2,
    )(*[pltpu.with_memory_space_constraint(x, pltpu.HBM) for x in inputs])
    (gain,) = call(growth_kernel, 3, [(NDIR, 2) + tile], name="growth")(own, local, consts)
    west, east = call(unpack_kernel, 3, [slabs] * 2, name="unpack")(cols_first, cols_second, consts)
    (rim_second,) = call(functools.partial(rim_kernel, True), 2, [(SENT + 1,) + tile], name="rim_far")(west, east)
    rims_second = swap(rim_second, "lat", 1)
    (rim_first,) = call(functools.partial(rim_kernel, False), 5, [sent], name="rim_near")(
        west, east, rows_second, rows_first, rim_second
    )
    rims_first = swap(rim_first, "lat", 0)
    south, north = call(unpack_rows_kernel, 2, [slabs] * 2, name="unpack_rows")(rows_second, rows_first)
    (partial,) = call(
        place_kernel,
        6,
        [(SLABS,) + block],
        [pltpu.VMEM((8 * SLABS + 8, 1536), bf16)],
        name="place",
    )(own, west, east, south, north, place)
    q, kx, ky, tx, ty = call(
        rims_kernel,
        5,
        [(NDIR,) + block, (2,) + block] + [block] * 3,
        [pltpu.VMEM((8 * NDIR, 512), bf16)] + [pltpu.VMEM(slabs, f32)] * 2,
        name="rims",
    )(partial, rims_second, rims_first, consts, rims)
    cells = [(NDIR,) + block]
    for substep in range(ITERS):
        if substep == 0:
            q, taps = call(first_lon_kernel, 3, cells + [(10, 2, 4) + block], name="first_lon")(q, kx, shifts)
        else:
            (q,) = call(lon_kernel, 3, cells, name="lon")(q, taps, shifts)
        if substep == ITERS - 1:
            q, sums = call(lat_kernel, 3, cells + [tile], name="lat_sums")(q, ky, consts)
        else:
            (q,) = call(lat_kernel, 3, cells, name="lat")(q, ky, consts)
            (q,) = call(turn_kernel, 3, cells, name="turn")(q, tx, ty)
    other = swap(sums, "band", 0)
    (last,) = call(
        gather_kernel, 2, [(2, NDIR) + tile], [pltpu.VMEM((8 * NDIR, 2048), bf16)], name="gather"
    )(q, gather)
    static = own[:, STATIC:]
    (early,) = call(last_turn_kernel, 4, [(2, NDIR) + tile], name="last_turn")(last, static, gain, consts)
    (out,) = call(
        finish_kernel, 5, [spectrum.shape], [pltpu.VMEM((NDIR * FREQ, 128), f32)] * 2, name="finish"
    )(early, local, sums, other, consts)
    return out


def solution(mesh):
    return jax.shard_map(
        per_device,
        mesh=mesh,
        in_specs=(
            P("lat", "lon", "band"),
            P("lat", "lon"),
            P("lat", "lon"),
            P("lat", "lon"),
            P(),
            P(),
            P(None, "lat", "lon"),
            P("lat", "lon"),
            P("lat", "lon"),
            P(),
        ),
        out_specs=P("lat", "lon", "band"),
        check_vma=False,
    )
```
